32 devices in a mesh: dp: 8 (over z, y), bal: 4 (over x, core).
Axes of the slice: x: 2, y: 2, z: 4, core: 2. Of those that a mesh axis runs over, the one named last changes fastest.
Arguments:
- tokens: bfloat16 [4, 128, 225, 768], P(None, ('dp', 'bal')), may hold values from -6 to 6
- cotangent: bfloat16 [4, 128, 225, 768], P(None, ('dp', 'bal')), may hold values from -6 to 6
- counts: int32 [4, 128], P(None, ('dp', 'bal')), may hold values from 56 to 225, as said below
- rows: int32 [4, 128, 225], P(None, ('dp', 'bal')), may hold values from 0 to 14, as said below
- cols: int32 [4, 128, 225], P(None, ('dp', 'bal')), may hold values from 0 to 14, as said below
- present: int32 [4, 128], P(None, ('dp', 'bal')), may hold values 0 or 1
- slots: int32 [4, 128], P(None, ('dp', 'bal')), may hold values from 0 to 15, as said below
- first_gain: float32 [768], replicated, may hold values from 0.25 to 1.75
- first_shift: float32 [768], replicated, may hold values from -1.75 to 1.75
- qkv_weight: bfloat16 [768, 2304], replicated, may hold values from -0.21875 to 0.21875
- query_bias: float32 [768], replicated, may hold values from -1.75 to 1.75
- value_bias: float32 [768], replicated, may hold values from -1.75 to 1.75
- out_weight: bfloat16 [768, 768], replicated, may hold values from -0.625 to 0.625
- out_bias: float32 [768], replicated, may hold values from -1.75 to 1.75
- second_gain: float32 [768], replicated, may hold values from 0.25 to 1.75
- second_shift: float32 [768], replicated, may hold values from -1.75 to 1.75
- up_weight: bfloat16 [768, 3072], replicated, may hold values from -0.21875 to 0.21875
- up_bias: float32 [3072], replicated, may hold values from -1.75 to 1.75
- down_weight: bfloat16 [3072, 768], replicated, may hold values from -0.109375 to 0.109375
- down_bias: float32 [768], replicated, may hold values from -1.75 to 1.75
Outputs:
- block_output: bfloat16 [4, 128, 225, 768], P(None, ('dp', 'bal'))
- tokens_grad: float32 [4, 128, 225, 768], P(None, ('dp', 'bal'))
- first_gain_grad: float32 [768], replicated
- first_shift_grad: float32 [768], replicated
- qkv_weight_grad: float32 [768, 2304], P('dp')
- query_bias_grad: float32 [768], replicated
- value_bias_grad: float32 [768], replicated
- out_weight_grad: float32 [768, 768], P('dp')
- out_bias_grad: float32 [768], replicated
- second_gain_grad: float32 [768], replicated
- second_shift_grad: float32 [768], replicated
- up_weight_grad: float32 [768, 3072], P('dp')
- up_bias_grad: float32 [3072], replicated
- down_weight_grad: float32 [3072, 768], P('dp')
- down_bias_grad: float32 [768], replicated
The draws below stay inside these ranges and needn't reach their ends.
Inputs may be any that keep to these rules, and one draw needn't show every extreme that they name: `counts`: every image has at least 56 visible patches; in every draw some image has all 225. In each image the pairs (rows, cols) over the 225 slots are the cells of a 15 x 15 grid, each once. `cols`: paired with rows as stated there. Within each aligned block of 16 images of a micro-batch the slots are a permutation of 0 to 15. Split such a block into runs of 4 images in order. For every pair of runs a and b, exactly one image of run a has a slot in [b * 4, (b + 1) * 4).
All inputs are finite; a program needn't handle non-finite values. No bound on the sum of `present` on one device may be relied on, other than what follows from the above.
Results may differ from the reference program's by a relative error of at most 0.014.
Values may be sent and summed in bfloat16 or wider, within the bound.
A program may use at most 512 MiB of HBM per device.

```python
import math
import jax
import jax.numpy as jnp
from jax import lax

D = 768
HEADS = 12
HEAD_DIM = 64
FF = 3072
GRID = 15
MB = 4
IMG = 4
S = 225
GROUP = 16
IMAGES = 128


def draw_counts(key, part):
    picks = jax.random.randint(jax.random.fold_in(key, 11), (MB, IMAGES), S // 4, S + 1)
    chosen_spot = jax.random.randint(jax.random.fold_in(key, 12), (), 0, MB * IMAGES)
    ordinal = jnp.arange(MB * IMAGES, dtype=jnp.int32).reshape(MB, IMAGES)
    return jnp.where(ordinal == chosen_spot, S, picks).astype(jnp.int32)


def grid_cells(key):
    noise = jax.random.randint(jax.random.fold_in(key, 21), (MB, IMAGES, S), 0, 1 << 20)
    ranked = noise * S + jnp.arange(S, dtype=jnp.int32)
    return jnp.argsort(ranked, axis=-1).astype(jnp.int32)


def draw_rows(key, part):
    return (grid_cells(key) // GRID).astype(jnp.int32)


def draw_cols(key, part):
    return (grid_cells(key) % GRID).astype(jnp.int32)


def draw_slots(key, part):
    blocks = MB * IMAGES // GROUP
    peers = GROUP // IMG
    per_peer = IMG // peers
    first_noise = jax.random.randint(jax.random.fold_in(key, 31), (blocks, peers, IMG), 0, 1 << 20)
    dealt = jnp.argsort(first_noise * IMG + jnp.arange(IMG, dtype=jnp.int32), axis=-1).astype(jnp.int32)
    target_peer = dealt % peers
    within = dealt // peers
    source_peer = jnp.arange(peers, dtype=jnp.int32)[None, :, None]
    arrival = source_peer * per_peer + within
    second_noise = jax.random.randint(jax.random.fold_in(key, 32), (blocks, peers, IMG), 0, 1 << 20)
    placing = jnp.argsort(second_noise * IMG + jnp.arange(IMG, dtype=jnp.int32), axis=-1).astype(jnp.int32)
    flat_placing = placing.reshape(blocks, peers * IMG)
    lookup = (target_peer * IMG + arrival).reshape(blocks, peers * IMG)
    local_place = jnp.take_along_axis(flat_placing, lookup, axis=1).reshape(blocks, peers, IMG)
    return (target_peer * IMG + local_place).astype(jnp.int32).reshape(MB, IMAGES)


def set_ends(drawn, own_key, low, top_value):
    longest = drawn.shape.index(max(drawn.shape))
    spots = []
    for shift in (0, 1):
        where = [jax.random.randint(jax.random.fold_in(own_key, axis), (), 0, length) for axis, length in enumerate(drawn.shape)]
        where[longest] = (where[longest] + shift) % drawn.shape[longest]
        spots.append(tuple(where))
    return drawn.at[spots[0]].set(low).at[spots[1]].set(top_value)


def block_levels(own_key, dims, cuts, smallest, high):
    def one(position, parts):
        heights = jax.random.uniform(jax.random.fold_in(jax.random.fold_in(own_key, 6), position), (parts,), jnp.float32, smallest / len(cuts), high / len(cuts))
        return jnp.repeat(jnp.exp(heights), dims[position] // parts).reshape((-1,) + (1,) * (len(dims) - position - 1))

    factor_of = one(*cuts[0])
    for cut in cuts[1:]:
        factor_of = factor_of * one(*cut)
    return factor_of


def normal_values(stream_key, extent, width, most, cuts=(), kind=jnp.bfloat16):
    loudness = block_levels(stream_key, extent, cuts, -0.22, 0.18) if cuts else 1.0
    values = jax.random.normal(stream_key, extent, jnp.float32) * width * loudness
    return jnp.minimum(jnp.maximum(values, -most), most).astype(kind)


def setup_inputs(seed: int = 0) -> dict:
    key_list = jax.random.split(jax.random.key(seed), 21)
    tokens = normal_values(key_list[0], (MB, IMAGES, S, D), 1.0, 6.0, ((1, 32),))
    cotangent = normal_values(key_list[1], (MB, IMAGES, S, D), 1.0, 6.0, ((1, 32),))
    counts = draw_counts(jax.random.fold_in(key_list[20], 71), 0)
    rows = draw_rows(jax.random.fold_in(key_list[20], 71), 0)
    cols = draw_cols(jax.random.fold_in(key_list[20], 71), 0)
    present = set_ends((jax.random.randint(key_list[5], (MB, IMAGES), 0, 4) < 3).astype(jnp.int32), jax.random.fold_in(key_list[5], 1), 0, 1)
    slots = draw_slots(jax.random.fold_in(key_list[20], 71), 0)
    first_gain = jnp.clip(1.0 + 0.15 * jax.random.normal(key_list[7], (D,), jnp.float32), 0.25, 1.75)
    first_shift = normal_values(key_list[8], (D,), 0.3, 1.75, (), jnp.float32)
    qkv_weight = normal_values(key_list[9], (D, 3 * D), D ** -0.5, 0.21875)
    query_bias = normal_values(key_list[10], (D,), 0.3, 1.75, (), jnp.float32)
    value_bias = normal_values(key_list[11], (D,), 0.3, 1.75, (), jnp.float32)
    out_weight = normal_values(key_list[12], (D, D), (D // 8) ** -0.5, 0.625)
    out_bias = normal_values(key_list[13], (D,), 0.3, 1.75, (), jnp.float32)
    second_gain = jnp.clip(1.0 + 0.15 * jax.random.normal(key_list[14], (D,), jnp.float32), 0.25, 1.75)
    second_shift = normal_values(key_list[15], (D,), 0.3, 1.75, (), jnp.float32)
    up_weight = normal_values(key_list[16], (D, FF), D ** -0.5, 0.21875)
    up_bias = normal_values(key_list[17], (FF,), 0.3, 1.75, (), jnp.float32)
    down_weight = normal_values(key_list[18], (FF, D), FF ** -0.5, 0.109375)
    down_bias = normal_values(key_list[19], (D,), 0.3, 1.75, (), jnp.float32)
    return dict(tokens=tokens, cotangent=cotangent, counts=counts, rows=rows, cols=cols, present=present, slots=slots, first_gain=first_gain, first_shift=first_shift, qkv_weight=qkv_weight, query_bias=query_bias, value_bias=value_bias, out_weight=out_weight, out_bias=out_bias, second_gain=second_gain, second_shift=second_shift, up_weight=up_weight, up_bias=up_bias, down_weight=down_weight, down_bias=down_bias)


exact_precision = lax.Precision.HIGHEST
norm_eps = 1e-06
masked_score = -1000000000.0

@jax.custom_vjp
def low(v):
    return lax.optimization_barrier(v.astype(jnp.bfloat16)).astype(jnp.float32)

@jax.custom_vjp
def low_back(v):
    return v

def low_keep(v):
    return (low(v), None)

def low_pass(kept, grad):
    return (grad,)

def back_keep(v):
    return (v, None)

def back_low(kept, grad):
    return (low(grad),)
low.defvjp(low_keep, low_pass)
low_back.defvjp(back_keep, back_low)

def normalize(values, norm_gain, norm_shift):
    average = lax.optimization_barrier(jnp.mean(values, axis=-1, keepdims=True))
    centred = values - average
    spread = lax.optimization_barrier(jnp.mean(centred * centred, axis=-1, keepdims=True))
    return centred * lax.rsqrt(spread + norm_eps) * norm_gain + norm_shift

def alibi_term(row_pos, col_pos, heads):
    row_f = row_pos.astype(jnp.float32)
    col_f = col_pos.astype(jnp.float32)
    row_gap = row_f[:, :, None] - row_f[:, None, :]
    col_gap = col_f[:, :, None] - col_f[:, None, :]
    distance = jnp.sqrt(row_gap * row_gap + col_gap * col_gap)
    slopes = jnp.exp2(-8.0 * (jnp.arange(heads, dtype=jnp.float32) + 1.0) / heads)
    return -slopes[None, :, None, None] * distance[:, None, :, :]

def project(values, matrix):
    return jnp.einsum('bsd,de->bse', values, matrix, precision=exact_precision)

def layer(params, inputs, alibi, visible):
    first_gain, first_shift, qkv_weight, query_bias, value_bias, out_weight, out_bias, second_gain, second_shift, up_weight, up_bias, down_weight, down_bias = params
    count = inputs.shape[0]
    hidden_one = low(normalize(inputs, first_gain, first_shift))
    shift_all = jnp.concatenate([query_bias, jnp.zeros_like(query_bias), value_bias])
    projected = low(low_back(project(hidden_one, qkv_weight) + shift_all))
    split = projected.reshape(count, S, 3, HEADS, HEAD_DIM)
    query_heads = split[:, :, 0]
    key_heads = split[:, :, 1]
    value_heads = split[:, :, 2]
    scale = 1.0 / math.sqrt(HEAD_DIM)
    raw = low_back(scale * jnp.einsum('bqhd,bkhd->bhqk', query_heads, key_heads, precision=exact_precision))
    scores = jnp.where(visible[:, None, None, :] > 0, raw + alibi, masked_score)
    row_max = lax.optimization_barrier(jnp.max(scores, axis=-1, keepdims=True))
    exp_terms = jnp.exp(scores - row_max)
    probs = exp_terms / lax.optimization_barrier(jnp.sum(exp_terms, axis=-1, keepdims=True))
    heads_out = jnp.einsum('bhqk,bkhd->bqhd', low(probs), value_heads, precision=exact_precision)
    attended = low(low_back(heads_out.reshape(count, S, D)))
    branch = low_back(project(attended, out_weight) + out_bias)
    middle = inputs + branch
    hidden_two = low(normalize(middle, second_gain, second_shift))
    pre_act = low_back(project(hidden_two, up_weight) + up_bias)
    act_low = low(jax.nn.gelu(pre_act, approximate=False))
    mlp_out = low_back(project(act_low, down_weight) + down_bias)
    return (middle + mlp_out) * visible[:, :, None]

def reference(tokens, cotangent, counts, rows, cols, present, slots, first_gain, first_shift, qkv_weight, query_bias, value_bias, out_weight, out_bias, second_gain, second_shift, up_weight, up_bias, down_weight, down_bias):
    params = tuple((member.astype(jnp.float32) for member in (first_gain, first_shift, qkv_weight, query_bias, value_bias, out_weight, out_bias, second_gain, second_shift, up_weight, up_bias, down_weight, down_bias)))
    total_images = MB * IMAGES
    flat_tokens = tokens.reshape(total_images, S, D).astype(jnp.float32)
    flat_slots = slots.reshape(total_images).astype(jnp.int32)
    ordinal = jnp.arange(total_images, dtype=jnp.int32)
    destination = ordinal // GROUP * GROUP + flat_slots
    flags = present.reshape(total_images).astype(jnp.float32)
    flat_cot = cotangent.reshape(total_images, S, D).astype(jnp.float32)[destination] * flags[:, None, None]
    visible = (jnp.arange(S, dtype=jnp.int32)[None, :] < counts.reshape(total_images, 1).astype(jnp.int32)).astype(jnp.float32)
    blocks = total_images // GROUP

    def in_blocks(array):
        return array.reshape((blocks, GROUP) + array.shape[1:])
    inputs = (in_blocks(flat_tokens), in_blocks(flat_cot), in_blocks(visible), in_blocks(rows.reshape(total_images, S)), in_blocks(cols.reshape(total_images, S)))
    initial = tuple((jnp.zeros_like(member) for member in params))

    def advance(running, pieces):
        block_tokens, block_cot, block_visible, block_rows, block_cols = pieces
        alibi = alibi_term(block_rows, block_cols, HEADS)

        def apply_layer(weights, values):
            return layer(weights, values, alibi, block_visible)
        result, pullback = jax.vjp(apply_layer, params, block_tokens)
        param_grads, input_grad = pullback(block_cot)
        return (tuple((acc + new for acc, new in zip(running, param_grads))), (result, input_grad))
    grads, (results, input_grads) = lax.scan(advance, initial, inputs)
    results = results.reshape(total_images, S, D)
    placed = jnp.zeros((total_images, S, D), jnp.float32).at[destination].set(results)
    block_output = placed.astype(jnp.bfloat16).reshape(MB, IMAGES, S, D)
    tokens_grad = input_grads.reshape(MB, IMAGES, S, D)
    return (block_output, tokens_grad, grads[0], grads[1], grads[2], grads[3], grads[4], grads[5], grads[6], grads[7], grads[8], grads[9], grads[10], grads[11], grads[12])
```

```python
import functools
import math

import jax
import jax.numpy as jnp
from jax import lax
from jax.experimental import pallas as pl
from jax.experimental.pallas import tpu as pltpu
from jax.sharding import PartitionSpec as P

HEADS = 12
TILE = 256
WINDOW = 256
FAR = 1e12
EPS = 1e-06
VMEM_LIMIT = 60 * 1024 * 1024

F32 = jnp.float32
BF16 = jnp.bfloat16

OFF, CNT, IMG, LIVE, PEER, MISC = 0, 16, 32, 48, 64, 80
N_FWD, N_BWD, ROWS_FWD, ROWS_BWD, N_LIVE = MISC, MISC + 1, MISC + 2, MISC + 3, MISC + 4


def dot(a, b):
    return jnp.dot(a, b, preferred_element_type=F32)


def dot_bt(a, b):
    return lax.dot_general(a, b, (((1,), (1,)), ((), ())), preferred_element_type=F32)


def turned(block):
    size = 256 if block.shape[1] % 256 == 0 else 128
    row = lax.broadcasted_iota(jnp.int32, (size, size), 0)
    col = lax.broadcasted_iota(jnp.int32, (size, size), 1)
    eye = jnp.where(row == col, 1.0, 0.0).astype(BF16)
    parts = [
        dot_bt(eye, block[:, start : start + size]).astype(BF16)
        for start in range(0, block.shape[1], size)
    ]
    return parts[0] if len(parts) == 1 else jnp.concatenate(parts, axis=0)


def layer_norm(values):
    average = jnp.mean(values, axis=-1, keepdims=True)
    centred = values - average
    spread = jnp.mean(centred * centred, axis=-1, keepdims=True)
    inverse = lax.rsqrt(spread + EPS)
    return centred * inverse, inverse


def norm_back(out_grad, gain, unit, inverse):
    e = out_grad * gain
    mean_e = jnp.mean(e, axis=-1, keepdims=True)
    mean_eu = jnp.mean(e * unit, axis=-1, keepdims=True)
    return inverse * (e - mean_e - unit * mean_eu)


def gelu_parts(u):
    size = jnp.abs(u)
    t = 1.0 / (1.0 + (0.3275911 * math.sqrt(0.5)) * size)
    bell = jnp.exp(-0.5 * (u * u))
    poly = t * (
        0.5 * 0.254829592
        + t
        * (
            0.5 * -0.284496736
            + t * (0.5 * 1.421413741 + t * (0.5 * -1.453152027 + t * (0.5 * 1.061405429)))
        )
    )
    tail = poly * bell
    phi_sum = jnp.where(u >= 0, 1.0 - tail, tail)
    return phi_sum, u * bell * (1.0 / math.sqrt(2.0 * math.pi))


def row_ids(start, rows):
    return start + lax.broadcasted_iota(jnp.int32, (rows, 1), 0)


def aligned(value, step=16):
    return pl.multiple_of(value, step)


def by_count(count, run):
    @pl.when(count <= 128)
    def _():
        run(128, 128)

    @pl.when(jnp.logical_and(count > 128, count <= 192))
    def _():
        run(192, 256)

    @pl.when(count > 192)
    def _():
        run(256, 256)


def distances(spot_rows, spot_cols, count, keys, queries):
    down = spot_cols[:keys, 0:1] - spot_rows[0:1, :queries]
    across = spot_cols[:keys, 1:2] - spot_rows[1:2, :queries]
    far = row_ids(0, keys) >= count
    return jnp.where(far, FAR, jnp.sqrt(down * down + across * across))


def attend_kernel(
    meta, slopes, tokens, spot_rows, spot_cols, gain, shift, weight, bias,
    packed_out, qkv_out, att_out, total_out,
    packed, qkv, att, gaps, sem_packed, sem_qkv, sem_att,
):
    step = pl.program_id(0)
    images = pl.num_programs(0) // 2
    length, width = tokens.shape[1], tokens.shape[2]

    def tile_copy(which, t):
        src, dst, sem = (
            (packed, packed_out, sem_packed),
            (qkv, qkv_out, sem_qkv),
            (att, att_out, sem_att),
        )[which]
        rows = pl.ds(aligned(t * TILE, TILE), TILE)
        return pltpu.make_async_copy(src.at[rows], dst.at[rows], sem.at[t])

    @pl.when(step == 0)
    def _():
        packed[...] = jnp.zeros_like(packed)

    @pl.when(step < images)
    def _():
        off = aligned(meta[OFF + step])
        packed[pl.ds(off, length), :] = tokens[0]
        begin = off // TILE
        after = aligned(meta[OFF + jnp.minimum(step + 1, images - 1)])
        end = jnp.where(step == images - 1, meta[N_FWD], after // TILE)

        def project(t, carry):
            rows = pl.ds(aligned(t * TILE, TILE), TILE)
            unit, _ = layer_norm(packed[rows, :].astype(F32))
            hidden = (unit * gain[...] + shift[...]).astype(BF16)
            for part in range(3):
                cols = slice(part * width, (part + 1) * width)
                qkv[rows, cols] = (dot(hidden, weight[:, cols]) + bias[:, cols]).astype(BF16)
            tile_copy(0, t).start()
            tile_copy(1, t).start()
            return carry

        lax.fori_loop(begin, end, project, 0)

    @pl.when(step >= images)
    def _():
        spot = step - images
        off = aligned(meta[OFF + spot])
        count = meta[CNT + spot]

        def run(keys, queries):
            gaps[:keys, :queries] = distances(spot_rows[0], spot_cols[0], count, keys, queries)
            key_seen = row_ids(0, keys) < count
            query_seen = row_ids(0, queries) < count
            left = lax.broadcasted_iota(jnp.int32, (queries, 128), 1) < 64

            def pair(p, carry):
                lanes = aligned(p * 128, 128)
                q2 = qkv[pl.ds(off, queries), pl.ds(lanes, 128)] * 0.125
                k2 = qkv[pl.ds(off, keys), pl.ds(width + lanes, 128)]
                v2 = qkv[pl.ds(off, keys), pl.ds(2 * width + lanes, 128)]
                q2 = jnp.where(query_seen, q2, jnp.zeros_like(q2))
                k2 = jnp.where(key_seen, k2, jnp.zeros_like(k2))
                v2 = jnp.where(key_seen, v2, jnp.zeros_like(v2))
                v2t = turned(v2)
                outs = []
                for half in range(2):
                    head = 2 * p + half
                    mine = left if half == 0 else jnp.logical_not(left)
                    qh = jnp.where(mine, q2, jnp.zeros_like(q2))
                    scores = dot_bt(k2, qh) - slopes[head] * gaps[:keys, :queries]
                    top = jnp.max(scores, axis=0, keepdims=True)
                    terms = jnp.exp(scores - top)
                    total = jnp.sum(terms, axis=0, keepdims=True)
                    heads_out = dot(v2t[half * 64 : half * 64 + 64], terms.astype(BF16))
                    outs.append((heads_out * (1.0 / total)).astype(BF16))
                    total_out[0, p, half : half + 1, :queries] = top + jnp.log(total)
                both = jnp.concatenate(outs, axis=0)
                att[pl.ds(off, queries), pl.ds(lanes, 128)] = turned_back(both)
                return carry

            lax.fori_loop(0, HEADS // 2, pair, 0)

        by_count(count, run)
        after = meta[OFF + jnp.minimum(spot + 1, images - 1)]
        end = jnp.where(spot == images - 1, meta[N_FWD], after // TILE)

        def send(t, carry):
            tile_copy(2, t).start()
            return carry

        lax.fori_loop(off // TILE, end, send, 0)

    @pl.when(step == 2 * images - 1)
    def _():
        def finish(t, carry):
            for which in range(3):
                tile_copy(which, t).wait()
            return carry

        lax.fori_loop(0, meta[N_FWD], finish, 0)


def turned_back(block):
    size = block.shape[1]
    parts = []
    for start in range(0, size, 128):
        row = lax.broadcasted_iota(jnp.int32, (128, size), 0)
        col = lax.broadcasted_iota(jnp.int32, (128, size), 1)
        eye = jnp.where(row + start == col, 1.0, 0.0).astype(BF16)
        parts.append(dot_bt(eye, block).astype(BF16))
    return parts[0] if len(parts) == 1 else jnp.concatenate(parts, axis=0)


def mlp_kernel(
    chunk, meta, cot_in, att_in, tokens_in,
    out_w, out_b, gain, shift, up_w, up_b, down_w, down_b,
    y_send, mid_grad, att_grad, up_g, down_g, out_g, vec_g, upb_g,
    cot, y_all, up_acc, down_acc, out_acc, h2_s, h2t_s, dzt_s, z_s, g_s, stage, sem,
):
    step = pl.program_id(0)
    images = 16
    tiles = pl.num_programs(0) - 2 * images
    length, width = cot_in.shape[1], cot_in.shape[2]
    hidden = up_w.shape[1]

    @pl.when(step == 0)
    def _():
        up_acc[...] = jnp.zeros_like(up_acc)
        down_acc[...] = jnp.zeros_like(down_acc)
        out_acc[...] = jnp.zeros_like(out_acc)
        vec_g[...] = jnp.zeros_like(vec_g)
        upb_g[...] = jnp.zeros_like(upb_g)

    @pl.when(jnp.logical_and(step < images, step < meta[N_LIVE]))
    def _():
        spot = step
        off = aligned(meta[OFF + spot])
        seen = row_ids(0, length) < meta[CNT + spot]
        block = cot_in[0]
        edge = length // 16 * 16
        cot[pl.ds(aligned(off + edge), 16), :] = jnp.zeros((16, width), BF16)
        cot[pl.ds(off, length), :] = jnp.where(seen, block, jnp.zeros_like(block))

    def run_tile(t, both):
        rows = aligned(t * TILE, TILE)
        ids = row_ids(rows, TILE)
        att = att_in[...]
        att = jnp.where(ids < meta[ROWS_FWD], att, jnp.zeros_like(att))
        mid = tokens_in[...].astype(F32) + (dot(att, out_w[...]) + out_b[...])
        unit, inverse = layer_norm(mid)
        h2 = (unit * gain[...] + shift[...]).astype(BF16)
        h2_s[...] = h2
        z_s[...] = mid + down_b[...]
        if both:
            dz = cot[pl.ds(rows, TILE), :]
            dz = jnp.where(ids < meta[ROWS_BWD], dz, jnp.zeros_like(dz))
            h2t_s[...] = turned(h2)
            dzt_s[...] = turned(dz)
            g_s[...] = jnp.zeros_like(g_s)

        def part(c, carry):
            cols = pl.ds(aligned(c * chunk, chunk), chunk)
            pre = dot(h2_s[...], up_w[:, cols]) + up_b[:, cols]
            share, slope = gelu_parts(pre)
            act = (pre * share).astype(BF16)
            z_s[...] += dot(act, down_w[cols, :])
            if both:
                pre_g = (dot_bt(dz, down_w[cols, :]) * (share + slope)).astype(BF16)
                up_acc[:, cols] += dot(h2t_s[...], pre_g)
                down_acc[:, cols] += dot(dzt_s[...], act)
                upb_g[0:1, cols] += jnp.sum(pre_g.astype(F32), axis=0, keepdims=True)
                g_s[...] += dot_bt(pre_g, up_w[:, cols])
            return carry

        lax.fori_loop(0, hidden // chunk, part, 0)
        y_all[pl.ds(rows, TILE), :] = z_s[...].astype(BF16)
        if both:
            dzf = dz.astype(F32)
            g2 = g_s[...]
            dmid = dzf + norm_back(g2, gain[...], unit, inverse)
            branch = dmid.astype(BF16)
            mid_grad[...] = dmid
            att_grad[...] = dot_bt(branch, out_w[...]).astype(BF16)
            out_acc[...] += dot(turned(att), branch)
            vec_g[0:1, :] += jnp.sum(g2 * unit, axis=0, keepdims=True)
            vec_g[1:2, :] += jnp.sum(g2, axis=0, keepdims=True)
            vec_g[2:3, :] += jnp.sum(branch.astype(F32), axis=0, keepdims=True)
            vec_g[3:4, :] += jnp.sum(dzf, axis=0, keepdims=True)

    tile = step - images

    @pl.when(jnp.logical_and(tile >= 0, tile < meta[N_BWD]))
    def _():
        run_tile(tile, True)

    @pl.when(
        jnp.logical_and(
            jnp.logical_and(tile >= meta[N_BWD], tile >= 0),
            jnp.logical_and(tile < meta[N_FWD], tile < tiles),
        )
    )
    def _():
        run_tile(tile, False)

    @pl.when(step == images + tiles)
    def _():
        size = stage.shape[1]
        jobs = []
        for start in range(0, width, size):
            jobs.append((up_acc, start, up_g, False))
            jobs.append((out_acc, start, out_g, False))
        for start in range(0, hidden, size):
            jobs.append((down_acc, start, down_g, True))

        def copy(n):
            source, start, target, _ = jobs[n]
            columns = target.shape[1]
            return pltpu.make_async_copy(
                stage.at[n % 2, :, pl.ds(0, columns)], target.at[pl.ds(start, size)], sem.at[n % 2]
            )

        for n, (source, start, target, flip) in enumerate(jobs):
            if n >= 2:
                copy(n - 2).wait()
            if flip:
                for low in range(0, width, 256):
                    block = source[pl.ds(low, 256), pl.ds(start, size)].astype(BF16)
                    stage[n % 2, :, pl.ds(low, 256)] = turned(block)
            else:
                columns = target.shape[1]
                stage[n % 2, :, pl.ds(0, columns)] = source[pl.ds(start, size), :].astype(BF16)
            copy(n).start()
        copy(len(jobs) - 2).wait()
        copy(len(jobs) - 1).wait()

    spot = step - images - tiles

    @pl.when(spot >= 0)
    def _():
        off = aligned(meta[OFF + spot])
        seen = row_ids(0, length) < meta[CNT + spot]
        block = y_all[pl.ds(off, length), :]
        y_send[0] = jnp.where(seen, block, jnp.zeros_like(block))


def attend_back_kernel(
    meta, slopes, qkv, att_grad, totals, spot_rows, spot_cols, tokens, gain, shift,
    packed_grad, weight_g, bias_g,
    grads, gaps, acc, stage, sem,
):
    step = pl.program_id(0)
    images = 16
    width = tokens.shape[1]
    length = 225

    @pl.when(step == 0)
    def _():
        acc[...] = jnp.zeros_like(acc)
        bias_g[...] = jnp.zeros_like(bias_g)

    @pl.when(jnp.logical_and(step < images, step < meta[N_LIVE]))
    def _():
        spot = step
        off = aligned(meta[OFF + spot])
        count = meta[CNT + spot]

        def run(keys, queries):
            gaps[:keys, :queries] = distances(spot_rows[0], spot_cols[0], count, keys, queries)
            key_seen = row_ids(0, keys) < count
            query_seen = row_ids(0, queries) < count
            left = lax.broadcasted_iota(jnp.int32, (queries, 128), 1) < 64

            def pair(p, carry):
                lanes = aligned(p * 128, 128)
                q2 = qkv[:queries, pl.ds(lanes, 128)] * 0.125
                k2 = qkv[:keys, pl.ds(width + lanes, 128)]
                v2 = qkv[:keys, pl.ds(2 * width + lanes, 128)]
                o2 = att_grad[:queries, pl.ds(lanes, 128)]
                q2 = jnp.where(query_seen, q2, jnp.zeros_like(q2))
                o2 = jnp.where(query_seen, o2, jnp.zeros_like(o2))
                k2 = jnp.where(key_seen, k2, jnp.zeros_like(k2))
                v2 = jnp.where(key_seen, v2, jnp.zeros_like(v2))
                k2t = turned(k2)
                dq_parts = []
                dk = dv = None
                for half in range(2):
                    head = 2 * p + half
                    mine = left if half == 0 else jnp.logical_not(left)
                    qh = jnp.where(mine, q2, jnp.zeros_like(q2))
                    oh = jnp.where(mine, o2, jnp.zeros_like(o2))
                    scores = dot_bt(k2, qh) - slopes[head] * gaps[:keys, :queries]
                    probs = jnp.exp(scores - totals[0, p, half : half + 1, :queries])
                    prob_g = dot_bt(v2, oh)
                    inner = jnp.sum(probs * prob_g, axis=0, keepdims=True)
                    score_g = (probs * (prob_g - inner)).astype(BF16)
                    dv_part = dot(probs.astype(BF16), oh)
                    dk_part = dot(score_g, qh)
                    dq_parts.append(
                        (dot(k2t[half * 64 : half * 64 + 64], score_g) * 0.125).astype(BF16)
                    )
                    dk = dk_part if dk is None else dk + dk_part
                    dv = dv_part if dv is None else dv + dv_part
                dq = turned_back(jnp.concatenate(dq_parts, axis=0))
                grads[pl.ds(off, queries), pl.ds(lanes, 128)] = dq
                grads[pl.ds(off, keys), pl.ds(width + lanes, 128)] = dk.astype(BF16)
                grads[pl.ds(off, keys), pl.ds(2 * width + lanes, 128)] = dv.astype(BF16)
                return carry

            lax.fori_loop(0, HEADS // 2, pair, 0)

        by_count(count, run)

    tile = step - images

    @pl.when(jnp.logical_and(tile >= 0, tile < meta[N_BWD]))
    def _():
        rows = aligned(tile * TILE, TILE)
        ids = row_ids(rows, TILE)
        unit, _ = layer_norm(tokens[...].astype(F32))
        hidden = (unit * gain[...] + shift[...]).astype(BF16)
        hidden_t = turned(hidden)
        for part in range(3):
            cols = slice(part * width, (part + 1) * width)
            block = grads[pl.ds(rows, TILE), cols]
            block = jnp.where(ids < meta[ROWS_BWD], block, jnp.zeros_like(block))
            packed_grad[:, cols] = block
            acc[:, cols] += dot(hidden_t, block)
            bias_g[0:1, cols] += jnp.sum(block.astype(F32), axis=0, keepdims=True)

    @pl.when(step == pl.num_programs(0) - 1)
    def _():
        size = stage.shape[1]
        count = width // size

        def copy(n):
            return pltpu.make_async_copy(
                stage.at[n % 2], weight_g.at[pl.ds(n * size, size)], sem.at[n % 2]
            )

        for n in range(count):
            if n >= 2:
                copy(n - 2).wait()
            stage[n % 2] = acc[pl.ds(n * size, size), :].astype(BF16)
            copy(n).start()
        copy(count - 2).wait()
        copy(count - 1).wait()


def token_grad_kernel(
    meta, packed_grad, tokens, mid_grad, gain, weight, out, vec_g, held,
):
    step = pl.program_id(0)
    images = 16
    tiles = pl.num_programs(0) - images
    length = out.shape[1]

    @pl.when(step == 0)
    def _():
        vec_g[...] = jnp.zeros_like(vec_g)

    @pl.when(jnp.logical_and(step < tiles, step < meta[N_BWD]))
    def _():
        rows = aligned(step * TILE, TILE)
        unit, inverse = layer_norm(tokens[...].astype(F32))
        g1 = dot_bt(packed_grad[...], weight[...])
        held[pl.ds(rows, TILE), :] = mid_grad[...] + norm_back(g1, gain[...], unit, inverse)
        vec_g[0:1, :] += jnp.sum(g1 * unit, axis=0, keepdims=True)
        vec_g[1:2, :] += jnp.sum(g1, axis=0, keepdims=True)

    @pl.when(step >= tiles)
    def _():
        spot = step - tiles
        off = aligned(meta[OFF + spot])
        limit = meta[CNT + spot] * meta[LIVE + spot]
        block = held[pl.ds(off, length), :]
        out[0] = jnp.where(row_ids(0, length) < limit, block, 0.0)


def move_kernel(table, source, target):
    del table
    target[...] = source[...]


def move_images(source, table):
    count, length, width = source.shape
    return pl.pallas_call(
        move_kernel,
        out_shape=jax.ShapeDtypeStruct(source.shape, source.dtype),
        grid_spec=pltpu.PrefetchScalarGridSpec(
            num_scalar_prefetch=1,
            grid=(count,),
            in_specs=[pl.BlockSpec((1, length, width), lambda s, table: (table[s], 0, 0))],
            out_specs=pl.BlockSpec((1, length, width), lambda s, table: (s, 0, 0)),
        ),
    )(table, source)


def whole(*shape):
    return pl.BlockSpec(shape, lambda *_: (0,) * len(shape), pipeline_mode=pl.Buffered(1))


def params():
    return pltpu.CompilerParams(vmem_limit_bytes=VMEM_LIMIT)


def make_meta(counts, present, peer):
    images = counts.shape[0]
    ordinal = jnp.arange(images, dtype=jnp.int32)
    padded = (counts + 15) // 16 * 16
    key = (1 - present) * images + ordinal
    before = (key[None, :] < key[:, None]).astype(jnp.int32)
    place = jnp.sum(before, axis=1)
    start = jnp.sum(before * padded[None, :], axis=1)
    pick = (place[None, :] == ordinal[:, None]).astype(jnp.int32)

    def ordered(values):
        return jnp.sum(pick * values[None, :], axis=1)

    rows_fwd = jnp.sum(padded)
    rows_bwd = jnp.sum(padded * present)
    misc = jnp.stack(
        [
            (rows_fwd + TILE - 1) // TILE,
            (rows_bwd + TILE - 1) // TILE,
            rows_fwd,
            rows_bwd,
            jnp.sum(present),
        ]
    )
    return jnp.concatenate(
        [
            ordered(start),
            ordered(counts),
            ordered(ordinal),
            ordered(present),
            ordered(peer),
            jnp.pad(misc, (0, 11)),
        ]
    ).astype(jnp.int32)


def first_half(meta, slopes, tokens, spot_rows, spot_cols, gain, shift, weight, bias):
    images, length, width = tokens.shape
    full = images * ((length + 15) // 16 * 16)
    tiles = -(-full // TILE)
    rows = tiles * TILE + WINDOW
    last = images - 1

    def by_spot(step, meta, slopes):
        return (meta[IMG + jnp.maximum(step - images, 0)], 0, 0)

    return pl.pallas_call(
        attend_kernel,
        out_shape=(
            jax.ShapeDtypeStruct((rows, width), BF16),
            jax.ShapeDtypeStruct((rows, 3 * width), BF16),
            jax.ShapeDtypeStruct((rows, width), BF16),
            jax.ShapeDtypeStruct((images, HEADS // 2, 8, WINDOW), F32),
        ),
        grid_spec=pltpu.PrefetchScalarGridSpec(
            num_scalar_prefetch=2,
            grid=(2 * images,),
            in_specs=[
                pl.BlockSpec(
                    (1, length, width), lambda s, meta, sl: (meta[IMG + jnp.minimum(s, last)], 0, 0)
                ),
                pl.BlockSpec((1, 8, WINDOW), by_spot),
                pl.BlockSpec((1, WINDOW, 128), by_spot),
                whole(1, width),
                whole(1, width),
                whole(width, 3 * width),
                whole(1, 3 * width),
            ],
            out_specs=[
                pl.BlockSpec(memory_space=pl.ANY),
                pl.BlockSpec(memory_space=pl.ANY),
                pl.BlockSpec(memory_space=pl.ANY),
                pl.BlockSpec(
                    (1, HEADS // 2, 8, WINDOW),
                    lambda s, meta, sl: (jnp.maximum(s - images, 0), 0, 0, 0),
                ),
            ],
            scratch_shapes=[
                pltpu.VMEM((rows, width), BF16),
                pltpu.VMEM((rows, 3 * width), BF16),
                pltpu.VMEM((rows, width), BF16),
                pltpu.VMEM((WINDOW, WINDOW), F32),
                pltpu.SemaphoreType.DMA((tiles,)),
                pltpu.SemaphoreType.DMA((tiles,)),
                pltpu.SemaphoreType.DMA((tiles,)),
            ],
        ),
        compiler_params=params(),
    )(meta, slopes, tokens, spot_rows, spot_cols, gain, shift, weight, bias)


def mlp(meta, cot, att, packed, out_w, out_b, gain, shift, up_w, up_b, down_w, down_b):
    images, length, width = cot.shape
    rows = packed.shape[0]
    tiles = (rows - WINDOW) // TILE
    hidden = up_w.shape[1]
    stage_rows = 256
    last = images - 1

    def fwd_tile(s, meta):
        return (jnp.clip(s - images, 0, meta[N_FWD] - 1), 0)

    def bwd_tile(s, meta):
        return (jnp.clip(s - images, 0, jnp.maximum(meta[N_BWD] - 1, 0)), 0)

    return pl.pallas_call(
        functools.partial(mlp_kernel, 512),
        out_shape=(
            jax.ShapeDtypeStruct((images, length, width), BF16),
            jax.ShapeDtypeStruct((rows, width), F32),
            jax.ShapeDtypeStruct((rows, width), BF16),
            jax.ShapeDtypeStruct((width, hidden), BF16),
            jax.ShapeDtypeStruct((hidden, width), BF16),
            jax.ShapeDtypeStruct((width, width), BF16),
            jax.ShapeDtypeStruct((8, width), F32),
            jax.ShapeDtypeStruct((8, hidden), F32),
        ),
        grid_spec=pltpu.PrefetchScalarGridSpec(
            num_scalar_prefetch=1,
            grid=(2 * images + tiles,),
            in_specs=[
                pl.BlockSpec(
                    (1, length, width), lambda s, meta: (meta[PEER + jnp.minimum(s, last)], 0, 0)
                ),
                pl.BlockSpec((TILE, width), fwd_tile),
                pl.BlockSpec((TILE, width), fwd_tile),
                whole(width, width),
                whole(1, width),
                whole(1, width),
                whole(1, width),
                whole(width, hidden),
                whole(1, hidden),
                whole(hidden, width),
                whole(1, width),
            ],
            out_specs=[
                pl.BlockSpec(
                    (1, length, width),
                    lambda s, meta: (meta[PEER + jnp.clip(s - images - tiles, 0, last)], 0, 0),
                ),
                pl.BlockSpec((TILE, width), bwd_tile),
                pl.BlockSpec((TILE, width), bwd_tile),
                pl.BlockSpec(memory_space=pl.ANY),
                pl.BlockSpec(memory_space=pl.ANY),
                pl.BlockSpec(memory_space=pl.ANY),
                whole(8, width),
                whole(8, hidden),
            ],
            scratch_shapes=[
                pltpu.VMEM((rows, width), BF16),
                pltpu.VMEM((rows, width), BF16),
                pltpu.VMEM((width, hidden), F32),
                pltpu.VMEM((width, hidden), F32),
                pltpu.VMEM((width, width), F32),
                pltpu.VMEM((TILE, width), BF16),
                pltpu.VMEM((width, TILE), BF16),
                pltpu.VMEM((width, TILE), BF16),
                pltpu.VMEM((TILE, width), F32),
                pltpu.VMEM((TILE, width), F32),
                pltpu.VMEM((2, stage_rows, hidden), BF16),
                pltpu.SemaphoreType.DMA((2,)),
            ],
        ),
        compiler_params=params(),
    )(meta, cot, att, packed, out_w, out_b, gain, shift, up_w, up_b, down_w, down_b)


def attend_back(meta, slopes, qkv, att_grad, totals, spot_rows, spot_cols, packed, gain, shift):
    images = totals.shape[0]
    rows, width = packed.shape
    tiles = (rows - WINDOW) // TILE
    last = images - 1

    def spot_of(s, meta):
        return jnp.clip(s, 0, jnp.maximum(jnp.minimum(last, meta[N_LIVE] - 1), 0))

    def by_offset(s, meta, slopes):
        return (aligned(meta[OFF + spot_of(s, meta)]), 0)

    def by_spot(s, meta, slopes):
        return (spot_of(s, meta), 0, 0, 0)

    def by_image(s, meta, slopes):
        return (meta[IMG + spot_of(s, meta)], 0, 0)

    def bwd_tile(s, meta, slopes):
        return (jnp.clip(s - images, 0, jnp.maximum(meta[N_BWD] - 1, 0)), 0)

    return pl.pallas_call(
        attend_back_kernel,
        out_shape=(
            jax.ShapeDtypeStruct((rows, 3 * width), BF16),
            jax.ShapeDtypeStruct((width, 3 * width), BF16),
            jax.ShapeDtypeStruct((8, 3 * width), F32),
        ),
        grid_spec=pltpu.PrefetchScalarGridSpec(
            num_scalar_prefetch=2,
            grid=(images + tiles,),
            in_specs=[
                pl.BlockSpec((pl.Element(WINDOW), pl.Element(3 * width)), by_offset),
                pl.BlockSpec((pl.Element(WINDOW), pl.Element(width)), by_offset),
                pl.BlockSpec((1, HEADS // 2, 8, WINDOW), by_spot),
                pl.BlockSpec((1, 8, WINDOW), by_image),
                pl.BlockSpec((1, WINDOW, 128), by_image),
                pl.BlockSpec((TILE, width), bwd_tile),
                whole(1, width),
                whole(1, width),
            ],
            out_specs=[
                pl.BlockSpec((TILE, 3 * width), bwd_tile),
                pl.BlockSpec(memory_space=pl.ANY),
                whole(8, 3 * width),
            ],
            scratch_shapes=[
                pltpu.VMEM((rows, 3 * width), BF16),
                pltpu.VMEM((WINDOW, WINDOW), F32),
                pltpu.VMEM((width, 3 * width), F32),
                pltpu.VMEM((2, 256, 3 * width), BF16),
                pltpu.SemaphoreType.DMA((2,)),
            ],
        ),
        compiler_params=params(),
    )(meta, slopes, qkv, att_grad, totals, spot_rows, spot_cols, packed, gain, shift)


def token_grad(meta, packed_grad, packed, mid_grad, gain, weight, images, length):
    rows, width = packed.shape
    tiles = (rows - WINDOW) // TILE
    last = images - 1

    def bwd_tile(s, meta):
        return (jnp.clip(s, 0, jnp.maximum(meta[N_BWD] - 1, 0)), 0)

    return pl.pallas_call(
        token_grad_kernel,
        out_shape=(
            jax.ShapeDtypeStruct((images, length, width), F32),
            jax.ShapeDtypeStruct((8, width), F32),
        ),
        grid_spec=pltpu.PrefetchScalarGridSpec(
            num_scalar_prefetch=1,
            grid=(images + tiles,),
            in_specs=[
                pl.BlockSpec((TILE, 3 * width), bwd_tile),
                pl.BlockSpec((TILE, width), bwd_tile),
                pl.BlockSpec((TILE, width), bwd_tile),
                whole(1, width),
                whole(width, 3 * width),
            ],
            out_specs=[
                pl.BlockSpec(
                    (1, length, width),
                    lambda s, meta: (meta[IMG + jnp.clip(s - tiles, 0, last)], 0, 0),
                ),
                whole(8, width),
            ],
            scratch_shapes=[pltpu.VMEM((rows, width), F32)],
        ),
        compiler_params=params(),
    )(meta, packed_grad, packed, mid_grad, gain, weight)


def prepare(counts, rows, cols, present, peer):
    images, length = rows.shape
    meta = make_meta(counts, present, peer)
    spots = jnp.stack([rows, cols], axis=1).astype(F32)
    spot_rows = jnp.pad(spots, ((0, 0), (0, 6), (0, WINDOW - length)))
    spot_cols = jnp.pad(
        jnp.swapaxes(spots, 1, 2), ((0, 0), (0, WINDOW - length), (0, 126))
    )
    slopes = jnp.exp2(-8.0 * (jnp.arange(HEADS, dtype=F32) + 1.0) / HEADS)
    return meta, spot_rows, spot_cols, jnp.pad(slopes, (0, 4))


def line(vector):
    return vector.reshape(1, -1)


def per_device(
    tokens,
    cotangent,
    counts,
    rows,
    cols,
    present,
    slots,
    first_gain,
    first_shift,
    qkv_weight,
    query_bias,
    value_bias,
    out_weight,
    out_bias,
    second_gain,
    second_shift,
    up_weight,
    up_bias,
    down_weight,
    down_bias,
):
    steps, images, length, width = tokens.shape
    hidden = up_weight.shape[1]
    group = lax.axis_size("bal")
    total = steps * images
    step_ids = jnp.arange(steps, dtype=jnp.int32)

    peer = slots // images * steps + step_ids[:, None]
    every = lax.all_gather(slots, "bal")
    here = (every // images == lax.axis_index("bal")).astype(jnp.int32)
    place = jnp.sum(here * (every % images), axis=2)
    send_cot_from = (step_ids[None, :] * images + place).reshape(total)
    source = jnp.arange(group, dtype=jnp.int32)[:, None] * steps + step_ids[None, :]
    lands = (place.T[:, None, :] == jnp.arange(images, dtype=jnp.int32)[None, :, None]).astype(jnp.int32)
    take_from = jnp.sum(lands * source.T[:, None, :], axis=2).reshape(total)

    meta, spot_rows, spot_cols, slopes = prepare(
        counts.reshape(total),
        rows.reshape(total, length),
        cols.reshape(total, length),
        present.reshape(total),
        peer.reshape(total),
    )

    def exchange(blocks):
        return lax.all_to_all(blocks, "bal", split_axis=0, concat_axis=0, tiled=True)

    cot_send = move_images(cotangent.reshape(total, length, width), send_cot_from)
    cot_home = exchange(cot_send.reshape(group, steps, length, width)).reshape(total, length, width)
    shift_all = jnp.concatenate([query_bias, jnp.zeros_like(query_bias), value_bias])
    packed, qkv, att, totals = first_half(
        meta, slopes, tokens.reshape(total, length, width), spot_rows, spot_cols,
        line(first_gain), line(first_shift), qkv_weight, line(shift_all),
    )
    y_send, mid_grad, att_grad, up_g, down_g, out_g, vec_two, upb_g = mlp(
        meta, cot_home, att, packed, out_weight, line(out_bias), line(second_gain),
        line(second_shift), up_weight, line(up_bias), down_weight, line(down_bias),
    )
    y_got = exchange(y_send.reshape(group, steps, length, width)).reshape(total, length, width)

    def over_dp(matrix):
        return lax.psum_scatter(matrix, "dp", scatter_dimension=0, tiled=True)

    up_rows, down_rows, out_rows = over_dp(up_g), over_dp(down_g), over_dp(out_g)
    packed_grad, qkv_g, bias_g = attend_back(
        meta, slopes, qkv, att_grad, totals, spot_rows, spot_cols, packed,
        line(first_gain), line(first_shift),
    )
    qkv_rows = over_dp(qkv_g)
    input_grad, vec_one = token_grad(
        meta, packed_grad, packed, mid_grad, line(first_gain), qkv_weight, total, length
    )
    qkv_rows, out_rows, up_rows, down_rows = [
        lax.psum(share, "bal").astype(F32) for share in (qkv_rows, out_rows, up_rows, down_rows)
    ]
    vectors = lax.psum(
        jnp.concatenate(
            [vec_one[0], vec_one[1], bias_g[0], vec_two[0], vec_two[1], vec_two[2], vec_two[3], upb_g[0]]
        ),
        ("dp", "bal"),
    )

    def vector(n):
        return vectors[n * width : (n + 1) * width]

    output = move_images(y_got, take_from)
    return (
        output.reshape(steps, images, length, width),
        input_grad.reshape(steps, images, length, width),
        vector(0),
        vector(1),
        qkv_rows,
        vector(2),
        vector(4),
        out_rows,
        vector(7),
        vector(5),
        vector(6),
        up_rows,
        vectors[9 * width : 9 * width + hidden],
        down_rows,
        vector(8),
    )


def solution(mesh):
    images = P(None, ("dp", "bal"), None, None)
    spots = P(None, ("dp", "bal"), None)
    flags = P(None, ("dp", "bal"))
    matrix = P("dp", None)
    return jax.shard_map(
        per_device,
        mesh=mesh,
        in_specs=(images, images, flags, spots, spots, flags, flags) + (P(),) * 13,
        out_specs=(
            images, images, P(), P(), matrix, P(), P(), matrix, P(), P(), P(), matrix, P(), matrix, P(),
        ),
        check_vma=False,
    )
```

```python
import functools
import math

import jax
import jax.numpy as jnp
from jax import lax
from jax.experimental import pallas as pl
from jax.experimental.pallas import tpu as pltpu
from jax.sharding import PartitionSpec as P

HEADS = 12
TILE = 256
WINDOW = 256
FAR = 1e12
EPS = 1e-06
VMEM_LIMIT = 60 * 1024 * 1024

F32 = jnp.float32
BF16 = jnp.bfloat16

OFF, CNT, IMG, LIVE, PEER, SPOT, MISC = 0, 16, 32, 48, 64, 80, 96
N_FWD, N_BWD, ROWS_FWD, ROWS_BWD, N_LIVE = MISC, MISC + 1, MISC + 2, MISC + 3, MISC + 4
PLACES = 128

GAIN_ONE, SHIFT_ONE, QKV_B, OUT_B, GAIN_TWO, SHIFT_TWO, DOWN_B, UP_B = 0, 1, 2, 5, 6, 7, 8, 9


def dot(a, b):
    return jnp.dot(a, b, preferred_element_type=F32)


def dot_bt(a, b):
    return lax.dot_general(a, b, (((1,), (1,)), ((), ())), preferred_element_type=F32)


def turned(block):
    size = 256 if block.shape[1] % 256 == 0 else 128
    row = lax.broadcasted_iota(jnp.int32, (size, size), 0)
    col = lax.broadcasted_iota(jnp.int32, (size, size), 1)
    eye = jnp.where(row == col, 1.0, 0.0).astype(BF16)
    parts = [
        dot_bt(eye, block[:, start : start + size]).astype(BF16)
        for start in range(0, block.shape[1], size)
    ]
    return parts[0] if len(parts) == 1 else jnp.concatenate(parts, axis=0)


def layer_norm(values):
    average = jnp.mean(values, axis=-1, keepdims=True)
    centred = values - average
    spread = jnp.mean(centred * centred, axis=-1, keepdims=True)
    inverse = lax.rsqrt(spread + EPS)
    return centred * inverse, inverse


def norm_back(out_grad, gain, unit, inverse):
    e = out_grad * gain
    mean_e = jnp.mean(e, axis=-1, keepdims=True)
    mean_eu = jnp.mean(e * unit, axis=-1, keepdims=True)
    return inverse * (e - mean_e - unit * mean_eu)


def gelu_parts(u):
    size = jnp.abs(u)
    t = 1.0 / (1.0 + (0.3275911 * math.sqrt(0.5)) * size)
    bell = jnp.exp(-0.5 * (u * u))
    poly = t * (
        0.5 * 0.254829592
        + t
        * (
            0.5 * -0.284496736
            + t * (0.5 * 1.421413741 + t * (0.5 * -1.453152027 + t * (0.5 * 1.061405429)))
        )
    )
    tail = poly * bell
    phi_sum = jnp.where(u >= 0, 1.0 - tail, tail)
    return phi_sum, u * bell * (1.0 / math.sqrt(2.0 * math.pi))


def row_ids(start, rows):
    return start + lax.broadcasted_iota(jnp.int32, (rows, 1), 0)


def aligned(value, step=16):
    return pl.multiple_of(value, step)


def by_count(count, run):
    @pl.when(count <= 128)
    def _():
        run(128, 128)

    @pl.when(jnp.logical_and(count > 128, count <= 192))
    def _():
        run(192, 256)

    @pl.when(count > 192)
    def _():
        run(256, 256)


def distances(rows, cols, which, count, keys, queries):
    mine = lax.broadcasted_iota(jnp.int32, rows.shape, 0) == which
    row = jnp.sum(jnp.where(mine, rows, 0).astype(F32), axis=0, keepdims=True)
    col = jnp.sum(jnp.where(mine, cols, 0).astype(F32), axis=0, keepdims=True)
    spots = jnp.concatenate([row, col, jnp.zeros((6, row.shape[1]), F32)], axis=0)
    spots = jnp.concatenate([spots, jnp.zeros((8, WINDOW - row.shape[1]), F32)], axis=1)
    eye = jnp.where(
        lax.broadcasted_iota(jnp.int32, (keys, WINDOW), 0)
        == lax.broadcasted_iota(jnp.int32, (keys, WINDOW), 1),
        1.0,
        0.0,
    ).astype(BF16)
    turned_spots = dot_bt(eye, spots.astype(BF16))
    down = turned_spots[:, 0:1] - spots[0:1, :queries]
    across = turned_spots[:, 1:2] - spots[1:2, :queries]
    far = row_ids(0, keys) >= count
    return jnp.where(far, FAR, jnp.sqrt(down * down + across * across))


def prepare_kernel(every, counts, present, slots, me, cot, meta, take, send):
    step = pl.program_id(0)
    steps, length, images, width = pl.num_programs(0), cot.shape[1], cot.shape[2], cot.shape[3]
    group = every.shape[0]

    @pl.when(step == 0)
    def _():
        def fill(live):
            def body(img, carry):
                spot, off = carry
                m, i = img // images, img % images
                count = counts[m, i]
                mine = present[m, i] == live

                @pl.when(mine)
                def _():
                    meta[OFF + spot] = off
                    meta[CNT + spot] = count
                    meta[IMG + spot] = img
                    meta[LIVE + spot] = live
                    meta[PEER + spot] = slots[m, i] // images * steps + m
                    meta[SPOT + img] = spot

                padded = (count + 15) // 16 * 16
                return spot + mine.astype(jnp.int32), off + jnp.where(mine, padded, 0)

            return body

        zero = jnp.int32(0)
        total = counts.shape[0] * images
        spot, off = lax.fori_loop(0, total, fill(1), (zero, zero))
        meta[N_LIVE] = spot
        meta[ROWS_BWD] = off
        meta[N_BWD] = (off + TILE - 1) // TILE
        spot, off = lax.fori_loop(0, total, fill(0), (spot, off))
        meta[ROWS_FWD] = off
        meta[N_FWD] = (off + TILE - 1) // TILE

        def land(n, carry):
            a, m, i = n // total, n % total // images, n % images
            slot = every[a, m, i]

            @pl.when(slot // images == me[0])
            def _():
                take[m * images + slot % images] = a * steps + m

            return carry

        lax.fori_loop(0, group * total, land, 0)

    block = jnp.swapaxes(cot[0].astype(F32), 0, 1).astype(BF16)
    for place in range(images):
        peer = take[step * images + place] // steps
        send[peer, 0, :length, :] = block[place]


def place_kernel(take, got, out):
    step = pl.program_id(0)
    length, images = out.shape[1], out.shape[2]
    steps = pl.num_programs(0)
    parts = [
        got[take[step * images + place] // steps, 0, :length, :].astype(F32)
        for place in range(images)
    ]
    out[0] = jnp.swapaxes(jnp.stack(parts, axis=0), 0, 1).astype(out.dtype)


def attend_kernel(
    meta, slopes, tokens, rows_in, cols_in, vecs, weight,
    packed_out, qkv_out, att_out, total_out,
    held, packed, qkv, att, gaps, sem_packed, sem_qkv, sem_att,
):
    length, per, width = tokens.shape[1], tokens.shape[2], tokens.shape[3]
    images = held.shape[0]
    steps = images // per
    now = pl.program_id(0)

    def tile_copy(which, t):
        src, dst, sem = (
            (packed, packed_out, sem_packed),
            (qkv, qkv_out, sem_qkv),
            (att, att_out, sem_att),
        )[which]
        rows = pl.ds(aligned(t * TILE, TILE), TILE)
        return pltpu.make_async_copy(src.at[rows], dst.at[rows], sem.at[t])

    @pl.when(now == 0)
    def _():
        packed[...] = jnp.zeros_like(packed)

    @pl.when(now < steps)
    def _():
        block = jnp.swapaxes(tokens[0].astype(F32), 0, 1).astype(BF16)
        for i in range(per):
            held[now * per + i, :length, :] = block[i]

    step = now - steps

    @pl.when(jnp.logical_and(step >= 0, step < images))
    def _():
        off = aligned(meta[OFF + step])
        packed[pl.ds(off, length), :] = held[meta[IMG + step], :length, :]
        begin = off // TILE
        after = aligned(meta[OFF + jnp.minimum(step + 1, images - 1)])
        end = jnp.where(step == images - 1, meta[N_FWD], after // TILE)

        def project(t, carry):
            rows = pl.ds(aligned(t * TILE, TILE), TILE)
            unit, _ = layer_norm(packed[rows, :].astype(F32))
            hidden = (
                unit * vecs[GAIN_ONE : GAIN_ONE + 1] + vecs[SHIFT_ONE : SHIFT_ONE + 1]
            ).astype(BF16)
            for part in range(3):
                cols = slice(part * width, (part + 1) * width)
                bias = vecs[QKV_B + part : QKV_B + part + 1]
                qkv[rows, cols] = (dot(hidden, weight[:, cols]) + bias).astype(BF16)
            tile_copy(0, t).start()
            tile_copy(1, t).start()
            return carry

        lax.fori_loop(begin, end, project, 0)

    @pl.when(step >= images)
    def _():
        spot = step - images
        off = aligned(meta[OFF + spot])
        count = meta[CNT + spot]

        def run(keys, queries):
            which = meta[IMG + spot] % per
            gaps[:keys, :queries] = distances(rows_in[0], cols_in[0], which, count, keys, queries)
            key_seen = row_ids(0, keys) < count
            query_seen = row_ids(0, queries) < count
            left = lax.broadcasted_iota(jnp.int32, (queries, 128), 1) < 64

            def pair(p, carry):
                lanes = aligned(p * 128, 128)
                q2 = qkv[pl.ds(off, queries), pl.ds(lanes, 128)] * 0.125
                k2 = qkv[pl.ds(off, keys), pl.ds(width + lanes, 128)]
                v2 = qkv[pl.ds(off, keys), pl.ds(2 * width + lanes, 128)]
                q2 = jnp.where(query_seen, q2, jnp.zeros_like(q2))
                k2 = jnp.where(key_seen, k2, jnp.zeros_like(k2))
                v2 = jnp.where(key_seen, v2, jnp.zeros_like(v2))
                v2t = turned(v2)
                outs = []
                for half in range(2):
                    head = 2 * p + half
                    mine = left if half == 0 else jnp.logical_not(left)
                    qh = jnp.where(mine, q2, jnp.zeros_like(q2))
                    scores = dot_bt(k2, qh) - slopes[head] * gaps[:keys, :queries]
                    top = jnp.max(scores, axis=0, keepdims=True)
                    terms = jnp.exp(scores - top)
                    total = jnp.sum(terms, axis=0, keepdims=True)
                    heads_out = dot(v2t[half * 64 : half * 64 + 64], terms.astype(BF16))
                    outs.append((heads_out * (1.0 / total)).astype(BF16))
                    total_out[0, p, half : half + 1, :queries] = top + jnp.log(total)
                both = jnp.concatenate(outs, axis=0)
                att[pl.ds(off, queries), pl.ds(lanes, 128)] = turned_back(both)
                return carry

            lax.fori_loop(0, HEADS // 2, pair, 0)

        by_count(count, run)
        after = meta[OFF + jnp.minimum(spot + 1, images - 1)]
        end = jnp.where(spot == images - 1, meta[N_FWD], after // TILE)

        def send(t, carry):
            tile_copy(2, t).start()
            return carry

        lax.fori_loop(off // TILE, end, send, 0)

    @pl.when(now == pl.num_programs(0) - 1)
    def _():
        def finish(t, carry):
            for which in range(3):
                tile_copy(which, t).wait()
            return carry

        lax.fori_loop(0, meta[N_FWD], finish, 0)


def turned_back(block):
    size = block.shape[1]
    parts = []
    for start in range(0, size, 128):
        row = lax.broadcasted_iota(jnp.int32, (128, size), 0)
        col = lax.broadcasted_iota(jnp.int32, (128, size), 1)
        eye = jnp.where(row + start == col, 1.0, 0.0).astype(BF16)
        parts.append(dot_bt(eye, block).astype(BF16))
    return parts[0] if len(parts) == 1 else jnp.concatenate(parts, axis=0)


def mlp_kernel(
    chunk, length, meta, cot_in, att_in, tokens_in,
    vecs, out_w, up_w, down_w,
    y_send, mid_grad, att_grad, up_g, down_g, out_g, vec_g, upb_g,
    up_b, cot, y_all, up_acc, down_acc, out_acc, h2_s, h2t_s, dzt_s, z_s, g_s, stage, sem,
):
    step = pl.program_id(0)
    tiles = cot.shape[0] // TILE - WINDOW // TILE
    images = (pl.num_programs(0) - tiles) // 2
    width = cot_in.shape[2]
    hidden = up_w.shape[1]
    out_b, gain, shift, down_b = [
        vecs.at[pl.ds(n, 1)] for n in (OUT_B, GAIN_TWO, SHIFT_TWO, DOWN_B)
    ]

    @pl.when(step == 0)
    def _():
        up_acc[...] = jnp.zeros_like(up_acc)
        down_acc[...] = jnp.zeros_like(down_acc)
        out_acc[...] = jnp.zeros_like(out_acc)
        vec_g[...] = jnp.zeros_like(vec_g)
        upb_g[...] = jnp.zeros_like(upb_g)
        for n in range(hidden // width):
            up_b[0:1, n * width : (n + 1) * width] = vecs[UP_B + n : UP_B + n + 1, :]

    @pl.when(jnp.logical_and(step < images, step < meta[N_LIVE]))
    def _():
        spot = step
        off = aligned(meta[OFF + spot])
        seen = row_ids(0, length) < meta[CNT + spot]
        block = cot_in[0, :length, :]
        edge = (length - 1) // 16 * 16
        cot[pl.ds(aligned(off + edge), 16), :] = jnp.zeros((16, width), BF16)
        cot[pl.ds(off, length), :] = jnp.where(seen, block, jnp.zeros_like(block))

    def run_tile(t, both):
        rows = aligned(t * TILE, TILE)
        ids = row_ids(rows, TILE)
        att = att_in[...]
        att = jnp.where(ids < meta[ROWS_FWD], att, jnp.zeros_like(att))
        mid = tokens_in[...].astype(F32) + (dot(att, out_w[...]) + out_b[...])
        unit, inverse = layer_norm(mid)
        h2 = (unit * gain[...] + shift[...]).astype(BF16)
        h2_s[...] = h2
        z_s[...] = mid + down_b[...]
        if both:
            dz = cot[pl.ds(rows, TILE), :]
            dz = jnp.where(ids < meta[ROWS_BWD], dz, jnp.zeros_like(dz))
            h2t_s[...] = turned(h2)
            dzt_s[...] = turned(dz)
            g_s[...] = jnp.zeros_like(g_s)

        def part(c, carry):
            cols = pl.ds(aligned(c * chunk, chunk), chunk)
            pre = dot(h2_s[...], up_w[:, cols]) + up_b[0:1, cols]
            share, slope = gelu_parts(pre)
            act = (pre * share).astype(BF16)
            z_s[...] += dot(act, down_w[cols, :])
            if both:
                pre_g = (dot_bt(dz, down_w[cols, :]) * (share + slope)).astype(BF16)
                up_acc[:, cols] += dot(h2t_s[...], pre_g)
                down_acc[:, cols] += dot(dzt_s[...], act)
                upb_g[0:1, cols] += jnp.sum(pre_g.astype(F32), axis=0, keepdims=True)
                g_s[...] += dot_bt(pre_g, up_w[:, cols])
            return carry

        lax.fori_loop(0, hidden // chunk, part, 0)
        y_all[pl.ds(rows, TILE), :] = z_s[...].astype(BF16)
        if both:
            dzf = dz.astype(F32)
            g2 = g_s[...]
            dmid = dzf + norm_back(g2, gain[...], unit, inverse)
            branch = dmid.astype(BF16)
            mid_grad[...] = dmid
            att_grad[...] = dot_bt(branch, out_w[...]).astype(BF16)
            out_acc[...] += dot(turned(att), branch)
            vec_g[0:1, :] += jnp.sum(g2 * unit, axis=0, keepdims=True)
            vec_g[1:2, :] += jnp.sum(g2, axis=0, keepdims=True)
            vec_g[2:3, :] += jnp.sum(branch.astype(F32), axis=0, keepdims=True)
            vec_g[3:4, :] += jnp.sum(dzf, axis=0, keepdims=True)

    tile = step - images

    @pl.when(jnp.logical_and(tile >= 0, tile < meta[N_BWD]))
    def _():
        run_tile(tile, True)

    @pl.when(
        jnp.logical_and(
            jnp.logical_and(tile >= meta[N_BWD], tile >= 0),
            jnp.logical_and(tile < meta[N_FWD], tile < tiles),
        )
    )
    def _():
        run_tile(tile, False)

    @pl.when(step == images + tiles)
    def _():
        size = stage.shape[1]
        jobs = []
        for start in range(0, width, size):
            jobs.append((up_acc, start, up_g, False))
            jobs.append((out_acc, start, out_g, False))
        for start in range(0, hidden, size):
            jobs.append((down_acc, start, down_g, True))

        def copy(n):
            source, start, target, _ = jobs[n]
            columns = target.shape[1]
            return pltpu.make_async_copy(
                stage.at[n % 2, :, pl.ds(0, columns)], target.at[pl.ds(start, size)], sem.at[n % 2]
            )

        for n, (source, start, target, flip) in enumerate(jobs):
            if n >= 2:
                copy(n - 2).wait()
            if flip:
                for low in range(0, width, 256):
                    block = source[pl.ds(low, 256), pl.ds(start, size)].astype(BF16)
                    stage[n % 2, :, pl.ds(low, 256)] = turned(block)
            else:
                columns = target.shape[1]
                stage[n % 2, :, pl.ds(0, columns)] = source[pl.ds(start, size), :].astype(BF16)
            copy(n).start()
        copy(len(jobs) - 2).wait()
        copy(len(jobs) - 1).wait()

    spot = step - images - tiles

    @pl.when(spot >= 0)
    def _():
        off = aligned(meta[OFF + spot])
        seen = row_ids(0, length) < meta[CNT + spot]
        block = y_all[pl.ds(off, length), :]
        y_send[0, :length, :] = jnp.where(seen, block, jnp.zeros_like(block))


def attend_back_kernel(
    first, per, meta, slopes, qkv, att_grad, totals, rows_in, cols_in, *rest
):
    grads_out, grads, gaps, sem = rest[-4:]
    step = pl.program_id(0)
    width = att_grad.shape[1]
    spot = first + step
    live = spot < meta[N_LIVE]
    slot = step % 2

    def copy(at):
        rows = pl.ds(aligned(meta[OFF + first + at]), WINDOW)
        return pltpu.make_async_copy(grads.at[at % 2], grads_out.at[rows], sem.at[at % 2])

    @pl.when(live)
    def _():
        count = meta[CNT + spot]

        def run(keys, queries):
            which = meta[IMG + spot] % per
            gaps[:keys, :queries] = distances(rows_in[0], cols_in[0], which, count, keys, queries)
            key_seen = row_ids(0, keys) < count
            query_seen = row_ids(0, queries) < count
            left = lax.broadcasted_iota(jnp.int32, (queries, 128), 1) < 64

            def pair(p, carry):
                lanes = aligned(p * 128, 128)
                q2 = qkv[:queries, pl.ds(lanes, 128)] * 0.125
                k2 = qkv[:keys, pl.ds(width + lanes, 128)]
                v2 = qkv[:keys, pl.ds(2 * width + lanes, 128)]
                o2 = att_grad[:queries, pl.ds(lanes, 128)]
                q2 = jnp.where(query_seen, q2, jnp.zeros_like(q2))
                o2 = jnp.where(query_seen, o2, jnp.zeros_like(o2))
                k2 = jnp.where(key_seen, k2, jnp.zeros_like(k2))
                v2 = jnp.where(key_seen, v2, jnp.zeros_like(v2))
                k2t = turned(k2)
                dq_parts = []
                dk = dv = None
                for half in range(2):
                    head = 2 * p + half
                    mine = left if half == 0 else jnp.logical_not(left)
                    qh = jnp.where(mine, q2, jnp.zeros_like(q2))
                    oh = jnp.where(mine, o2, jnp.zeros_like(o2))
                    scores = dot_bt(k2, qh) - slopes[head] * gaps[:keys, :queries]
                    probs = jnp.exp(scores - totals[0, p, half : half + 1, :queries])
                    prob_g = dot_bt(v2, oh)
                    inner = jnp.sum(probs * prob_g, axis=0, keepdims=True)
                    score_g = (probs * (prob_g - inner)).astype(BF16)
                    dv_part = dot(probs.astype(BF16), oh)
                    dk_part = dot(score_g, qh)
                    dq_parts.append(
                        (dot(k2t[half * 64 : half * 64 + 64], score_g) * 0.125).astype(BF16)
                    )
                    dk = dk_part if dk is None else dk + dk_part
                    dv = dv_part if dv is None else dv + dv_part
                dq = turned_back(jnp.concatenate(dq_parts, axis=0))
                grads[slot, :queries, pl.ds(lanes, 128)] = dq
                grads[slot, :keys, pl.ds(width + lanes, 128)] = dk.astype(BF16)
                grads[slot, :keys, pl.ds(2 * width + lanes, 128)] = dv.astype(BF16)
                return carry

            lax.fori_loop(0, HEADS // 2, pair, 0)

        by_count(count, run)

        @pl.when(step > 0)
        def _():
            copy(step - 1).wait()

        copy(step).start()

        @pl.when(jnp.logical_or(step == pl.num_programs(0) - 1, spot == meta[N_LIVE] - 1))
        def _():
            copy(step).wait()


def qkv_grad_kernel(meta, packed_grad, tokens, vecs, weight_g, bias_g, acc, stage, sem):
    tile = pl.program_id(0)
    width = tokens.shape[1]

    @pl.when(tile == 0)
    def _():
        acc[...] = jnp.zeros_like(acc)
        bias_g[...] = jnp.zeros_like(bias_g)

    @pl.when(tile < meta[N_BWD])
    def _():
        ids = row_ids(tile * TILE, TILE)
        unit, _ = layer_norm(tokens[...].astype(F32))
        hidden = (
            unit * vecs[GAIN_ONE : GAIN_ONE + 1] + vecs[SHIFT_ONE : SHIFT_ONE + 1]
        ).astype(BF16)
        hidden_t = turned(hidden)
        for part in range(3):
            cols = slice(part * width, (part + 1) * width)
            block = packed_grad[:, cols]
            block = jnp.where(ids < meta[ROWS_BWD], block, jnp.zeros_like(block))
            acc[:, cols] += dot(hidden_t, block)
            bias_g[0:1, cols] += jnp.sum(block.astype(F32), axis=0, keepdims=True)

    @pl.when(tile == pl.num_programs(0) - 1)
    def _():
        size = stage.shape[1]
        count = width // size

        def copy(n):
            return pltpu.make_async_copy(
                stage.at[n % 2], weight_g.at[pl.ds(n * size, size)], sem.at[n % 2]
            )

        for n in range(count):
            if n >= 2:
                copy(n - 2).wait()
            stage[n % 2] = acc[pl.ds(n * size, size), :].astype(BF16)
            copy(n).start()
        copy(count - 2).wait()
        copy(count - 1).wait()


def token_grad_kernel(meta, packed_grad, tokens, mid_grad, vecs, weight, out, vec_g, held):
    step = pl.program_id(0)
    tiles = held.shape[0] // TILE - WINDOW // TILE
    length, images = out.shape[1], out.shape[2]

    @pl.when(step == 0)
    def _():
        vec_g[...] = jnp.zeros_like(vec_g)

    @pl.when(jnp.logical_and(step < tiles, step < meta[N_BWD]))
    def _():
        rows = aligned(step * TILE, TILE)
        ids = row_ids(rows, TILE)
        unit, inverse = layer_norm(tokens[...].astype(F32))
        block = packed_grad[...]
        block = jnp.where(ids < meta[ROWS_BWD], block, jnp.zeros_like(block))
        g1 = dot_bt(block, weight[...])
        back = norm_back(g1, vecs[GAIN_ONE : GAIN_ONE + 1], unit, inverse)
        held[pl.ds(rows, TILE), :] = mid_grad[...] + back
        vec_g[0:1, :] += jnp.sum(g1 * unit, axis=0, keepdims=True)
        vec_g[1:2, :] += jnp.sum(g1, axis=0, keepdims=True)

    @pl.when(step >= tiles)
    def _():
        parts = []
        for i in range(images):
            spot = meta[SPOT + (step - tiles) * images + i]
            off = aligned(meta[OFF + spot])
            limit = meta[CNT + spot] * meta[LIVE + spot]
            block = held[pl.ds(off, length), :]
            parts.append(jnp.where(row_ids(0, length) < limit, block, 0.0))
        out[0] = jnp.swapaxes(jnp.stack(parts, axis=0), 0, 1)


def whole(*shape):
    return pl.BlockSpec(shape, lambda *_: (0,) * len(shape), pipeline_mode=pl.Buffered(1))


def params():
    return pltpu.CompilerParams(vmem_limit_bytes=VMEM_LIMIT)


def small():
    return pl.BlockSpec(memory_space=pltpu.SMEM)


def prepare(every, counts, present, slots, me, cotangent):
    steps, length, images, width = cotangent.shape
    group = every.shape[0]
    padded = (length + 7) // 8 * 8
    return pl.pallas_call(
        prepare_kernel,
        out_shape=(
            jax.ShapeDtypeStruct((PLACES,), jnp.int32),
            jax.ShapeDtypeStruct((steps * images,), jnp.int32),
            jax.ShapeDtypeStruct((group, steps, padded, width), BF16),
        ),
        grid=(steps,),
        in_specs=[small()] * 5 + [pl.BlockSpec((1, length, images, width), lambda m: (m, 0, 0, 0))],
        out_specs=[
            small(),
            small(),
            pl.BlockSpec((group, 1, padded, width), lambda m: (0, m, 0, 0)),
        ],
        compiler_params=params(),
    )(every, counts, present, slots, me, cotangent)


def place(take, got, length):
    group, steps, padded, width = got.shape
    return pl.pallas_call(
        place_kernel,
        out_shape=jax.ShapeDtypeStruct((steps, length, group, width), BF16),
        grid=(steps,),
        in_specs=[small(), pl.BlockSpec((group, 1, padded, width), lambda m: (0, m, 0, 0))],
        out_specs=pl.BlockSpec((1, length, group, width), lambda m: (m, 0, 0, 0)),
        compiler_params=params(),
    )(take, got)


def first_half(meta, slopes, tokens, rows, cols, vecs, weight):
    steps, length, per, width = tokens.shape
    images = steps * per
    tiles = -(-images * ((length + 15) // 16 * 16) // TILE)
    total = tiles * TILE + WINDOW
    spots = pl.BlockSpec(
        (1, per, length),
        lambda s, meta, slopes: (meta[IMG + jnp.maximum(s - steps - images, 0)] // per, 0, 0),
    )
    return pl.pallas_call(
        attend_kernel,
        out_shape=(
            jax.ShapeDtypeStruct((total, width), BF16),
            jax.ShapeDtypeStruct((total, 3 * width), BF16),
            jax.ShapeDtypeStruct((total, width), BF16),
            jax.ShapeDtypeStruct((images, HEADS // 2, 8, WINDOW), F32),
        ),
        grid_spec=pltpu.PrefetchScalarGridSpec(
            num_scalar_prefetch=2,
            grid=(steps + 2 * images,),
            in_specs=[
                pl.BlockSpec(
                    (1, length, per, width),
                    lambda s, meta, slopes: (jnp.minimum(s, steps - 1), 0, 0, 0),
                ),
                spots,
                spots,
                whole(*vecs.shape),
                whole(width, 3 * width),
            ],
            out_specs=[
                pl.BlockSpec(memory_space=pl.ANY),
                pl.BlockSpec(memory_space=pl.ANY),
                pl.BlockSpec(memory_space=pl.ANY),
                pl.BlockSpec(
                    (1, HEADS // 2, 8, WINDOW),
                    lambda s, meta, slopes: (jnp.maximum(s - steps - images, 0), 0, 0, 0),
                ),
            ],
            scratch_shapes=[
                pltpu.VMEM((images, (length + 15) // 16 * 16, width), BF16),
                pltpu.VMEM((total, width), BF16),
                pltpu.VMEM((total, 3 * width), BF16),
                pltpu.VMEM((total, width), BF16),
                pltpu.VMEM((WINDOW, WINDOW), F32),
                pltpu.SemaphoreType.DMA((tiles,)),
                pltpu.SemaphoreType.DMA((tiles,)),
                pltpu.SemaphoreType.DMA((tiles,)),
            ],
        ),
        compiler_params=params(),
        cost_estimate=cost(40),
    )(meta, slopes, tokens, rows, cols, vecs, weight)


def mlp(meta, cot, att, packed, vecs, out_w, up_w, down_w, length):
    images, padded, width = cot.shape
    rows = packed.shape[0]
    tiles = (rows - WINDOW) // TILE
    hidden = up_w.shape[1]
    last = images - 1

    def fwd_tile(s, meta):
        return (jnp.clip(s - images, 0, meta[N_FWD] - 1), 0)

    def bwd_tile(s, meta):
        return (jnp.clip(s - images, 0, jnp.maximum(meta[N_BWD] - 1, 0)), 0)

    return pl.pallas_call(
        functools.partial(mlp_kernel, 512, length),
        out_shape=(
            jax.ShapeDtypeStruct((images, padded, width), BF16),
            jax.ShapeDtypeStruct((rows, width), F32),
            jax.ShapeDtypeStruct((rows, width), BF16),
            jax.ShapeDtypeStruct((width, hidden), BF16),
            jax.ShapeDtypeStruct((hidden, width), BF16),
            jax.ShapeDtypeStruct((width, width), BF16),
            jax.ShapeDtypeStruct((8, width), F32),
            jax.ShapeDtypeStruct((8, hidden), F32),
        ),
        grid_spec=pltpu.PrefetchScalarGridSpec(
            num_scalar_prefetch=1,
            grid=(2 * images + tiles,),
            in_specs=[
                pl.BlockSpec(
                    (1, padded, width), lambda s, meta: (meta[PEER + jnp.minimum(s, last)], 0, 0)
                ),
                pl.BlockSpec((TILE, width), fwd_tile),
                pl.BlockSpec((TILE, width), fwd_tile),
                whole(*vecs.shape),
                whole(width, width),
                whole(width, hidden),
                whole(hidden, width),
            ],
            out_specs=[
                pl.BlockSpec(
                    (1, padded, width),
                    lambda s, meta: (meta[PEER + jnp.clip(s - images - tiles, 0, last)], 0, 0),
                ),
                pl.BlockSpec((TILE, width), bwd_tile),
                pl.BlockSpec((TILE, width), bwd_tile),
                pl.BlockSpec(memory_space=pl.ANY),
                pl.BlockSpec(memory_space=pl.ANY),
                pl.BlockSpec(memory_space=pl.ANY),
                whole(8, width),
                whole(8, hidden),
            ],
            scratch_shapes=[
                pltpu.VMEM((8, hidden), F32),
                pltpu.VMEM((rows, width), BF16),
                pltpu.VMEM((rows, width), BF16),
                pltpu.VMEM((width, hidden), F32),
                pltpu.VMEM((width, hidden), F32),
                pltpu.VMEM((width, width), F32),
                pltpu.VMEM((TILE, width), BF16),
                pltpu.VMEM((width, TILE), BF16),
                pltpu.VMEM((width, TILE), BF16),
                pltpu.VMEM((TILE, width), F32),
                pltpu.VMEM((TILE, width), F32),
                pltpu.VMEM((2, 256, hidden), BF16),
                pltpu.SemaphoreType.DMA((2,)),
            ],
        ),
        compiler_params=params(),
        cost_estimate=cost(110),
    )(meta, cot, att, packed, vecs, out_w, up_w, down_w)


def attend_back(first, count, meta, slopes, qkv, att_grad, totals, rows_in, cols_in, earlier):
    total, wide = qkv.shape
    width = wide // 3
    per, length = rows_in.shape[1:]

    def spot_of(s, meta):
        return jnp.clip(first + s, 0, jnp.maximum(meta[N_LIVE] - 1, 0))

    def by_offset(s, meta, slopes):
        return (aligned(meta[OFF + spot_of(s, meta)]), 0)

    spots = pl.BlockSpec(
        (1, per, length),
        lambda s, meta, slopes: (meta[IMG + spot_of(s, meta)] // per, 0, 0),
    )
    anywhere = pl.BlockSpec(memory_space=pl.ANY)
    return pl.pallas_call(
        functools.partial(attend_back_kernel, first, per),
        out_shape=jax.ShapeDtypeStruct((total, wide), BF16),
        grid_spec=pltpu.PrefetchScalarGridSpec(
            num_scalar_prefetch=2,
            grid=(count,),
            in_specs=[
                pl.BlockSpec((pl.Element(WINDOW), pl.Element(wide)), by_offset),
                pl.BlockSpec((pl.Element(WINDOW), pl.Element(width)), by_offset),
                pl.BlockSpec(
                    (1, HEADS // 2, 8, WINDOW),
                    lambda s, meta, slopes: (spot_of(s, meta), 0, 0, 0),
                ),
                spots,
                spots,
            ]
            + [anywhere] * len(earlier),
            out_specs=anywhere,
            scratch_shapes=[
                pltpu.VMEM((2, WINDOW, wide), BF16),
                pltpu.VMEM((WINDOW, WINDOW), F32),
                pltpu.SemaphoreType.DMA((2,)),
            ],
        ),
        input_output_aliases={7: 0} if earlier else {},
        compiler_params=params(),
        cost_estimate=cost(15),
    )(meta, slopes, qkv, att_grad, totals, rows_in, cols_in, *earlier)


def bwd_tile(s, meta):
    return (jnp.clip(s, 0, jnp.maximum(meta[N_BWD] - 1, 0)), 0)


def qkv_grad(meta, packed_grad, packed, vecs):
    rows, width = packed.shape
    tiles = (rows - WINDOW) // TILE
    return pl.pallas_call(
        qkv_grad_kernel,
        out_shape=(
            jax.ShapeDtypeStruct((width, 3 * width), BF16),
            jax.ShapeDtypeStruct((8, 3 * width), F32),
        ),
        grid_spec=pltpu.PrefetchScalarGridSpec(
            num_scalar_prefetch=1,
            grid=(tiles,),
            in_specs=[
                pl.BlockSpec((TILE, 3 * width), bwd_tile),
                pl.BlockSpec((TILE, width), bwd_tile),
                whole(*vecs.shape),
            ],
            out_specs=[pl.BlockSpec(memory_space=pl.ANY), whole(8, 3 * width)],
            scratch_shapes=[
                pltpu.VMEM((width, 3 * width), F32),
                pltpu.VMEM((2, 256, 3 * width), BF16),
                pltpu.SemaphoreType.DMA((2,)),
            ],
        ),
        compiler_params=params(),
        cost_estimate=cost(15),
    )(meta, packed_grad, packed, vecs)


def token_grad(meta, packed_grad, packed, mid_grad, vecs, weight, steps, length, images):
    rows, width = packed.shape
    tiles = (rows - WINDOW) // TILE
    return pl.pallas_call(
        token_grad_kernel,
        out_shape=(
            jax.ShapeDtypeStruct((steps, length, images, width), F32),
            jax.ShapeDtypeStruct((8, width), F32),
        ),
        grid_spec=pltpu.PrefetchScalarGridSpec(
            num_scalar_prefetch=1,
            grid=(tiles + steps,),
            in_specs=[
                pl.BlockSpec((TILE, 3 * width), bwd_tile),
                pl.BlockSpec((TILE, width), bwd_tile),
                pl.BlockSpec((TILE, width), bwd_tile),
                whole(*vecs.shape),
                whole(width, 3 * width),
            ],
            out_specs=[
                pl.BlockSpec(
                    (1, length, images, width),
                    lambda s, meta: (jnp.clip(s - tiles, 0, steps - 1), 0, 0, 0),
                ),
                whole(8, width),
            ],
            scratch_shapes=[pltpu.VMEM((rows, width), F32)],
        ),
        compiler_params=params(),
        cost_estimate=cost(20),
    )(meta, packed_grad, packed, mid_grad, vecs, weight)


def cost(microseconds):
    return pl.CostEstimate(
        flops=int(microseconds * 1e9), bytes_accessed=int(microseconds * 1e5), transcendentals=0
    )


def swap(block, axis, bit):
    size = lax.axis_size(axis)
    return lax.ppermute(block, axis, [(n, n ^ bit) for n in range(size)])


def bit_of(axis, bit):
    return lax.axis_index(axis) // bit % 2


def added(a, b):
    return (a.astype(F32) + b.astype(F32)).astype(BF16)


def half_sums(block, axis, bit, dim):
    mine = bit_of(axis, bit)
    keep = lax.dynamic_index_in_dim(block, mine, dim, keepdims=False)
    send = lax.dynamic_index_in_dim(block, 1 - mine, dim, keepdims=False)
    return added(keep, swap(send, axis, bit))


def summed_rows(matrix):
    size = lax.axis_size("dp")
    rows, columns = matrix.shape
    mine = bit_of("bal", 1)
    half = columns // 2
    keep = lax.dynamic_slice(matrix, (0, mine * half), (rows, half))
    send = lax.dynamic_slice(matrix, (0, (1 - mine) * half), (rows, half))
    block = added(keep, swap(send, "bal", 1))
    bit = 1
    while bit < size:
        left = size // bit
        block = half_sums(block.reshape(left // 2, 2, rows // size, half), "dp", bit, 1)
        bit *= 2
    block = block.reshape(rows // size, half)
    block = added(block, swap(block, "bal", 2))
    other = swap(block, "bal", 1)
    first = jnp.where(mine == 0, block, other)
    second = jnp.where(mine == 0, other, block)
    return jnp.concatenate([first, second], axis=1).astype(F32)


def summed(block):
    for axis in ("bal", "dp"):
        bit = 1
        while bit < lax.axis_size(axis):
            block = block + swap(block, axis, bit)
            bit *= 2
    return block


def per_device(
    tokens,
    cotangent,
    counts,
    rows,
    cols,
    present,
    slots,
    first_gain,
    first_shift,
    qkv_weight,
    query_bias,
    value_bias,
    out_weight,
    out_bias,
    second_gain,
    second_shift,
    up_weight,
    up_bias,
    down_weight,
    down_bias,
):
    steps, images, length, width = tokens.shape
    hidden = up_weight.shape[1]
    group = lax.axis_size("bal")
    total = steps * images
    vecs = jnp.concatenate(
        [
            first_gain, first_shift, query_bias, jnp.zeros_like(query_bias), value_bias,
            out_bias, second_gain, second_shift, down_bias, up_bias,
            jnp.zeros((7 * width - hidden,), F32),
        ]
    ).reshape(16, width)
    slopes = jnp.exp2(-8.0 * (jnp.arange(16, dtype=F32) + 1.0) / HEADS)

    def exchange(blocks):
        flat = blocks.reshape(group, -1, width)
        return lax.all_to_all(flat, "bal", split_axis=0, concat_axis=0, tiled=True)

    def turn(array):
        return jnp.transpose(array, (0, 2, 1, 3))

    meta, take, cot_send = prepare(
        lax.all_gather(slots, "bal"), counts, present, slots,
        lax.axis_index("bal").astype(jnp.int32).reshape(1), turn(cotangent),
    )
    cot_home = exchange(cot_send).reshape(total, -1, width)
    packed, qkv, att, totals = first_half(meta, slopes, turn(tokens), rows, cols, vecs, qkv_weight)
    y_send, mid_grad, att_grad, up_g, down_g, out_g, vec_two, upb_g = mlp(
        meta, cot_home, att, packed, vecs, out_weight, up_weight, down_weight, length
    )
    y_got = exchange(y_send).reshape(group, steps, -1, width)
    up_rows, down_rows, out_rows = summed_rows(up_g), summed_rows(down_g), summed_rows(out_g)
    vec_two = summed(jnp.concatenate([vec_two[:4].reshape(-1), upb_g[0]]))

    quarter = images
    earlier = ()
    for first in range(0, total, quarter):
        packed_grad = attend_back(
            first, quarter, meta, slopes, qkv, att_grad, totals, rows, cols, earlier
        )
        earlier = (packed_grad,)
    qkv_g, bias_g = qkv_grad(meta, packed_grad, packed, vecs)
    qkv_rows = summed_rows(qkv_g)
    input_grad, vec_one = token_grad(
        meta, packed_grad, packed, mid_grad, vecs, qkv_weight, steps, length, images
    )
    vec_one = summed(
        jnp.concatenate([vec_one[:2].reshape(-1), bias_g[0, :width], bias_g[0, 2 * width :]])
    )

    def vector(array, n):
        return array[n * width : (n + 1) * width]

    return (
        turn(place(take, y_got, length)),
        turn(input_grad),
        vector(vec_one, 0),
        vector(vec_one, 1),
        qkv_rows,
        vector(vec_one, 2),
        vector(vec_one, 3),
        out_rows,
        vector(vec_two, 2),
        vector(vec_two, 0),
        vector(vec_two, 1),
        up_rows,
        vec_two[4 * width :],
        down_rows,
        vector(vec_two, 3),
    )


def solution(mesh):
    images = P(None, ("dp", "bal"), None, None)
    spots = P(None, ("dp", "bal"), None)
    flags = P(None, ("dp", "bal"))
    matrix = P("dp", None)
    return jax.shard_map(
        per_device,
        mesh=mesh,
        in_specs=(images, images, flags, spots, spots, flags, flags) + (P(),) * 13,
        out_specs=(
            images, images, P(), P(), matrix, P(), P(), matrix, P(), P(), P(), matrix, P(), matrix, P(),
        ),
        check_vma=False,
    )
```

```python
import functools
import math

import jax
import jax.numpy as jnp
from jax import lax
from jax.experimental import pallas as pl
from jax.experimental.pallas import tpu as pltpu
from jax.sharding import PartitionSpec as P

HEADS = 12
TILE = 256
WINDOW = 256
FAR = 1e12
EPS = 1e-06
BLOCKS = 8
VMEM_LIMIT = 60 * 1024 * 1024

F32 = jnp.float32
BF16 = jnp.bfloat16

OFF, CNT, IMG, LIVE, PEER, SPOT, MISC = 0, 16, 32, 48, 64, 80, 96
N_FWD, N_BWD, ROWS_FWD, ROWS_BWD, N_LIVE, CORE = range(MISC, MISC + 6)
PLACES = 128

GAIN_ONE, SHIFT_ONE, QKV_B, OUT_B, GAIN_TWO, SHIFT_TWO, DOWN_B, UP_B = 0, 1, 2, 5, 6, 7, 8, 9
VECTORS = (GAIN_ONE, SHIFT_ONE, QKV_B, QKV_B + 2, OUT_B, GAIN_TWO, SHIFT_TWO, DOWN_B, UP_B)


def dot(a, b):
    return jnp.dot(a, b, preferred_element_type=F32)


def dot_bt(a, b):
    return lax.dot_general(a, b, (((1,), (1,)), ((), ())), preferred_element_type=F32)


def turned(block):
    size = 256 if block.shape[1] % 256 == 0 else 128
    row = lax.broadcasted_iota(jnp.int32, (size, size), 0)
    col = lax.broadcasted_iota(jnp.int32, (size, size), 1)
    eye = jnp.where(row == col, 1.0, 0.0).astype(BF16)
    parts = [
        dot_bt(eye, block[:, start : start + size]).astype(BF16)
        for start in range(0, block.shape[1], size)
    ]
    return parts[0] if len(parts) == 1 else jnp.concatenate(parts, axis=0)


def layer_norm(values):
    average = jnp.mean(values, axis=-1, keepdims=True)
    centred = values - average
    spread = jnp.mean(centred * centred, axis=-1, keepdims=True)
    inverse = lax.rsqrt(spread + EPS)
    return centred * inverse, inverse


def norm_back(out_grad, gain, unit, inverse):
    e = out_grad * gain
    mean_e = jnp.mean(e, axis=-1, keepdims=True)
    mean_eu = jnp.mean(e * unit, axis=-1, keepdims=True)
    return inverse * (e - mean_e - unit * mean_eu)


def gelu_parts(u):
    size = jnp.abs(u)
    t = 1.0 / (1.0 + (0.3275911 * math.sqrt(0.5)) * size)
    bell = jnp.exp(-0.5 * (u * u))
    poly = t * (
        0.5 * 0.254829592
        + t
        * (
            0.5 * -0.284496736
            + t * (0.5 * 1.421413741 + t * (0.5 * -1.453152027 + t * (0.5 * 1.061405429)))
        )
    )
    tail = poly * bell
    phi_sum = jnp.where(u >= 0, 1.0 - tail, tail)
    return phi_sum, u * bell * (1.0 / math.sqrt(2.0 * math.pi))


def row_ids(start, rows):
    return start + lax.broadcasted_iota(jnp.int32, (rows, 1), 0)


def aligned(value, step=16):
    return pl.multiple_of(value, step)


def by_count(count, run):
    @pl.when(count <= 128)
    def _():
        run(128, 128)

    @pl.when(jnp.logical_and(count > 128, count <= 192))
    def _():
        run(192, 256)

    @pl.when(count > 192)
    def _():
        run(256, 256)


def distances(rows, cols, which, count, keys, queries):
    mine = lax.broadcasted_iota(jnp.int32, rows.shape, 0) == which
    row = jnp.sum(jnp.where(mine, rows, 0).astype(F32), axis=0, keepdims=True)
    col = jnp.sum(jnp.where(mine, cols, 0).astype(F32), axis=0, keepdims=True)
    spots = jnp.concatenate([row, col, jnp.zeros((6, row.shape[1]), F32)], axis=0)
    spots = jnp.concatenate([spots, jnp.zeros((8, WINDOW - row.shape[1]), F32)], axis=1)
    eye = jnp.where(
        lax.broadcasted_iota(jnp.int32, (keys, WINDOW), 0)
        == lax.broadcasted_iota(jnp.int32, (keys, WINDOW), 1),
        1.0,
        0.0,
    ).astype(BF16)
    turned_spots = dot_bt(eye, spots.astype(BF16))
    down = turned_spots[:, 0:1] - spots[0:1, :queries]
    across = turned_spots[:, 1:2] - spots[1:2, :queries]
    far = row_ids(0, keys) >= count
    return jnp.where(far, FAR, jnp.sqrt(down * down + across * across))


def prepare_kernel(every, counts, present, slots, me, cot, *rest):
    *lines, meta, take, vecs, send = rest
    step = pl.program_id(0)
    steps, length, images, width = pl.num_programs(0), cot.shape[1], cot.shape[2], cot.shape[3]
    group = every.shape[0]

    @pl.when(step == 0)
    def _():
        def fill(live):
            def body(img, carry):
                spot, off = carry
                m, i = img // images, img % images
                count = counts[m, i]
                mine = present[m, i] == live

                @pl.when(mine)
                def _():
                    meta[OFF + spot] = off
                    meta[CNT + spot] = count
                    meta[IMG + spot] = img
                    meta[LIVE + spot] = live
                    meta[PEER + spot] = slots[m, i] // images * steps + m
                    meta[SPOT + img] = spot

                padded = (count + 15) // 16 * 16
                return spot + mine.astype(jnp.int32), off + jnp.where(mine, padded, 0)

            return body

        meta[CORE] = me[0] % 2
        vecs[...] = jnp.zeros_like(vecs)
        for row, values in zip(VECTORS, lines):
            for n in range(values.shape[0] // width):
                piece = values[n * width : (n + 1) * width]
                vecs[row + n : row + n + 1, :] = piece.reshape(1, width)
        zero = jnp.int32(0)
        total = counts.shape[0] * images
        spot, off = lax.fori_loop(0, total, fill(1), (zero, zero))
        meta[N_LIVE] = spot
        meta[ROWS_BWD] = off
        meta[N_BWD] = (off + TILE - 1) // TILE
        spot, off = lax.fori_loop(0, total, fill(0), (spot, off))
        meta[ROWS_FWD] = off
        meta[N_FWD] = (off + TILE - 1) // TILE

        def land(n, carry):
            a, m, i = n // total, n % total // images, n % images
            slot = every[a, m, i]

            @pl.when(slot // images == me[0])
            def _():
                take[m * images + slot % images] = a * steps + m

            return carry

        lax.fori_loop(0, group * total, land, 0)

    block = jnp.swapaxes(cot[0].astype(F32), 0, 1).astype(BF16)
    for place in range(images):
        peer = take[step * images + place] // steps
        send[peer, 0, :length, :] = block[place]


def place_kernel(take, got, out):
    step = pl.program_id(0)
    length, images = out.shape[1], out.shape[2]
    steps = pl.num_programs(0)
    parts = [
        got[take[step * images + place] // steps, 0, :length, :].astype(F32)
        for place in range(images)
    ]
    out[0] = jnp.swapaxes(jnp.stack(parts, axis=0), 0, 1).astype(out.dtype)


def attend_kernel(
    meta, slopes, tokens, rows_in, cols_in, vecs, weight,
    packed_out, qkv_out, att_out, total_out,
    held, packed, qkv, att, gaps, sem_packed, sem_qkv, sem_att,
):
    length, per, width = tokens.shape[1], tokens.shape[2], tokens.shape[3]
    images = held.shape[0]
    steps = images // per
    now = pl.program_id(0)

    def tile_copy(which, t):
        src, dst, sem = (
            (packed, packed_out, sem_packed),
            (qkv, qkv_out, sem_qkv),
            (att, att_out, sem_att),
        )[which]
        rows = pl.ds(aligned(t * TILE, TILE), TILE)
        return pltpu.make_async_copy(src.at[rows], dst.at[rows], sem.at[t])

    @pl.when(now == 0)
    def _():
        packed[...] = jnp.zeros_like(packed)

    @pl.when(now < steps)
    def _():
        block = jnp.swapaxes(tokens[0].astype(F32), 0, 1).astype(BF16)
        for i in range(per):
            held[now * per + i, :length, :] = block[i]

    step = now - steps

    @pl.when(jnp.logical_and(step >= 0, step < images))
    def _():
        off = aligned(meta[OFF + step])
        packed[pl.ds(off, length), :] = held[meta[IMG + step], :length, :]
        begin = off // TILE
        after = aligned(meta[OFF + jnp.minimum(step + 1, images - 1)])
        end = jnp.where(step == images - 1, meta[N_FWD], after // TILE)

        def project(t, carry):
            rows = pl.ds(aligned(t * TILE, TILE), TILE)
            unit, _ = layer_norm(packed[rows, :].astype(F32))
            hidden = (
                unit * vecs[GAIN_ONE : GAIN_ONE + 1] + vecs[SHIFT_ONE : SHIFT_ONE + 1]
            ).astype(BF16)
            for part in range(3):
                cols = slice(part * width, (part + 1) * width)
                bias = vecs[QKV_B + part : QKV_B + part + 1]
                qkv[rows, cols] = (dot(hidden, weight[:, cols]) + bias).astype(BF16)
            tile_copy(0, t).start()
            tile_copy(1, t).start()
            return carry

        lax.fori_loop(begin, end, project, 0)

    @pl.when(step >= images)
    def _():
        spot = step - images
        off = aligned(meta[OFF + spot])
        count = meta[CNT + spot]

        def run(keys, queries):
            which = meta[IMG + spot] % per
            gaps[:keys, :queries] = distances(rows_in[0], cols_in[0], which, count, keys, queries)
            key_seen = row_ids(0, keys) < count
            query_seen = row_ids(0, queries) < count
            left = lax.broadcasted_iota(jnp.int32, (queries, 128), 1) < 64

            def pair(p, carry):
                lanes = aligned(p * 128, 128)
                q2 = qkv[pl.ds(off, queries), pl.ds(lanes, 128)] * 0.125
                k2 = qkv[pl.ds(off, keys), pl.ds(width + lanes, 128)]
                v2 = qkv[pl.ds(off, keys), pl.ds(2 * width + lanes, 128)]
                q2 = jnp.where(query_seen, q2, jnp.zeros_like(q2))
                k2 = jnp.where(key_seen, k2, jnp.zeros_like(k2))
                v2 = jnp.where(key_seen, v2, jnp.zeros_like(v2))
                v2t = turned(v2)
                outs = []
                for half in range(2):
                    head = 2 * p + half
                    mine = left if half == 0 else jnp.logical_not(left)
                    qh = jnp.where(mine, q2, jnp.zeros_like(q2))
                    scores = dot_bt(k2, qh) - slopes[head] * gaps[:keys, :queries]
                    top = jnp.max(scores, axis=0, keepdims=True)
                    terms = jnp.exp(scores - top)
                    total = jnp.sum(terms, axis=0, keepdims=True)
                    heads_out = dot(v2t[half * 64 : half * 64 + 64], terms.astype(BF16))
                    outs.append((heads_out * (1.0 / total)).astype(BF16))
                    total_out[0, p, half : half + 1, :queries] = top + jnp.log(total)
                both = jnp.concatenate(outs, axis=0)
                att[pl.ds(off, queries), pl.ds(lanes, 128)] = turned_back(both)
                return carry

            lax.fori_loop(0, HEADS // 2, pair, 0)

        by_count(count, run)
        after = meta[OFF + jnp.minimum(spot + 1, images - 1)]
        end = jnp.where(spot == images - 1, meta[N_FWD], after // TILE)

        def send(t, carry):
            tile_copy(2, t).start()
            return carry

        lax.fori_loop(off // TILE, end, send, 0)

    @pl.when(now == pl.num_programs(0) - 1)
    def _():
        def finish(t, carry):
            for which in range(3):
                tile_copy(which, t).wait()
            return carry

        lax.fori_loop(0, meta[N_FWD], finish, 0)


def turned_back(block):
    size = block.shape[1]
    parts = []
    for start in range(0, size, 128):
        row = lax.broadcasted_iota(jnp.int32, (128, size), 0)
        col = lax.broadcasted_iota(jnp.int32, (128, size), 1)
        eye = jnp.where(row + start == col, 1.0, 0.0).astype(BF16)
        parts.append(dot_bt(eye, block).astype(BF16))
    return parts[0] if len(parts) == 1 else jnp.concatenate(parts, axis=0)


def mlp_kernel(
    chunk, length, meta, cot_in, att_in, tokens_in,
    vecs, out_w, up_w, down_w,
    y_send, mid_grad, att_grad, keep_g, send_g, vec_g, upb_g,
    up_b, cot, y_all, up_acc, down_acc, out_acc, h2_s, h2t_s, dzt_s, z_s, g_s, stage, spare, sem,
):
    step = pl.program_id(0)
    tiles = cot.shape[0] // TILE - WINDOW // TILE
    images = (pl.num_programs(0) - tiles) // 2
    width = cot_in.shape[2]
    hidden = up_w.shape[1]
    out_b, gain, shift, down_b = [
        vecs.at[pl.ds(n, 1)] for n in (OUT_B, GAIN_TWO, SHIFT_TWO, DOWN_B)
    ]

    @pl.when(step == 0)
    def _():
        up_acc[...] = jnp.zeros_like(up_acc)
        down_acc[...] = jnp.zeros_like(down_acc)
        out_acc[...] = jnp.zeros_like(out_acc)
        vec_g[...] = jnp.zeros_like(vec_g)
        upb_g[...] = jnp.zeros_like(upb_g)
        for n in range(hidden // width):
            up_b[0:1, n * width : (n + 1) * width] = vecs[UP_B + n : UP_B + n + 1, :]

    @pl.when(jnp.logical_and(step < images, step < meta[N_LIVE]))
    def _():
        spot = step
        off = aligned(meta[OFF + spot])
        seen = row_ids(0, length) < meta[CNT + spot]
        block = cot_in[0, :length, :]
        edge = (length - 1) // 16 * 16
        cot[pl.ds(aligned(off + edge), 16), :] = jnp.zeros((16, width), BF16)
        cot[pl.ds(off, length), :] = jnp.where(seen, block, jnp.zeros_like(block))

    def run_tile(t, both):
        rows = aligned(t * TILE, TILE)
        ids = row_ids(rows, TILE)
        att = att_in[...]
        att = jnp.where(ids < meta[ROWS_FWD], att, jnp.zeros_like(att))
        mid = tokens_in[...].astype(F32) + (dot(att, out_w[...]) + out_b[...])
        unit, inverse = layer_norm(mid)
        h2 = (unit * gain[...] + shift[...]).astype(BF16)
        h2_s[...] = h2
        z_s[...] = mid + down_b[...]
        if both:
            dz = cot[pl.ds(rows, TILE), :]
            dz = jnp.where(ids < meta[ROWS_BWD], dz, jnp.zeros_like(dz))
            h2t_s[...] = turned(h2)
            dzt_s[...] = turned(dz)
            g_s[...] = jnp.zeros_like(g_s)

        def part(c, carry):
            cols = pl.ds(aligned(c * chunk, chunk), chunk)
            pre = dot(h2_s[...], up_w[:, cols]) + up_b[0:1, cols]
            share, slope = gelu_parts(pre)
            act = (pre * share).astype(BF16)
            z_s[...] += dot(act, down_w[cols, :])
            if both:
                pre_g = (dot_bt(dz, down_w[cols, :]) * (share + slope)).astype(BF16)
                up_acc[:, cols] += dot(h2t_s[...], pre_g)
                down_acc[:, cols] += dot(dzt_s[...], act)
                upb_g[0:1, cols] += jnp.sum(pre_g.astype(F32), axis=0, keepdims=True)
                g_s[...] += dot_bt(pre_g, up_w[:, cols])
            return carry

        lax.fori_loop(0, hidden // chunk, part, 0)
        y_all[pl.ds(rows, TILE), :] = z_s[...].astype(BF16)
        if both:
            dzf = dz.astype(F32)
            g2 = g_s[...]
            dmid = dzf + norm_back(g2, gain[...], unit, inverse)
            branch = dmid.astype(BF16)
            mid_grad[...] = dmid
            att_grad[...] = dot_bt(branch, out_w[...]).astype(BF16)
            out_acc[...] += dot(turned(att), branch)
            vec_g[0:1, :] += jnp.sum(g2 * unit, axis=0, keepdims=True)
            vec_g[1:2, :] += jnp.sum(g2, axis=0, keepdims=True)
            vec_g[2:3, :] += jnp.sum(branch.astype(F32), axis=0, keepdims=True)
            vec_g[3:4, :] += jnp.sum(dzf, axis=0, keepdims=True)

    tile = step - images

    @pl.when(jnp.logical_and(tile >= 0, tile < meta[N_BWD]))
    def _():
        run_tile(tile, True)

    @pl.when(
        jnp.logical_and(
            jnp.logical_and(tile >= meta[N_BWD], tile >= 0),
            jnp.logical_and(tile < meta[N_FWD], tile < tiles),
        )
    )
    def _():
        run_tile(tile, False)

    @pl.when(step == images + tiles)
    def _():
        share = width // BLOCKS
        long = hidden // BLOCKS
        half = long // 2
        jobs = []
        for n in range(BLOCKS):
            for c in range(hidden // width):
                jobs.append(("up", n, c // 2, c % 2 * share, share, c))
            for h in range(2):
                jobs.append(("down", n, h, 2 * share, half, 0))
                jobs.append(("out", n, h, 2 * share + half, share // 2, 0))

        def copy(n, target):
            _, block, _, at, rows, _ = jobs[n]
            src = stage.at[n % 2, pl.ds(0, rows)]
            return pltpu.make_async_copy(src, target.at[block, pl.ds(at, rows)], sem.at[n % 2])

        def start(n):
            h = jobs[n][2]

            @pl.when(meta[CORE] == h)
            def _():
                copy(n, keep_g).start()

            @pl.when(meta[CORE] != h)
            def _():
                copy(n, send_g).start()

        for n, (kind, block, h, _, rows, c) in enumerate(jobs):
            if n >= 2:
                copy(n - 2, keep_g).wait()
            if kind == "up":
                piece = up_acc[block * share : (block + 1) * share, c * width : (c + 1) * width]
                stage[n % 2, :rows, :] = piece.astype(BF16)
            elif kind == "out":
                first = block * share + h * rows
                stage[n % 2, :rows, :] = out_acc[first : first + rows, :].astype(BF16)
            elif h == 0:
                for low in range(0, width, 256):
                    cols = slice(low, low + 256)
                    piece = down_acc[cols, block * long : (block + 1) * long].astype(BF16)
                    flipped = turned(piece)
                    stage[n % 2, :half, cols] = flipped[:half]
                    spare[:, cols] = flipped[half:]
            else:
                stage[n % 2, :half, :] = spare[...]
            start(n)
        copy(len(jobs) - 2, keep_g).wait()
        copy(len(jobs) - 1, keep_g).wait()

    spot = step - images - tiles

    @pl.when(spot >= 0)
    def _():
        off = aligned(meta[OFF + spot])
        seen = row_ids(0, length) < meta[CNT + spot]
        block = y_all[pl.ds(off, length), :]
        y_send[0, :length, :] = jnp.where(seen, block, jnp.zeros_like(block))


def attend_back_kernel(
    first, per, meta, slopes, qkv, att_grad, totals, rows_in, cols_in, *rest
):
    grads_out, grads, gaps, sem = rest[-4:]
    step = pl.program_id(0)
    width = att_grad.shape[1]
    spot = first + step
    live = spot < meta[N_LIVE]
    slot = step % 2

    def copy(at):
        rows = pl.ds(aligned(meta[OFF + first + at]), WINDOW)
        return pltpu.make_async_copy(grads.at[at % 2], grads_out.at[rows], sem.at[at % 2])

    @pl.when(live)
    def _():
        count = meta[CNT + spot]

        def run(keys, queries):
            which = meta[IMG + spot] % per
            gaps[:keys, :queries] = distances(rows_in[0], cols_in[0], which, count, keys, queries)
            key_seen = row_ids(0, keys) < count
            query_seen = row_ids(0, queries) < count
            left = lax.broadcasted_iota(jnp.int32, (queries, 128), 1) < 64

            def pair(p, carry):
                lanes = aligned(p * 128, 128)
                q2 = qkv[:queries, pl.ds(lanes, 128)] * 0.125
                k2 = qkv[:keys, pl.ds(width + lanes, 128)]
                v2 = qkv[:keys, pl.ds(2 * width + lanes, 128)]
                o2 = att_grad[:queries, pl.ds(lanes, 128)]
                q2 = jnp.where(query_seen, q2, jnp.zeros_like(q2))
                o2 = jnp.where(query_seen, o2, jnp.zeros_like(o2))
                k2 = jnp.where(key_seen, k2, jnp.zeros_like(k2))
                v2 = jnp.where(key_seen, v2, jnp.zeros_like(v2))
                k2t = turned(k2)
                dq_parts = []
                dk = dv = None
                for half in range(2):
                    head = 2 * p + half
                    mine = left if half == 0 else jnp.logical_not(left)
                    qh = jnp.where(mine, q2, jnp.zeros_like(q2))
                    oh = jnp.where(mine, o2, jnp.zeros_like(o2))
                    scores = dot_bt(k2, qh) - slopes[head] * gaps[:keys, :queries]
                    probs = jnp.exp(scores - totals[0, p, half : half + 1, :queries])
                    prob_g = dot_bt(v2, oh)
                    inner = jnp.sum(probs * prob_g, axis=0, keepdims=True)
                    score_g = (probs * (prob_g - inner)).astype(BF16)
                    dv_part = dot(probs.astype(BF16), oh)
                    dk_part = dot(score_g, qh)
                    dq_parts.append(
                        (dot(k2t[half * 64 : half * 64 + 64], score_g) * 0.125).astype(BF16)
                    )
                    dk = dk_part if dk is None else dk + dk_part
                    dv = dv_part if dv is None else dv + dv_part
                dq = turned_back(jnp.concatenate(dq_parts, axis=0))
                grads[slot, :queries, pl.ds(lanes, 128)] = dq
                grads[slot, :keys, pl.ds(width + lanes, 128)] = dk.astype(BF16)
                grads[slot, :keys, pl.ds(2 * width + lanes, 128)] = dv.astype(BF16)
                return carry

            lax.fori_loop(0, HEADS // 2, pair, 0)

        by_count(count, run)

        @pl.when(step > 0)
        def _():
            copy(step - 1).wait()

        copy(step).start()

        @pl.when(jnp.logical_or(step == pl.num_programs(0) - 1, spot == meta[N_LIVE] - 1))
        def _():
            copy(step).wait()


def qkv_grad_kernel(meta, packed_grad, tokens, vecs, keep_g, send_g, bias_g, acc, stage, sem):
    tile = pl.program_id(0)
    width = tokens.shape[1]

    @pl.when(tile == 0)
    def _():
        acc[...] = jnp.zeros_like(acc)
        bias_g[...] = jnp.zeros_like(bias_g)

    @pl.when(tile < meta[N_BWD])
    def _():
        ids = row_ids(tile * TILE, TILE)
        unit, _ = layer_norm(tokens[...].astype(F32))
        hidden = (
            unit * vecs[GAIN_ONE : GAIN_ONE + 1] + vecs[SHIFT_ONE : SHIFT_ONE + 1]
        ).astype(BF16)
        hidden_t = turned(hidden)
        for part in range(3):
            cols = slice(part * width, (part + 1) * width)
            block = packed_grad[:, cols]
            block = jnp.where(ids < meta[ROWS_BWD], block, jnp.zeros_like(block))
            acc[:, cols] += dot(hidden_t, block)
            bias_g[0:1, cols] += jnp.sum(block.astype(F32), axis=0, keepdims=True)

    @pl.when(tile == pl.num_programs(0) - 1)
    def _():
        rows = width // BLOCKS // 2
        jobs = [(n, h, c) for n in range(BLOCKS) for h in range(2) for c in range(3)]

        def copy(n, target):
            block, _, c = jobs[n]
            return pltpu.make_async_copy(
                stage.at[n % 2], target.at[block, pl.ds(c * rows, rows)], sem.at[n % 2]
            )

        def start(n):
            h = jobs[n][1]

            @pl.when(meta[CORE] == h)
            def _():
                copy(n, keep_g).start()

            @pl.when(meta[CORE] != h)
            def _():
                copy(n, send_g).start()

        for n, (block, h, c) in enumerate(jobs):
            if n >= 2:
                copy(n - 2, keep_g).wait()
            first = (2 * block + h) * rows
            piece = acc[first : first + rows, c * width : (c + 1) * width]
            stage[n % 2] = piece.astype(BF16)
            start(n)
        copy(len(jobs) - 2, keep_g).wait()
        copy(len(jobs) - 1, keep_g).wait()


def token_grad_kernel(meta, packed_grad, tokens, mid_grad, vecs, weight, out, vec_g, held):
    step = pl.program_id(0)
    tiles = held.shape[0] // TILE - WINDOW // TILE
    length, images = out.shape[1], out.shape[2]

    @pl.when(step == 0)
    def _():
        vec_g[...] = jnp.zeros_like(vec_g)

    @pl.when(jnp.logical_and(step < tiles, step < meta[N_BWD]))
    def _():
        rows = aligned(step * TILE, TILE)
        ids = row_ids(rows, TILE)
        unit, inverse = layer_norm(tokens[...].astype(F32))
        block = packed_grad[...]
        block = jnp.where(ids < meta[ROWS_BWD], block, jnp.zeros_like(block))
        g1 = dot_bt(block, weight[...])
        back = norm_back(g1, vecs[GAIN_ONE : GAIN_ONE + 1], unit, inverse)
        held[pl.ds(rows, TILE), :] = mid_grad[...] + back
        vec_g[0:1, :] += jnp.sum(g1 * unit, axis=0, keepdims=True)
        vec_g[1:2, :] += jnp.sum(g1, axis=0, keepdims=True)

    @pl.when(step >= tiles)
    def _():
        parts = []
        for i in range(images):
            spot = meta[SPOT + (step - tiles) * images + i]
            off = aligned(meta[OFF + spot])
            limit = meta[CNT + spot] * meta[LIVE + spot]
            block = held[pl.ds(off, length), :]
            parts.append(jnp.where(row_ids(0, length) < limit, block, 0.0))
        out[0] = jnp.swapaxes(jnp.stack(parts, axis=0), 0, 1)


def whole(*shape):
    return pl.BlockSpec(shape, lambda *_: (0,) * len(shape), pipeline_mode=pl.Buffered(1))


def params():
    return pltpu.CompilerParams(vmem_limit_bytes=VMEM_LIMIT)


def small():
    return pl.BlockSpec(memory_space=pltpu.SMEM)


def prepare(every, counts, present, slots, me, cotangent, *vectors):
    steps, length, images, width = cotangent.shape
    group = every.shape[0]
    padded = (length + 7) // 8 * 8
    return pl.pallas_call(
        prepare_kernel,
        out_shape=(
            jax.ShapeDtypeStruct((PLACES,), jnp.int32),
            jax.ShapeDtypeStruct((steps * images,), jnp.int32),
            jax.ShapeDtypeStruct((16, width), F32),
            jax.ShapeDtypeStruct((group, steps, padded, width), BF16),
        ),
        grid=(steps,),
        in_specs=[small()] * 5
        + [pl.BlockSpec((1, length, images, width), lambda m: (m, 0, 0, 0))]
        + [whole(*vector.shape) for vector in vectors],
        out_specs=[
            small(),
            small(),
            whole(16, width),
            pl.BlockSpec((group, 1, padded, width), lambda m: (0, m, 0, 0)),
        ],
        compiler_params=params(),
    )(every, counts, present, slots, me, cotangent, *vectors)


def place(take, got, length):
    group, steps, padded, width = got.shape
    return pl.pallas_call(
        place_kernel,
        out_shape=jax.ShapeDtypeStruct((steps, length, group, width), BF16),
        grid=(steps,),
        in_specs=[small(), pl.BlockSpec((group, 1, padded, width), lambda m: (0, m, 0, 0))],
        out_specs=pl.BlockSpec((1, length, group, width), lambda m: (m, 0, 0, 0)),
        compiler_params=params(),
    )(take, got)


def first_half(meta, slopes, tokens, rows, cols, vecs, weight):
    steps, length, per, width = tokens.shape
    images = steps * per
    tiles = -(-images * ((length + 15) // 16 * 16) // TILE)
    total = tiles * TILE + WINDOW
    spots = pl.BlockSpec(
        (1, per, length),
        lambda s, meta, slopes: (meta[IMG + jnp.maximum(s - steps - images, 0)] // per, 0, 0),
    )
    return pl.pallas_call(
        attend_kernel,
        out_shape=(
            jax.ShapeDtypeStruct((total, width), BF16),
            jax.ShapeDtypeStruct((total, 3 * width), BF16),
            jax.ShapeDtypeStruct((total, width), BF16),
            jax.ShapeDtypeStruct((images, HEADS // 2, 8, WINDOW), F32),
        ),
        grid_spec=pltpu.PrefetchScalarGridSpec(
            num_scalar_prefetch=2,
            grid=(steps + 2 * images,),
            in_specs=[
                pl.BlockSpec(
                    (1, length, per, width),
                    lambda s, meta, slopes: (jnp.minimum(s, steps - 1), 0, 0, 0),
                ),
                spots,
                spots,
                whole(*vecs.shape),
                whole(width, 3 * width),
            ],
            out_specs=[
                pl.BlockSpec(memory_space=pl.ANY),
                pl.BlockSpec(memory_space=pl.ANY),
                pl.BlockSpec(memory_space=pl.ANY),
                pl.BlockSpec(
                    (1, HEADS // 2, 8, WINDOW),
                    lambda s, meta, slopes: (jnp.maximum(s - steps - images, 0), 0, 0, 0),
                ),
            ],
            scratch_shapes=[
                pltpu.VMEM((images, (length + 15) // 16 * 16, width), BF16),
                pltpu.VMEM((total, width), BF16),
                pltpu.VMEM((total, 3 * width), BF16),
                pltpu.VMEM((total, width), BF16),
                pltpu.VMEM((WINDOW, WINDOW), F32),
                pltpu.SemaphoreType.DMA((tiles,)),
                pltpu.SemaphoreType.DMA((tiles,)),
                pltpu.SemaphoreType.DMA((tiles,)),
            ],
        ),
        compiler_params=params(),
        cost_estimate=cost(40),
    )(meta, slopes, tokens, rows, cols, vecs, weight)


def mlp(meta, cot, att, packed, vecs, out_w, up_w, down_w, length):
    images, padded, width = cot.shape
    rows = packed.shape[0]
    tiles = (rows - WINDOW) // TILE
    hidden = up_w.shape[1]
    parcel = (2 * width + hidden // 2 + width // 2) // BLOCKS
    last = images - 1

    def fwd_tile(s, meta):
        return (jnp.clip(s - images, 0, meta[N_FWD] - 1), 0)

    def bwd_tile(s, meta):
        return (jnp.clip(s - images, 0, jnp.maximum(meta[N_BWD] - 1, 0)), 0)

    return pl.pallas_call(
        functools.partial(mlp_kernel, 512, length),
        out_shape=(
            jax.ShapeDtypeStruct((images, padded, width), BF16),
            jax.ShapeDtypeStruct((rows, width), F32),
            jax.ShapeDtypeStruct((rows, width), BF16),
            jax.ShapeDtypeStruct((BLOCKS, parcel, width), BF16),
            jax.ShapeDtypeStruct((BLOCKS, parcel, width), BF16),
            jax.ShapeDtypeStruct((8, width), F32),
            jax.ShapeDtypeStruct((8, hidden), F32),
        ),
        grid_spec=pltpu.PrefetchScalarGridSpec(
            num_scalar_prefetch=1,
            grid=(2 * images + tiles,),
            in_specs=[
                pl.BlockSpec(
                    (1, padded, width), lambda s, meta: (meta[PEER + jnp.minimum(s, last)], 0, 0)
                ),
                pl.BlockSpec((TILE, width), fwd_tile),
                pl.BlockSpec((TILE, width), fwd_tile),
                whole(*vecs.shape),
                whole(width, width),
                whole(width, hidden),
                whole(hidden, width),
            ],
            out_specs=[
                pl.BlockSpec(
                    (1, padded, width),
                    lambda s, meta: (meta[PEER + jnp.clip(s - images - tiles, 0, last)], 0, 0),
                ),
                pl.BlockSpec((TILE, width), bwd_tile),
                pl.BlockSpec((TILE, width), bwd_tile),
                pl.BlockSpec(memory_space=pl.ANY),
                pl.BlockSpec(memory_space=pl.ANY),
                whole(8, width),
                whole(8, hidden),
            ],
            scratch_shapes=[
                pltpu.VMEM((8, hidden), F32),
                pltpu.VMEM((rows, width), BF16),
                pltpu.VMEM((rows, width), BF16),
                pltpu.VMEM((width, hidden), F32),
                pltpu.VMEM((width, hidden), F32),
                pltpu.VMEM((width, width), F32),
                pltpu.VMEM((TILE, width), BF16),
                pltpu.VMEM((width, TILE), BF16),
                pltpu.VMEM((width, TILE), BF16),
                pltpu.VMEM((TILE, width), F32),
                pltpu.VMEM((TILE, width), F32),
                pltpu.VMEM((2, hidden // BLOCKS // 2, width), BF16),
                pltpu.VMEM((hidden // BLOCKS // 2, width), BF16),
                pltpu.SemaphoreType.DMA((2,)),
            ],
        ),
        compiler_params=params(),
        cost_estimate=cost(110),
    )(meta, cot, att, packed, vecs, out_w, up_w, down_w)


def attend_back(first, count, expected, meta, slopes, qkv, att_grad, totals, rows_in, cols_in, earlier):
    total, wide = qkv.shape
    width = wide // 3
    per, length = rows_in.shape[1:]

    def spot_of(s, meta):
        return jnp.clip(first + s, 0, jnp.maximum(meta[N_LIVE] - 1, 0))

    def by_offset(s, meta, slopes):
        return (aligned(meta[OFF + spot_of(s, meta)]), 0)

    spots = pl.BlockSpec(
        (1, per, length),
        lambda s, meta, slopes: (meta[IMG + spot_of(s, meta)] // per, 0, 0),
    )
    anywhere = pl.BlockSpec(memory_space=pl.ANY)
    return pl.pallas_call(
        functools.partial(attend_back_kernel, first, per),
        out_shape=jax.ShapeDtypeStruct((total, wide), BF16),
        grid_spec=pltpu.PrefetchScalarGridSpec(
            num_scalar_prefetch=2,
            grid=(count,),
            in_specs=[
                pl.BlockSpec((pl.Element(WINDOW), pl.Element(wide)), by_offset),
                pl.BlockSpec((pl.Element(WINDOW), pl.Element(width)), by_offset),
                pl.BlockSpec(
                    (1, HEADS // 2, 8, WINDOW),
                    lambda s, meta, slopes: (spot_of(s, meta), 0, 0, 0),
                ),
                spots,
                spots,
            ]
            + [anywhere] * len(earlier),
            out_specs=anywhere,
            scratch_shapes=[
                pltpu.VMEM((2, WINDOW, wide), BF16),
                pltpu.VMEM((WINDOW, WINDOW), F32),
                pltpu.SemaphoreType.DMA((2,)),
            ],
        ),
        input_output_aliases={7: 0} if earlier else {},
        compiler_params=params(),
        cost_estimate=cost(expected),
    )(meta, slopes, qkv, att_grad, totals, rows_in, cols_in, *earlier)


def bwd_tile(s, meta):
    return (jnp.clip(s, 0, jnp.maximum(meta[N_BWD] - 1, 0)), 0)


def qkv_grad(meta, packed_grad, packed, vecs):
    rows, width = packed.shape
    parcel = 3 * width // 2 // BLOCKS
    tiles = (rows - WINDOW) // TILE
    return pl.pallas_call(
        qkv_grad_kernel,
        out_shape=(
            jax.ShapeDtypeStruct((BLOCKS, parcel, width), BF16),
            jax.ShapeDtypeStruct((BLOCKS, parcel, width), BF16),
            jax.ShapeDtypeStruct((8, 3 * width), F32),
        ),
        grid_spec=pltpu.PrefetchScalarGridSpec(
            num_scalar_prefetch=1,
            grid=(tiles,),
            in_specs=[
                pl.BlockSpec((TILE, 3 * width), bwd_tile),
                pl.BlockSpec((TILE, width), bwd_tile),
                whole(*vecs.shape),
            ],
            out_specs=[
                pl.BlockSpec(memory_space=pl.ANY),
                pl.BlockSpec(memory_space=pl.ANY),
                whole(8, 3 * width),
            ],
            scratch_shapes=[
                pltpu.VMEM((width, 3 * width), F32),
                pltpu.VMEM((2, width // BLOCKS // 2, width), BF16),
                pltpu.SemaphoreType.DMA((2,)),
            ],
        ),
        compiler_params=params(),
        cost_estimate=cost(15),
    )(meta, packed_grad, packed, vecs)


def token_grad(meta, packed_grad, packed, mid_grad, vecs, weight, steps, length, images):
    rows, width = packed.shape
    tiles = (rows - WINDOW) // TILE
    return pl.pallas_call(
        token_grad_kernel,
        out_shape=(
            jax.ShapeDtypeStruct((steps, length, images, width), F32),
            jax.ShapeDtypeStruct((8, width), F32),
        ),
        grid_spec=pltpu.PrefetchScalarGridSpec(
            num_scalar_prefetch=1,
            grid=(tiles + steps,),
            in_specs=[
                pl.BlockSpec((TILE, 3 * width), bwd_tile),
                pl.BlockSpec((TILE, width), bwd_tile),
                pl.BlockSpec((TILE, width), bwd_tile),
                whole(*vecs.shape),
                whole(width, 3 * width),
            ],
            out_specs=[
                pl.BlockSpec(
                    (1, length, images, width),
                    lambda s, meta: (jnp.clip(s - tiles, 0, steps - 1), 0, 0, 0),
                ),
                whole(8, width),
            ],
            scratch_shapes=[pltpu.VMEM((rows, width), F32)],
        ),
        compiler_params=params(),
        cost_estimate=cost(20),
    )(meta, packed_grad, packed, mid_grad, vecs, weight)


def cost(microseconds):
    return pl.CostEstimate(
        flops=int(microseconds * 1e9), bytes_accessed=int(microseconds * 1e5), transcendentals=0
    )


def swap(block, axis, bit):
    size = lax.axis_size(axis)
    return lax.ppermute(block, axis, [(n, n ^ bit) for n in range(size)])


def bit_of(axis, bit):
    return lax.axis_index(axis) // bit % 2


def added(a, b):
    return (a.astype(F32) + b.astype(F32)).astype(BF16)


def half_sums(block, axis, bit, dim):
    mine = bit_of(axis, bit)
    keep = lax.dynamic_index_in_dim(block, mine, dim, keepdims=False)
    send = lax.dynamic_index_in_dim(block, 1 - mine, dim, keepdims=False)
    return added(keep, swap(send, axis, bit))


def unpacked(mine, other, shapes):
    swapped = bit_of("bal", 1) == 1
    first = jnp.where(swapped, other, mine)
    second = jnp.where(swapped, mine, other)
    lead, width = mine.shape[:-2], mine.shape[-1]
    out, at = [], 0
    for rows, columns, by_rows in shapes:
        wide = columns // width
        part = rows * wide // 2
        if by_rows:
            parts = [
                jnp.concatenate(
                    [half[..., at + c * (rows // 2) : at + (c + 1) * (rows // 2), :] for c in range(wide)],
                    axis=-1,
                )
                for half in (first, second)
            ]
            out.append(jnp.concatenate(parts, axis=-2))
        else:
            parts = [
                half[..., at + c * rows : at + (c + 1) * rows, :]
                for half in (first, second)
                for c in range(wide // 2)
            ]
            out.append(jnp.concatenate(parts, axis=-1))
        at += part
    return [matrix.reshape(lead[:-1] + (-1, matrix.shape[-1])) if lead else matrix for matrix in out]


def spread_sum(keep, send, shapes):
    return [
        lax.psum(lax.psum_scatter(matrix, "dp", scatter_dimension=0, tiled=True), "bal").astype(F32)
        for matrix in unpacked(keep, send, shapes)
    ]


def joined(block, shapes):
    block = added(block, swap(block, "bal", 2))
    return [matrix.astype(F32) for matrix in unpacked(block, swap(block, "bal", 1), shapes)]


def halved(block):
    bit = 1
    while bit < lax.axis_size("dp"):
        block = half_sums(block.reshape((-1, 2) + block.shape[-2:]), "dp", bit, 1)
        bit *= 2
    return block.reshape(block.shape[-2:])


def after(value, *others):
    return lax.optimization_barrier((value,) + others)[0]


def summed(block):
    for axis in ("bal", "dp"):
        bit = 1
        while bit < lax.axis_size(axis):
            block = block + swap(block, axis, bit)
            bit *= 2
    return block


def per_device(
    tokens,
    cotangent,
    counts,
    rows,
    cols,
    present,
    slots,
    first_gain,
    first_shift,
    qkv_weight,
    query_bias,
    value_bias,
    out_weight,
    out_bias,
    second_gain,
    second_shift,
    up_weight,
    up_bias,
    down_weight,
    down_bias,
):
    steps, images, length, width = tokens.shape
    hidden = up_weight.shape[1]
    group = lax.axis_size("bal")
    total = steps * images
    slopes = jnp.exp2(-8.0 * (jnp.arange(16, dtype=F32) + 1.0) / HEADS)

    def exchange(blocks):
        flat = blocks.reshape(group, -1, width)
        return lax.all_to_all(flat, "bal", split_axis=0, concat_axis=0, tiled=True)

    def turn(array):
        return jnp.transpose(array, (0, 2, 1, 3))

    meta, take, vecs, cot_send = prepare(
        lax.all_gather(slots, "bal"), counts, present, slots,
        lax.axis_index("bal").astype(jnp.int32).reshape(1), turn(cotangent),
        first_gain, first_shift, query_bias, value_bias, out_bias, second_gain, second_shift,
        down_bias, up_bias,
    )
    cot_home = exchange(cot_send).reshape(total, -1, width)
    packed, qkv, att, totals = first_half(meta, slopes, turn(tokens), rows, cols, vecs, qkv_weight)
    y_send, mid_grad, att_grad, keep_two, send_two, vec_two, upb_g = mlp(
        meta, cot_home, att, packed, vecs, out_weight, up_weight, down_weight, length
    )
    y_got = exchange(y_send)

    share, long = width // BLOCKS, hidden // BLOCKS
    shapes_two = ((share, hidden, False), (long, width, True), (share, width, True))
    shapes_one = ((share, 3 * width, True),)
    direct = lax.axis_size("dp") == BLOCKS

    def back(first, count, expected, table, earlier):
        return attend_back(
            first, count, expected, table, slopes, qkv, att_grad, totals, rows, cols, earlier
        )

    lead = max(images // 2, 1)
    packed_grad = back(0, lead, 15, meta, ())
    table = meta
    if direct:
        sum_two = added(after(keep_two, packed_grad), swap(send_two, "bal", 1))
        share_two = lax.psum_scatter(sum_two, "dp", scatter_dimension=0, tiled=True)[0]
        table = after(meta, sum_two)
    packed_grad = back(lead, total - lead, 500, table, (packed_grad,))
    keep_one, send_one, bias_g = qkv_grad(after(table, y_got), packed_grad, packed, vecs)
    output = place(after(take, keep_one), y_got.reshape(group, steps, -1, width), length)
    table = after(table, output)
    if direct:
        sum_one = added(keep_one, swap(send_one, "bal", 1))
        table = after(table, sum_one)
    input_grad, vec_one = token_grad(
        table, packed_grad, packed, mid_grad, vecs, qkv_weight, steps, length, images
    )
    if direct:
        (qkv_rows,) = joined(halved(sum_one), shapes_one)
        up_rows, down_rows, out_rows = joined(share_two, shapes_two)
    else:
        (qkv_rows,) = spread_sum(keep_one, send_one, shapes_one)
        up_rows, down_rows, out_rows = spread_sum(keep_two, send_two, shapes_two)
    vectors = summed(
        jnp.concatenate(
            [
                vec_one[:2].reshape(-1), bias_g[0, :width], bias_g[0, 2 * width :],
                vec_two[:4].reshape(-1), upb_g[0],
            ]
        )
    )

    def vector(n):
        return vectors[n * width : (n + 1) * width]

    return (
        turn(output),
        turn(input_grad),
        vector(0),
        vector(1),
        qkv_rows,
        vector(2),
        vector(3),
        out_rows,
        vector(6),
        vector(4),
        vector(5),
        up_rows,
        vectors[8 * width :],
        down_rows,
        vector(7),
    )


def solution(mesh):
    images = P(None, ("dp", "bal"), None, None)
    spots = P(None, ("dp", "bal"), None)
    flags = P(None, ("dp", "bal"))
    matrix = P("dp", None)
    return jax.shard_map(
        per_device,
        mesh=mesh,
        in_specs=(images, images, flags, spots, spots, flags, flags) + (P(),) * 13,
        out_specs=(
            images, images, P(), P(), matrix, P(), P(), matrix, P(), P(), P(), matrix, P(), matrix, P(),
        ),
        check_vma=False,
    )
```

```python
import functools
import math

import jax
import jax.numpy as jnp
from jax import lax
from jax.experimental import pallas as pl
from jax.experimental.pallas import tpu as pltpu
from jax.sharding import PartitionSpec as P

HEADS = 12
TILE = 256
WINDOW = 256
FAR = 1e12
EPS = 1e-06
BLOCKS = 8
CHUNK = 1536
VMEM_LIMIT = 60 * 1024 * 1024

F32 = jnp.float32
BF16 = jnp.bfloat16

OFF, CNT, IMG, LIVE, PEER, SPOT, MISC = 0, 16, 32, 48, 64, 80, 96
N_FWD, N_BWD, ROWS_FWD, ROWS_BWD, N_LIVE, CORE = range(MISC, MISC + 6)
PLACES = 128

GAIN_ONE, SHIFT_ONE, QKV_B, OUT_B, GAIN_TWO, SHIFT_TWO, DOWN_B, UP_B = 0, 1, 2, 5, 6, 7, 8, 9
VECTORS = (GAIN_ONE, SHIFT_ONE, QKV_B, QKV_B + 2, OUT_B, GAIN_TWO, SHIFT_TWO, DOWN_B, UP_B)


def dot(a, b):
    return jnp.dot(a, b, preferred_element_type=F32)


def dot_bt(a, b):
    return lax.dot_general(a, b, (((1,), (1,)), ((), ())), preferred_element_type=F32)


def turned(block):
    size = 256 if block.shape[1] % 256 == 0 else 128
    row = lax.broadcasted_iota(jnp.int32, (size, size), 0)
    col = lax.broadcasted_iota(jnp.int32, (size, size), 1)
    eye = jnp.where(row == col, 1.0, 0.0).astype(BF16)
    parts = [
        dot_bt(eye, block[:, start : start + size]).astype(BF16)
        for start in range(0, block.shape[1], size)
    ]
    return parts[0] if len(parts) == 1 else jnp.concatenate(parts, axis=0)


def layer_norm(values):
    average = jnp.mean(values, axis=-1, keepdims=True)
    centred = values - average
    spread = jnp.mean(centred * centred, axis=-1, keepdims=True)
    inverse = lax.rsqrt(spread + EPS)
    return centred * inverse, inverse


def norm_back(out_grad, gain, unit, inverse):
    e = out_grad * gain
    mean_e = jnp.mean(e, axis=-1, keepdims=True)
    mean_eu = jnp.mean(e * unit, axis=-1, keepdims=True)
    return inverse * (e - mean_e - unit * mean_eu)


def gelu_parts(u):
    size = jnp.abs(u)
    t = 1.0 / (1.0 + (0.3275911 * math.sqrt(0.5)) * size)
    bell = jnp.exp(-0.5 * (u * u))
    poly = t * (
        0.5 * 0.254829592
        + t
        * (
            0.5 * -0.284496736
            + t * (0.5 * 1.421413741 + t * (0.5 * -1.453152027 + t * (0.5 * 1.061405429)))
        )
    )
    tail = poly * bell
    phi_sum = jnp.where(u >= 0, 1.0 - tail, tail)
    return phi_sum, u * bell * (1.0 / math.sqrt(2.0 * math.pi))


def row_ids(start, rows):
    return start + lax.broadcasted_iota(jnp.int32, (rows, 1), 0)


def aligned(value, step=16):
    return pl.multiple_of(value, step)


def by_count(count, run):
    @pl.when(count <= 128)
    def _():
        run(128, 128)

    @pl.when(jnp.logical_and(count > 128, count <= 192))
    def _():
        run(192, 256)

    @pl.when(count > 192)
    def _():
        run(256, 256)


def distances(rows, cols, which, count, keys, queries):
    mine = lax.broadcasted_iota(jnp.int32, rows.shape, 0) == which
    row = jnp.sum(jnp.where(mine, rows, 0).astype(F32), axis=0, keepdims=True)
    col = jnp.sum(jnp.where(mine, cols, 0).astype(F32), axis=0, keepdims=True)
    spots = jnp.concatenate([row, col, jnp.zeros((6, row.shape[1]), F32)], axis=0)
    spots = jnp.concatenate([spots, jnp.zeros((8, WINDOW - row.shape[1]), F32)], axis=1)
    eye = jnp.where(
        lax.broadcasted_iota(jnp.int32, (keys, WINDOW), 0)
        == lax.broadcasted_iota(jnp.int32, (keys, WINDOW), 1),
        1.0,
        0.0,
    ).astype(BF16)
    turned_spots = dot_bt(eye, spots.astype(BF16))
    down = turned_spots[:, 0:1] - spots[0:1, :queries]
    across = turned_spots[:, 1:2] - spots[1:2, :queries]
    far = row_ids(0, keys) >= count
    return jnp.where(far, FAR, jnp.sqrt(down * down + across * across))


def prepare_kernel(every, counts, present, slots, me, cot, *rest):
    *lines, meta, take, vecs, send = rest
    step = pl.program_id(0)
    steps, length, images, width = pl.num_programs(0), cot.shape[1], cot.shape[2], cot.shape[3]
    group = every.shape[0]

    @pl.when(step == 0)
    def _():
        def fill(live):
            def body(img, carry):
                spot, off = carry
                m, i = img // images, img % images
                count = counts[m, i]
                mine = present[m, i] == live

                @pl.when(mine)
                def _():
                    meta[OFF + spot] = off
                    meta[CNT + spot] = count
                    meta[IMG + spot] = img
                    meta[LIVE + spot] = live
                    meta[PEER + spot] = slots[m, i] // images * steps + m
                    meta[SPOT + img] = spot

                padded = (count + 15) // 16 * 16
                return spot + mine.astype(jnp.int32), off + jnp.where(mine, padded, 0)

            return body

        meta[CORE] = me[0] % 2
        vecs[...] = jnp.zeros_like(vecs)
        for row, values in zip(VECTORS, lines):
            for n in range(values.shape[0] // width):
                piece = values[n * width : (n + 1) * width]
                vecs[row + n : row + n + 1, :] = piece.reshape(1, width)
        zero = jnp.int32(0)
        total = counts.shape[0] * images
        spot, off = lax.fori_loop(0, total, fill(1), (zero, zero))
        meta[N_LIVE] = spot
        meta[ROWS_BWD] = off
        meta[N_BWD] = (off + TILE - 1) // TILE
        spot, off = lax.fori_loop(0, total, fill(0), (spot, off))
        meta[ROWS_FWD] = off
        meta[N_FWD] = (off + TILE - 1) // TILE

        def land(n, carry):
            a, m, i = n // total, n % total // images, n % images
            slot = every[a, m, i]

            @pl.when(slot // images == me[0])
            def _():
                take[m * images + slot % images] = a * steps + m

            return carry

        lax.fori_loop(0, group * total, land, 0)

    block = jnp.swapaxes(cot[0].astype(F32), 0, 1).astype(BF16)
    for place in range(images):
        peer = take[step * images + place] // steps
        send[peer, 0, :length, :] = block[place]


def place_kernel(take, got, out):
    step = pl.program_id(0)
    length, images = out.shape[1], out.shape[2]
    steps = pl.num_programs(0)
    parts = [
        got[take[step * images + place] // steps, 0, :length, :].astype(F32)
        for place in range(images)
    ]
    out[0] = jnp.swapaxes(jnp.stack(parts, axis=0), 0, 1).astype(out.dtype)


def attend_kernel(
    meta, slopes, tokens, rows_in, cols_in, vecs, weight,
    packed_out, qkv_out, att_out, total_out,
    held, packed, qkv, att, gaps, sem_packed, sem_qkv, sem_att,
):
    length, per, width = tokens.shape[1], tokens.shape[2], tokens.shape[3]
    images = held.shape[0]
    steps = images // per
    now = pl.program_id(0)

    def tile_copy(which, t):
        src, dst, sem = (
            (packed, packed_out, sem_packed),
            (qkv, qkv_out, sem_qkv),
            (att, att_out, sem_att),
        )[which]
        rows = pl.ds(aligned(t * TILE, TILE), TILE)
        return pltpu.make_async_copy(src.at[rows], dst.at[rows], sem.at[t])

    @pl.when(now == 0)
    def _():
        packed[...] = jnp.zeros_like(packed)

    @pl.when(now < steps)
    def _():
        block = jnp.swapaxes(tokens[0].astype(F32), 0, 1).astype(BF16)
        for i in range(per):
            held[now * per + i, :length, :] = block[i]

    step = now - steps

    @pl.when(jnp.logical_and(step >= 0, step < images))
    def _():
        off = aligned(meta[OFF + step])
        packed[pl.ds(off, length), :] = held[meta[IMG + step], :length, :]
        begin = off // TILE
        after = aligned(meta[OFF + jnp.minimum(step + 1, images - 1)])
        end = jnp.where(step == images - 1, meta[N_FWD], after // TILE)

        def project(t, carry):
            rows = pl.ds(aligned(t * TILE, TILE), TILE)
            unit, _ = layer_norm(packed[rows, :].astype(F32))
            hidden = (
                unit * vecs[GAIN_ONE : GAIN_ONE + 1] + vecs[SHIFT_ONE : SHIFT_ONE + 1]
            ).astype(BF16)
            for part in range(3):
                cols = slice(part * width, (part + 1) * width)
                bias = vecs[QKV_B + part : QKV_B + part + 1]
                qkv[rows, cols] = (dot(hidden, weight[:, cols]) + bias).astype(BF16)
            tile_copy(0, t).start()
            tile_copy(1, t).start()
            return carry

        lax.fori_loop(begin, end, project, 0)

    @pl.when(step >= images)
    def _():
        spot = step - images
        off = aligned(meta[OFF + spot])
        count = meta[CNT + spot]

        def run(keys, queries):
            which = meta[IMG + spot] % per
            gaps[:keys, :queries] = distances(rows_in[0], cols_in[0], which, count, keys, queries)
            key_seen = row_ids(0, keys) < count
            query_seen = row_ids(0, queries) < count
            left = lax.broadcasted_iota(jnp.int32, (queries, 128), 1) < 64

            def pair(p, carry):
                lanes = aligned(p * 128, 128)
                q2 = qkv[pl.ds(off, queries), pl.ds(lanes, 128)] * 0.125
                k2 = qkv[pl.ds(off, keys), pl.ds(width + lanes, 128)]
                v2 = qkv[pl.ds(off, keys), pl.ds(2 * width + lanes, 128)]
                q2 = jnp.where(query_seen, q2, jnp.zeros_like(q2))
                k2 = jnp.where(key_seen, k2, jnp.zeros_like(k2))
                v2 = jnp.where(key_seen, v2, jnp.zeros_like(v2))
                v2t = turned(v2)
                outs = []
                for half in range(2):
                    head = 2 * p + half
                    mine = left if half == 0 else jnp.logical_not(left)
                    qh = jnp.where(mine, q2, jnp.zeros_like(q2))
                    scores = dot_bt(k2, qh) - slopes[head] * gaps[:keys, :queries]
                    top = jnp.max(scores, axis=0, keepdims=True)
                    terms = jnp.exp(scores - top)
                    total = jnp.sum(terms, axis=0, keepdims=True)
                    heads_out = dot(v2t[half * 64 : half * 64 + 64], terms.astype(BF16))
                    outs.append((heads_out * (1.0 / total)).astype(BF16))
                    total_out[0, p, half : half + 1, :queries] = top + jnp.log(total)
                both = jnp.concatenate(outs, axis=0)
                att[pl.ds(off, queries), pl.ds(lanes, 128)] = turned_back(both)
                return carry

            lax.fori_loop(0, HEADS // 2, pair, 0, unroll=HEADS // 2)

        by_count(count, run)
        after = meta[OFF + jnp.minimum(spot + 1, images - 1)]
        end = jnp.where(spot == images - 1, meta[N_FWD], after // TILE)

        def send(t, carry):
            tile_copy(2, t).start()
            return carry

        lax.fori_loop(off // TILE, end, send, 0)

    @pl.when(now == pl.num_programs(0) - 1)
    def _():
        def finish(t, carry):
            for which in range(3):
                tile_copy(which, t).wait()
            return carry

        lax.fori_loop(0, meta[N_FWD], finish, 0)


def turned_back(block):
    size = block.shape[1]
    parts = []
    for start in range(0, size, 128):
        row = lax.broadcasted_iota(jnp.int32, (128, size), 0)
        col = lax.broadcasted_iota(jnp.int32, (128, size), 1)
        eye = jnp.where(row + start == col, 1.0, 0.0).astype(BF16)
        parts.append(dot_bt(eye, block).astype(BF16))
    return parts[0] if len(parts) == 1 else jnp.concatenate(parts, axis=0)


def mlp_kernel(
    chunk, length, meta, cot_in, att_in, tokens_in,
    vecs, out_w, up_w, down_w,
    y_send, mid_grad, att_grad, keep_g, send_g, vec_g, upb_g,
    up_b, cot, y_all, up_acc, down_acc, out_acc, h2_s, h2t_s, dzt_s, z_s, g_s, sem,
):
    step = pl.program_id(0)
    tiles = cot.shape[0] // TILE - WINDOW // TILE
    images = (pl.num_programs(0) - tiles) // 2
    width = cot_in.shape[2]
    hidden = up_w.shape[1]
    out_b, gain, shift, down_b = [
        vecs.at[pl.ds(n, 1)] for n in (OUT_B, GAIN_TWO, SHIFT_TWO, DOWN_B)
    ]

    @pl.when(step == 0)
    def _():
        up_acc[...] = jnp.zeros_like(up_acc)
        down_acc[...] = jnp.zeros_like(down_acc)
        out_acc[...] = jnp.zeros_like(out_acc)
        vec_g[...] = jnp.zeros_like(vec_g)
        upb_g[...] = jnp.zeros_like(upb_g)
        for n in range(hidden // width):
            up_b[0:1, n * width : (n + 1) * width] = vecs[UP_B + n : UP_B + n + 1, :]

    @pl.when(jnp.logical_and(step < images, step < meta[N_LIVE]))
    def _():
        spot = step
        off = aligned(meta[OFF + spot])
        seen = row_ids(0, length) < meta[CNT + spot]
        block = cot_in[0, :length, :]
        edge = (length - 1) // 16 * 16
        cot[pl.ds(aligned(off + edge), 16), :] = jnp.zeros((16, width), BF16)
        cot[pl.ds(off, length), :] = jnp.where(seen, block, jnp.zeros_like(block))

    def run_tile(t, both):
        rows = aligned(t * TILE, TILE)
        ids = row_ids(rows, TILE)
        att = att_in[...]
        att = jnp.where(ids < meta[ROWS_FWD], att, jnp.zeros_like(att))
        mid = tokens_in[...].astype(F32) + (dot(att, out_w[...]) + out_b[...])
        unit, inverse = layer_norm(mid)
        h2 = (unit * gain[...] + shift[...]).astype(BF16)
        h2_s[...] = h2
        z_s[...] = mid + down_b[...]
        if both:
            dz = cot[pl.ds(rows, TILE), :]
            dz = jnp.where(ids < meta[ROWS_BWD], dz, jnp.zeros_like(dz))
            h2t_s[...] = turned(h2)
            dzt_s[...] = turned(dz)
            g_s[...] = jnp.zeros_like(g_s)

        def part(c, carry):
            cols = pl.ds(aligned(c * chunk, chunk), chunk)
            pre = dot(h2_s[...], up_w[:, cols]) + up_b[0:1, cols]
            share, slope = gelu_parts(pre)
            act = (pre * share).astype(BF16)
            z_s[...] += dot(act, down_w[cols, :])
            if both:
                pre_g = (dot_bt(dz, down_w[cols, :]) * (share + slope)).astype(BF16)
                up_acc[:, cols] += dot(h2t_s[...], pre_g)
                down_acc[:, cols] += dot(dzt_s[...], act)
                upb_g[0:1, cols] += jnp.sum(pre_g.astype(F32), axis=0, keepdims=True)
                g_s[...] += dot_bt(pre_g, up_w[:, cols])
            return carry

        lax.fori_loop(0, hidden // chunk, part, 0)
        y_all[pl.ds(rows, TILE), :] = z_s[...].astype(BF16)
        if both:
            dzf = dz.astype(F32)
            g2 = g_s[...]
            dmid = dzf + norm_back(g2, gain[...], unit, inverse)
            branch = dmid.astype(BF16)
            mid_grad[...] = dmid
            att_grad[...] = dot_bt(branch, out_w[...]).astype(BF16)
            out_acc[...] += dot(turned(att), branch)
            vec_g[0:1, :] += jnp.sum(g2 * unit, axis=0, keepdims=True)
            vec_g[1:2, :] += jnp.sum(g2, axis=0, keepdims=True)
            vec_g[2:3, :] += jnp.sum(branch.astype(F32), axis=0, keepdims=True)
            vec_g[3:4, :] += jnp.sum(dzf, axis=0, keepdims=True)

    tile = step - images

    @pl.when(jnp.logical_and(tile >= 0, tile < meta[N_BWD]))
    def _():
        run_tile(tile, True)

    @pl.when(
        jnp.logical_and(
            jnp.logical_and(tile >= meta[N_BWD], tile >= 0),
            jnp.logical_and(tile < meta[N_FWD], tile < tiles),
        )
    )
    def _():
        run_tile(tile, False)

    spot = step - images - tiles

    @pl.when(spot >= 0)
    def _():
        off = aligned(meta[OFF + spot])
        seen = row_ids(0, length) < meta[CNT + spot]
        block = y_all[pl.ds(off, length), :]
        y_send[0, :length, :] = jnp.where(seen, block, jnp.zeros_like(block))

    @pl.when(step == pl.num_programs(0) - 1)
    def _():
        share = width // BLOCKS
        long = hidden // BLOCKS
        size = 2 * share + long // 2 + share // 2
        for turn, target in enumerate((send_g, keep_g)):
            h = meta[CORE] if turn else 1 - meta[CORE]
            side = aligned(h * (width // 2), 128)
            copies = []
            for n in range(BLOCKS):
                base = n * size
                if turn:
                    earlier[n].wait()
                for c in range(2):
                    cols = pl.ds(aligned((2 * h + c) * width, 128), width)
                    piece = up_acc[n * share : (n + 1) * share, cols]
                    y_all[base + c * share : base + (c + 1) * share, :] = piece.astype(BF16)
                base += 2 * share
                piece = down_acc[pl.ds(side, width // 2), n * long : (n + 1) * long]
                flipped = turned(piece.astype(BF16))
                y_all[base : base + long // 2, : width // 2] = flipped[: long // 2]
                y_all[base : base + long // 2, width // 2 :] = flipped[long // 2 :]
                base += long // 2
                rows = pl.ds(pl.multiple_of(n * share + h * (share // 2), 8), share // 2)
                y_all[base : base + share // 2, :] = out_acc[rows, :].astype(BF16)
                copy = pltpu.make_async_copy(
                    y_all.at[pl.ds(n * size, size)], target.at[n], sem.at[turn, n]
                )
                copy.start()
                copies.append(copy)
            earlier = copies
        for copy in earlier:
            copy.wait()


def attend_back_kernel(
    first, per, meta, slopes, qkv, att_grad, totals, rows_in, cols_in, *rest
):
    grads_out, grads, gaps, sem = rest[-4:]
    step = pl.program_id(0)
    width = att_grad.shape[1]
    spot = first + step
    live = spot < meta[N_LIVE]
    slot = step % 2

    def copy(at):
        rows = pl.ds(aligned(meta[OFF + first + at]), WINDOW)
        return pltpu.make_async_copy(grads.at[at % 2], grads_out.at[rows], sem.at[at % 2])

    @pl.when(live)
    def _():
        count = meta[CNT + spot]

        def run(keys, queries):
            which = meta[IMG + spot] % per
            gaps[:keys, :queries] = distances(rows_in[0], cols_in[0], which, count, keys, queries)
            key_seen = row_ids(0, keys) < count
            query_seen = row_ids(0, queries) < count
            left = lax.broadcasted_iota(jnp.int32, (queries, 128), 1) < 64

            def pair(p, carry):
                lanes = aligned(p * 128, 128)
                q2 = qkv[:queries, pl.ds(lanes, 128)] * 0.125
                k2 = qkv[:keys, pl.ds(width + lanes, 128)]
                v2 = qkv[:keys, pl.ds(2 * width + lanes, 128)]
                o2 = att_grad[:queries, pl.ds(lanes, 128)]
                q2 = jnp.where(query_seen, q2, jnp.zeros_like(q2))
                o2 = jnp.where(query_seen, o2, jnp.zeros_like(o2))
                k2 = jnp.where(key_seen, k2, jnp.zeros_like(k2))
                v2 = jnp.where(key_seen, v2, jnp.zeros_like(v2))
                k2t = turned(k2)
                dq_parts = []
                dk = dv = None
                for half in range(2):
                    head = 2 * p + half
                    mine = left if half == 0 else jnp.logical_not(left)
                    qh = jnp.where(mine, q2, jnp.zeros_like(q2))
                    oh = jnp.where(mine, o2, jnp.zeros_like(o2))
                    scores = dot_bt(k2, qh) - slopes[head] * gaps[:keys, :queries]
                    probs = jnp.exp(scores - totals[0, p, half : half + 1, :queries])
                    prob_g = dot_bt(v2, oh)
                    inner = jnp.sum(probs * prob_g, axis=0, keepdims=True)
                    score_g = (probs * (prob_g - inner)).astype(BF16)
                    dv_part = dot(probs.astype(BF16), oh)
                    dk_part = dot(score_g, qh)
                    dq_parts.append(
                        (dot(k2t[half * 64 : half * 64 + 64], score_g) * 0.125).astype(BF16)
                    )
                    dk = dk_part if dk is None else dk + dk_part
                    dv = dv_part if dv is None else dv + dv_part
                dq = turned_back(jnp.concatenate(dq_parts, axis=0))
                grads[slot, :queries, pl.ds(lanes, 128)] = dq
                grads[slot, :keys, pl.ds(width + lanes, 128)] = dk.astype(BF16)
                grads[slot, :keys, pl.ds(2 * width + lanes, 128)] = dv.astype(BF16)
                return carry

            lax.fori_loop(0, HEADS // 2, pair, 0, unroll=HEADS // 2)

        by_count(count, run)

        @pl.when(step > 0)
        def _():
            copy(step - 1).wait()

        copy(step).start()

        @pl.when(jnp.logical_or(step == pl.num_programs(0) - 1, spot == meta[N_LIVE] - 1))
        def _():
            copy(step).wait()


def qkv_grad_kernel(meta, packed_grad, tokens, vecs, keep_g, send_g, bias_g, acc, stage, sem):
    tile = pl.program_id(0)
    width = tokens.shape[1]

    @pl.when(tile == 0)
    def _():
        acc[...] = jnp.zeros_like(acc)
        bias_g[...] = jnp.zeros_like(bias_g)

    @pl.when(tile < meta[N_BWD])
    def _():
        ids = row_ids(tile * TILE, TILE)
        unit, _ = layer_norm(tokens[...].astype(F32))
        hidden = (
            unit * vecs[GAIN_ONE : GAIN_ONE + 1] + vecs[SHIFT_ONE : SHIFT_ONE + 1]
        ).astype(BF16)
        hidden_t = turned(hidden)
        for part in range(3):
            cols = slice(part * width, (part + 1) * width)
            block = packed_grad[:, cols]
            block = jnp.where(ids < meta[ROWS_BWD], block, jnp.zeros_like(block))
            acc[:, cols] += dot(hidden_t, block)
            bias_g[0:1, cols] += jnp.sum(block.astype(F32), axis=0, keepdims=True)

    @pl.when(tile == pl.num_programs(0) - 1)
    def _():
        rows = width // BLOCKS // 2
        for block in range(BLOCKS):
            for h in range(2):
                for c in range(3):
                    first = (2 * block + h) * rows
                    piece = acc[first : first + rows, c * width : (c + 1) * width]
                    stage[h, block, c * rows : (c + 1) * rows, :] = piece.astype(BF16)
        mine = meta[CORE]
        keep = pltpu.make_async_copy(stage.at[mine], keep_g, sem.at[0])
        send = pltpu.make_async_copy(stage.at[1 - mine], send_g, sem.at[1])
        keep.start()
        send.start()
        keep.wait()
        send.wait()


def token_grad_kernel(meta, packed_grad, tokens, mid_grad, vecs, weight, out, vec_g, held):
    step = pl.program_id(0)
    tiles = held.shape[0] // TILE - WINDOW // TILE
    length, images = out.shape[1], out.shape[2]

    @pl.when(step == 0)
    def _():
        vec_g[...] = jnp.zeros_like(vec_g)

    @pl.when(jnp.logical_and(step < tiles, step < meta[N_BWD]))
    def _():
        rows = aligned(step * TILE, TILE)
        ids = row_ids(rows, TILE)
        unit, inverse = layer_norm(tokens[...].astype(F32))
        block = packed_grad[...]
        block = jnp.where(ids < meta[ROWS_BWD], block, jnp.zeros_like(block))
        g1 = dot_bt(block, weight[...])
        back = norm_back(g1, vecs[GAIN_ONE : GAIN_ONE + 1], unit, inverse)
        held[pl.ds(rows, TILE), :] = mid_grad[...] + back
        vec_g[0:1, :] += jnp.sum(g1 * unit, axis=0, keepdims=True)
        vec_g[1:2, :] += jnp.sum(g1, axis=0, keepdims=True)

    @pl.when(step >= tiles)
    def _():
        parts = []
        for i in range(images):
            spot = meta[SPOT + (step - tiles) * images + i]
            off = aligned(meta[OFF + spot])
            limit = meta[CNT + spot] * meta[LIVE + spot]
            block = held[pl.ds(off, length), :]
            parts.append(jnp.where(row_ids(0, length) < limit, block, 0.0))
        out[0] = jnp.swapaxes(jnp.stack(parts, axis=0), 0, 1)


def whole(*shape):
    return pl.BlockSpec(shape, lambda *_: (0,) * len(shape), pipeline_mode=pl.Buffered(1))


def params():
    return pltpu.CompilerParams(vmem_limit_bytes=VMEM_LIMIT)


def small():
    return pl.BlockSpec(memory_space=pltpu.SMEM)


def prepare(every, counts, present, slots, me, cotangent, *vectors):
    steps, length, images, width = cotangent.shape
    group = every.shape[0]
    padded = (length + 7) // 8 * 8
    return pl.pallas_call(
        prepare_kernel,
        out_shape=(
            jax.ShapeDtypeStruct((PLACES,), jnp.int32),
            jax.ShapeDtypeStruct((steps * images,), jnp.int32),
            jax.ShapeDtypeStruct((16, width), F32),
            jax.ShapeDtypeStruct((group, steps, padded, width), BF16),
        ),
        grid=(steps,),
        in_specs=[small()] * 5
        + [pl.BlockSpec((1, length, images, width), lambda m: (m, 0, 0, 0))]
        + [whole(*vector.shape) for vector in vectors],
        out_specs=[
            small(),
            small(),
            whole(16, width),
            pl.BlockSpec((group, 1, padded, width), lambda m: (0, m, 0, 0)),
        ],
        compiler_params=params(),
    )(every, counts, present, slots, me, cotangent, *vectors)


def place(take, got, length):
    group, steps, padded, width = got.shape
    return pl.pallas_call(
        place_kernel,
        out_shape=jax.ShapeDtypeStruct((steps, length, group, width), BF16),
        grid=(steps,),
        in_specs=[small(), pl.BlockSpec((group, 1, padded, width), lambda m: (0, m, 0, 0))],
        out_specs=pl.BlockSpec((1, length, group, width), lambda m: (m, 0, 0, 0)),
        compiler_params=params(),
    )(take, got)


def first_half(meta, slopes, tokens, rows, cols, vecs, weight):
    steps, length, per, width = tokens.shape
    images = steps * per
    tiles = -(-images * ((length + 15) // 16 * 16) // TILE)
    total = tiles * TILE + WINDOW
    spots = pl.BlockSpec(
        (1, per, length),
        lambda s, meta, slopes: (meta[IMG + jnp.maximum(s - steps - images, 0)] // per, 0, 0),
    )
    return pl.pallas_call(
        attend_kernel,
        out_shape=(
            jax.ShapeDtypeStruct((total, width), BF16),
            jax.ShapeDtypeStruct((total, 3 * width), BF16),
            jax.ShapeDtypeStruct((total, width), BF16),
            jax.ShapeDtypeStruct((images, HEADS // 2, 8, WINDOW), F32),
        ),
        grid_spec=pltpu.PrefetchScalarGridSpec(
            num_scalar_prefetch=2,
            grid=(steps + 2 * images,),
            in_specs=[
                pl.BlockSpec(
                    (1, length, per, width),
                    lambda s, meta, slopes: (jnp.minimum(s, steps - 1), 0, 0, 0),
                ),
                spots,
                spots,
                whole(*vecs.shape),
                whole(width, 3 * width),
            ],
            out_specs=[
                pl.BlockSpec(memory_space=pl.ANY),
                pl.BlockSpec(memory_space=pl.ANY),
                pl.BlockSpec(memory_space=pl.ANY),
                pl.BlockSpec(
                    (1, HEADS // 2, 8, WINDOW),
                    lambda s, meta, slopes: (jnp.maximum(s - steps - images, 0), 0, 0, 0),
                ),
            ],
            scratch_shapes=[
                pltpu.VMEM((images, (length + 15) // 16 * 16, width), BF16),
                pltpu.VMEM((total, width), BF16),
                pltpu.VMEM((total, 3 * width), BF16),
                pltpu.VMEM((total, width), BF16),
                pltpu.VMEM((WINDOW, WINDOW), F32),
                pltpu.SemaphoreType.DMA((tiles,)),
                pltpu.SemaphoreType.DMA((tiles,)),
                pltpu.SemaphoreType.DMA((tiles,)),
            ],
        ),
        compiler_params=params(),
        cost_estimate=cost(40),
    )(meta, slopes, tokens, rows, cols, vecs, weight)


def mlp(meta, cot, att, packed, vecs, out_w, up_w, down_w, length):
    images, padded, width = cot.shape
    rows = packed.shape[0]
    tiles = (rows - WINDOW) // TILE
    hidden = up_w.shape[1]
    parcel = (2 * width + hidden // 2 + width // 2) // BLOCKS
    last = images - 1

    def fwd_tile(s, meta):
        return (jnp.clip(s - images, 0, meta[N_FWD] - 1), 0)

    def bwd_tile(s, meta):
        return (jnp.clip(s - images, 0, jnp.maximum(meta[N_BWD] - 1, 0)), 0)

    return pl.pallas_call(
        functools.partial(mlp_kernel, CHUNK, length),
        out_shape=(
            jax.ShapeDtypeStruct((images, padded, width), BF16),
            jax.ShapeDtypeStruct((rows, width), F32),
            jax.ShapeDtypeStruct((rows, width), BF16),
            jax.ShapeDtypeStruct((BLOCKS, parcel, width), BF16),
            jax.ShapeDtypeStruct((BLOCKS, parcel, width), BF16),
            jax.ShapeDtypeStruct((8, width), F32),
            jax.ShapeDtypeStruct((8, hidden), F32),
        ),
        grid_spec=pltpu.PrefetchScalarGridSpec(
            num_scalar_prefetch=1,
            grid=(2 * images + tiles,),
            in_specs=[
                pl.BlockSpec(
                    (1, padded, width), lambda s, meta: (meta[PEER + jnp.minimum(s, last)], 0, 0)
                ),
                pl.BlockSpec((TILE, width), fwd_tile),
                pl.BlockSpec((TILE, width), fwd_tile),
                whole(*vecs.shape),
                whole(width, width),
                whole(width, hidden),
                whole(hidden, width),
            ],
            out_specs=[
                pl.BlockSpec(
                    (1, padded, width),
                    lambda s, meta: (meta[PEER + jnp.clip(s - images - tiles, 0, last)], 0, 0),
                ),
                pl.BlockSpec((TILE, width), bwd_tile),
                pl.BlockSpec((TILE, width), bwd_tile),
                pl.BlockSpec(memory_space=pl.ANY),
                pl.BlockSpec(memory_space=pl.ANY),
                whole(8, width),
                whole(8, hidden),
            ],
            scratch_shapes=[
                pltpu.VMEM((8, hidden), F32),
                pltpu.VMEM((rows, width), BF16),
                pltpu.VMEM((rows, width), BF16),
                pltpu.VMEM((width, hidden), F32),
                pltpu.VMEM((width, hidden), F32),
                pltpu.VMEM((width, width), F32),
                pltpu.VMEM((TILE, width), BF16),
                pltpu.VMEM((width, TILE), BF16),
                pltpu.VMEM((width, TILE), BF16),
                pltpu.VMEM((TILE, width), F32),
                pltpu.VMEM((TILE, width), F32),
                pltpu.SemaphoreType.DMA((2, BLOCKS)),
            ],
        ),
        compiler_params=params(),
        cost_estimate=cost(110),
    )(meta, cot, att, packed, vecs, out_w, up_w, down_w)


def attend_back(first, count, expected, meta, slopes, qkv, att_grad, totals, rows_in, cols_in, earlier):
    total, wide = qkv.shape
    width = wide // 3
    per, length = rows_in.shape[1:]

    def spot_of(s, meta):
        return jnp.clip(first + s, 0, jnp.maximum(meta[N_LIVE] - 1, 0))

    def by_offset(s, meta, slopes):
        return (aligned(meta[OFF + spot_of(s, meta)]), 0)

    spots = pl.BlockSpec(
        (1, per, length),
        lambda s, meta, slopes: (meta[IMG + spot_of(s, meta)] // per, 0, 0),
    )
    anywhere = pl.BlockSpec(memory_space=pl.ANY)
    return pl.pallas_call(
        functools.partial(attend_back_kernel, first, per),
        out_shape=jax.ShapeDtypeStruct((total, wide), BF16),
        grid_spec=pltpu.PrefetchScalarGridSpec(
            num_scalar_prefetch=2,
            grid=(count,),
            in_specs=[
                pl.BlockSpec((pl.Element(WINDOW), pl.Element(wide)), by_offset),
                pl.BlockSpec((pl.Element(WINDOW), pl.Element(width)), by_offset),
                pl.BlockSpec(
                    (1, HEADS // 2, 8, WINDOW),
                    lambda s, meta, slopes: (spot_of(s, meta), 0, 0, 0),
                ),
                spots,
                spots,
            ]
            + [anywhere] * len(earlier),
            out_specs=anywhere,
            scratch_shapes=[
                pltpu.VMEM((2, WINDOW, wide), BF16),
                pltpu.VMEM((WINDOW, WINDOW), F32),
                pltpu.SemaphoreType.DMA((2,)),
            ],
        ),
        input_output_aliases={7: 0} if earlier else {},
        compiler_params=params(),
        cost_estimate=cost(expected),
    )(meta, slopes, qkv, att_grad, totals, rows_in, cols_in, *earlier)


def bwd_tile(s, meta):
    return (jnp.clip(s, 0, jnp.maximum(meta[N_BWD] - 1, 0)), 0)


def qkv_grad(meta, packed_grad, packed, vecs):
    rows, width = packed.shape
    parcel = 3 * width // 2 // BLOCKS
    tiles = (rows - WINDOW) // TILE
    return pl.pallas_call(
        qkv_grad_kernel,
        out_shape=(
            jax.ShapeDtypeStruct((BLOCKS, parcel, width), BF16),
            jax.ShapeDtypeStruct((BLOCKS, parcel, width), BF16),
            jax.ShapeDtypeStruct((8, 3 * width), F32),
        ),
        grid_spec=pltpu.PrefetchScalarGridSpec(
            num_scalar_prefetch=1,
            grid=(tiles,),
            in_specs=[
                pl.BlockSpec((TILE, 3 * width), bwd_tile),
                pl.BlockSpec((TILE, width), bwd_tile),
                whole(*vecs.shape),
            ],
            out_specs=[
                pl.BlockSpec(memory_space=pl.ANY),
                pl.BlockSpec(memory_space=pl.ANY),
                whole(8, 3 * width),
            ],
            scratch_shapes=[
                pltpu.VMEM((width, 3 * width), F32),
                pltpu.VMEM((2, BLOCKS, parcel, width), BF16),
                pltpu.SemaphoreType.DMA((2,)),
            ],
        ),
        compiler_params=params(),
        cost_estimate=cost(15),
    )(meta, packed_grad, packed, vecs)


def token_grad(meta, packed_grad, packed, mid_grad, vecs, weight, steps, length, images):
    rows, width = packed.shape
    tiles = (rows - WINDOW) // TILE
    return pl.pallas_call(
        token_grad_kernel,
        out_shape=(
            jax.ShapeDtypeStruct((steps, length, images, width), F32),
            jax.ShapeDtypeStruct((8, width), F32),
        ),
        grid_spec=pltpu.PrefetchScalarGridSpec(
            num_scalar_prefetch=1,
            grid=(tiles + steps,),
            in_specs=[
                pl.BlockSpec((TILE, 3 * width), bwd_tile),
                pl.BlockSpec((TILE, width), bwd_tile),
                pl.BlockSpec((TILE, width), bwd_tile),
                whole(*vecs.shape),
                whole(width, 3 * width),
            ],
            out_specs=[
                pl.BlockSpec(
                    (1, length, images, width),
                    lambda s, meta: (jnp.clip(s - tiles, 0, steps - 1), 0, 0, 0),
                ),
                whole(8, width),
            ],
            scratch_shapes=[pltpu.VMEM((rows, width), F32)],
        ),
        compiler_params=params(),
        cost_estimate=cost(20),
    )(meta, packed_grad, packed, mid_grad, vecs, weight)


def cost(microseconds):
    return pl.CostEstimate(
        flops=int(microseconds * 1e9), bytes_accessed=int(microseconds * 1e5), transcendentals=0
    )


def swap(block, axis, bit):
    size = lax.axis_size(axis)
    return lax.ppermute(block, axis, [(n, n ^ bit) for n in range(size)])


def bit_of(axis, bit):
    return lax.axis_index(axis) // bit % 2


def added(a, b):
    return (a.astype(F32) + b.astype(F32)).astype(BF16)


def half_sums(block, axis, bit, dim):
    mine = bit_of(axis, bit)
    keep = lax.dynamic_index_in_dim(block, mine, dim, keepdims=False)
    send = lax.dynamic_index_in_dim(block, 1 - mine, dim, keepdims=False)
    return added(keep, swap(send, axis, bit))


def unpacked(mine, other, shapes):
    swapped = bit_of("bal", 1) == 1
    first = jnp.where(swapped, other, mine)
    second = jnp.where(swapped, mine, other)
    lead, width = mine.shape[:-2], mine.shape[-1]
    out, at = [], 0
    for rows, columns, kind in shapes:
        wide = columns // width
        part = rows * wide // 2
        held = [half[..., at : at + part, :] for half in (first, second)]
        if kind == "rows":
            size = rows // 2
            parts = [
                jnp.concatenate(
                    [half[..., c * size : (c + 1) * size, :] for c in range(wide)], axis=-1
                )
                for half in held
            ]
            out.append(jnp.concatenate(parts, axis=-2))
        elif kind == "columns":
            parts = [
                half[..., c * rows : (c + 1) * rows, :] for half in held for c in range(wide // 2)
            ]
            out.append(jnp.concatenate(parts, axis=-1))
        else:
            size = width // 2
            tops = [half[..., :size] for half in held]
            bottoms = [half[..., size:] for half in held]
            out.append(
                jnp.concatenate(
                    [jnp.concatenate(tops, axis=-1), jnp.concatenate(bottoms, axis=-1)], axis=-2
                )
            )
        at += part
    return [matrix.reshape(lead[:-1] + (-1, matrix.shape[-1])) if lead else matrix for matrix in out]


def spread_sum(keep, send, shapes):
    return [
        lax.psum(lax.psum_scatter(matrix, "dp", scatter_dimension=0, tiled=True), "bal").astype(F32)
        for matrix in unpacked(keep, send, shapes)
    ]


def joined(block, shapes):
    block = added(block, swap(block, "bal", 2))
    return [matrix.astype(F32) for matrix in unpacked(block, swap(block, "bal", 1), shapes)]


def halved(block):
    bit = 1
    while bit < lax.axis_size("dp"):
        block = half_sums(block.reshape((-1, 2) + block.shape[-2:]), "dp", bit, 1)
        bit *= 2
    return block.reshape(block.shape[-2:])


def after(value, *others):
    return lax.optimization_barrier((value,) + others)[0]


def summed(block):
    for axis in ("bal", "dp"):
        bit = 1
        while bit < lax.axis_size(axis):
            block = block + swap(block, axis, bit)
            bit *= 2
    return block


def per_device(
    tokens,
    cotangent,
    counts,
    rows,
    cols,
    present,
    slots,
    first_gain,
    first_shift,
    qkv_weight,
    query_bias,
    value_bias,
    out_weight,
    out_bias,
    second_gain,
    second_shift,
    up_weight,
    up_bias,
    down_weight,
    down_bias,
):
    steps, images, length, width = tokens.shape
    hidden = up_weight.shape[1]
    group = lax.axis_size("bal")
    total = steps * images
    slopes = jnp.exp2(-8.0 * (jnp.arange(16, dtype=F32) + 1.0) / HEADS)

    def exchange(blocks):
        flat = blocks.reshape(group, -1, width)
        return lax.all_to_all(flat, "bal", split_axis=0, concat_axis=0, tiled=True)

    def turn(array):
        return jnp.transpose(array, (0, 2, 1, 3))

    meta, take, vecs, cot_send = prepare(
        lax.all_gather(slots, "bal"), counts, present, slots,
        lax.axis_index("bal").astype(jnp.int32).reshape(1), turn(cotangent),
        first_gain, first_shift, query_bias, value_bias, out_bias, second_gain, second_shift,
        down_bias, up_bias,
    )
    cot_home = exchange(cot_send).reshape(total, -1, width)
    packed, qkv, att, totals = first_half(meta, slopes, turn(tokens), rows, cols, vecs, qkv_weight)
    y_send, mid_grad, att_grad, keep_two, send_two, vec_two, upb_g = mlp(
        meta, cot_home, att, packed, vecs, out_weight, up_weight, down_weight, length
    )
    y_got = exchange(y_send)

    share, long = width // BLOCKS, hidden // BLOCKS
    shapes_two = ((share, hidden, "columns"), (long, width, "side"), (share, width, "rows"))
    shapes_one = ((share, 3 * width, "rows"),)
    direct = lax.axis_size("dp") == BLOCKS

    def back(first, count, expected, table, earlier):
        return attend_back(
            first, count, expected, table, slopes, qkv, att_grad, totals, rows, cols, earlier
        )

    lead = max(images // 2, 1)
    packed_grad = back(0, lead, 15, meta, ())
    table = meta
    if direct:
        sum_two = added(after(keep_two, packed_grad), swap(send_two, "bal", 1))
        share_two = lax.psum_scatter(sum_two, "dp", scatter_dimension=0, tiled=True)[0]
        table = after(meta, sum_two)
    packed_grad = back(lead, total - lead, 500, table, (packed_grad,))
    keep_one, send_one, bias_g = qkv_grad(after(table, y_got), packed_grad, packed, vecs)
    output = place(after(take, keep_one), y_got.reshape(group, steps, -1, width), length)
    table = after(table, output)
    if direct:
        sum_one = added(keep_one, swap(send_one, "bal", 1))
        table = after(table, sum_one)
    input_grad, vec_one = token_grad(
        table, packed_grad, packed, mid_grad, vecs, qkv_weight, steps, length, images
    )
    if direct:
        (qkv_rows,) = joined(halved(sum_one), shapes_one)
        up_rows, down_rows, out_rows = joined(share_two, shapes_two)
    else:
        (qkv_rows,) = spread_sum(keep_one, send_one, shapes_one)
        up_rows, down_rows, out_rows = spread_sum(keep_two, send_two, shapes_two)
    vectors = summed(
        jnp.concatenate(
            [
                vec_one[:2].reshape(-1), bias_g[0, :width], bias_g[0, 2 * width :],
                vec_two[:4].reshape(-1), upb_g[0],
            ]
        )
    )

    def vector(n):
        return vectors[n * width : (n + 1) * width]

    return (
        turn(output),
        turn(input_grad),
        vector(0),
        vector(1),
        qkv_rows,
        vector(2),
        vector(3),
        out_rows,
        vector(6),
        vector(4),
        vector(5),
        up_rows,
        vectors[8 * width :],
        down_rows,
        vector(7),
    )


def solution(mesh):
    images = P(None, ("dp", "bal"), None, None)
    spots = P(None, ("dp", "bal"), None)
    flags = P(None, ("dp", "bal"))
    matrix = P("dp", None)
    return jax.shard_map(
        per_device,
        mesh=mesh,
        in_specs=(images, images, flags, spots, spots, flags, flags) + (P(),) * 13,
        out_specs=(
            images, images, P(), P(), matrix, P(), P(), matrix, P(), P(), P(), matrix, P(), matrix, P(),
        ),
        check_vma=False,
    )
```

```python
import functools
import math

import jax
import jax.numpy as jnp
from jax import lax
from jax.experimental import pallas as pl
from jax.experimental.pallas import tpu as pltpu
from jax.sharding import PartitionSpec as P

HEADS = 12
TILE = 256
WINDOW = 256
FAR = 1e12
EPS = 1e-06
BLOCKS = 8
CHUNK = 1536
VMEM_LIMIT = 60 * 1024 * 1024

F32 = jnp.float32
BF16 = jnp.bfloat16

OFF, CNT, IMG, LIVE, PEER, SPOT, MISC = 0, 16, 32, 48, 64, 80, 96
N_FWD, N_BWD, ROWS_FWD, ROWS_BWD, N_LIVE, CORE = range(MISC, MISC + 6)
PLACES = 128

GAIN_ONE, SHIFT_ONE, QKV_B, OUT_B, GAIN_TWO, SHIFT_TWO, DOWN_B, UP_B = 0, 1, 2, 5, 6, 7, 8, 9
VECTORS = (GAIN_ONE, SHIFT_ONE, QKV_B, QKV_B + 2, OUT_B, GAIN_TWO, SHIFT_TWO, DOWN_B, UP_B)


def dot(a, b):
    return jnp.dot(a, b, preferred_element_type=F32)


def dot_bt(a, b):
    return lax.dot_general(a, b, (((1,), (1,)), ((), ())), preferred_element_type=F32)


def turned(block):
    size = 256 if block.shape[1] % 256 == 0 else 128
    row = lax.broadcasted_iota(jnp.int32, (size, size), 0)
    col = lax.broadcasted_iota(jnp.int32, (size, size), 1)
    eye = jnp.where(row == col, 1.0, 0.0).astype(BF16)
    parts = [
        dot_bt(eye, block[:, start : start + size]).astype(BF16)
        for start in range(0, block.shape[1], size)
    ]
    return parts[0] if len(parts) == 1 else jnp.concatenate(parts, axis=0)


def layer_norm(values):
    average = jnp.mean(values, axis=-1, keepdims=True)
    centred = values - average
    spread = jnp.mean(centred * centred, axis=-1, keepdims=True)
    inverse = lax.rsqrt(spread + EPS)
    return centred * inverse, inverse


def norm_back(out_grad, gain, unit, inverse):
    e = out_grad * gain
    mean_e = jnp.mean(e, axis=-1, keepdims=True)
    mean_eu = jnp.mean(e * unit, axis=-1, keepdims=True)
    return inverse * (e - mean_e - unit * mean_eu)


def gelu_parts(u):
    size = jnp.abs(u)
    t = 1.0 / (1.0 + (0.3275911 * math.sqrt(0.5)) * size)
    bell = jnp.exp(-0.5 * (u * u))
    poly = t * (
        0.5 * 0.254829592
        + t
        * (
            0.5 * -0.284496736
            + t * (0.5 * 1.421413741 + t * (0.5 * -1.453152027 + t * (0.5 * 1.061405429)))
        )
    )
    tail = poly * bell
    phi_sum = jnp.where(u >= 0, 1.0 - tail, tail)
    return phi_sum, u * bell * (1.0 / math.sqrt(2.0 * math.pi))


def put_rows(packed, off, count, block):
    rows = (block.shape[0] + 15) // 16 * 16
    if rows > block.shape[0]:
        more = jnp.zeros((rows - block.shape[0], block.shape[1]), block.dtype)
        block = jnp.concatenate([block, more], axis=0)
    ids = row_ids(0, rows)
    window = pl.ds(off, rows)
    block = jnp.where(ids < count, block, jnp.zeros_like(block))
    packed[window, :] = jnp.where(ids < (count + 15) // 16 * 16, block, packed[window, :])


def row_ids(start, rows):
    return start + lax.broadcasted_iota(jnp.int32, (rows, 1), 0)


def aligned(value, step=16):
    return pl.multiple_of(value, step)


def by_count(count, run):
    @pl.when(count <= 128)
    def _():
        run(128, 128)

    @pl.when(jnp.logical_and(count > 128, count <= 192))
    def _():
        run(192, 256)

    @pl.when(count > 192)
    def _():
        run(256, 256)


def distances(rows, cols, which, count, keys, queries):
    mine = lax.broadcasted_iota(jnp.int32, rows.shape, 0) == which
    row = jnp.sum(jnp.where(mine, rows, 0).astype(F32), axis=0, keepdims=True)
    col = jnp.sum(jnp.where(mine, cols, 0).astype(F32), axis=0, keepdims=True)
    spots = jnp.concatenate([row, col, jnp.zeros((6, row.shape[1]), F32)], axis=0)
    spots = jnp.concatenate([spots, jnp.zeros((8, WINDOW - row.shape[1]), F32)], axis=1)
    eye = jnp.where(
        lax.broadcasted_iota(jnp.int32, (keys, WINDOW), 0)
        == lax.broadcasted_iota(jnp.int32, (keys, WINDOW), 1),
        1.0,
        0.0,
    ).astype(BF16)
    turned_spots = dot_bt(eye, spots.astype(BF16))
    down = turned_spots[:, 0:1] - spots[0:1, :queries]
    across = turned_spots[:, 1:2] - spots[1:2, :queries]
    far = row_ids(0, keys) >= count
    return jnp.where(far, FAR, jnp.sqrt(down * down + across * across))


def prepare_kernel(every, counts, present, slots, me, cot, *rest):
    *lines, meta, take, vecs, send = rest
    step = pl.program_id(0)
    steps, length, images, width = pl.num_programs(0), cot.shape[1], cot.shape[2], cot.shape[3]
    group = every.shape[0]

    @pl.when(step == 0)
    def _():
        def fill(live):
            def body(img, carry):
                spot, off = carry
                m, i = img // images, img % images
                count = counts[m, i]
                mine = present[m, i] == live

                @pl.when(mine)
                def _():
                    meta[OFF + spot] = off
                    meta[CNT + spot] = count
                    meta[IMG + spot] = img
                    meta[LIVE + spot] = live
                    meta[PEER + spot] = slots[m, i] // images * steps + m
                    meta[SPOT + img] = spot

                padded = (count + 15) // 16 * 16
                return spot + mine.astype(jnp.int32), off + jnp.where(mine, padded, 0)

            return body

        meta[CORE] = me[0] % 2
        vecs[...] = jnp.zeros_like(vecs)
        for row, values in zip(VECTORS, lines):
            for n in range(values.shape[0] // width):
                piece = values[n * width : (n + 1) * width]
                vecs[row + n : row + n + 1, :] = piece.reshape(1, width)
        zero = jnp.int32(0)
        total = counts.shape[0] * images
        spot, off = lax.fori_loop(0, total, fill(1), (zero, zero))
        meta[N_LIVE] = spot
        meta[ROWS_BWD] = off
        meta[N_BWD] = (off + TILE - 1) // TILE
        spot, off = lax.fori_loop(0, total, fill(0), (spot, off))
        meta[ROWS_FWD] = off
        meta[N_FWD] = (off + TILE - 1) // TILE

        def land(n, carry):
            a, m, i = n // total, n % total // images, n % images
            slot = every[a, m, i]

            @pl.when(slot // images == me[0])
            def _():
                take[m * images + slot % images] = a * steps + m

            return carry

        lax.fori_loop(0, group * total, land, 0)

    block = jnp.swapaxes(cot[0].astype(F32), 0, 1).astype(BF16)
    for place in range(images):
        peer = take[step * images + place] // steps
        send[peer, 0, :length, :] = block[place]


def place_kernel(take, got, out):
    step = pl.program_id(0)
    length, images = out.shape[1], out.shape[2]
    steps = pl.num_programs(0)
    parts = [
        got[take[step * images + place] // steps, 0, :length, :].astype(F32)
        for place in range(images)
    ]
    out[0] = jnp.swapaxes(jnp.stack(parts, axis=0), 0, 1).astype(out.dtype)


def attend_kernel(
    meta, slopes, tokens, rows_in, cols_in, vecs, weight,
    packed_out, qkv_out, att_out, total_out,
    packed, qkv, att, gaps, sem_packed, sem_qkv, sem_att,
):
    length, per, width = tokens.shape[1], tokens.shape[2], tokens.shape[3]
    steps = pl.num_programs(0) // (per + 1)
    images = steps * per
    now = pl.program_id(0)

    def tile_copy(which, t):
        src, dst, sem = (
            (packed, packed_out, sem_packed),
            (qkv, qkv_out, sem_qkv),
            (att, att_out, sem_att),
        )[which]
        rows = pl.ds(aligned(t * TILE, TILE), TILE)
        return pltpu.make_async_copy(src.at[rows], dst.at[rows], sem.at[t])

    @pl.when(now == 0)
    def _():
        packed[...] = jnp.zeros_like(packed)

    @pl.when(now < steps)
    def _():
        block = jnp.swapaxes(tokens[0].astype(F32), 0, 1).astype(BF16)
        for i in range(per):
            spot = meta[SPOT + now * per + i]
            put_rows(packed, aligned(meta[OFF + spot]), meta[CNT + spot], block[i])

    @pl.when(now == steps - 1)
    def _():

        def project(t, carry):
            rows = pl.ds(aligned(t * TILE, TILE), TILE)
            unit, _ = layer_norm(packed[rows, :].astype(F32))
            hidden = (
                unit * vecs[GAIN_ONE : GAIN_ONE + 1] + vecs[SHIFT_ONE : SHIFT_ONE + 1]
            ).astype(BF16)
            for part in range(3):
                cols = slice(part * width, (part + 1) * width)
                bias = vecs[QKV_B + part : QKV_B + part + 1]
                qkv[rows, cols] = (dot(hidden, weight[:, cols]) + bias).astype(BF16)
            tile_copy(0, t).start()
            tile_copy(1, t).start()
            return carry

        lax.fori_loop(0, meta[N_FWD], project, 0)

    @pl.when(now >= steps)
    def _():
        spot = now - steps
        off = aligned(meta[OFF + spot])
        count = meta[CNT + spot]

        def run(keys, queries):
            which = meta[IMG + spot] % per
            gaps[:keys, :queries] = distances(rows_in[0], cols_in[0], which, count, keys, queries)
            key_seen = row_ids(0, keys) < count
            query_seen = row_ids(0, queries) < count
            left = lax.broadcasted_iota(jnp.int32, (queries, 128), 1) < 64

            def pair(p, carry):
                lanes = aligned(p * 128, 128)
                q2 = qkv[pl.ds(off, queries), pl.ds(lanes, 128)] * 0.125
                k2 = qkv[pl.ds(off, keys), pl.ds(width + lanes, 128)]
                v2 = qkv[pl.ds(off, keys), pl.ds(2 * width + lanes, 128)]
                q2 = jnp.where(query_seen, q2, jnp.zeros_like(q2))
                k2 = jnp.where(key_seen, k2, jnp.zeros_like(k2))
                v2 = jnp.where(key_seen, v2, jnp.zeros_like(v2))
                v2t = turned(v2)
                outs = []
                for half in range(2):
                    head = 2 * p + half
                    mine = left if half == 0 else jnp.logical_not(left)
                    qh = jnp.where(mine, q2, jnp.zeros_like(q2))
                    scores = dot_bt(k2, qh) - slopes[head] * gaps[:keys, :queries]
                    top = jnp.max(scores, axis=0, keepdims=True)
                    terms = jnp.exp(scores - top)
                    total = jnp.sum(terms, axis=0, keepdims=True)
                    heads_out = dot(v2t[half * 64 : half * 64 + 64], terms.astype(BF16))
                    outs.append((heads_out * (1.0 / total)).astype(BF16))
                    total_out[0, p, half : half + 1, :queries] = top + jnp.log(total)
                both = jnp.concatenate(outs, axis=0)
                att[pl.ds(off, queries), pl.ds(lanes, 128)] = turned_back(both)
                return carry

            lax.fori_loop(0, HEADS // 2, pair, 0, unroll=HEADS // 2)

        by_count(count, run)
        after = meta[OFF + jnp.minimum(spot + 1, images - 1)]
        end = jnp.where(spot == images - 1, meta[N_FWD], after // TILE)

        def send(t, carry):
            tile_copy(2, t).start()
            return carry

        lax.fori_loop(off // TILE, end, send, 0)

    @pl.when(now == pl.num_programs(0) - 1)
    def _():
        def finish(t, carry):
            for which in range(3):
                tile_copy(which, t).wait()
            return carry

        lax.fori_loop(0, meta[N_FWD], finish, 0)


def turned_back(block):
    size = block.shape[1]
    parts = []
    for start in range(0, size, 128):
        row = lax.broadcasted_iota(jnp.int32, (128, size), 0)
        col = lax.broadcasted_iota(jnp.int32, (128, size), 1)
        eye = jnp.where(row + start == col, 1.0, 0.0).astype(BF16)
        parts.append(dot_bt(eye, block).astype(BF16))
    return parts[0] if len(parts) == 1 else jnp.concatenate(parts, axis=0)


def mlp_kernel(
    chunk, length, meta, cot_in, att_in, tokens_in,
    vecs, out_w, up_w, down_w,
    y_send, mid_grad, att_grad, keep_g, send_g, vec_g, upb_g,
    up_b, held, up_acc, down_acc, out_acc, h2_s, h2t_s, dzt_s, z_s, g_s, sem,
):
    step = pl.program_id(0)
    tiles = held.shape[0] // TILE - WINDOW // TILE
    images = (pl.num_programs(0) - tiles) // 2
    per = cot_in.shape[0]
    width = cot_in.shape[3]
    hidden = up_w.shape[1]
    out_b, gain, shift, down_b = [
        vecs.at[pl.ds(n, 1)] for n in (OUT_B, GAIN_TWO, SHIFT_TWO, DOWN_B)
    ]

    @pl.when(step == 0)
    def _():
        up_acc[...] = jnp.zeros_like(up_acc)
        down_acc[...] = jnp.zeros_like(down_acc)
        out_acc[...] = jnp.zeros_like(out_acc)
        vec_g[...] = jnp.zeros_like(vec_g)
        upb_g[...] = jnp.zeros_like(upb_g)
        for n in range(hidden // width):
            up_b[0:1, n * width : (n + 1) * width] = vecs[UP_B + n : UP_B + n + 1, :]

    @pl.when(step < images)
    def _():
        for i in range(per):
            spot = meta[SPOT + step * per + i]

            @pl.when(meta[LIVE + spot] == 1)
            def _():
                put_rows(
                    held, aligned(meta[OFF + spot]), meta[CNT + spot],
                    cot_in[meta[PEER + spot] // images, 0],
                )

    def run_tile(t, both):
        rows = aligned(t * TILE, TILE)
        ids = row_ids(rows, TILE)
        att = att_in[...]
        att = jnp.where(ids < meta[ROWS_FWD], att, jnp.zeros_like(att))
        mid = tokens_in[...].astype(F32) + (dot(att, out_w[...]) + out_b[...])
        unit, inverse = layer_norm(mid)
        h2 = (unit * gain[...] + shift[...]).astype(BF16)
        h2_s[...] = h2
        z_s[...] = mid + down_b[...]
        if both:
            dz = held[pl.ds(rows, TILE), :]
            dz = jnp.where(ids < meta[ROWS_BWD], dz, jnp.zeros_like(dz))
            h2t_s[...] = turned(h2)
            dzt_s[...] = turned(dz)
            g_s[...] = jnp.zeros_like(g_s)

        def part(c, carry):
            cols = pl.ds(aligned(c * chunk, chunk), chunk)
            pre = dot(h2_s[...], up_w[:, cols]) + up_b[0:1, cols]
            share, slope = gelu_parts(pre)
            act = (pre * share).astype(BF16)
            z_s[...] += dot(act, down_w[cols, :])
            if both:
                pre_g = (dot_bt(dz, down_w[cols, :]) * (share + slope)).astype(BF16)
                up_acc[:, cols] += dot(h2t_s[...], pre_g)
                down_acc[:, cols] += dot(dzt_s[...], act)
                upb_g[0:1, cols] += jnp.sum(pre_g.astype(F32), axis=0, keepdims=True)
                g_s[...] += dot_bt(pre_g, up_w[:, cols])
            return carry

        lax.fori_loop(0, hidden // chunk, part, 0)
        held[pl.ds(rows, TILE), :] = z_s[...].astype(BF16)
        if both:
            dzf = dz.astype(F32)
            g2 = g_s[...]
            dmid = dzf + norm_back(g2, gain[...], unit, inverse)
            branch = dmid.astype(BF16)
            mid_grad[...] = dmid
            att_grad[...] = dot_bt(branch, out_w[...]).astype(BF16)
            out_acc[...] += dot(turned(att), branch)
            vec_g[0:1, :] += jnp.sum(g2 * unit, axis=0, keepdims=True)
            vec_g[1:2, :] += jnp.sum(g2, axis=0, keepdims=True)
            vec_g[2:3, :] += jnp.sum(branch.astype(F32), axis=0, keepdims=True)
            vec_g[3:4, :] += jnp.sum(dzf, axis=0, keepdims=True)

    tile = step - images

    @pl.when(jnp.logical_and(tile >= 0, tile < meta[N_BWD]))
    def _():
        run_tile(tile, True)

    @pl.when(
        jnp.logical_and(
            jnp.logical_and(tile >= meta[N_BWD], tile >= 0),
            jnp.logical_and(tile < meta[N_FWD], tile < tiles),
        )
    )
    def _():
        run_tile(tile, False)

    turn = step - images - tiles

    @pl.when(turn >= 0)
    def _():
        for i in range(per):
            spot = meta[SPOT + turn * per + i]
            block = held[pl.ds(aligned(meta[OFF + spot]), length), :]
            seen = row_ids(0, length) < meta[CNT + spot]
            y_send[meta[PEER + spot] // images, 0, :length, :] = jnp.where(
                seen, block, jnp.zeros_like(block)
            )

    @pl.when(step == pl.num_programs(0) - 1)
    def _():
        share = width // BLOCKS
        long = hidden // BLOCKS
        size = 2 * share + long // 2 + share // 2
        for turn, target in enumerate((send_g, keep_g)):
            h = meta[CORE] if turn else 1 - meta[CORE]
            side = aligned(h * (width // 2), 128)
            copies = []
            for n in range(BLOCKS):
                base = n * size
                if turn:
                    earlier[n].wait()
                for c in range(2):
                    cols = pl.ds(aligned((2 * h + c) * width, 128), width)
                    piece = up_acc[n * share : (n + 1) * share, cols]
                    held[base + c * share : base + (c + 1) * share, :] = piece.astype(BF16)
                base += 2 * share
                piece = down_acc[pl.ds(side, width // 2), n * long : (n + 1) * long]
                flipped = turned(piece.astype(BF16))
                held[base : base + long // 2, : width // 2] = flipped[: long // 2]
                held[base : base + long // 2, width // 2 :] = flipped[long // 2 :]
                base += long // 2
                rows = pl.ds(pl.multiple_of(n * share + h * (share // 2), 8), share // 2)
                held[base : base + share // 2, :] = out_acc[rows, :].astype(BF16)
                copy = pltpu.make_async_copy(
                    held.at[pl.ds(n * size, size)], target.at[n], sem.at[turn, n]
                )
                copy.start()
                copies.append(copy)
            earlier = copies
        for copy in earlier:
            copy.wait()


def attend_back_kernel(
    first, per, meta, slopes, qkv, att_grad, totals, rows_in, cols_in, *rest
):
    grads_out, grads, gaps, sem = rest[-4:]
    step = pl.program_id(0)
    width = att_grad.shape[1]
    spot = first + step
    live = spot < meta[N_LIVE]
    slot = step % 2

    def copy(at):
        rows = pl.ds(aligned(meta[OFF + first + at]), WINDOW)
        return pltpu.make_async_copy(grads.at[at % 2], grads_out.at[rows], sem.at[at % 2])

    @pl.when(live)
    def _():
        count = meta[CNT + spot]

        def run(keys, queries):
            which = meta[IMG + spot] % per
            gaps[:keys, :queries] = distances(rows_in[0], cols_in[0], which, count, keys, queries)
            key_seen = row_ids(0, keys) < count
            query_seen = row_ids(0, queries) < count
            left = lax.broadcasted_iota(jnp.int32, (queries, 128), 1) < 64

            def pair(p, carry):
                lanes = aligned(p * 128, 128)
                q2 = qkv[:queries, pl.ds(lanes, 128)] * 0.125
                k2 = qkv[:keys, pl.ds(width + lanes, 128)]
                v2 = qkv[:keys, pl.ds(2 * width + lanes, 128)]
                o2 = att_grad[:queries, pl.ds(lanes, 128)]
                q2 = jnp.where(query_seen, q2, jnp.zeros_like(q2))
                o2 = jnp.where(query_seen, o2, jnp.zeros_like(o2))
                k2 = jnp.where(key_seen, k2, jnp.zeros_like(k2))
                v2 = jnp.where(key_seen, v2, jnp.zeros_like(v2))
                k2t = turned(k2)
                dq_parts = []
                dk = dv = None
                for half in range(2):
                    head = 2 * p + half
                    mine = left if half == 0 else jnp.logical_not(left)
                    qh = jnp.where(mine, q2, jnp.zeros_like(q2))
                    oh = jnp.where(mine, o2, jnp.zeros_like(o2))
                    scores = dot_bt(k2, qh) - slopes[head] * gaps[:keys, :queries]
                    probs = jnp.exp(scores - totals[0, p, half : half + 1, :queries])
                    prob_g = dot_bt(v2, oh)
                    inner = jnp.sum(probs * prob_g, axis=0, keepdims=True)
                    score_g = (probs * (prob_g - inner)).astype(BF16)
                    dv_part = dot(probs.astype(BF16), oh)
                    dk_part = dot(score_g, qh)
                    dq_parts.append(
                        (dot(k2t[half * 64 : half * 64 + 64], score_g) * 0.125).astype(BF16)
                    )
                    dk = dk_part if dk is None else dk + dk_part
                    dv = dv_part if dv is None else dv + dv_part
                dq = turned_back(jnp.concatenate(dq_parts, axis=0))
                grads[slot, :queries, pl.ds(lanes, 128)] = dq
                grads[slot, :keys, pl.ds(width + lanes, 128)] = dk.astype(BF16)
                grads[slot, :keys, pl.ds(2 * width + lanes, 128)] = dv.astype(BF16)
                return carry

            lax.fori_loop(0, HEADS // 2, pair, 0, unroll=HEADS // 2)

        by_count(count, run)

        @pl.when(step > 0)
        def _():
            copy(step - 1).wait()

        copy(step).start()

        @pl.when(jnp.logical_or(step == pl.num_programs(0) - 1, spot == meta[N_LIVE] - 1))
        def _():
            copy(step).wait()


def qkv_grad_kernel(meta, packed_grad, tokens, vecs, keep_g, send_g, bias_g, acc, stage, sem):
    tile = pl.program_id(0)
    width = tokens.shape[1]

    @pl.when(tile == 0)
    def _():
        acc[...] = jnp.zeros_like(acc)
        bias_g[...] = jnp.zeros_like(bias_g)

    @pl.when(tile < meta[N_BWD])
    def _():
        ids = row_ids(tile * TILE, TILE)
        unit, _ = layer_norm(tokens[...].astype(F32))
        hidden = (
            unit * vecs[GAIN_ONE : GAIN_ONE + 1] + vecs[SHIFT_ONE : SHIFT_ONE + 1]
        ).astype(BF16)
        hidden_t = turned(hidden)
        for part in range(3):
            cols = slice(part * width, (part + 1) * width)
            block = packed_grad[:, cols]
            block = jnp.where(ids < meta[ROWS_BWD], block, jnp.zeros_like(block))
            acc[:, cols] += dot(hidden_t, block)
            bias_g[0:1, cols] += jnp.sum(block.astype(F32), axis=0, keepdims=True)

    @pl.when(tile == pl.num_programs(0) - 1)
    def _():
        rows = width // BLOCKS // 2
        for block in range(BLOCKS):
            for h in range(2):
                for c in range(3):
                    first = (2 * block + h) * rows
                    piece = acc[first : first + rows, c * width : (c + 1) * width]
                    stage[h, block, c * rows : (c + 1) * rows, :] = piece.astype(BF16)
        mine = meta[CORE]
        keep = pltpu.make_async_copy(stage.at[mine], keep_g, sem.at[0])
        send = pltpu.make_async_copy(stage.at[1 - mine], send_g, sem.at[1])
        keep.start()
        send.start()
        keep.wait()
        send.wait()


def token_grad_kernel(meta, packed_grad, tokens, mid_grad, vecs, weight, out, vec_g, held):
    step = pl.program_id(0)
    tiles = held.shape[0] // TILE - WINDOW // TILE
    length, images = out.shape[1], out.shape[2]

    @pl.when(step == 0)
    def _():
        vec_g[...] = jnp.zeros_like(vec_g)

    @pl.when(jnp.logical_and(step < tiles, step < meta[N_BWD]))
    def _():
        rows = aligned(step * TILE, TILE)
        ids = row_ids(rows, TILE)
        unit, inverse = layer_norm(tokens[...].astype(F32))
        block = packed_grad[...]
        block = jnp.where(ids < meta[ROWS_BWD], block, jnp.zeros_like(block))
        g1 = dot_bt(block, weight[...])
        back = norm_back(g1, vecs[GAIN_ONE : GAIN_ONE + 1], unit, inverse)
        held[pl.ds(rows, TILE), :] = mid_grad[...] + back
        vec_g[0:1, :] += jnp.sum(g1 * unit, axis=0, keepdims=True)
        vec_g[1:2, :] += jnp.sum(g1, axis=0, keepdims=True)

    @pl.when(step >= tiles)
    def _():
        parts = []
        for i in range(images):
            spot = meta[SPOT + (step - tiles) * images + i]
            off = aligned(meta[OFF + spot])
            limit = meta[CNT + spot] * meta[LIVE + spot]
            block = held[pl.ds(off, length), :]
            parts.append(jnp.where(row_ids(0, length) < limit, block, 0.0))
        out[0] = jnp.swapaxes(jnp.stack(parts, axis=0), 0, 1)


def whole(*shape):
    return pl.BlockSpec(shape, lambda *_: (0,) * len(shape), pipeline_mode=pl.Buffered(1))


def params():
    return pltpu.CompilerParams(vmem_limit_bytes=VMEM_LIMIT)


def small():
    return pl.BlockSpec(memory_space=pltpu.SMEM)


def prepare(every, counts, present, slots, me, cotangent, *vectors):
    steps, length, images, width = cotangent.shape
    group = every.shape[0]
    padded = (length + 7) // 8 * 8
    return pl.pallas_call(
        prepare_kernel,
        out_shape=(
            jax.ShapeDtypeStruct((PLACES,), jnp.int32),
            jax.ShapeDtypeStruct((steps * images,), jnp.int32),
            jax.ShapeDtypeStruct((16, width), F32),
            jax.ShapeDtypeStruct((group, steps, padded, width), BF16),
        ),
        grid=(steps,),
        in_specs=[small()] * 5
        + [pl.BlockSpec((1, length, images, width), lambda m: (m, 0, 0, 0))]
        + [whole(*vector.shape) for vector in vectors],
        out_specs=[
            small(),
            small(),
            whole(16, width),
            pl.BlockSpec((group, 1, padded, width), lambda m: (0, m, 0, 0)),
        ],
        compiler_params=params(),
    )(every, counts, present, slots, me, cotangent, *vectors)


def place(take, got, length):
    group, steps, padded, width = got.shape
    return pl.pallas_call(
        place_kernel,
        out_shape=jax.ShapeDtypeStruct((steps, length, group, width), BF16),
        grid=(steps,),
        in_specs=[small(), pl.BlockSpec((group, 1, padded, width), lambda m: (0, m, 0, 0))],
        out_specs=pl.BlockSpec((1, length, group, width), lambda m: (m, 0, 0, 0)),
        compiler_params=params(),
    )(take, got)


def first_half(meta, slopes, tokens, rows, cols, vecs, weight):
    steps, length, per, width = tokens.shape
    images = steps * per
    tiles = -(-images * ((length + 15) // 16 * 16) // TILE)
    total = tiles * TILE + WINDOW
    spots = pl.BlockSpec(
        (1, per, length),
        lambda s, meta, slopes: (meta[IMG + jnp.maximum(s - steps, 0)] // per, 0, 0),
    )
    return pl.pallas_call(
        attend_kernel,
        out_shape=(
            jax.ShapeDtypeStruct((total, width), BF16),
            jax.ShapeDtypeStruct((total, 3 * width), BF16),
            jax.ShapeDtypeStruct((total, width), BF16),
            jax.ShapeDtypeStruct((images, HEADS // 2, 8, WINDOW), F32),
        ),
        grid_spec=pltpu.PrefetchScalarGridSpec(
            num_scalar_prefetch=2,
            grid=(steps + images,),
            in_specs=[
                pl.BlockSpec(
                    (1, length, per, width),
                    lambda s, meta, slopes: (jnp.minimum(s, steps - 1), 0, 0, 0),
                ),
                spots,
                spots,
                whole(*vecs.shape),
                whole(width, 3 * width),
            ],
            out_specs=[
                pl.BlockSpec(memory_space=pl.ANY),
                pl.BlockSpec(memory_space=pl.ANY),
                pl.BlockSpec(memory_space=pl.ANY),
                pl.BlockSpec(
                    (1, HEADS // 2, 8, WINDOW),
                    lambda s, meta, slopes: (jnp.maximum(s - steps, 0), 0, 0, 0),
                ),
            ],
            scratch_shapes=[
                pltpu.VMEM((total, width), BF16),
                pltpu.VMEM((total, 3 * width), BF16),
                pltpu.VMEM((total, width), BF16),
                pltpu.VMEM((WINDOW, WINDOW), F32),
                pltpu.SemaphoreType.DMA((tiles,)),
                pltpu.SemaphoreType.DMA((tiles,)),
                pltpu.SemaphoreType.DMA((tiles,)),
            ],
        ),
        compiler_params=params(),
        cost_estimate=cost(40),
    )(meta, slopes, tokens, rows, cols, vecs, weight)


def mlp(meta, cot, att, packed, vecs, out_w, up_w, down_w, length):
    group, steps, padded, width = cot.shape
    rows = packed.shape[0]
    tiles = (rows - WINDOW) // TILE
    hidden = up_w.shape[1]
    parcel = (2 * width + hidden // 2 + width // 2) // BLOCKS
    def fwd_tile(s, meta):
        return (jnp.clip(s - steps, 0, meta[N_FWD] - 1), 0)

    def bwd_tile(s, meta):
        return (jnp.clip(s - steps, 0, jnp.maximum(meta[N_BWD] - 1, 0)), 0)

    return pl.pallas_call(
        functools.partial(mlp_kernel, CHUNK, length),
        out_shape=(
            jax.ShapeDtypeStruct(cot.shape, BF16),
            jax.ShapeDtypeStruct((rows, width), F32),
            jax.ShapeDtypeStruct((rows, width), BF16),
            jax.ShapeDtypeStruct((BLOCKS, parcel, width), BF16),
            jax.ShapeDtypeStruct((BLOCKS, parcel, width), BF16),
            jax.ShapeDtypeStruct((8, width), F32),
            jax.ShapeDtypeStruct((8, hidden), F32),
        ),
        grid_spec=pltpu.PrefetchScalarGridSpec(
            num_scalar_prefetch=1,
            grid=(2 * steps + tiles,),
            in_specs=[
                pl.BlockSpec(
                    (group, 1, padded, width), lambda s, meta: (0, jnp.minimum(s, steps - 1), 0, 0)
                ),
                pl.BlockSpec((TILE, width), fwd_tile),
                pl.BlockSpec((TILE, width), fwd_tile),
                whole(*vecs.shape),
                whole(width, width),
                whole(width, hidden),
                whole(hidden, width),
            ],
            out_specs=[
                pl.BlockSpec(
                    (group, 1, padded, width),
                    lambda s, meta: (0, jnp.clip(s - steps - tiles, 0, steps - 1), 0, 0),
                ),
                pl.BlockSpec((TILE, width), bwd_tile),
                pl.BlockSpec((TILE, width), bwd_tile),
                pl.BlockSpec(memory_space=pl.ANY),
                pl.BlockSpec(memory_space=pl.ANY),
                whole(8, width),
                whole(8, hidden),
            ],
            scratch_shapes=[
                pltpu.VMEM((8, hidden), F32),
                pltpu.VMEM((rows, width), BF16),
                pltpu.VMEM((width, hidden), F32),
                pltpu.VMEM((width, hidden), F32),
                pltpu.VMEM((width, width), F32),
                pltpu.VMEM((TILE, width), BF16),
                pltpu.VMEM((width, TILE), BF16),
                pltpu.VMEM((width, TILE), BF16),
                pltpu.VMEM((TILE, width), F32),
                pltpu.VMEM((TILE, width), F32),
                pltpu.SemaphoreType.DMA((2, BLOCKS)),
            ],
        ),
        compiler_params=params(),
        cost_estimate=cost(110),
    )(meta, cot, att, packed, vecs, out_w, up_w, down_w)


def attend_back(first, count, expected, meta, slopes, qkv, att_grad, totals, rows_in, cols_in, earlier):
    total, wide = qkv.shape
    width = wide // 3
    per, length = rows_in.shape[1:]

    def spot_of(s, meta):
        return jnp.clip(first + s, 0, jnp.maximum(meta[N_LIVE] - 1, 0))

    def by_offset(s, meta, slopes):
        return (aligned(meta[OFF + spot_of(s, meta)]), 0)

    spots = pl.BlockSpec(
        (1, per, length),
        lambda s, meta, slopes: (meta[IMG + spot_of(s, meta)] // per, 0, 0),
    )
    anywhere = pl.BlockSpec(memory_space=pl.ANY)
    return pl.pallas_call(
        functools.partial(attend_back_kernel, first, per),
        out_shape=jax.ShapeDtypeStruct((total, wide), BF16),
        grid_spec=pltpu.PrefetchScalarGridSpec(
            num_scalar_prefetch=2,
            grid=(count,),
            in_specs=[
                pl.BlockSpec((pl.Element(WINDOW), pl.Element(wide)), by_offset),
                pl.BlockSpec((pl.Element(WINDOW), pl.Element(width)), by_offset),
                pl.BlockSpec(
                    (1, HEADS // 2, 8, WINDOW),
                    lambda s, meta, slopes: (spot_of(s, meta), 0, 0, 0),
                ),
                spots,
                spots,
            ]
            + [anywhere] * len(earlier),
            out_specs=anywhere,
            scratch_shapes=[
                pltpu.VMEM((2, WINDOW, wide), BF16),
                pltpu.VMEM((WINDOW, WINDOW), F32),
                pltpu.SemaphoreType.DMA((2,)),
            ],
        ),
        input_output_aliases={7: 0} if earlier else {},
        compiler_params=params(),
        cost_estimate=cost(expected),
    )(meta, slopes, qkv, att_grad, totals, rows_in, cols_in, *earlier)


def bwd_tile(s, meta):
    return (jnp.clip(s, 0, jnp.maximum(meta[N_BWD] - 1, 0)), 0)


def qkv_grad(meta, packed_grad, packed, vecs):
    rows, width = packed.shape
    parcel = 3 * width // 2 // BLOCKS
    tiles = (rows - WINDOW) // TILE
    return pl.pallas_call(
        qkv_grad_kernel,
        out_shape=(
            jax.ShapeDtypeStruct((BLOCKS, parcel, width), BF16),
            jax.ShapeDtypeStruct((BLOCKS, parcel, width), BF16),
            jax.ShapeDtypeStruct((8, 3 * width), F32),
        ),
        grid_spec=pltpu.PrefetchScalarGridSpec(
            num_scalar_prefetch=1,
            grid=(tiles,),
            in_specs=[
                pl.BlockSpec((TILE, 3 * width), bwd_tile),
                pl.BlockSpec((TILE, width), bwd_tile),
                whole(*vecs.shape),
            ],
            out_specs=[
                pl.BlockSpec(memory_space=pl.ANY),
                pl.BlockSpec(memory_space=pl.ANY),
                whole(8, 3 * width),
            ],
            scratch_shapes=[
                pltpu.VMEM((width, 3 * width), F32),
                pltpu.VMEM((2, BLOCKS, parcel, width), BF16),
                pltpu.SemaphoreType.DMA((2,)),
            ],
        ),
        compiler_params=params(),
        cost_estimate=cost(15),
    )(meta, packed_grad, packed, vecs)


def token_grad(meta, packed_grad, packed, mid_grad, vecs, weight, steps, length, images):
    rows, width = packed.shape
    tiles = (rows - WINDOW) // TILE
    return pl.pallas_call(
        token_grad_kernel,
        out_shape=(
            jax.ShapeDtypeStruct((steps, length, images, width), F32),
            jax.ShapeDtypeStruct((8, width), F32),
        ),
        grid_spec=pltpu.PrefetchScalarGridSpec(
            num_scalar_prefetch=1,
            grid=(tiles + steps,),
            in_specs=[
                pl.BlockSpec((TILE, 3 * width), bwd_tile),
                pl.BlockSpec((TILE, width), bwd_tile),
                pl.BlockSpec((TILE, width), bwd_tile),
                whole(*vecs.shape),
                whole(width, 3 * width),
            ],
            out_specs=[
                pl.BlockSpec(
                    (1, length, images, width),
                    lambda s, meta: (jnp.clip(s - tiles, 0, steps - 1), 0, 0, 0),
                ),
                whole(8, width),
            ],
            scratch_shapes=[pltpu.VMEM((rows, width), F32)],
        ),
        compiler_params=params(),
        cost_estimate=cost(20),
    )(meta, packed_grad, packed, mid_grad, vecs, weight)


def cost(microseconds):
    return pl.CostEstimate(
        flops=int(microseconds * 1e9), bytes_accessed=int(microseconds * 1e5), transcendentals=0
    )


def swap(block, axis, bit):
    size = lax.axis_size(axis)
    return lax.ppermute(block, axis, [(n, n ^ bit) for n in range(size)])


def bit_of(axis, bit):
    return lax.axis_index(axis) // bit % 2


def added(a, b):
    return (a.astype(F32) + b.astype(F32)).astype(BF16)


def unpacked(mine, other, shapes):
    swapped = bit_of("bal", 1) == 1
    first = jnp.where(swapped, other, mine)
    second = jnp.where(swapped, mine, other)
    lead, width = mine.shape[:-2], mine.shape[-1]
    out, at = [], 0
    for rows, columns, kind in shapes:
        wide = columns // width
        part = rows * wide // 2
        held = [half[..., at : at + part, :] for half in (first, second)]
        if kind == "rows":
            size = rows // 2
            parts = [
                jnp.concatenate(
                    [half[..., c * size : (c + 1) * size, :] for c in range(wide)], axis=-1
                )
                for half in held
            ]
            out.append(jnp.concatenate(parts, axis=-2))
        elif kind == "columns":
            parts = [
                half[..., c * rows : (c + 1) * rows, :] for half in held for c in range(wide // 2)
            ]
            out.append(jnp.concatenate(parts, axis=-1))
        else:
            size = width // 2
            tops = [half[..., :size] for half in held]
            bottoms = [half[..., size:] for half in held]
            out.append(
                jnp.concatenate(
                    [jnp.concatenate(tops, axis=-1), jnp.concatenate(bottoms, axis=-1)], axis=-2
                )
            )
        at += part
    return [matrix.reshape(lead[:-1] + (-1, matrix.shape[-1])) if lead else matrix for matrix in out]


def spread_sum(keep, send, shapes):
    return [
        lax.psum(lax.psum_scatter(matrix, "dp", scatter_dimension=0, tiled=True), "bal").astype(F32)
        for matrix in unpacked(keep, send, shapes)
    ]


def start_fold(block, bit):
    block = block.reshape((-1, 2) + block.shape[-2:])
    mine = bit_of("dp", bit)
    keep = lax.dynamic_index_in_dim(block, mine, 1, keepdims=False)
    send = lax.dynamic_index_in_dim(block, 1 - mine, 1, keepdims=False)
    return keep, swap(send, "dp", bit)


def fold(block, bit):
    return added(*start_fold(block, bit))


def after(value, *others):
    return lax.optimization_barrier((value,) + others)[0]


def doubled(block, round_no):
    bits = []
    for axis in ("bal", "dp"):
        bit = 1
        while bit < lax.axis_size(axis):
            bits.append((axis, bit))
            bit *= 2
    if round_no is None:
        return len(bits)
    axis, bit = bits[round_no]
    return block + swap(block, axis, bit)


def per_device(
    tokens,
    cotangent,
    counts,
    rows,
    cols,
    present,
    slots,
    first_gain,
    first_shift,
    qkv_weight,
    query_bias,
    value_bias,
    out_weight,
    out_bias,
    second_gain,
    second_shift,
    up_weight,
    up_bias,
    down_weight,
    down_bias,
):
    steps, images, length, width = tokens.shape
    hidden = up_weight.shape[1]
    group = lax.axis_size("bal")
    total = steps * images
    slopes = jnp.exp2(-8.0 * (jnp.arange(16, dtype=F32) + 1.0) / HEADS)

    def exchange(blocks):
        flat = blocks.reshape(group, -1, width)
        return lax.all_to_all(flat, "bal", split_axis=0, concat_axis=0, tiled=True)

    def turn(array):
        return jnp.transpose(array, (0, 2, 1, 3))

    meta, take, vecs, cot_send = prepare(
        lax.all_gather(slots, "bal"), counts, present, slots,
        lax.axis_index("bal").astype(jnp.int32).reshape(1), turn(cotangent),
        first_gain, first_shift, query_bias, value_bias, out_bias, second_gain, second_shift,
        down_bias, up_bias,
    )
    cot_home = exchange(cot_send).reshape(group, steps, -1, width)
    packed, qkv, att, totals = first_half(meta, slopes, turn(tokens), rows, cols, vecs, qkv_weight)
    y_send, mid_grad, att_grad, keep_two, send_two, vec_two, upb_g = mlp(
        meta, cot_home, att, packed, vecs, out_weight, up_weight, down_weight, length
    )
    y_got = exchange(y_send)

    share, long = width // BLOCKS, hidden // BLOCKS
    shapes_two = ((share, hidden, "columns"), (long, width, "side"), (share, width, "rows"))
    shapes_one = ((share, 3 * width, "rows"),)
    direct = lax.axis_size("dp") == BLOCKS

    def back(first, count, expected, table, earlier):
        return attend_back(
            first, count, expected, table, slopes, qkv, att_grad, totals, rows, cols, earlier
        )

    lead = max(images // 2, 1)
    packed_grad = back(0, lead, 15, meta, ())
    table = meta
    if direct:
        sum_two = added(after(keep_two, packed_grad), swap(send_two, "bal", 1))
        share_two = lax.psum_scatter(sum_two, "dp", scatter_dimension=0, tiled=True)[0]
        table = after(meta, sum_two)
    packed_grad = back(lead, total - lead, 500, table, (packed_grad,))
    keep_one, send_one, bias_g = qkv_grad(after(table, y_got), packed_grad, packed, vecs)
    output = place(after(take, keep_one), y_got.reshape(group, steps, -1, width), length)
    table = after(table, output)
    if direct:
        sum_one = added(keep_one, swap(send_one, "bal", 1))
        table = after(table, sum_one)
    input_grad, vec_one = token_grad(
        table, packed_grad, packed, mid_grad, vecs, qkv_weight, steps, length, images
    )
    vectors = jnp.concatenate(
        [
            vec_one[:2].reshape(-1), bias_g[0, :width], bias_g[0, 2 * width :],
            vec_two[:4].reshape(-1), upb_g[0],
        ]
    )
    rounds = doubled(vectors, None)
    if direct:
        half_one = fold(sum_one, 1)
        keep, crossing = start_fold(half_one, 2)
        across = swap(share_two, "bal", 2)
        for n in range(3):
            vectors = doubled(vectors, n)
        block = added(after(keep, vectors), crossing)
        keep, crossing = start_fold(block, 4)
        vectors = after(vectors, block)
        for n in range(3, rounds):
            vectors = doubled(vectors, n)
        full_two = added(after(share_two, vectors), across)
        other_two = swap(full_two, "bal", 1)
        up_rows, down_rows, out_rows = [
            matrix.astype(F32) for matrix in unpacked(full_two, other_two, shapes_two)
        ]
        block = added(after(keep, full_two), crossing).reshape(sum_one.shape[-2:])
        full_one = added(block, swap(block, "bal", 2))
        (qkv_rows,) = [
            matrix.astype(F32)
            for matrix in unpacked(full_one, swap(full_one, "bal", 1), shapes_one)
        ]
    else:
        (qkv_rows,) = spread_sum(keep_one, send_one, shapes_one)
        up_rows, down_rows, out_rows = spread_sum(keep_two, send_two, shapes_two)
        for n in range(rounds):
            vectors = doubled(vectors, n)

    def vector(n):
        return vectors[n * width : (n + 1) * width]

    return (
        turn(output),
        turn(input_grad),
        vector(0),
        vector(1),
        qkv_rows,
        vector(2),
        vector(3),
        out_rows,
        vector(6),
        vector(4),
        vector(5),
        up_rows,
        vectors[8 * width :],
        down_rows,
        vector(7),
    )


def solution(mesh):
    images = P(None, ("dp", "bal"), None, None)
    spots = P(None, ("dp", "bal"), None)
    flags = P(None, ("dp", "bal"))
    matrix = P("dp", None)
    return jax.shard_map(
        per_device,
        mesh=mesh,
        in_specs=(images, images, flags, spots, spots, flags, flags) + (P(),) * 13,
        out_specs=(
            images, images, P(), P(), matrix, P(), P(), matrix, P(), P(), P(), matrix, P(), matrix, P(),
        ),
        check_vma=False,
    )
```

```python
import functools
import math

import jax
import jax.numpy as jnp
from jax import lax
from jax.experimental import pallas as pl
from jax.experimental.pallas import tpu as pltpu
from jax.sharding import PartitionSpec as P

HEADS = 12
TILE = 256
WINDOW = 256
FAR = 1e12
EPS = 1e-06
BLOCKS = 8
CHUNK = 1536
VMEM_LIMIT = 60 * 1024 * 1024

F32 = jnp.float32
BF16 = jnp.bfloat16

OFF, CNT, IMG, LIVE, PEER, SPOT, MISC = 0, 16, 32, 48, 64, 80, 96
N_FWD, N_BWD, ROWS_FWD, ROWS_BWD, N_LIVE, CORE = range(MISC, MISC + 6)
PLACES = 128

GAIN_ONE, SHIFT_ONE, QKV_B, OUT_B, GAIN_TWO, SHIFT_TWO, DOWN_B, UP_B = 0, 1, 2, 5, 6, 7, 8, 9
VECTORS = (GAIN_ONE, SHIFT_ONE, QKV_B, QKV_B + 2, OUT_B, GAIN_TWO, SHIFT_TWO, DOWN_B, UP_B)


def dot(a, b):
    return jnp.dot(a, b, preferred_element_type=F32)


def dot_bt(a, b):
    return lax.dot_general(a, b, (((1,), (1,)), ((), ())), preferred_element_type=F32)


def turned(block):
    return block.astype(F32).T.astype(BF16)


def layer_norm(values):
    average = jnp.mean(values, axis=-1, keepdims=True)
    centred = values - average
    spread = jnp.mean(centred * centred, axis=-1, keepdims=True)
    inverse = lax.rsqrt(spread + EPS)
    return centred * inverse, inverse


def norm_back(out_grad, gain, unit, inverse):
    e = out_grad * gain
    mean_e = jnp.mean(e, axis=-1, keepdims=True)
    mean_eu = jnp.mean(e * unit, axis=-1, keepdims=True)
    return inverse * (e - mean_e - unit * mean_eu)


def gelu_parts(u):
    size = jnp.abs(u)
    t = 1.0 / (1.0 + (0.3275911 * math.sqrt(0.5)) * size)
    bell = jnp.exp(-0.5 * (u * u))
    poly = t * (
        0.5 * 0.254829592
        + t
        * (
            0.5 * -0.284496736
            + t * (0.5 * 1.421413741 + t * (0.5 * -1.453152027 + t * (0.5 * 1.061405429)))
        )
    )
    tail = poly * bell
    phi_sum = jnp.where(u >= 0, 1.0 - tail, tail)
    return phi_sum, u * bell * (1.0 / math.sqrt(2.0 * math.pi))


def put_rows(packed, off, count, block):
    rows = (block.shape[0] + 15) // 16 * 16
    if rows > block.shape[0]:
        more = jnp.zeros((rows - block.shape[0], block.shape[1]), block.dtype)
        block = jnp.concatenate([block, more], axis=0)
    ids = row_ids(0, rows)
    window = pl.ds(off, rows)
    block = jnp.where(ids < count, block, jnp.zeros_like(block))
    packed[window, :] = jnp.where(ids < (count + 15) // 16 * 16, block, packed[window, :])


def row_ids(start, rows):
    return start + lax.broadcasted_iota(jnp.int32, (rows, 1), 0)


def aligned(value, step=16):
    return pl.multiple_of(value, step)


def by_count(count, run):
    @pl.when(count <= 128)
    def _():
        run(128, 128)

    @pl.when(jnp.logical_and(count > 128, count <= 192))
    def _():
        run(192, 256)

    @pl.when(count > 192)
    def _():
        run(256, 256)


def distances(rows, cols, which, count, keys, queries):
    mine = lax.broadcasted_iota(jnp.int32, rows.shape, 0) == which
    row = jnp.sum(jnp.where(mine, rows, 0).astype(F32), axis=0, keepdims=True)
    col = jnp.sum(jnp.where(mine, cols, 0).astype(F32), axis=0, keepdims=True)
    spots = jnp.concatenate([row, col, jnp.zeros((6, row.shape[1]), F32)], axis=0)
    spots = jnp.concatenate([spots, jnp.zeros((8, WINDOW - row.shape[1]), F32)], axis=1)
    eye = jnp.where(
        lax.broadcasted_iota(jnp.int32, (keys, WINDOW), 0)
        == lax.broadcasted_iota(jnp.int32, (keys, WINDOW), 1),
        1.0,
        0.0,
    ).astype(BF16)
    turned_spots = dot_bt(eye, spots.astype(BF16))
    down = turned_spots[:, 0:1] - spots[0:1, :queries]
    across = turned_spots[:, 1:2] - spots[1:2, :queries]
    far = row_ids(0, keys) >= count
    return jnp.where(far, FAR, jnp.sqrt(down * down + across * across))


def prepare_kernel(every, counts, present, slots, me, cot, *rest):
    *lines, meta, take, vecs, send = rest
    step = pl.program_id(0)
    steps, length, images, width = pl.num_programs(0), cot.shape[1], cot.shape[2], cot.shape[3]
    group = every.shape[0]

    @pl.when(step == 0)
    def _():
        def fill(live):
            def body(img, carry):
                spot, off = carry
                m, i = img // images, img % images
                count = counts[m, i]
                mine = present[m, i] == live

                @pl.when(mine)
                def _():
                    meta[OFF + spot] = off
                    meta[CNT + spot] = count
                    meta[IMG + spot] = img
                    meta[LIVE + spot] = live
                    meta[PEER + spot] = slots[m, i] // images * steps + m
                    meta[SPOT + img] = spot

                padded = (count + 15) // 16 * 16
                return spot + mine.astype(jnp.int32), off + jnp.where(mine, padded, 0)

            return body

        meta[CORE] = me[0] % 2
        vecs[...] = jnp.zeros_like(vecs)
        for row, values in zip(VECTORS, lines):
            for n in range(values.shape[0] // width):
                piece = values[n * width : (n + 1) * width]
                vecs[row + n : row + n + 1, :] = piece.reshape(1, width)
        zero = jnp.int32(0)
        total = counts.shape[0] * images
        spot, off = lax.fori_loop(0, total, fill(1), (zero, zero))
        meta[N_LIVE] = spot
        meta[ROWS_BWD] = off
        meta[N_BWD] = (off + TILE - 1) // TILE
        spot, off = lax.fori_loop(0, total, fill(0), (spot, off))
        meta[ROWS_FWD] = off
        meta[N_FWD] = (off + TILE - 1) // TILE

        def land(n, carry):
            a, m, i = n // total, n % total // images, n % images
            slot = every[a, m, i]

            @pl.when(slot // images == me[0])
            def _():
                take[m * images + slot % images] = a * steps + m

            return carry

        lax.fori_loop(0, group * total, land, 0)

    block = jnp.swapaxes(cot[0].astype(F32), 0, 1).astype(BF16)
    for place in range(images):
        peer = take[step * images + place] // steps
        send[peer, 0, :length, :] = block[place]


def place_kernel(take, got, out):
    step = pl.program_id(0)
    length, images = out.shape[1], out.shape[2]
    steps = pl.num_programs(0)
    parts = [
        got[take[step * images + place] // steps, 0, :length, :].astype(F32)
        for place in range(images)
    ]
    out[0] = jnp.swapaxes(jnp.stack(parts, axis=0), 0, 1).astype(out.dtype)


def attend_kernel(
    meta, slopes, tokens, rows_in, cols_in, vecs, weight,
    packed_out, qkv_out, att_out, total_out,
    packed, qkv, att, gaps, sem_packed, sem_qkv, sem_att,
):
    length, per, width = tokens.shape[1], tokens.shape[2], tokens.shape[3]
    steps = pl.num_programs(0) // (per + 1)
    images = steps * per
    now = pl.program_id(0)

    def tile_copy(which, t):
        src, dst, sem = (
            (packed, packed_out, sem_packed),
            (qkv, qkv_out, sem_qkv),
            (att, att_out, sem_att),
        )[which]
        rows = pl.ds(aligned(t * TILE, TILE), TILE)
        return pltpu.make_async_copy(src.at[rows], dst.at[rows], sem.at[t])

    @pl.when(now == 0)
    def _():
        packed[...] = jnp.zeros_like(packed)

    @pl.when(now < steps)
    def _():
        block = jnp.swapaxes(tokens[0].astype(F32), 0, 1).astype(BF16)
        for i in range(per):
            spot = meta[SPOT + now * per + i]
            put_rows(packed, aligned(meta[OFF + spot]), meta[CNT + spot], block[i])

    @pl.when(now == steps - 1)
    def _():

        def project(t, carry):
            rows = pl.ds(aligned(t * TILE, TILE), TILE)
            unit, _ = layer_norm(packed[rows, :].astype(F32))
            hidden = (
                unit * vecs[GAIN_ONE : GAIN_ONE + 1] + vecs[SHIFT_ONE : SHIFT_ONE + 1]
            ).astype(BF16)
            for part in range(3):
                cols = slice(part * width, (part + 1) * width)
                bias = vecs[QKV_B + part : QKV_B + part + 1]
                qkv[rows, cols] = (dot(hidden, weight[:, cols]) + bias).astype(BF16)
            tile_copy(0, t).start()
            tile_copy(1, t).start()
            return carry

        lax.fori_loop(0, meta[N_FWD], project, 0)

    @pl.when(now >= steps)
    def _():
        spot = now - steps
        off = aligned(meta[OFF + spot])
        count = meta[CNT + spot]

        def run(keys, queries):
            which = meta[IMG + spot] % per
            gaps[:keys, :queries] = distances(rows_in[0], cols_in[0], which, count, keys, queries)
            key_seen = row_ids(0, keys) < count
            query_seen = row_ids(0, queries) < count
            left = lax.broadcasted_iota(jnp.int32, (keys, 128), 1) < 64

            def pair(p, carry):
                lanes = aligned(p * 128, 128)
                q2 = qkv[pl.ds(off, queries), pl.ds(lanes, 128)] * 0.125
                k2 = qkv[pl.ds(off, keys), pl.ds(width + lanes, 128)]
                v2 = qkv[pl.ds(off, keys), pl.ds(2 * width + lanes, 128)]
                q2 = jnp.where(query_seen, q2, jnp.zeros_like(q2))
                k2 = jnp.where(key_seen, k2, jnp.zeros_like(k2))
                v2 = jnp.where(key_seen, v2, jnp.zeros_like(v2))
                v2t = v2.astype(F32).T.astype(BF16)
                raw = dot_bt(by_head(k2, left), q2)
                outs = []
                for half in range(2):
                    head = 2 * p + half
                    scores = raw[half * keys : (half + 1) * keys]
                    scores = scores - slopes[head] * gaps[:keys, :queries]
                    top = jnp.max(scores, axis=0, keepdims=True)
                    terms = jnp.exp(scores - top)
                    total = jnp.sum(terms, axis=0, keepdims=True)
                    heads_out = dot(v2t[half * 64 : half * 64 + 64], terms.astype(BF16))
                    outs.append(heads_out * (1.0 / total))
                    total_out[0, p, half : half + 1, :queries] = top + jnp.log(total)
                both = jnp.concatenate(outs, axis=0)
                att[pl.ds(off, queries), pl.ds(lanes, 128)] = both.T.astype(BF16)
                return carry

            lax.fori_loop(0, HEADS // 2, pair, 0, unroll=HEADS // 2)

        by_count(count, run)
        after = meta[OFF + jnp.minimum(spot + 1, images - 1)]
        end = jnp.where(spot == images - 1, meta[N_FWD], after // TILE)

        def send(t, carry):
            tile_copy(2, t).start()
            return carry

        lax.fori_loop(off // TILE, end, send, 0)

    @pl.when(now == pl.num_programs(0) - 1)
    def _():
        def finish(t, carry):
            for which in range(3):
                tile_copy(which, t).wait()
            return carry

        lax.fori_loop(0, meta[N_FWD], finish, 0)


def by_head(block, left):
    none = jnp.zeros_like(block)
    return jnp.concatenate([jnp.where(left, block, none), jnp.where(left, none, block)], axis=0)


def mlp_kernel(
    chunk, length, meta, cot_in, att_in, tokens_in,
    vecs, out_w, up_w, down_w,
    y_send, mid_grad, att_grad, keep_g, send_g, vec_g, upb_g,
    up_b, held, up_acc, down_acc, out_acc, h2_s, h2t_s, dzt_s, z_s, g_s, sem,
):
    step = pl.program_id(0)
    tiles = held.shape[0] // TILE - WINDOW // TILE
    images = (pl.num_programs(0) - tiles) // 2
    per = cot_in.shape[0]
    width = cot_in.shape[3]
    hidden = up_w.shape[1]
    out_b, gain, shift, down_b = [
        vecs.at[pl.ds(n, 1)] for n in (OUT_B, GAIN_TWO, SHIFT_TWO, DOWN_B)
    ]

    @pl.when(step == 0)
    def _():
        up_acc[...] = jnp.zeros_like(up_acc)
        down_acc[...] = jnp.zeros_like(down_acc)
        out_acc[...] = jnp.zeros_like(out_acc)
        vec_g[...] = jnp.zeros_like(vec_g)
        upb_g[...] = jnp.zeros_like(upb_g)
        for n in range(hidden // width):
            up_b[0:1, n * width : (n + 1) * width] = vecs[UP_B + n : UP_B + n + 1, :]

    @pl.when(step < images)
    def _():
        for i in range(per):
            spot = meta[SPOT + step * per + i]

            @pl.when(meta[LIVE + spot] == 1)
            def _():
                put_rows(
                    held, aligned(meta[OFF + spot]), meta[CNT + spot],
                    cot_in[meta[PEER + spot] // images, 0],
                )

    def run_tile(t, both):
        rows = aligned(t * TILE, TILE)
        ids = row_ids(rows, TILE)
        att = att_in[...]
        att = jnp.where(ids < meta[ROWS_FWD], att, jnp.zeros_like(att))
        mid = tokens_in[...].astype(F32) + (dot(att, out_w[...]) + out_b[...])
        unit, inverse = layer_norm(mid)
        h2 = (unit * gain[...] + shift[...]).astype(BF16)
        h2_s[...] = h2
        z_s[...] = mid + down_b[...]
        if both:
            dz = held[pl.ds(rows, TILE), :]
            dz = jnp.where(ids < meta[ROWS_BWD], dz, jnp.zeros_like(dz))
            h2t_s[...] = turned(h2)
            dzt_s[...] = turned(dz)
            g_s[...] = jnp.zeros_like(g_s)

        def part(c, carry):
            cols = pl.ds(aligned(c * chunk, chunk), chunk)
            pre = dot(h2_s[...], up_w[:, cols]) + up_b[0:1, cols]
            share, slope = gelu_parts(pre)
            act = (pre * share).astype(BF16)
            z_s[...] += dot(act, down_w[cols, :])
            if both:
                pre_g = (dot_bt(dz, down_w[cols, :]) * (share + slope)).astype(BF16)
                up_acc[:, cols] += dot(h2t_s[...], pre_g)
                down_acc[:, cols] += dot(dzt_s[...], act)
                upb_g[0:1, cols] += jnp.sum(pre_g.astype(F32), axis=0, keepdims=True)
                g_s[...] += dot_bt(pre_g, up_w[:, cols])
            return carry

        lax.fori_loop(0, hidden // chunk, part, 0)
        held[pl.ds(rows, TILE), :] = z_s[...].astype(BF16)
        if both:
            dzf = dz.astype(F32)
            g2 = g_s[...]
            dmid = dzf + norm_back(g2, gain[...], unit, inverse)
            branch = dmid.astype(BF16)
            mid_grad[...] = dmid
            att_grad[...] = dot_bt(branch, out_w[...]).astype(BF16)
            out_acc[...] += dot(turned(att), branch)
            vec_g[0:1, :] += jnp.sum(g2 * unit, axis=0, keepdims=True)
            vec_g[1:2, :] += jnp.sum(g2, axis=0, keepdims=True)
            vec_g[2:3, :] += jnp.sum(branch.astype(F32), axis=0, keepdims=True)
            vec_g[3:4, :] += jnp.sum(dzf, axis=0, keepdims=True)

    tile = step - images

    @pl.when(jnp.logical_and(tile >= 0, tile < meta[N_BWD]))
    def _():
        run_tile(tile, True)

    @pl.when(
        jnp.logical_and(
            jnp.logical_and(tile >= meta[N_BWD], tile >= 0),
            jnp.logical_and(tile < meta[N_FWD], tile < tiles),
        )
    )
    def _():
        run_tile(tile, False)

    turn = step - images - tiles

    @pl.when(turn >= 0)
    def _():
        for i in range(per):
            spot = meta[SPOT + turn * per + i]
            block = held[pl.ds(aligned(meta[OFF + spot]), length), :]
            seen = row_ids(0, length) < meta[CNT + spot]
            y_send[meta[PEER + spot] // images, 0, :length, :] = jnp.where(
                seen, block, jnp.zeros_like(block)
            )

    @pl.when(step == pl.num_programs(0) - 1)
    def _():
        share = width // BLOCKS
        long = hidden // BLOCKS
        size = 2 * share + long // 2 + share // 2
        for turn, target in enumerate((send_g, keep_g)):
            h = meta[CORE] if turn else 1 - meta[CORE]
            side = aligned(h * (width // 2), 128)
            copies = []
            for n in range(BLOCKS):
                base = n * size
                if turn:
                    earlier[n].wait()
                for c in range(2):
                    cols = pl.ds(aligned((2 * h + c) * width, 128), width)
                    piece = up_acc[n * share : (n + 1) * share, cols]
                    held[base + c * share : base + (c + 1) * share, :] = piece.astype(BF16)
                base += 2 * share
                piece = down_acc[pl.ds(side, width // 2), n * long : (n + 1) * long]
                flipped = turned(piece.astype(BF16))
                held[base : base + long // 2, : width // 2] = flipped[: long // 2]
                held[base : base + long // 2, width // 2 :] = flipped[long // 2 :]
                base += long // 2
                rows = pl.ds(pl.multiple_of(n * share + h * (share // 2), 8), share // 2)
                held[base : base + share // 2, :] = out_acc[rows, :].astype(BF16)
                copy = pltpu.make_async_copy(
                    held.at[pl.ds(n * size, size)], target.at[n], sem.at[turn, n]
                )
                copy.start()
                copies.append(copy)
            earlier = copies
        for copy in earlier:
            copy.wait()


def attend_back_kernel(
    first, per, meta, slopes, qkv, att_grad, totals, rows_in, cols_in, *rest
):
    grads_out, grads, gaps, sem = rest[-4:]
    step = pl.program_id(0)
    width = att_grad.shape[1]
    spot = first + step
    live = spot < meta[N_LIVE]
    slot = step % 2

    def copy(at):
        rows = pl.ds(aligned(meta[OFF + first + at]), WINDOW)
        return pltpu.make_async_copy(grads.at[at % 2], grads_out.at[rows], sem.at[at % 2])

    @pl.when(live)
    def _():
        count = meta[CNT + spot]

        def run(keys, queries):
            which = meta[IMG + spot] % per
            gaps[:keys, :queries] = distances(rows_in[0], cols_in[0], which, count, keys, queries)
            key_seen = row_ids(0, keys) < count
            query_seen = row_ids(0, queries) < count
            left = lax.broadcasted_iota(jnp.int32, (keys, 128), 1) < 64

            def pair(p, carry):
                lanes = aligned(p * 128, 128)
                q2 = qkv[:queries, pl.ds(lanes, 128)] * 0.125
                k2 = qkv[:keys, pl.ds(width + lanes, 128)]
                v2 = qkv[:keys, pl.ds(2 * width + lanes, 128)]
                o2 = att_grad[:queries, pl.ds(lanes, 128)]
                q2 = jnp.where(query_seen, q2, jnp.zeros_like(q2))
                o2 = jnp.where(query_seen, o2, jnp.zeros_like(o2))
                k2 = jnp.where(key_seen, k2, jnp.zeros_like(k2))
                v2 = jnp.where(key_seen, v2, jnp.zeros_like(v2))
                k2t = k2.astype(F32).T.astype(BF16)
                raw = dot_bt(by_head(k2, left), q2)
                raw_g = dot_bt(by_head(v2, left), o2)
                dq_parts, probs_low, score_low = [], [], []
                for half in range(2):
                    head = 2 * p + half
                    rows = slice(half * keys, (half + 1) * keys)
                    scores = raw[rows] - slopes[head] * gaps[:keys, :queries]
                    probs = jnp.exp(scores - totals[0, p, half : half + 1, :queries])
                    prob_g = raw_g[rows]
                    inner = jnp.sum(probs * prob_g, axis=0, keepdims=True)
                    score_g = (probs * (prob_g - inner)).astype(BF16)
                    dq_parts.append(dot(k2t[half * 64 : half * 64 + 64], score_g) * 0.125)
                    probs_low.append(probs.astype(BF16))
                    score_low.append(score_g)
                dv = dot(jnp.concatenate(probs_low, axis=0), o2)
                dk = dot(jnp.concatenate(score_low, axis=0), q2)
                dv = jnp.where(left, dv[:keys], dv[keys:])
                dk = jnp.where(left, dk[:keys], dk[keys:])
                dq = jnp.concatenate(dq_parts, axis=0).T.astype(BF16)
                grads[slot, :queries, pl.ds(lanes, 128)] = dq
                grads[slot, :keys, pl.ds(width + lanes, 128)] = dk.astype(BF16)
                grads[slot, :keys, pl.ds(2 * width + lanes, 128)] = dv.astype(BF16)
                return carry

            lax.fori_loop(0, HEADS // 2, pair, 0, unroll=HEADS // 2)

        by_count(count, run)

        @pl.when(step > 0)
        def _():
            copy(step - 1).wait()

        copy(step).start()

        @pl.when(jnp.logical_or(step == pl.num_programs(0) - 1, spot == meta[N_LIVE] - 1))
        def _():
            copy(step).wait()


def qkv_grad_kernel(meta, packed_grad, tokens, vecs, keep_g, send_g, bias_g, acc, stage, sem):
    tile = pl.program_id(0)
    width = tokens.shape[1]

    @pl.when(tile == 0)
    def _():
        acc[...] = jnp.zeros_like(acc)
        bias_g[...] = jnp.zeros_like(bias_g)

    @pl.when(tile < meta[N_BWD])
    def _():
        ids = row_ids(tile * TILE, TILE)
        unit, _ = layer_norm(tokens[...].astype(F32))
        hidden = (
            unit * vecs[GAIN_ONE : GAIN_ONE + 1] + vecs[SHIFT_ONE : SHIFT_ONE + 1]
        ).astype(BF16)
        hidden_t = turned(hidden)
        for part in range(3):
            cols = slice(part * width, (part + 1) * width)
            block = packed_grad[:, cols]
            block = jnp.where(ids < meta[ROWS_BWD], block, jnp.zeros_like(block))
            acc[:, cols] += dot(hidden_t, block)
            bias_g[0:1, cols] += jnp.sum(block.astype(F32), axis=0, keepdims=True)

    @pl.when(tile == pl.num_programs(0) - 1)
    def _():
        rows = width // BLOCKS // 2
        for block in range(BLOCKS):
            for h in range(2):
                for c in range(3):
                    first = (2 * block + h) * rows
                    piece = acc[first : first + rows, c * width : (c + 1) * width]
                    stage[h, block, c * rows : (c + 1) * rows, :] = piece.astype(BF16)
        mine = meta[CORE]
        keep = pltpu.make_async_copy(stage.at[mine], keep_g, sem.at[0])
        send = pltpu.make_async_copy(stage.at[1 - mine], send_g, sem.at[1])
        keep.start()
        send.start()
        keep.wait()
        send.wait()


def token_grad_kernel(
    meta, packed_grad, tokens, mid_grad, vecs, weight, bias_g, vec_two, upb_g, out, vec_g, held
):
    step = pl.program_id(0)
    tiles = held.shape[0] // TILE - WINDOW // TILE
    length, images = out.shape[1], out.shape[2]

    @pl.when(step == 0)
    def _():
        width = vec_g.shape[1]
        vec_g[...] = jnp.zeros_like(vec_g)
        vec_g[2:3, :] = bias_g[0:1, :width]
        vec_g[3:4, :] = bias_g[0:1, 2 * width :]
        vec_g[4:8, :] = vec_two[0:4, :]
        for n in range(upb_g.shape[1] // width):
            vec_g[8 + n : 9 + n, :] = upb_g[0:1, n * width : (n + 1) * width]

    @pl.when(jnp.logical_and(step < tiles, step < meta[N_BWD]))
    def _():
        rows = aligned(step * TILE, TILE)
        ids = row_ids(rows, TILE)
        unit, inverse = layer_norm(tokens[...].astype(F32))
        block = packed_grad[...]
        block = jnp.where(ids < meta[ROWS_BWD], block, jnp.zeros_like(block))
        g1 = dot_bt(block, weight[...])
        back = norm_back(g1, vecs[GAIN_ONE : GAIN_ONE + 1], unit, inverse)
        held[pl.ds(rows, TILE), :] = mid_grad[...] + back
        vec_g[0:1, :] += jnp.sum(g1 * unit, axis=0, keepdims=True)
        vec_g[1:2, :] += jnp.sum(g1, axis=0, keepdims=True)

    @pl.when(step >= tiles)
    def _():
        parts = []
        for i in range(images):
            spot = meta[SPOT + (step - tiles) * images + i]
            off = aligned(meta[OFF + spot])
            limit = meta[CNT + spot] * meta[LIVE + spot]
            block = held[pl.ds(off, length), :]
            parts.append(jnp.where(row_ids(0, length) < limit, block, 0.0))
        out[0] = jnp.swapaxes(jnp.stack(parts, axis=0), 0, 1)


def whole(*shape):
    return pl.BlockSpec(shape, lambda *_: (0,) * len(shape), pipeline_mode=pl.Buffered(1))


def params():
    return pltpu.CompilerParams(vmem_limit_bytes=VMEM_LIMIT)


def small():
    return pl.BlockSpec(memory_space=pltpu.SMEM)


def prepare(every, counts, present, slots, me, cotangent, *vectors):
    steps, length, images, width = cotangent.shape
    group = every.shape[0]
    padded = (length + 7) // 8 * 8
    return pl.pallas_call(
        prepare_kernel,
        out_shape=(
            jax.ShapeDtypeStruct((PLACES,), jnp.int32),
            jax.ShapeDtypeStruct((steps * images,), jnp.int32),
            jax.ShapeDtypeStruct((16, width), F32),
            jax.ShapeDtypeStruct((group, steps, padded, width), BF16),
        ),
        grid=(steps,),
        in_specs=[small()] * 5
        + [pl.BlockSpec((1, length, images, width), lambda m: (m, 0, 0, 0))]
        + [whole(*vector.shape) for vector in vectors],
        out_specs=[
            small(),
            small(),
            whole(16, width),
            pl.BlockSpec((group, 1, padded, width), lambda m: (0, m, 0, 0)),
        ],
        compiler_params=params(),
    )(every, counts, present, slots, me, cotangent, *vectors)


def place(take, got, length):
    group, steps, padded, width = got.shape
    return pl.pallas_call(
        place_kernel,
        out_shape=jax.ShapeDtypeStruct((steps, length, group, width), BF16),
        grid=(steps,),
        in_specs=[small(), pl.BlockSpec((group, 1, padded, width), lambda m: (0, m, 0, 0))],
        out_specs=pl.BlockSpec((1, length, group, width), lambda m: (m, 0, 0, 0)),
        compiler_params=params(),
    )(take, got)


def first_half(meta, slopes, tokens, rows, cols, vecs, weight):
    steps, length, per, width = tokens.shape
    images = steps * per
    tiles = -(-images * ((length + 15) // 16 * 16) // TILE)
    total = tiles * TILE + WINDOW
    spots = pl.BlockSpec(
        (1, per, length),
        lambda s, meta, slopes: (meta[IMG + jnp.maximum(s - steps, 0)] // per, 0, 0),
    )
    return pl.pallas_call(
        attend_kernel,
        out_shape=(
            jax.ShapeDtypeStruct((total, width), BF16),
            jax.ShapeDtypeStruct((total, 3 * width), BF16),
            jax.ShapeDtypeStruct((total, width), BF16),
            jax.ShapeDtypeStruct((images, HEADS // 2, 8, WINDOW), F32),
        ),
        grid_spec=pltpu.PrefetchScalarGridSpec(
            num_scalar_prefetch=2,
            grid=(steps + images,),
            in_specs=[
                pl.BlockSpec(
                    (1, length, per, width),
                    lambda s, meta, slopes: (jnp.minimum(s, steps - 1), 0, 0, 0),
                ),
                spots,
                spots,
                whole(*vecs.shape),
                whole(width, 3 * width),
            ],
            out_specs=[
                pl.BlockSpec(memory_space=pl.ANY),
                pl.BlockSpec(memory_space=pl.ANY),
                pl.BlockSpec(memory_space=pl.ANY),
                pl.BlockSpec(
                    (1, HEADS // 2, 8, WINDOW),
                    lambda s, meta, slopes: (jnp.maximum(s - steps, 0), 0, 0, 0),
                ),
            ],
            scratch_shapes=[
                pltpu.VMEM((total, width), BF16),
                pltpu.VMEM((total, 3 * width), BF16),
                pltpu.VMEM((total, width), BF16),
                pltpu.VMEM((WINDOW, WINDOW), F32),
                pltpu.SemaphoreType.DMA((tiles,)),
                pltpu.SemaphoreType.DMA((tiles,)),
                pltpu.SemaphoreType.DMA((tiles,)),
            ],
        ),
        compiler_params=params(),
        cost_estimate=cost(40),
    )(meta, slopes, tokens, rows, cols, vecs, weight)


def mlp(meta, cot, att, packed, vecs, out_w, up_w, down_w, length):
    group, steps, padded, width = cot.shape
    rows = packed.shape[0]
    tiles = (rows - WINDOW) // TILE
    hidden = up_w.shape[1]
    parcel = (2 * width + hidden // 2 + width // 2) // BLOCKS
    def fwd_tile(s, meta):
        return (jnp.clip(s - steps, 0, meta[N_FWD] - 1), 0)

    def bwd_tile(s, meta):
        return (jnp.clip(s - steps, 0, jnp.maximum(meta[N_BWD] - 1, 0)), 0)

    return pl.pallas_call(
        functools.partial(mlp_kernel, CHUNK, length),
        out_shape=(
            jax.ShapeDtypeStruct(cot.shape, BF16),
            jax.ShapeDtypeStruct((rows, width), F32),
            jax.ShapeDtypeStruct((rows, width), BF16),
            jax.ShapeDtypeStruct((BLOCKS, parcel, width), BF16),
            jax.ShapeDtypeStruct((BLOCKS, parcel, width), BF16),
            jax.ShapeDtypeStruct((8, width), F32),
            jax.ShapeDtypeStruct((8, hidden), F32),
        ),
        grid_spec=pltpu.PrefetchScalarGridSpec(
            num_scalar_prefetch=1,
            grid=(2 * steps + tiles,),
            in_specs=[
                pl.BlockSpec(
                    (group, 1, padded, width), lambda s, meta: (0, jnp.minimum(s, steps - 1), 0, 0)
                ),
                pl.BlockSpec((TILE, width), fwd_tile),
                pl.BlockSpec((TILE, width), fwd_tile),
                whole(*vecs.shape),
                whole(width, width),
                whole(width, hidden),
                whole(hidden, width),
            ],
            out_specs=[
                pl.BlockSpec(
                    (group, 1, padded, width),
                    lambda s, meta: (0, jnp.clip(s - steps - tiles, 0, steps - 1), 0, 0),
                ),
                pl.BlockSpec((TILE, width), bwd_tile),
                pl.BlockSpec((TILE, width), bwd_tile),
                pl.BlockSpec(memory_space=pl.ANY),
                pl.BlockSpec(memory_space=pl.ANY),
                whole(8, width),
                whole(8, hidden),
            ],
            scratch_shapes=[
                pltpu.VMEM((8, hidden), F32),
                pltpu.VMEM((rows, width), BF16),
                pltpu.VMEM((width, hidden), F32),
                pltpu.VMEM((width, hidden), F32),
                pltpu.VMEM((width, width), F32),
                pltpu.VMEM((TILE, width), BF16),
                pltpu.VMEM((width, TILE), BF16),
                pltpu.VMEM((width, TILE), BF16),
                pltpu.VMEM((TILE, width), F32),
                pltpu.VMEM((TILE, width), F32),
                pltpu.SemaphoreType.DMA((2, BLOCKS)),
            ],
        ),
        compiler_params=params(),
        cost_estimate=cost(110),
    )(meta, cot, att, packed, vecs, out_w, up_w, down_w)


def attend_back(first, count, expected, meta, slopes, qkv, att_grad, totals, rows_in, cols_in, earlier):
    total, wide = qkv.shape
    width = wide // 3
    per, length = rows_in.shape[1:]

    def spot_of(s, meta):
        return jnp.clip(first + s, 0, jnp.maximum(meta[N_LIVE] - 1, 0))

    def by_offset(s, meta, slopes):
        return (aligned(meta[OFF + spot_of(s, meta)]), 0)

    spots = pl.BlockSpec(
        (1, per, length),
        lambda s, meta, slopes: (meta[IMG + spot_of(s, meta)] // per, 0, 0),
    )
    anywhere = pl.BlockSpec(memory_space=pl.ANY)
    return pl.pallas_call(
        functools.partial(attend_back_kernel, first, per),
        out_shape=jax.ShapeDtypeStruct((total, wide), BF16),
        grid_spec=pltpu.PrefetchScalarGridSpec(
            num_scalar_prefetch=2,
            grid=(count,),
            in_specs=[
                pl.BlockSpec((pl.Element(WINDOW), pl.Element(wide)), by_offset),
                pl.BlockSpec((pl.Element(WINDOW), pl.Element(width)), by_offset),
                pl.BlockSpec(
                    (1, HEADS // 2, 8, WINDOW),
                    lambda s, meta, slopes: (spot_of(s, meta), 0, 0, 0),
                ),
                spots,
                spots,
            ]
            + [anywhere] * len(earlier),
            out_specs=anywhere,
            scratch_shapes=[
                pltpu.VMEM((2, WINDOW, wide), BF16),
                pltpu.VMEM((WINDOW, WINDOW), F32),
                pltpu.SemaphoreType.DMA((2,)),
            ],
        ),
        input_output_aliases={7: 0} if earlier else {},
        compiler_params=params(),
        cost_estimate=cost(expected),
    )(meta, slopes, qkv, att_grad, totals, rows_in, cols_in, *earlier)


def bwd_tile(s, meta):
    return (jnp.clip(s, 0, jnp.maximum(meta[N_BWD] - 1, 0)), 0)


def qkv_grad(meta, packed_grad, packed, vecs):
    rows, width = packed.shape
    parcel = 3 * width // 2 // BLOCKS
    tiles = (rows - WINDOW) // TILE
    return pl.pallas_call(
        qkv_grad_kernel,
        out_shape=(
            jax.ShapeDtypeStruct((BLOCKS, parcel, width), BF16),
            jax.ShapeDtypeStruct((BLOCKS, parcel, width), BF16),
            jax.ShapeDtypeStruct((8, 3 * width), F32),
        ),
        grid_spec=pltpu.PrefetchScalarGridSpec(
            num_scalar_prefetch=1,
            grid=(tiles,),
            in_specs=[
                pl.BlockSpec((TILE, 3 * width), bwd_tile),
                pl.BlockSpec((TILE, width), bwd_tile),
                whole(*vecs.shape),
            ],
            out_specs=[
                pl.BlockSpec(memory_space=pl.ANY),
                pl.BlockSpec(memory_space=pl.ANY),
                whole(8, 3 * width),
            ],
            scratch_shapes=[
                pltpu.VMEM((width, 3 * width), F32),
                pltpu.VMEM((2, BLOCKS, parcel, width), BF16),
                pltpu.SemaphoreType.DMA((2,)),
            ],
        ),
        compiler_params=params(),
        cost_estimate=cost(15),
    )(meta, packed_grad, packed, vecs)


def token_grad(
    meta, packed_grad, packed, mid_grad, vecs, weight, bias_g, vec_two, upb_g, steps, length, images
):
    rows, width = packed.shape
    tiles = (rows - WINDOW) // TILE
    return pl.pallas_call(
        token_grad_kernel,
        out_shape=(
            jax.ShapeDtypeStruct((steps, length, images, width), F32),
            jax.ShapeDtypeStruct((16, width), F32),
        ),
        grid_spec=pltpu.PrefetchScalarGridSpec(
            num_scalar_prefetch=1,
            grid=(tiles + steps,),
            in_specs=[
                pl.BlockSpec((TILE, 3 * width), bwd_tile),
                pl.BlockSpec((TILE, width), bwd_tile),
                pl.BlockSpec((TILE, width), bwd_tile),
                whole(*vecs.shape),
                whole(width, 3 * width),
                whole(*bias_g.shape),
                whole(*vec_two.shape),
                whole(*upb_g.shape),
            ],
            out_specs=[
                pl.BlockSpec(
                    (1, length, images, width),
                    lambda s, meta: (jnp.clip(s - tiles, 0, steps - 1), 0, 0, 0),
                ),
                whole(16, width),
            ],
            scratch_shapes=[pltpu.VMEM((rows, width), F32)],
        ),
        compiler_params=params(),
        cost_estimate=cost(20),
    )(meta, packed_grad, packed, mid_grad, vecs, weight, bias_g, vec_two, upb_g)


def cost(microseconds):
    return pl.CostEstimate(
        flops=int(microseconds * 1e9), bytes_accessed=int(microseconds * 1e5), transcendentals=0
    )


def swap(block, axis, bit):
    size = lax.axis_size(axis)
    return lax.ppermute(block, axis, [(n, n ^ bit) for n in range(size)])


def bit_of(axis, bit):
    return lax.axis_index(axis) // bit % 2


def added(a, b):
    return (a.astype(F32) + b.astype(F32)).astype(BF16)


def unpacked(mine, other, shapes):
    swapped = bit_of("bal", 1) == 1
    first = jnp.where(swapped, other, mine)
    second = jnp.where(swapped, mine, other)
    lead, width = mine.shape[:-2], mine.shape[-1]
    out, at = [], 0
    for rows, columns, kind in shapes:
        wide = columns // width
        part = rows * wide // 2
        held = [half[..., at : at + part, :] for half in (first, second)]
        if kind == "rows":
            size = rows // 2
            parts = [
                jnp.concatenate(
                    [half[..., c * size : (c + 1) * size, :] for c in range(wide)], axis=-1
                )
                for half in held
            ]
            out.append(jnp.concatenate(parts, axis=-2))
        elif kind == "columns":
            parts = [
                half[..., c * rows : (c + 1) * rows, :] for half in held for c in range(wide // 2)
            ]
            out.append(jnp.concatenate(parts, axis=-1))
        else:
            size = width // 2
            tops = [half[..., :size] for half in held]
            bottoms = [half[..., size:] for half in held]
            out.append(
                jnp.concatenate(
                    [jnp.concatenate(tops, axis=-1), jnp.concatenate(bottoms, axis=-1)], axis=-2
                )
            )
        at += part
    return [matrix.reshape(lead[:-1] + (-1, matrix.shape[-1])) if lead else matrix for matrix in out]


def spread_sum(keep, send, shapes):
    return [
        lax.psum(lax.psum_scatter(matrix, "dp", scatter_dimension=0, tiled=True), "bal").astype(F32)
        for matrix in unpacked(keep, send, shapes)
    ]


def start_fold(block, bit):
    block = block.reshape((-1, 2) + block.shape[-2:])
    mine = bit_of("dp", bit)
    keep = lax.dynamic_index_in_dim(block, mine, 1, keepdims=False)
    send = lax.dynamic_index_in_dim(block, 1 - mine, 1, keepdims=False)
    return keep, swap(send, "dp", bit)


def after(value, *others):
    return lax.optimization_barrier((value,) + others)[0]


def doubled(block, round_no):
    bits = [("bal", 1)]
    bit = 1
    while bit < lax.axis_size("dp"):
        bits.append(("dp", bit))
        bit *= 2
    bits.append(("bal", 2))
    if round_no is None:
        return len(bits)
    axis, bit = bits[round_no]
    return block + swap(block, axis, bit)


def per_device(
    tokens,
    cotangent,
    counts,
    rows,
    cols,
    present,
    slots,
    first_gain,
    first_shift,
    qkv_weight,
    query_bias,
    value_bias,
    out_weight,
    out_bias,
    second_gain,
    second_shift,
    up_weight,
    up_bias,
    down_weight,
    down_bias,
):
    steps, images, length, width = tokens.shape
    hidden = up_weight.shape[1]
    group = lax.axis_size("bal")
    total = steps * images
    slopes = jnp.exp2(-8.0 * (jnp.arange(16, dtype=F32) + 1.0) / HEADS)

    def exchange(blocks):
        flat = blocks.reshape(group, -1, width)
        return lax.all_to_all(flat, "bal", split_axis=0, concat_axis=0, tiled=True)

    def turn(array):
        return jnp.transpose(array, (0, 2, 1, 3))

    meta, take, vecs, cot_send = prepare(
        lax.all_gather(slots, "bal"), counts, present, slots,
        lax.axis_index("bal").astype(jnp.int32).reshape(1), turn(cotangent),
        first_gain, first_shift, query_bias, value_bias, out_bias, second_gain, second_shift,
        down_bias, up_bias,
    )
    cot_home = exchange(cot_send).reshape(group, steps, -1, width)
    packed, qkv, att, totals = first_half(meta, slopes, turn(tokens), rows, cols, vecs, qkv_weight)
    y_send, mid_grad, att_grad, keep_two, send_two, vec_two, upb_g = mlp(
        meta, cot_home, att, packed, vecs, out_weight, up_weight, down_weight, length
    )
    y_got = exchange(y_send)

    share, long = width // BLOCKS, hidden // BLOCKS
    shapes_two = ((share, hidden, "columns"), (long, width, "side"), (share, width, "rows"))
    shapes_one = ((share, 3 * width, "rows"),)
    direct = lax.axis_size("dp") == BLOCKS

    def back(first, count, expected, table, earlier):
        return attend_back(
            first, count, expected, table, slopes, qkv, att_grad, totals, rows, cols, earlier
        )

    lead = max(images // 2, 1)
    packed_grad = back(0, lead, 15, meta, ())
    table = meta
    if direct:
        sum_two = added(after(keep_two, packed_grad), swap(send_two, "bal", 1))
        share_two = lax.psum_scatter(sum_two, "dp", scatter_dimension=0, tiled=True)[0]
        table = after(meta, sum_two)
    packed_grad = back(lead, total - lead, 500, table, (packed_grad,))
    keep_one, send_one, bias_g = qkv_grad(table, packed_grad, packed, vecs)
    output = place(after(take, keep_one), y_got.reshape(group, steps, -1, width), length)
    table = after(table, output)
    if direct:
        sum_one = added(keep_one, swap(send_one, "bal", 1))
        keep_y, crossing_y = start_fold(sum_one, 1)
        table = after(table, sum_one)
    input_grad, vectors = token_grad(
        table, packed_grad, packed, mid_grad, vecs, qkv_weight, bias_g, vec_two, upb_g,
        steps, length, images,
    )
    rounds = doubled(vectors, None)
    if direct:
        half_one = added(after(keep_y, vectors), crossing_y)
        keep, crossing = start_fold(half_one, 2)
        for n in range(rounds - 2):
            vectors = doubled(vectors, n)
        block = added(after(keep, vectors), crossing)
        keep, crossing = start_fold(block, 4)
        vectors = doubled(after(vectors, block), rounds - 2)
        block = added(after(keep, vectors), crossing).reshape(sum_one.shape[-2:])
        across_one = swap(block, "bal", 2)
        across_two = swap(after(share_two, block), "bal", 2)
        vectors = doubled(after(vectors, block), rounds - 1)
        full_one = added(after(block, vectors), across_one)
        full_two = added(after(share_two, full_one), across_two)
        (qkv_rows,) = [
            matrix.astype(F32)
            for matrix in unpacked(full_one, swap(full_one, "bal", 1), shapes_one)
        ]
        up_rows, down_rows, out_rows = [
            matrix.astype(F32)
            for matrix in unpacked(full_two, swap(full_two, "bal", 1), shapes_two)
        ]
    else:
        (qkv_rows,) = spread_sum(keep_one, send_one, shapes_one)
        up_rows, down_rows, out_rows = spread_sum(keep_two, send_two, shapes_two)
        for n in range(rounds):
            vectors = doubled(vectors, n)

    def vector(n):
        return vectors[n]

    return (
        turn(output),
        turn(input_grad),
        vector(0),
        vector(1),
        qkv_rows,
        vector(2),
        vector(3),
        out_rows,
        vector(6),
        vector(4),
        vector(5),
        up_rows,
        vectors[8 : 8 + hidden // width].reshape(-1),
        down_rows,
        vector(7),
    )


def solution(mesh):
    images = P(None, ("dp", "bal"), None, None)
    spots = P(None, ("dp", "bal"), None)
    flags = P(None, ("dp", "bal"))
    matrix = P("dp", None)
    return jax.shard_map(
        per_device,
        mesh=mesh,
        in_specs=(images, images, flags, spots, spots, flags, flags) + (P(),) * 13,
        out_specs=(
            images, images, P(), P(), matrix, P(), P(), matrix, P(), P(), P(), matrix, P(), matrix, P(),
        ),
        check_vma=False,
    )
```

```python
import functools
import math

import jax
import jax.numpy as jnp
from jax import lax
from jax.experimental import pallas as pl
from jax.experimental.pallas import tpu as pltpu
from jax.sharding import PartitionSpec as P

HEADS = 12
TILE = 256
WINDOW = 256
FAR = 1e12
EPS = 1e-06
BLOCKS = 8
CHUNK = 1024
VMEM_LIMIT = 60 * 1024 * 1024

F32 = jnp.float32
BF16 = jnp.bfloat16

OFF, CNT, IMG, LIVE, PEER, SPOT, MISC = 0, 16, 32, 48, 64, 80, 96
N_FWD, N_BWD, ROWS_FWD, ROWS_BWD, N_LIVE, CORE = range(MISC, MISC + 6)
PLACES = 128

GAIN_ONE, SHIFT_ONE, QKV_B, OUT_B, GAIN_TWO, SHIFT_TWO, DOWN_B, UP_B = 0, 1, 2, 5, 6, 7, 8, 9
VECTORS = (GAIN_ONE, SHIFT_ONE, QKV_B, QKV_B + 2, OUT_B, GAIN_TWO, SHIFT_TWO, DOWN_B, UP_B)


def dot(a, b):
    return jnp.dot(a, b, preferred_element_type=F32)


def dot_bt(a, b):
    return lax.dot_general(a, b, (((1,), (1,)), ((), ())), preferred_element_type=F32)


def turned(block):
    return block.astype(F32).T.astype(BF16)


def layer_norm(values):
    average = jnp.mean(values, axis=-1, keepdims=True)
    centred = values - average
    spread = jnp.mean(centred * centred, axis=-1, keepdims=True)
    inverse = lax.rsqrt(spread + EPS)
    return centred * inverse, inverse


def norm_back(out_grad, gain, unit, inverse):
    e = out_grad * gain
    mean_e = jnp.mean(e, axis=-1, keepdims=True)
    mean_eu = jnp.mean(e * unit, axis=-1, keepdims=True)
    return inverse * (e - mean_e - unit * mean_eu)


def gelu_parts(u):
    size = jnp.abs(u)
    t = 1.0 / (1.0 + (0.3275911 * math.sqrt(0.5)) * size)
    bell = jnp.exp2((-0.5 * math.log2(math.e)) * (u * u))
    poly = t * (
        0.5 * 0.254829592
        + t
        * (
            0.5 * -0.284496736
            + t * (0.5 * 1.421413741 + t * (0.5 * -1.453152027 + t * (0.5 * 1.061405429)))
        )
    )
    tail = poly * bell
    phi_sum = jnp.where(u >= 0, 1.0 - tail, tail)
    return phi_sum, u * bell * (1.0 / math.sqrt(2.0 * math.pi))


def put_rows(packed, off, count, block):
    rows = (block.shape[0] + 15) // 16 * 16
    if rows > block.shape[0]:
        more = jnp.zeros((rows - block.shape[0], block.shape[1]), block.dtype)
        block = jnp.concatenate([block, more], axis=0)
    ids = row_ids(0, rows)
    window = pl.ds(off, rows)
    block = jnp.where(ids < count, block, jnp.zeros_like(block))
    packed[window, :] = jnp.where(ids < (count + 15) // 16 * 16, block, packed[window, :])


def row_ids(start, rows):
    return start + lax.broadcasted_iota(jnp.int32, (rows, 1), 0)


def aligned(value, step=16):
    return pl.multiple_of(value, step)


def by_count(count, run):
    @pl.when(count <= 128)
    def _():
        run(128, 128)

    @pl.when(jnp.logical_and(count > 128, count <= 192))
    def _():
        run(192, 256)

    @pl.when(count > 192)
    def _():
        run(256, 256)


def distances(rows, cols, which, count, keys, queries):
    mine = lax.broadcasted_iota(jnp.int32, rows.shape, 0) == which
    row = jnp.sum(jnp.where(mine, rows, 0).astype(F32), axis=0, keepdims=True)
    col = jnp.sum(jnp.where(mine, cols, 0).astype(F32), axis=0, keepdims=True)
    spots = jnp.concatenate([row, col, jnp.zeros((6, row.shape[1]), F32)], axis=0)
    spots = jnp.concatenate([spots, jnp.zeros((8, WINDOW - row.shape[1]), F32)], axis=1)
    eye = jnp.where(
        lax.broadcasted_iota(jnp.int32, (keys, WINDOW), 0)
        == lax.broadcasted_iota(jnp.int32, (keys, WINDOW), 1),
        1.0,
        0.0,
    ).astype(BF16)
    turned_spots = dot_bt(eye, spots.astype(BF16))
    down = turned_spots[:, 0:1] - spots[0:1, :queries]
    across = turned_spots[:, 1:2] - spots[1:2, :queries]
    far = row_ids(0, keys) >= count
    return jnp.where(far, FAR, jnp.sqrt(down * down + across * across))


def prepare_kernel(group, counts, present, slots, me, cot, *rest):
    *rest, meta, take, vecs, send = rest
    every, lines = (slots,) + tuple(rest[: group - 1]), rest[group - 1 :]
    step = pl.program_id(0)
    steps, length, images, width = pl.num_programs(0), cot.shape[1], cot.shape[2], cot.shape[3]
    @pl.when(step == 0)
    def _():
        def fill(live):
            def body(img, carry):
                spot, off = carry
                m, i = img // images, img % images
                count = counts[m, i]
                mine = present[m, i] == live

                @pl.when(mine)
                def _():
                    meta[OFF + spot] = off
                    meta[CNT + spot] = count
                    meta[IMG + spot] = img
                    meta[LIVE + spot] = live
                    meta[PEER + spot] = slots[m, i] // images * steps + m
                    meta[SPOT + img] = spot

                padded = (count + 15) // 16 * 16
                return spot + mine.astype(jnp.int32), off + jnp.where(mine, padded, 0)

            return body

        meta[CORE] = me[0] % 2
        vecs[...] = jnp.zeros_like(vecs)
        for row, values in zip(VECTORS, lines):
            for n in range(values.shape[0] // width):
                piece = values[n * width : (n + 1) * width]
                vecs[row + n : row + n + 1, :] = piece.reshape(1, width)
        zero = jnp.int32(0)
        total = counts.shape[0] * images
        spot, off = lax.fori_loop(0, total, fill(1), (zero, zero))
        meta[N_LIVE] = spot
        meta[ROWS_BWD] = off
        meta[N_BWD] = (off + TILE - 1) // TILE
        spot, off = lax.fori_loop(0, total, fill(0), (spot, off))
        meta[ROWS_FWD] = off
        meta[N_FWD] = (off + TILE - 1) // TILE

        for back, theirs in enumerate(every):
            a = (me[0] + group - back) % group

            def land(n, carry):
                m, i = n // images, n % images
                slot = theirs[m, i]

                @pl.when(slot // images == me[0])
                def _():
                    take[m * images + slot % images] = a * steps + m

                return carry

            lax.fori_loop(0, total, land, 0)

    block = jnp.swapaxes(cot[0].astype(F32), 0, 1).astype(BF16)
    for place in range(images):
        peer = take[step * images + place] // steps
        send[peer, 0, :length, :] = block[place]


def place_kernel(take, got, out):
    step = pl.program_id(0)
    length, images = out.shape[1], out.shape[2]
    steps = pl.num_programs(0)
    parts = [
        got[take[step * images + place] // steps, 0, :length, :].astype(F32)
        for place in range(images)
    ]
    out[0] = jnp.swapaxes(jnp.stack(parts, axis=0), 0, 1).astype(out.dtype)


def attend_kernel(
    meta, slopes, tokens, rows_in, cols_in, vecs, weight,
    packed_out, qkv_out, att_out, total_out,
    packed, qkv, att, gaps, sem_packed, sem_qkv, sem_att,
):
    length, per, width = tokens.shape[1], tokens.shape[2], tokens.shape[3]
    steps = pl.num_programs(0) // (per + 1)
    images = steps * per
    now = pl.program_id(0)

    def tile_copy(which, t):
        src, dst, sem = (
            (packed, packed_out, sem_packed),
            (qkv, qkv_out, sem_qkv),
            (att, att_out, sem_att),
        )[which]
        rows = pl.ds(aligned(t * TILE, TILE), TILE)
        return pltpu.make_async_copy(src.at[rows], dst.at[rows], sem.at[t])

    @pl.when(now == 0)
    def _():
        packed[...] = jnp.zeros_like(packed)

    @pl.when(now < steps)
    def _():
        block = jnp.swapaxes(tokens[0].astype(F32), 0, 1).astype(BF16)
        for i in range(per):
            spot = meta[SPOT + now * per + i]
            put_rows(packed, aligned(meta[OFF + spot]), meta[CNT + spot], block[i])

    @pl.when(now == steps - 1)
    def _():

        def project(t, carry):
            rows = pl.ds(aligned(t * TILE, TILE), TILE)
            unit, _ = layer_norm(packed[rows, :].astype(F32))
            hidden = (
                unit * vecs[GAIN_ONE : GAIN_ONE + 1] + vecs[SHIFT_ONE : SHIFT_ONE + 1]
            ).astype(BF16)
            for part in range(3):
                cols = slice(part * width, (part + 1) * width)
                bias = vecs[QKV_B + part : QKV_B + part + 1]
                qkv[rows, cols] = (dot(hidden, weight[:, cols]) + bias).astype(BF16)
            tile_copy(0, t).start()
            tile_copy(1, t).start()
            return carry

        lax.fori_loop(0, meta[N_FWD], project, 0)

    @pl.when(now >= steps)
    def _():
        spot = now - steps
        off = aligned(meta[OFF + spot])
        count = meta[CNT + spot]

        def run(keys, queries):
            which = meta[IMG + spot] % per
            gaps[:keys, :queries] = distances(rows_in[0], cols_in[0], which, count, keys, queries)
            key_seen = row_ids(0, keys) < count
            query_seen = row_ids(0, queries) < count
            left = lax.broadcasted_iota(jnp.int32, (keys, 128), 1) < 64

            def pair(p, carry):
                lanes = aligned(p * 128, 128)
                q2 = qkv[pl.ds(off, queries), pl.ds(lanes, 128)] * 0.125
                k2 = qkv[pl.ds(off, keys), pl.ds(width + lanes, 128)]
                v2 = qkv[pl.ds(off, keys), pl.ds(2 * width + lanes, 128)]
                q2 = jnp.where(query_seen, q2, jnp.zeros_like(q2))
                k2 = jnp.where(key_seen, k2, jnp.zeros_like(k2))
                v2 = jnp.where(key_seen, v2, jnp.zeros_like(v2))
                v2t = v2.astype(F32).T.astype(BF16)
                raw = dot_bt(by_head(k2, left), q2)
                outs = []
                for half in range(2):
                    head = 2 * p + half
                    scores = raw[half * keys : (half + 1) * keys]
                    scores = scores - slopes[head] * gaps[:keys, :queries]
                    top = jnp.max(scores, axis=0, keepdims=True)
                    terms = jnp.exp(scores - top)
                    total = jnp.sum(terms, axis=0, keepdims=True)
                    heads_out = dot(v2t[half * 64 : half * 64 + 64], terms.astype(BF16))
                    outs.append(heads_out * (1.0 / total))
                    total_out[0, p, half : half + 1, :queries] = top + jnp.log(total)
                both = jnp.concatenate(outs, axis=0)
                att[pl.ds(off, queries), pl.ds(lanes, 128)] = both.T.astype(BF16)
                return carry

            lax.fori_loop(0, HEADS // 2, pair, 0, unroll=HEADS // 2)

        by_count(count, run)
        after = meta[OFF + jnp.minimum(spot + 1, images - 1)]
        end = jnp.where(spot == images - 1, meta[N_FWD], after // TILE)

        def send(t, carry):
            tile_copy(2, t).start()
            return carry

        lax.fori_loop(off // TILE, end, send, 0)

    @pl.when(now == pl.num_programs(0) - 1)
    def _():
        def finish(t, carry):
            for which in range(3):
                tile_copy(which, t).wait()
            return carry

        lax.fori_loop(0, meta[N_FWD], finish, 0)


def by_head(block, left):
    none = jnp.zeros_like(block)
    return jnp.concatenate([jnp.where(left, block, none), jnp.where(left, none, block)], axis=0)


def mlp_kernel(
    chunk, length, meta, cot_in, att_in, tokens_in,
    vecs, out_hbm, up_hbm, down_hbm,
    y_send, mid_grad, att_grad, keep_g, send_g, vec_g, upb_g,
    up_b, held, up_acc, down_acc, out_acc, h2_s, h2t_s, dzt_s, z_s, g_s,
    out_w, up_w, down_w, sem, sem_w,
):
    step = pl.program_id(0)
    tiles = held.shape[0] // TILE - WINDOW // TILE
    images = (pl.num_programs(0) - tiles) // 2
    per = cot_in.shape[0]
    width = cot_in.shape[3]
    hidden = up_w.shape[1]
    out_b, gain, shift, down_b = [
        vecs.at[pl.ds(n, 1)] for n in (OUT_B, GAIN_TWO, SHIFT_TWO, DOWN_B)
    ]

    def weight_copies():
        pairs = ((out_hbm, out_w), (up_hbm, up_w), (down_hbm, down_w))
        return [pltpu.make_async_copy(a, b, sem_w.at[n]) for n, (a, b) in enumerate(pairs)]

    @pl.when(step == 0)
    def _():
        for copy in weight_copies():
            copy.start()
        up_acc[...] = jnp.zeros_like(up_acc)
        down_acc[...] = jnp.zeros_like(down_acc)
        out_acc[...] = jnp.zeros_like(out_acc)
        vec_g[...] = jnp.zeros_like(vec_g)
        upb_g[...] = jnp.zeros_like(upb_g)
        for n in range(hidden // width):
            up_b[0:1, n * width : (n + 1) * width] = vecs[UP_B + n : UP_B + n + 1, :]

    @pl.when(step < images)
    def _():
        for i in range(per):
            spot = meta[SPOT + step * per + i]

            @pl.when(meta[LIVE + spot] == 1)
            def _():
                put_rows(
                    held, aligned(meta[OFF + spot]), meta[CNT + spot],
                    cot_in[meta[PEER + spot] // images, 0],
                )

    @pl.when(step == images)
    def _():
        for copy in weight_copies():
            copy.wait()

    def run_tile(t, both):
        rows = aligned(t * TILE, TILE)
        ids = row_ids(rows, TILE)
        att = att_in[...]
        att = jnp.where(ids < meta[ROWS_FWD], att, jnp.zeros_like(att))
        mid = tokens_in[...].astype(F32) + (dot(att, out_w[...]) + out_b[...])
        unit, inverse = layer_norm(mid)
        h2 = (unit * gain[...] + shift[...]).astype(BF16)
        h2_s[...] = h2
        z_s[...] = mid + down_b[...]
        if both:
            dz = held[pl.ds(rows, TILE), :]
            dz = jnp.where(ids < meta[ROWS_BWD], dz, jnp.zeros_like(dz))
            h2t_s[...] = turned(h2)
            dzt_s[...] = turned(dz)
            g_s[...] = jnp.zeros_like(g_s)

        def part(c, carry):
            cols = pl.ds(aligned(c * chunk, chunk), chunk)
            pre = dot(h2_s[...], up_w[:, cols]) + up_b[0:1, cols]
            share, slope = gelu_parts(pre)
            act = (pre * share).astype(BF16)
            z_s[...] += dot(act, down_w[cols, :])
            if both:
                pre_g = (dot_bt(dz, down_w[cols, :]) * (share + slope)).astype(BF16)
                up_acc[:, cols] += dot(h2t_s[...], pre_g)
                down_acc[:, cols] += dot(dzt_s[...], act)
                upb_g[0:1, cols] += jnp.sum(pre_g.astype(F32), axis=0, keepdims=True)
                g_s[...] += dot_bt(pre_g, up_w[:, cols])
            return carry

        lax.fori_loop(0, hidden // chunk, part, 0, unroll=True)
        held[pl.ds(rows, TILE), :] = z_s[...].astype(BF16)
        if both:
            dzf = dz.astype(F32)
            g2 = g_s[...]
            dmid = dzf + norm_back(g2, gain[...], unit, inverse)
            branch = dmid.astype(BF16)
            mid_grad[...] = dmid
            att_grad[...] = dot_bt(branch, out_w[...]).astype(BF16)
            out_acc[...] += dot(turned(att), branch)
            vec_g[0:1, :] += jnp.sum(g2 * unit, axis=0, keepdims=True)
            vec_g[1:2, :] += jnp.sum(g2, axis=0, keepdims=True)
            vec_g[2:3, :] += jnp.sum(branch.astype(F32), axis=0, keepdims=True)
            vec_g[3:4, :] += jnp.sum(dzf, axis=0, keepdims=True)

    tile = step - images

    @pl.when(jnp.logical_and(tile >= 0, tile < meta[N_BWD]))
    def _():
        run_tile(tile, True)

    @pl.when(
        jnp.logical_and(
            jnp.logical_and(tile >= meta[N_BWD], tile >= 0),
            jnp.logical_and(tile < meta[N_FWD], tile < tiles),
        )
    )
    def _():
        run_tile(tile, False)

    turn = step - images - tiles

    @pl.when(turn >= 0)
    def _():
        for i in range(per):
            spot = meta[SPOT + turn * per + i]
            block = held[pl.ds(aligned(meta[OFF + spot]), length), :]
            seen = row_ids(0, length) < meta[CNT + spot]
            y_send[meta[PEER + spot] // images, 0, :length, :] = jnp.where(
                seen, block, jnp.zeros_like(block)
            )

    @pl.when(step == pl.num_programs(0) - 1)
    def _():
        share = width // BLOCKS
        long = hidden // BLOCKS
        size = 2 * share + long // 2 + share // 2
        for turn, target in enumerate((send_g, keep_g)):
            h = meta[CORE] if turn else 1 - meta[CORE]
            side = aligned(h * (width // 2), 128)
            copies = []
            for n in range(BLOCKS):
                base = n * size
                if turn:
                    earlier[n].wait()
                for c in range(2):
                    cols = pl.ds(aligned((2 * h + c) * width, 128), width)
                    piece = up_acc[n * share : (n + 1) * share, cols]
                    held[base + c * share : base + (c + 1) * share, :] = piece.astype(BF16)
                base += 2 * share
                piece = down_acc[pl.ds(side, width // 2), n * long : (n + 1) * long]
                flipped = turned(piece.astype(BF16))
                held[base : base + long // 2, : width // 2] = flipped[: long // 2]
                held[base : base + long // 2, width // 2 :] = flipped[long // 2 :]
                base += long // 2
                rows = pl.ds(pl.multiple_of(n * share + h * (share // 2), 8), share // 2)
                held[base : base + share // 2, :] = out_acc[rows, :].astype(BF16)
                copy = pltpu.make_async_copy(
                    held.at[pl.ds(n * size, size)], target.at[n], sem.at[turn, n]
                )
                copy.start()
                copies.append(copy)
            earlier = copies
        for copy in earlier:
            copy.wait()


def attend_back_kernel(
    first, per, meta, slopes, qkv, att_grad, totals, rows_in, cols_in, *rest
):
    grads_out, grads, gaps, sem = rest[-4:]
    step = pl.program_id(0)
    width = att_grad.shape[1]
    spot = first + step
    live = spot < meta[N_LIVE]
    slot = step % 2

    def copy(at):
        rows = pl.ds(aligned(meta[OFF + first + at]), WINDOW)
        return pltpu.make_async_copy(grads.at[at % 2], grads_out.at[rows], sem.at[at % 2])

    @pl.when(live)
    def _():
        count = meta[CNT + spot]

        def run(keys, queries):
            which = meta[IMG + spot] % per
            gaps[:keys, :queries] = distances(rows_in[0], cols_in[0], which, count, keys, queries)
            key_seen = row_ids(0, keys) < count
            query_seen = row_ids(0, queries) < count
            left = lax.broadcasted_iota(jnp.int32, (keys, 128), 1) < 64

            def pair(p, carry):
                lanes = aligned(p * 128, 128)
                q2 = qkv[:queries, pl.ds(lanes, 128)] * 0.125
                k2 = qkv[:keys, pl.ds(width + lanes, 128)]
                v2 = qkv[:keys, pl.ds(2 * width + lanes, 128)]
                o2 = att_grad[:queries, pl.ds(lanes, 128)]
                q2 = jnp.where(query_seen, q2, jnp.zeros_like(q2))
                o2 = jnp.where(query_seen, o2, jnp.zeros_like(o2))
                k2 = jnp.where(key_seen, k2, jnp.zeros_like(k2))
                v2 = jnp.where(key_seen, v2, jnp.zeros_like(v2))
                k2t = k2.astype(F32).T.astype(BF16)
                raw = dot_bt(by_head(k2, left), q2)
                raw_g = dot_bt(by_head(v2, left), o2)
                dq_parts, probs_low, score_low = [], [], []
                for half in range(2):
                    head = 2 * p + half
                    rows = slice(half * keys, (half + 1) * keys)
                    scores = raw[rows] - slopes[head] * gaps[:keys, :queries]
                    probs = jnp.exp(scores - totals[0, p, half : half + 1, :queries])
                    prob_g = raw_g[rows]
                    inner = jnp.sum(probs * prob_g, axis=0, keepdims=True)
                    score_g = (probs * (prob_g - inner)).astype(BF16)
                    dq_parts.append(dot(k2t[half * 64 : half * 64 + 64], score_g) * 0.125)
                    probs_low.append(probs.astype(BF16))
                    score_low.append(score_g)
                dv = dot(jnp.concatenate(probs_low, axis=0), o2)
                dk = dot(jnp.concatenate(score_low, axis=0), q2)
                dv = jnp.where(left, dv[:keys], dv[keys:])
                dk = jnp.where(left, dk[:keys], dk[keys:])
                dq = jnp.concatenate(dq_parts, axis=0).T.astype(BF16)
                grads[slot, :queries, pl.ds(lanes, 128)] = dq
                grads[slot, :keys, pl.ds(width + lanes, 128)] = dk.astype(BF16)
                grads[slot, :keys, pl.ds(2 * width + lanes, 128)] = dv.astype(BF16)
                return carry

            lax.fori_loop(0, HEADS // 2, pair, 0, unroll=HEADS // 2)

        by_count(count, run)

        @pl.when(step > 0)
        def _():
            copy(step - 1).wait()

        copy(step).start()

        @pl.when(jnp.logical_or(step == pl.num_programs(0) - 1, spot == meta[N_LIVE] - 1))
        def _():
            copy(step).wait()


def qkv_grad_kernel(meta, packed_grad, tokens, vecs, keep_g, send_g, bias_g, acc, stage, sem):
    tile = pl.program_id(0)
    width = tokens.shape[1]

    @pl.when(tile == 0)
    def _():
        acc[...] = jnp.zeros_like(acc)
        bias_g[...] = jnp.zeros_like(bias_g)

    @pl.when(tile < meta[N_BWD])
    def _():
        ids = row_ids(tile * TILE, TILE)
        unit, _ = layer_norm(tokens[...].astype(F32))
        hidden = (
            unit * vecs[GAIN_ONE : GAIN_ONE + 1] + vecs[SHIFT_ONE : SHIFT_ONE + 1]
        ).astype(BF16)
        hidden_t = turned(hidden)
        for part in range(3):
            cols = slice(part * width, (part + 1) * width)
            block = packed_grad[:, cols]
            block = jnp.where(ids < meta[ROWS_BWD], block, jnp.zeros_like(block))
            acc[:, cols] += dot(hidden_t, block)
            bias_g[0:1, cols] += jnp.sum(block.astype(F32), axis=0, keepdims=True)

    @pl.when(tile == pl.num_programs(0) - 1)
    def _():
        rows = width // BLOCKS // 2
        for block in range(BLOCKS):
            for h in range(2):
                for c in range(3):
                    first = (2 * block + h) * rows
                    piece = acc[first : first + rows, c * width : (c + 1) * width]
                    stage[h, block, c * rows : (c + 1) * rows, :] = piece.astype(BF16)
        mine = meta[CORE]
        keep = pltpu.make_async_copy(stage.at[mine], keep_g, sem.at[0])
        send = pltpu.make_async_copy(stage.at[1 - mine], send_g, sem.at[1])
        keep.start()
        send.start()
        keep.wait()
        send.wait()


def token_grad_kernel(
    meta, packed_grad, tokens, mid_grad, vecs, weight, bias_g, vec_two, upb_g, out, vec_g, held
):
    step = pl.program_id(0)
    tiles = held.shape[0] // TILE - WINDOW // TILE
    length, images = out.shape[1], out.shape[2]

    @pl.when(step == 0)
    def _():
        width = vec_g.shape[1]
        vec_g[...] = jnp.zeros_like(vec_g)
        vec_g[2:3, :] = bias_g[0:1, :width]
        vec_g[3:4, :] = bias_g[0:1, 2 * width :]
        vec_g[4:8, :] = vec_two[0:4, :]
        for n in range(upb_g.shape[1] // width):
            vec_g[8 + n : 9 + n, :] = upb_g[0:1, n * width : (n + 1) * width]

    @pl.when(jnp.logical_and(step < tiles, step < meta[N_BWD]))
    def _():
        rows = aligned(step * TILE, TILE)
        ids = row_ids(rows, TILE)
        unit, inverse = layer_norm(tokens[...].astype(F32))
        block = packed_grad[...]
        block = jnp.where(ids < meta[ROWS_BWD], block, jnp.zeros_like(block))
        g1 = dot_bt(block, weight[...])
        back = norm_back(g1, vecs[GAIN_ONE : GAIN_ONE + 1], unit, inverse)
        held[pl.ds(rows, TILE), :] = mid_grad[...] + back
        vec_g[0:1, :] += jnp.sum(g1 * unit, axis=0, keepdims=True)
        vec_g[1:2, :] += jnp.sum(g1, axis=0, keepdims=True)

    @pl.when(step >= tiles)
    def _():
        parts = []
        for i in range(images):
            spot = meta[SPOT + (step - tiles) * images + i]
            off = aligned(meta[OFF + spot])
            limit = meta[CNT + spot] * meta[LIVE + spot]
            block = held[pl.ds(off, length), :]
            parts.append(jnp.where(row_ids(0, length) < limit, block, 0.0))
        out[0] = jnp.swapaxes(jnp.stack(parts, axis=0), 0, 1)


def whole(*shape):
    return pl.BlockSpec(shape, lambda *_: (0,) * len(shape), pipeline_mode=pl.Buffered(1))


def params():
    return pltpu.CompilerParams(vmem_limit_bytes=VMEM_LIMIT)


def small():
    return pl.BlockSpec(memory_space=pltpu.SMEM)


def prepare(others, counts, present, slots, me, cotangent, *vectors):
    steps, length, images, width = cotangent.shape
    group = len(others) + 1
    padded = (length + 7) // 8 * 8
    return pl.pallas_call(
        functools.partial(prepare_kernel, group),
        out_shape=(
            jax.ShapeDtypeStruct((PLACES,), jnp.int32),
            jax.ShapeDtypeStruct((steps * images,), jnp.int32),
            jax.ShapeDtypeStruct((16, width), F32),
            jax.ShapeDtypeStruct((group, steps, padded, width), BF16),
        ),
        grid=(steps,),
        in_specs=[small()] * 4
        + [pl.BlockSpec((1, length, images, width), lambda m: (m, 0, 0, 0))]
        + [small()] * len(others)
        + [whole(*vector.shape) for vector in vectors],
        out_specs=[
            small(),
            small(),
            whole(16, width),
            pl.BlockSpec((group, 1, padded, width), lambda m: (0, m, 0, 0)),
        ],
        compiler_params=params(),
    )(counts, present, slots, me, cotangent, *others, *vectors)


def place(take, got, length):
    group, steps, padded, width = got.shape
    return pl.pallas_call(
        place_kernel,
        out_shape=jax.ShapeDtypeStruct((steps, length, group, width), BF16),
        grid=(steps,),
        in_specs=[small(), pl.BlockSpec((group, 1, padded, width), lambda m: (0, m, 0, 0))],
        out_specs=pl.BlockSpec((1, length, group, width), lambda m: (m, 0, 0, 0)),
        compiler_params=params(),
    )(take, got)


def first_half(meta, slopes, tokens, rows, cols, vecs, weight):
    steps, length, per, width = tokens.shape
    images = steps * per
    tiles = -(-images * ((length + 15) // 16 * 16) // TILE)
    total = tiles * TILE + WINDOW
    spots = pl.BlockSpec(
        (1, per, length),
        lambda s, meta, slopes: (meta[IMG + jnp.maximum(s - steps, 0)] // per, 0, 0),
    )
    return pl.pallas_call(
        attend_kernel,
        out_shape=(
            jax.ShapeDtypeStruct((total, width), BF16),
            jax.ShapeDtypeStruct((total, 3 * width), BF16),
            jax.ShapeDtypeStruct((total, width), BF16),
            jax.ShapeDtypeStruct((images, HEADS // 2, 8, WINDOW), F32),
        ),
        grid_spec=pltpu.PrefetchScalarGridSpec(
            num_scalar_prefetch=2,
            grid=(steps + images,),
            in_specs=[
                pl.BlockSpec(
                    (1, length, per, width),
                    lambda s, meta, slopes: (jnp.minimum(s, steps - 1), 0, 0, 0),
                ),
                spots,
                spots,
                whole(*vecs.shape),
                whole(width, 3 * width),
            ],
            out_specs=[
                pl.BlockSpec(memory_space=pl.ANY),
                pl.BlockSpec(memory_space=pl.ANY),
                pl.BlockSpec(memory_space=pl.ANY),
                pl.BlockSpec(
                    (1, HEADS // 2, 8, WINDOW),
                    lambda s, meta, slopes: (jnp.maximum(s - steps, 0), 0, 0, 0),
                ),
            ],
            scratch_shapes=[
                pltpu.VMEM((total, width), BF16),
                pltpu.VMEM((total, 3 * width), BF16),
                pltpu.VMEM((total, width), BF16),
                pltpu.VMEM((WINDOW, WINDOW), F32),
                pltpu.SemaphoreType.DMA((tiles,)),
                pltpu.SemaphoreType.DMA((tiles,)),
                pltpu.SemaphoreType.DMA((tiles,)),
            ],
        ),
        compiler_params=params(),
        cost_estimate=cost(40),
    )(meta, slopes, tokens, rows, cols, vecs, weight)


def mlp(meta, cot, att, packed, vecs, out_w, up_w, down_w, length):
    group, steps, padded, width = cot.shape
    rows = packed.shape[0]
    tiles = (rows - WINDOW) // TILE
    hidden = up_w.shape[1]
    parcel = (2 * width + hidden // 2 + width // 2) // BLOCKS
    def fwd_tile(s, meta):
        return (jnp.clip(s - steps, 0, meta[N_FWD] - 1), 0)

    def bwd_tile(s, meta):
        return (jnp.clip(s - steps, 0, jnp.maximum(meta[N_BWD] - 1, 0)), 0)

    return pl.pallas_call(
        functools.partial(mlp_kernel, CHUNK, length),
        out_shape=(
            jax.ShapeDtypeStruct(cot.shape, BF16),
            jax.ShapeDtypeStruct((rows, width), F32),
            jax.ShapeDtypeStruct((rows, width), BF16),
            jax.ShapeDtypeStruct((BLOCKS, parcel, width), BF16),
            jax.ShapeDtypeStruct((BLOCKS, parcel, width), BF16),
            jax.ShapeDtypeStruct((8, width), F32),
            jax.ShapeDtypeStruct((8, hidden), F32),
        ),
        grid_spec=pltpu.PrefetchScalarGridSpec(
            num_scalar_prefetch=1,
            grid=(2 * steps + tiles,),
            in_specs=[
                pl.BlockSpec(
                    (group, 1, padded, width), lambda s, meta: (0, jnp.minimum(s, steps - 1), 0, 0)
                ),
                pl.BlockSpec((TILE, width), fwd_tile),
                pl.BlockSpec((TILE, width), fwd_tile),
                whole(*vecs.shape),
                pl.BlockSpec(memory_space=pl.ANY),
                pl.BlockSpec(memory_space=pl.ANY),
                pl.BlockSpec(memory_space=pl.ANY),
            ],
            out_specs=[
                pl.BlockSpec(
                    (group, 1, padded, width),
                    lambda s, meta: (0, jnp.clip(s - steps - tiles, 0, steps - 1), 0, 0),
                ),
                pl.BlockSpec((TILE, width), bwd_tile),
                pl.BlockSpec((TILE, width), bwd_tile),
                pl.BlockSpec(memory_space=pl.ANY),
                pl.BlockSpec(memory_space=pl.ANY),
                whole(8, width),
                whole(8, hidden),
            ],
            scratch_shapes=[
                pltpu.VMEM((8, hidden), F32),
                pltpu.VMEM((rows, width), BF16),
                pltpu.VMEM((width, hidden), F32),
                pltpu.VMEM((width, hidden), F32),
                pltpu.VMEM((width, width), F32),
                pltpu.VMEM((TILE, width), BF16),
                pltpu.VMEM((width, TILE), BF16),
                pltpu.VMEM((width, TILE), BF16),
                pltpu.VMEM((TILE, width), F32),
                pltpu.VMEM((TILE, width), F32),
                pltpu.VMEM((width, width), BF16),
                pltpu.VMEM((width, hidden), BF16),
                pltpu.VMEM((hidden, width), BF16),
                pltpu.SemaphoreType.DMA((2, BLOCKS)),
                pltpu.SemaphoreType.DMA((3,)),
            ],
        ),
        compiler_params=params(),
        cost_estimate=cost(110),
    )(meta, cot, att, packed, vecs, out_w, up_w, down_w)


def attend_back(first, count, expected, meta, slopes, qkv, att_grad, totals, rows_in, cols_in, earlier):
    total, wide = qkv.shape
    width = wide // 3
    per, length = rows_in.shape[1:]

    def spot_of(s, meta):
        return jnp.clip(first + s, 0, jnp.maximum(meta[N_LIVE] - 1, 0))

    def by_offset(s, meta, slopes):
        return (aligned(meta[OFF + spot_of(s, meta)]), 0)

    spots = pl.BlockSpec(
        (1, per, length),
        lambda s, meta, slopes: (meta[IMG + spot_of(s, meta)] // per, 0, 0),
    )
    anywhere = pl.BlockSpec(memory_space=pl.ANY)
    return pl.pallas_call(
        functools.partial(attend_back_kernel, first, per),
        out_shape=jax.ShapeDtypeStruct((total, wide), BF16),
        grid_spec=pltpu.PrefetchScalarGridSpec(
            num_scalar_prefetch=2,
            grid=(count,),
            in_specs=[
                pl.BlockSpec((pl.Element(WINDOW), pl.Element(wide)), by_offset),
                pl.BlockSpec((pl.Element(WINDOW), pl.Element(width)), by_offset),
                pl.BlockSpec(
                    (1, HEADS // 2, 8, WINDOW),
                    lambda s, meta, slopes: (spot_of(s, meta), 0, 0, 0),
                ),
                spots,
                spots,
            ]
            + [anywhere] * len(earlier),
            out_specs=anywhere,
            scratch_shapes=[
                pltpu.VMEM((2, WINDOW, wide), BF16),
                pltpu.VMEM((WINDOW, WINDOW), F32),
                pltpu.SemaphoreType.DMA((2,)),
            ],
        ),
        input_output_aliases={7: 0} if earlier else {},
        compiler_params=params(),
        cost_estimate=cost(expected),
    )(meta, slopes, qkv, att_grad, totals, rows_in, cols_in, *earlier)


def bwd_tile(s, meta):
    return (jnp.clip(s, 0, jnp.maximum(meta[N_BWD] - 1, 0)), 0)


def qkv_grad(meta, packed_grad, packed, vecs):
    rows, width = packed.shape
    parcel = 3 * width // 2 // BLOCKS
    tiles = (rows - WINDOW) // TILE
    return pl.pallas_call(
        qkv_grad_kernel,
        out_shape=(
            jax.ShapeDtypeStruct((BLOCKS, parcel, width), BF16),
            jax.ShapeDtypeStruct((BLOCKS, parcel, width), BF16),
            jax.ShapeDtypeStruct((8, 3 * width), F32),
        ),
        grid_spec=pltpu.PrefetchScalarGridSpec(
            num_scalar_prefetch=1,
            grid=(tiles,),
            in_specs=[
                pl.BlockSpec((TILE, 3 * width), bwd_tile),
                pl.BlockSpec((TILE, width), bwd_tile),
                whole(*vecs.shape),
            ],
            out_specs=[
                pl.BlockSpec(memory_space=pl.ANY),
                pl.BlockSpec(memory_space=pl.ANY),
                whole(8, 3 * width),
            ],
            scratch_shapes=[
                pltpu.VMEM((width, 3 * width), F32),
                pltpu.VMEM((2, BLOCKS, parcel, width), BF16),
                pltpu.SemaphoreType.DMA((2,)),
            ],
        ),
        compiler_params=params(),
        cost_estimate=cost(15),
    )(meta, packed_grad, packed, vecs)


def token_grad(
    meta, packed_grad, packed, mid_grad, vecs, weight, bias_g, vec_two, upb_g, steps, length, images
):
    rows, width = packed.shape
    tiles = (rows - WINDOW) // TILE
    return pl.pallas_call(
        token_grad_kernel,
        out_shape=(
            jax.ShapeDtypeStruct((steps, length, images, width), F32),
            jax.ShapeDtypeStruct((16, width), F32),
        ),
        grid_spec=pltpu.PrefetchScalarGridSpec(
            num_scalar_prefetch=1,
            grid=(tiles + steps,),
            in_specs=[
                pl.BlockSpec((TILE, 3 * width), bwd_tile),
                pl.BlockSpec((TILE, width), bwd_tile),
                pl.BlockSpec((TILE, width), bwd_tile),
                whole(*vecs.shape),
                whole(width, 3 * width),
                whole(*bias_g.shape),
                whole(*vec_two.shape),
                whole(*upb_g.shape),
            ],
            out_specs=[
                pl.BlockSpec(
                    (1, length, images, width),
                    lambda s, meta: (jnp.clip(s - tiles, 0, steps - 1), 0, 0, 0),
                ),
                whole(16, width),
            ],
            scratch_shapes=[pltpu.VMEM((rows, width), F32)],
        ),
        compiler_params=params(),
        cost_estimate=cost(20),
    )(meta, packed_grad, packed, mid_grad, vecs, weight, bias_g, vec_two, upb_g)


def cost(microseconds):
    return pl.CostEstimate(
        flops=int(microseconds * 1e9), bytes_accessed=int(microseconds * 1e5), transcendentals=0
    )


def swap(block, axis, bit):
    size = lax.axis_size(axis)
    return lax.ppermute(block, axis, [(n, n ^ bit) for n in range(size)])


def bit_of(axis, bit):
    return lax.axis_index(axis) // bit % 2


def added(a, b):
    return (a.astype(F32) + b.astype(F32)).astype(BF16)


def unpacked(mine, other, shapes):
    swapped = bit_of("bal", 1) == 1
    first = jnp.where(swapped, other, mine)
    second = jnp.where(swapped, mine, other)
    lead, width = mine.shape[:-2], mine.shape[-1]
    out, at = [], 0
    for rows, columns, kind in shapes:
        wide = columns // width
        part = rows * wide // 2
        held = [half[..., at : at + part, :] for half in (first, second)]
        if kind == "rows":
            size = rows // 2
            parts = [
                jnp.concatenate(
                    [half[..., c * size : (c + 1) * size, :] for c in range(wide)], axis=-1
                )
                for half in held
            ]
            out.append(jnp.concatenate(parts, axis=-2))
        elif kind == "columns":
            parts = [
                half[..., c * rows : (c + 1) * rows, :] for half in held for c in range(wide // 2)
            ]
            out.append(jnp.concatenate(parts, axis=-1))
        else:
            size = width // 2
            tops = [half[..., :size] for half in held]
            bottoms = [half[..., size:] for half in held]
            out.append(
                jnp.concatenate(
                    [jnp.concatenate(tops, axis=-1), jnp.concatenate(bottoms, axis=-1)], axis=-2
                )
            )
        at += part
    return [matrix.reshape(lead[:-1] + (-1, matrix.shape[-1])) if lead else matrix for matrix in out]


def spread_sum(keep, send, shapes):
    return [
        lax.psum(lax.psum_scatter(matrix, "dp", scatter_dimension=0, tiled=True), "bal").astype(F32)
        for matrix in unpacked(keep, send, shapes)
    ]


def start_fold(block, bit):
    block = block.reshape((-1, 2) + block.shape[-2:])
    mine = bit_of("dp", bit)
    keep = lax.dynamic_index_in_dim(block, mine, 1, keepdims=False)
    send = lax.dynamic_index_in_dim(block, 1 - mine, 1, keepdims=False)
    return keep, swap(send, "dp", bit)


def after(value, *others):
    return lax.optimization_barrier((value,) + others)[0]


def doubled(block, round_no):
    bits = [("bal", 1)]
    bit = 1
    while bit < lax.axis_size("dp"):
        bits.append(("dp", bit))
        bit *= 2
    bits.append(("bal", 2))
    if round_no is None:
        return len(bits)
    axis, bit = bits[round_no]
    return block + swap(block, axis, bit)


def per_device(
    tokens,
    cotangent,
    counts,
    rows,
    cols,
    present,
    slots,
    first_gain,
    first_shift,
    qkv_weight,
    query_bias,
    value_bias,
    out_weight,
    out_bias,
    second_gain,
    second_shift,
    up_weight,
    up_bias,
    down_weight,
    down_bias,
):
    steps, images, length, width = tokens.shape
    hidden = up_weight.shape[1]
    group = lax.axis_size("bal")
    total = steps * images
    slopes = jnp.exp2(-8.0 * (jnp.arange(16, dtype=F32) + 1.0) / HEADS)

    def exchange(blocks):
        flat = blocks.reshape(group, -1, width)
        return lax.all_to_all(flat, "bal", split_axis=0, concat_axis=0, tiled=True)

    def turn(array):
        return jnp.transpose(array, (0, 2, 1, 3))

    meta, take, vecs, cot_send = prepare(
        [
            lax.ppermute(slots, "bal", [(a, (a + k) % group) for a in range(group)])
            for k in range(1, group)
        ],
        counts, present, slots,
        lax.axis_index("bal").astype(jnp.int32).reshape(1), turn(cotangent),
        first_gain, first_shift, query_bias, value_bias, out_bias, second_gain, second_shift,
        down_bias, up_bias,
    )
    cot_home = exchange(cot_send).reshape(group, steps, -1, width)
    packed, qkv, att, totals = first_half(meta, slopes, turn(tokens), rows, cols, vecs, qkv_weight)
    y_send, mid_grad, att_grad, keep_two, send_two, vec_two, upb_g = mlp(
        meta, cot_home, att, packed, vecs, out_weight, up_weight, down_weight, length
    )
    share, long = width // BLOCKS, hidden // BLOCKS
    shapes_two = ((share, hidden, "columns"), (long, width, "side"), (share, width, "rows"))
    shapes_one = ((share, 3 * width, "rows"),)
    direct = lax.axis_size("dp") == BLOCKS

    def back(first, count, expected, table, earlier):
        return attend_back(
            first, count, expected, table, slopes, qkv, att_grad, totals, rows, cols, earlier
        )

    lead = max(images // 2, 1)
    packed_grad = back(0, lead, 15, meta, ())
    table = meta
    if direct:
        sum_two = added(after(keep_two, packed_grad), swap(send_two, "bal", 1))
        share_two = lax.psum_scatter(sum_two, "dp", scatter_dimension=0, tiled=True)[0]
        table = after(meta, sum_two)
        y_send = after(y_send, sum_two)
    y_got = exchange(y_send)
    packed_grad = back(lead, total - lead, 500, table, (packed_grad,))
    keep_one, send_one, bias_g = qkv_grad(table, packed_grad, packed, vecs)
    output = place(after(take, keep_one), y_got.reshape(group, steps, -1, width), length)
    table = after(table, output)
    if direct:
        sum_one = added(keep_one, swap(send_one, "bal", 1))
        keep_y, crossing_y = start_fold(sum_one, 1)
        table = after(table, sum_one)
    input_grad, vectors = token_grad(
        table, packed_grad, packed, mid_grad, vecs, qkv_weight, bias_g, vec_two, upb_g,
        steps, length, images,
    )
    rounds = doubled(vectors, None)
    if direct:
        half_one = added(after(keep_y, vectors), crossing_y)
        keep, crossing = start_fold(half_one, 2)
        for n in range(rounds - 2):
            vectors = doubled(vectors, n)
        block = added(after(keep, vectors), crossing)
        keep, crossing = start_fold(block, 4)
        vectors = doubled(after(vectors, block), rounds - 2)
        block = added(after(keep, vectors), crossing).reshape(sum_one.shape[-2:])
        across_one = swap(block, "bal", 2)
        across_two = swap(after(share_two, block), "bal", 2)
        vectors = doubled(after(vectors, block), rounds - 1)
        full_one = added(after(block, vectors), across_one)
        full_two = added(after(share_two, full_one), across_two)
        (qkv_rows,) = [
            matrix.astype(F32)
            for matrix in unpacked(full_one, swap(full_one, "bal", 1), shapes_one)
        ]
        up_rows, down_rows, out_rows = [
            matrix.astype(F32)
            for matrix in unpacked(full_two, swap(full_two, "bal", 1), shapes_two)
        ]
    else:
        (qkv_rows,) = spread_sum(keep_one, send_one, shapes_one)
        up_rows, down_rows, out_rows = spread_sum(keep_two, send_two, shapes_two)
        for n in range(rounds):
            vectors = doubled(vectors, n)

    def vector(n):
        return vectors[n]

    return (
        turn(output),
        turn(input_grad),
        vector(0),
        vector(1),
        qkv_rows,
        vector(2),
        vector(3),
        out_rows,
        vector(6),
        vector(4),
        vector(5),
        up_rows,
        vectors[8 : 8 + hidden // width].reshape(-1),
        down_rows,
        vector(7),
    )


def solution(mesh):
    images = P(None, ("dp", "bal"), None, None)
    spots = P(None, ("dp", "bal"), None)
    flags = P(None, ("dp", "bal"))
    matrix = P("dp", None)
    return jax.shard_map(
        per_device,
        mesh=mesh,
        in_specs=(images, images, flags, spots, spots, flags, flags) + (P(),) * 13,
        out_specs=(
            images, images, P(), P(), matrix, P(), P(), matrix, P(), P(), P(), matrix, P(), matrix, P(),
        ),
        check_vma=False,
    )
```

```python
import functools
import math

import jax
import jax.numpy as jnp
from jax import lax
from jax.experimental import pallas as pl
from jax.experimental.pallas import tpu as pltpu
from jax.sharding import PartitionSpec as P

HEADS = 12
TILE = 256
WINDOW = 256
FAR = 1e12
EPS = 1e-06
BLOCKS = 8
CHUNK = 1024
VMEM_LIMIT = 60 * 1024 * 1024

F32 = jnp.float32
BF16 = jnp.bfloat16

OFF, CNT, IMG, LIVE, PEER, SPOT, MISC = 0, 16, 32, 48, 64, 80, 96
N_FWD, N_BWD, ROWS_FWD, ROWS_BWD, N_LIVE, CORE = range(MISC, MISC + 6)
PLACES = 128

GAIN_ONE, SHIFT_ONE, QKV_B, OUT_B, GAIN_TWO, SHIFT_TWO, DOWN_B, UP_B = 0, 1, 2, 5, 6, 7, 8, 9
VECTORS = (GAIN_ONE, SHIFT_ONE, QKV_B, QKV_B + 2, OUT_B, GAIN_TWO, SHIFT_TWO, DOWN_B, UP_B)


def dot(a, b):
    return jnp.dot(a, b, preferred_element_type=F32)


def dot_bt(a, b):
    return lax.dot_general(a, b, (((1,), (1,)), ((), ())), preferred_element_type=F32)


def turned(block):
    return block.astype(F32).T.astype(BF16)


def layer_norm(values):
    average = jnp.mean(values, axis=-1, keepdims=True)
    centred = values - average
    spread = jnp.mean(centred * centred, axis=-1, keepdims=True)
    inverse = lax.rsqrt(spread + EPS)
    return centred * inverse, inverse


def norm_back(out_grad, gain, unit, inverse):
    e = out_grad * gain
    mean_e = jnp.mean(e, axis=-1, keepdims=True)
    mean_eu = jnp.mean(e * unit, axis=-1, keepdims=True)
    return inverse * (e - mean_e - unit * mean_eu)


def gelu_parts(u):
    size = jnp.abs(u)
    t = 1.0 / (1.0 + (0.3275911 * math.sqrt(0.5)) * size)
    bell = jnp.exp2((-0.5 * math.log2(math.e)) * (u * u))
    poly = t * (
        0.5 * 0.254829592
        + t
        * (
            0.5 * -0.284496736
            + t * (0.5 * 1.421413741 + t * (0.5 * -1.453152027 + t * (0.5 * 1.061405429)))
        )
    )
    tail = poly * bell
    phi_sum = jnp.where(u >= 0, 1.0 - tail, tail)
    return phi_sum, u * bell * (1.0 / math.sqrt(2.0 * math.pi))


def put_rows(packed, off, count, block):
    rows = (block.shape[0] + 15) // 16 * 16
    if rows > block.shape[0]:
        more = jnp.zeros((rows - block.shape[0], block.shape[1]), block.dtype)
        block = jnp.concatenate([block, more], axis=0)
    ids = row_ids(0, rows)
    window = pl.ds(off, rows)
    block = jnp.where(ids < count, block, jnp.zeros_like(block))
    packed[window, :] = jnp.where(ids < (count + 15) // 16 * 16, block, packed[window, :])


def row_ids(start, rows):
    return start + lax.broadcasted_iota(jnp.int32, (rows, 1), 0)


def aligned(value, step=16):
    return pl.multiple_of(value, step)


def by_count(count, run):
    @pl.when(count <= 128)
    def _():
        run(128, 128)

    @pl.when(jnp.logical_and(count > 128, count <= 192))
    def _():
        run(192, 256)

    @pl.when(count > 192)
    def _():
        run(256, 256)


def distances(rows, cols, which, count, keys, queries):
    mine = lax.broadcasted_iota(jnp.int32, rows.shape, 0) == which
    row = jnp.sum(jnp.where(mine, rows, 0).astype(F32), axis=0, keepdims=True)
    col = jnp.sum(jnp.where(mine, cols, 0).astype(F32), axis=0, keepdims=True)
    spots = jnp.concatenate([row, col, jnp.zeros((6, row.shape[1]), F32)], axis=0)
    spots = jnp.concatenate([spots, jnp.zeros((8, WINDOW - row.shape[1]), F32)], axis=1)
    eye = jnp.where(
        lax.broadcasted_iota(jnp.int32, (keys, WINDOW), 0)
        == lax.broadcasted_iota(jnp.int32, (keys, WINDOW), 1),
        1.0,
        0.0,
    ).astype(BF16)
    turned_spots = dot_bt(eye, spots.astype(BF16))
    down = turned_spots[:, 0:1] - spots[0:1, :queries]
    across = turned_spots[:, 1:2] - spots[1:2, :queries]
    far = row_ids(0, keys) >= count
    return jnp.where(far, FAR, jnp.sqrt(down * down + across * across))


def prepare_kernel(group, counts, present, slots, me, cot, *rest):
    *rest, meta, take, vecs, send = rest
    every, lines = (slots,) + tuple(rest[: group - 1]), rest[group - 1 :]
    step = pl.program_id(0)
    steps, length, images, width = pl.num_programs(0), cot.shape[1], cot.shape[2], cot.shape[3]
    @pl.when(step == 0)
    def _():
        def fill(live):
            def body(img, carry):
                spot, off = carry
                m, i = img // images, img % images
                count = counts[m, i]
                mine = present[m, i] == live

                @pl.when(mine)
                def _():
                    meta[OFF + spot] = off
                    meta[CNT + spot] = count
                    meta[IMG + spot] = img
                    meta[LIVE + spot] = live
                    meta[PEER + spot] = slots[m, i] // images * steps + m
                    meta[SPOT + img] = spot

                padded = (count + 15) // 16 * 16
                return spot + mine.astype(jnp.int32), off + jnp.where(mine, padded, 0)

            return body

        meta[CORE] = me[0] % 2
        vecs[...] = jnp.zeros_like(vecs)
        for row, values in zip(VECTORS, lines):
            for n in range(values.shape[0] // width):
                piece = values[n * width : (n + 1) * width]
                vecs[row + n : row + n + 1, :] = piece.reshape(1, width)
        zero = jnp.int32(0)
        total = counts.shape[0] * images
        spot, off = lax.fori_loop(0, total, fill(1), (zero, zero))
        meta[N_LIVE] = spot
        meta[ROWS_BWD] = off
        meta[N_BWD] = (off + TILE - 1) // TILE
        spot, off = lax.fori_loop(0, total, fill(0), (spot, off))
        meta[ROWS_FWD] = off
        meta[N_FWD] = (off + TILE - 1) // TILE

        for back, theirs in enumerate(every):
            a = (me[0] + group - back) % group

            def land(n, carry):
                m, i = n // images, n % images
                slot = theirs[m, i]

                @pl.when(slot // images == me[0])
                def _():
                    take[m * images + slot % images] = a * steps + m

                return carry

            lax.fori_loop(0, total, land, 0)

    block = jnp.swapaxes(cot[0].astype(F32), 0, 1).astype(BF16)
    for place in range(images):
        peer = take[step * images + place] // steps
        send[peer, 0, :length, :] = block[place]


def place_kernel(take, got, out):
    step = pl.program_id(0)
    length, images = out.shape[1], out.shape[2]
    steps = pl.num_programs(0)
    parts = [
        got[take[step * images + place] // steps, 0, :length, :].astype(F32)
        for place in range(images)
    ]
    out[0] = jnp.swapaxes(jnp.stack(parts, axis=0), 0, 1).astype(out.dtype)


def attend_kernel(
    meta, slopes, tokens, rows_in, cols_in, vecs, weight,
    packed_out, qkv_out, att_out, total_out,
    packed, qkv, att, gaps, sem_packed, sem_qkv, sem_att,
):
    length, per, width = tokens.shape[1], tokens.shape[2], tokens.shape[3]
    steps = pl.num_programs(0) // (per + 1)
    images = steps * per
    now = pl.program_id(0)

    def tile_copy(which, t):
        src, dst, sem = (
            (packed, packed_out, sem_packed),
            (qkv, qkv_out, sem_qkv),
            (att, att_out, sem_att),
        )[which]
        rows = pl.ds(aligned(t * TILE, TILE), TILE)
        return pltpu.make_async_copy(src.at[rows], dst.at[rows], sem.at[t])

    @pl.when(now == 0)
    def _():
        packed[...] = jnp.zeros_like(packed)

    @pl.when(now < steps)
    def _():
        block = jnp.swapaxes(tokens[0].astype(F32), 0, 1).astype(BF16)
        for i in range(per):
            spot = meta[SPOT + now * per + i]
            put_rows(packed, aligned(meta[OFF + spot]), meta[CNT + spot], block[i])

    @pl.when(now == steps - 1)
    def _():

        def project(t, carry):
            rows = pl.ds(aligned(t * TILE, TILE), TILE)
            unit, _ = layer_norm(packed[rows, :].astype(F32))
            hidden = (
                unit * vecs[GAIN_ONE : GAIN_ONE + 1] + vecs[SHIFT_ONE : SHIFT_ONE + 1]
            ).astype(BF16)
            for part in range(3):
                cols = slice(part * width, (part + 1) * width)
                bias = vecs[QKV_B + part : QKV_B + part + 1]
                qkv[rows, cols] = (dot(hidden, weight[:, cols]) + bias).astype(BF16)
            tile_copy(0, t).start()
            tile_copy(1, t).start()
            return carry

        lax.fori_loop(0, meta[N_FWD], project, 0)

    @pl.when(now >= steps)
    def _():
        spot = now - steps
        off = aligned(meta[OFF + spot])
        count = meta[CNT + spot]

        def run(keys, queries):
            which = meta[IMG + spot] % per
            gaps[:keys, :queries] = distances(rows_in[0], cols_in[0], which, count, keys, queries)
            key_seen = row_ids(0, keys) < count
            query_seen = row_ids(0, queries) < count
            left = lax.broadcasted_iota(jnp.int32, (keys, 128), 1) < 64

            def pair(p, carry):
                lanes = aligned(p * 128, 128)
                q2 = qkv[pl.ds(off, queries), pl.ds(lanes, 128)] * 0.125
                k2 = qkv[pl.ds(off, keys), pl.ds(width + lanes, 128)]
                v2 = qkv[pl.ds(off, keys), pl.ds(2 * width + lanes, 128)]
                q2 = jnp.where(query_seen, q2, jnp.zeros_like(q2))
                k2 = jnp.where(key_seen, k2, jnp.zeros_like(k2))
                v2 = jnp.where(key_seen, v2, jnp.zeros_like(v2))
                v2t = v2.astype(F32).T.astype(BF16)
                raw = dot_bt(by_head(k2, left), q2)
                outs = []
                for half in range(2):
                    head = 2 * p + half
                    scores = raw[half * keys : (half + 1) * keys]
                    scores = scores - slopes[head] * gaps[:keys, :queries]
                    top = jnp.max(scores, axis=0, keepdims=True)
                    terms = jnp.exp(scores - top)
                    total = jnp.sum(terms, axis=0, keepdims=True)
                    heads_out = dot(v2t[half * 64 : half * 64 + 64], terms.astype(BF16))
                    outs.append(heads_out * (1.0 / total))
                    total_out[0, p, half : half + 1, :queries] = top + jnp.log(total)
                both = jnp.concatenate(outs, axis=0)
                att[pl.ds(off, queries), pl.ds(lanes, 128)] = both.T.astype(BF16)
                return carry

            lax.fori_loop(0, HEADS // 2, pair, 0, unroll=HEADS // 2)

        by_count(count, run)
        after = meta[OFF + jnp.minimum(spot + 1, images - 1)]
        end = jnp.where(spot == images - 1, meta[N_FWD], after // TILE)

        def send(t, carry):
            tile_copy(2, t).start()
            return carry

        lax.fori_loop(off // TILE, end, send, 0)

    @pl.when(now == pl.num_programs(0) - 1)
    def _():
        def finish(t, carry):
            for which in range(3):
                tile_copy(which, t).wait()
            return carry

        lax.fori_loop(0, meta[N_FWD], finish, 0)


def by_head(block, left):
    none = jnp.zeros_like(block)
    return jnp.concatenate([jnp.where(left, block, none), jnp.where(left, none, block)], axis=0)


def mlp_kernel(
    chunk, length, meta, cot_in, att_in, tokens_in,
    vecs, out_hbm, up_hbm, down_hbm,
    y_send, mid_grad, att_grad, keep_g, send_g, vec_g, upb_g,
    up_b, held, up_acc, down_acc, out_acc, h2_s, h2t_s, dzt_s, z_s, g_s,
    out_w, up_w, down_w, sem, sem_w,
):
    step = pl.program_id(0)
    tiles = held.shape[0] // TILE - WINDOW // TILE
    images = (pl.num_programs(0) - tiles) // 2
    per = cot_in.shape[0]
    width = cot_in.shape[3]
    hidden = up_w.shape[1]
    out_b, gain, shift, down_b = [
        vecs.at[pl.ds(n, 1)] for n in (OUT_B, GAIN_TWO, SHIFT_TWO, DOWN_B)
    ]

    def weight_copies():
        pairs = ((out_hbm, out_w), (up_hbm, up_w), (down_hbm, down_w))
        return [pltpu.make_async_copy(a, b, sem_w.at[n]) for n, (a, b) in enumerate(pairs)]

    @pl.when(step == 0)
    def _():
        for copy in weight_copies():
            copy.start()
        up_acc[...] = jnp.zeros_like(up_acc)
        down_acc[...] = jnp.zeros_like(down_acc)
        out_acc[...] = jnp.zeros_like(out_acc)
        vec_g[...] = jnp.zeros_like(vec_g)
        upb_g[...] = jnp.zeros_like(upb_g)
        for n in range(hidden // width):
            up_b[0:1, n * width : (n + 1) * width] = vecs[UP_B + n : UP_B + n + 1, :]

    @pl.when(step < images)
    def _():
        for i in range(per):
            spot = meta[SPOT + step * per + i]

            @pl.when(meta[LIVE + spot] == 1)
            def _():
                put_rows(
                    held, aligned(meta[OFF + spot]), meta[CNT + spot],
                    cot_in[meta[PEER + spot] // images, 0],
                )

    @pl.when(step == images)
    def _():
        for copy in weight_copies():
            copy.wait()

    def run_tile(t, both):
        rows = aligned(t * TILE, TILE)
        ids = row_ids(rows, TILE)
        att = att_in[...]
        att = jnp.where(ids < meta[ROWS_FWD], att, jnp.zeros_like(att))
        mid = tokens_in[...].astype(F32) + (dot(att, out_w[...]) + out_b[...])
        unit, inverse = layer_norm(mid)
        h2 = (unit * gain[...] + shift[...]).astype(BF16)
        h2_s[...] = h2
        z_s[...] = mid + down_b[...]
        if both:
            dz = held[pl.ds(rows, TILE), :]
            dz = jnp.where(ids < meta[ROWS_BWD], dz, jnp.zeros_like(dz))
            h2t_s[...] = turned(h2)
            dzt_s[...] = turned(dz)
            g_s[...] = jnp.zeros_like(g_s)

        def part(c, carry):
            cols = pl.ds(aligned(c * chunk, chunk), chunk)
            pre = dot(h2_s[...], up_w[:, cols]) + up_b[0:1, cols]
            share, slope = gelu_parts(pre)
            act = (pre * share).astype(BF16)
            z_s[...] += dot(act, down_w[cols, :])
            if both:
                pre_g = (dot_bt(dz, down_w[cols, :]) * (share + slope)).astype(BF16)
                up_acc[:, cols] += dot(h2t_s[...], pre_g)
                down_acc[:, cols] += dot(dzt_s[...], act)
                upb_g[0:1, cols] += jnp.sum(pre_g.astype(F32), axis=0, keepdims=True)
                g_s[...] += dot_bt(pre_g, up_w[:, cols])
            return carry

        lax.fori_loop(0, hidden // chunk, part, 0, unroll=True)
        held[pl.ds(rows, TILE), :] = z_s[...].astype(BF16)
        if both:
            dzf = dz.astype(F32)
            g2 = g_s[...]
            dmid = dzf + norm_back(g2, gain[...], unit, inverse)
            branch = dmid.astype(BF16)
            mid_grad[...] = dmid
            att_grad[...] = dot_bt(branch, out_w[...]).astype(BF16)
            out_acc[...] += dot(turned(att), branch)
            vec_g[0:1, :] += jnp.sum(g2 * unit, axis=0, keepdims=True)
            vec_g[1:2, :] += jnp.sum(g2, axis=0, keepdims=True)
            vec_g[2:3, :] += jnp.sum(branch.astype(F32), axis=0, keepdims=True)
            vec_g[3:4, :] += jnp.sum(dzf, axis=0, keepdims=True)

    tile = step - images

    @pl.when(jnp.logical_and(tile >= 0, tile < meta[N_BWD]))
    def _():
        run_tile(tile, True)

    @pl.when(
        jnp.logical_and(
            jnp.logical_and(tile >= meta[N_BWD], tile >= 0),
            jnp.logical_and(tile < meta[N_FWD], tile < tiles),
        )
    )
    def _():
        run_tile(tile, False)

    turn = step - images - tiles

    @pl.when(turn >= 0)
    def _():
        for i in range(per):
            spot = meta[SPOT + turn * per + i]
            block = held[pl.ds(aligned(meta[OFF + spot]), length), :]
            seen = row_ids(0, length) < meta[CNT + spot]
            y_send[meta[PEER + spot] // images, 0, :length, :] = jnp.where(
                seen, block, jnp.zeros_like(block)
            )

    @pl.when(step == pl.num_programs(0) - 1)
    def _():
        share = width // BLOCKS
        long = hidden // BLOCKS
        size = 2 * share + long // 2 + share // 2
        for turn, target in enumerate((send_g, keep_g)):
            h = meta[CORE] if turn else 1 - meta[CORE]
            side = aligned(h * (width // 2), 128)
            copies = []
            for n in range(BLOCKS):
                base = n * size
                if turn:
                    earlier[n].wait()
                for c in range(2):
                    cols = pl.ds(aligned((2 * h + c) * width, 128), width)
                    piece = up_acc[n * share : (n + 1) * share, cols]
                    held[base + c * share : base + (c + 1) * share, :] = piece.astype(BF16)
                base += 2 * share
                piece = down_acc[pl.ds(side, width // 2), n * long : (n + 1) * long]
                flipped = turned(piece.astype(BF16))
                held[base : base + long // 2, : width // 2] = flipped[: long // 2]
                held[base : base + long // 2, width // 2 :] = flipped[long // 2 :]
                base += long // 2
                rows = pl.ds(pl.multiple_of(n * share + h * (share // 2), 8), share // 2)
                held[base : base + share // 2, :] = out_acc[rows, :].astype(BF16)
                copy = pltpu.make_async_copy(
                    held.at[pl.ds(n * size, size)], target.at[n], sem.at[turn, n]
                )
                copy.start()
                copies.append(copy)
            earlier = copies
        for copy in earlier:
            copy.wait()


def attend_back_kernel(
    first, per, meta, slopes, qkv, att_grad, totals, rows_in, cols_in, *rest
):
    grads_out, grads, gaps, sem = rest[-4:]
    step = pl.program_id(0)
    width = att_grad.shape[1]
    spot = first + step
    live = spot < meta[N_LIVE]
    slot = step % 2

    def copy(at):
        rows = pl.ds(aligned(meta[OFF + first + at]), WINDOW)
        return pltpu.make_async_copy(grads.at[at % 2], grads_out.at[rows], sem.at[at % 2])

    @pl.when(live)
    def _():
        count = meta[CNT + spot]

        def run(keys, queries):
            which = meta[IMG + spot] % per
            gaps[:keys, :queries] = distances(rows_in[0], cols_in[0], which, count, keys, queries)
            key_seen = row_ids(0, keys) < count
            query_seen = row_ids(0, queries) < count
            left = lax.broadcasted_iota(jnp.int32, (keys, 128), 1) < 64

            def pair(p, carry):
                lanes = aligned(p * 128, 128)
                q2 = qkv[:queries, pl.ds(lanes, 128)] * 0.125
                k2 = qkv[:keys, pl.ds(width + lanes, 128)]
                v2 = qkv[:keys, pl.ds(2 * width + lanes, 128)]
                o2 = att_grad[:queries, pl.ds(lanes, 128)]
                q2 = jnp.where(query_seen, q2, jnp.zeros_like(q2))
                o2 = jnp.where(query_seen, o2, jnp.zeros_like(o2))
                k2 = jnp.where(key_seen, k2, jnp.zeros_like(k2))
                v2 = jnp.where(key_seen, v2, jnp.zeros_like(v2))
                k2t = k2.astype(F32).T.astype(BF16)
                raw = dot_bt(by_head(k2, left), q2)
                raw_g = dot_bt(by_head(v2, left), o2)
                dq_parts, probs_low, score_low = [], [], []
                for half in range(2):
                    head = 2 * p + half
                    rows = slice(half * keys, (half + 1) * keys)
                    scores = raw[rows] - slopes[head] * gaps[:keys, :queries]
                    probs = jnp.exp(scores - totals[0, p, half : half + 1, :queries])
                    prob_g = raw_g[rows]
                    inner = jnp.sum(probs * prob_g, axis=0, keepdims=True)
                    score_g = (probs * (prob_g - inner)).astype(BF16)
                    dq_parts.append(dot(k2t[half * 64 : half * 64 + 64], score_g) * 0.125)
                    probs_low.append(probs.astype(BF16))
                    score_low.append(score_g)
                dv = dot(jnp.concatenate(probs_low, axis=0), o2)
                dk = dot(jnp.concatenate(score_low, axis=0), q2)
                dv = jnp.where(left, dv[:keys], dv[keys:])
                dk = jnp.where(left, dk[:keys], dk[keys:])
                dq = jnp.concatenate(dq_parts, axis=0).T.astype(BF16)
                grads[slot, :queries, pl.ds(lanes, 128)] = dq
                grads[slot, :keys, pl.ds(width + lanes, 128)] = dk.astype(BF16)
                grads[slot, :keys, pl.ds(2 * width + lanes, 128)] = dv.astype(BF16)
                return carry

            lax.fori_loop(0, HEADS // 2, pair, 0, unroll=HEADS // 2)

        by_count(count, run)

        @pl.when(step > 0)
        def _():
            copy(step - 1).wait()

        copy(step).start()

        @pl.when(jnp.logical_or(step == pl.num_programs(0) - 1, spot == meta[N_LIVE] - 1))
        def _():
            copy(step).wait()


def qkv_grad_kernel(meta, packed_grad, tokens, vecs, keep_g, send_g, bias_g, acc, stage, sem):
    tile = pl.program_id(0)
    width = tokens.shape[1]

    @pl.when(tile == 0)
    def _():
        acc[...] = jnp.zeros_like(acc)
        bias_g[...] = jnp.zeros_like(bias_g)

    @pl.when(tile < meta[N_BWD])
    def _():
        ids = row_ids(tile * TILE, TILE)
        unit, _ = layer_norm(tokens[...].astype(F32))
        hidden = (
            unit * vecs[GAIN_ONE : GAIN_ONE + 1] + vecs[SHIFT_ONE : SHIFT_ONE + 1]
        ).astype(BF16)
        hidden_t = turned(hidden)
        for part in range(3):
            cols = slice(part * width, (part + 1) * width)
            block = packed_grad[:, cols]
            block = jnp.where(ids < meta[ROWS_BWD], block, jnp.zeros_like(block))
            acc[:, cols] += dot(hidden_t, block)
            bias_g[0:1, cols] += jnp.sum(block.astype(F32), axis=0, keepdims=True)

    @pl.when(tile == pl.num_programs(0) - 1)
    def _():
        rows = width // BLOCKS // 2
        for block in range(BLOCKS):
            for h in range(2):
                for c in range(3):
                    first = (2 * block + h) * rows
                    piece = acc[first : first + rows, c * width : (c + 1) * width]
                    stage[h, block, c * rows : (c + 1) * rows, :] = piece.astype(BF16)
        mine = meta[CORE]
        keep = pltpu.make_async_copy(stage.at[mine], keep_g, sem.at[0])
        send = pltpu.make_async_copy(stage.at[1 - mine], send_g, sem.at[1])
        keep.start()
        send.start()
        keep.wait()
        send.wait()


def token_grad_kernel(
    meta, packed_grad, tokens, mid_grad, vecs, weight, bias_g, vec_two, upb_g, out, vec_g, held
):
    step = pl.program_id(0)
    tiles = held.shape[0] // TILE - WINDOW // TILE
    length, images = out.shape[1], out.shape[2]

    @pl.when(step == 0)
    def _():
        width = vec_g.shape[1]
        vec_g[...] = jnp.zeros_like(vec_g)
        vec_g[2:3, :] = bias_g[0:1, :width]
        vec_g[3:4, :] = bias_g[0:1, 2 * width :]
        vec_g[4:8, :] = vec_two[0:4, :]
        for n in range(upb_g.shape[1] // width):
            vec_g[8 + n : 9 + n, :] = upb_g[0:1, n * width : (n + 1) * width]

    @pl.when(jnp.logical_and(step < tiles, step < meta[N_BWD]))
    def _():
        rows = aligned(step * TILE, TILE)
        ids = row_ids(rows, TILE)
        unit, inverse = layer_norm(tokens[...].astype(F32))
        block = packed_grad[...]
        block = jnp.where(ids < meta[ROWS_BWD], block, jnp.zeros_like(block))
        g1 = dot_bt(block, weight[...])
        back = norm_back(g1, vecs[GAIN_ONE : GAIN_ONE + 1], unit, inverse)
        held[pl.ds(rows, TILE), :] = mid_grad[...] + back
        vec_g[0:1, :] += jnp.sum(g1 * unit, axis=0, keepdims=True)
        vec_g[1:2, :] += jnp.sum(g1, axis=0, keepdims=True)

    @pl.when(step >= tiles)
    def _():
        parts = []
        for i in range(images):
            spot = meta[SPOT + (step - tiles) * images + i]
            off = aligned(meta[OFF + spot])
            limit = meta[CNT + spot] * meta[LIVE + spot]
            block = held[pl.ds(off, length), :]
            parts.append(jnp.where(row_ids(0, length) < limit, block, 0.0))
        out[0] = jnp.swapaxes(jnp.stack(parts, axis=0), 0, 1)


def whole(*shape):
    return pl.BlockSpec(shape, lambda *_: (0,) * len(shape), pipeline_mode=pl.Buffered(1))


def params():
    return pltpu.CompilerParams(vmem_limit_bytes=VMEM_LIMIT)


def small():
    return pl.BlockSpec(memory_space=pltpu.SMEM)


def prepare(others, counts, present, slots, me, cotangent, *vectors):
    steps, length, images, width = cotangent.shape
    group = len(others) + 1
    padded = (length + 7) // 8 * 8
    return pl.pallas_call(
        functools.partial(prepare_kernel, group),
        out_shape=(
            jax.ShapeDtypeStruct((PLACES,), jnp.int32),
            jax.ShapeDtypeStruct((steps * images,), jnp.int32),
            jax.ShapeDtypeStruct((16, width), F32),
            jax.ShapeDtypeStruct((group, steps, padded, width), BF16),
        ),
        grid=(steps,),
        in_specs=[small()] * 4
        + [pl.BlockSpec((1, length, images, width), lambda m: (m, 0, 0, 0))]
        + [small()] * len(others)
        + [whole(*vector.shape) for vector in vectors],
        out_specs=[
            small(),
            small(),
            whole(16, width),
            pl.BlockSpec((group, 1, padded, width), lambda m: (0, m, 0, 0)),
        ],
        compiler_params=params(),
    )(counts, present, slots, me, cotangent, *others, *vectors)


def place(take, got, length):
    group, steps, padded, width = got.shape
    return pl.pallas_call(
        place_kernel,
        out_shape=jax.ShapeDtypeStruct((steps, length, group, width), BF16),
        grid=(steps,),
        in_specs=[small(), pl.BlockSpec((group, 1, padded, width), lambda m: (0, m, 0, 0))],
        out_specs=pl.BlockSpec((1, length, group, width), lambda m: (m, 0, 0, 0)),
        compiler_params=params(),
    )(take, got)


def first_half(meta, slopes, tokens, rows, cols, vecs, weight):
    steps, length, per, width = tokens.shape
    images = steps * per
    tiles = -(-images * ((length + 15) // 16 * 16) // TILE)
    total = tiles * TILE + WINDOW
    spots = pl.BlockSpec(
        (1, per, length),
        lambda s, meta, slopes: (meta[IMG + jnp.maximum(s - steps, 0)] // per, 0, 0),
    )
    return pl.pallas_call(
        attend_kernel,
        out_shape=(
            jax.ShapeDtypeStruct((total, width), BF16),
            jax.ShapeDtypeStruct((total, 3 * width), BF16),
            jax.ShapeDtypeStruct((total, width), BF16),
            jax.ShapeDtypeStruct((images, HEADS // 2, 8, WINDOW), F32),
        ),
        grid_spec=pltpu.PrefetchScalarGridSpec(
            num_scalar_prefetch=2,
            grid=(steps + images,),
            in_specs=[
                pl.BlockSpec(
                    (1, length, per, width),
                    lambda s, meta, slopes: (jnp.minimum(s, steps - 1), 0, 0, 0),
                ),
                spots,
                spots,
                whole(*vecs.shape),
                whole(width, 3 * width),
            ],
            out_specs=[
                pl.BlockSpec(memory_space=pl.ANY),
                pl.BlockSpec(memory_space=pl.ANY),
                pl.BlockSpec(memory_space=pl.ANY),
                pl.BlockSpec(
                    (1, HEADS // 2, 8, WINDOW),
                    lambda s, meta, slopes: (jnp.maximum(s - steps, 0), 0, 0, 0),
                ),
            ],
            scratch_shapes=[
                pltpu.VMEM((total, width), BF16),
                pltpu.VMEM((total, 3 * width), BF16),
                pltpu.VMEM((total, width), BF16),
                pltpu.VMEM((WINDOW, WINDOW), F32),
                pltpu.SemaphoreType.DMA((tiles,)),
                pltpu.SemaphoreType.DMA((tiles,)),
                pltpu.SemaphoreType.DMA((tiles,)),
            ],
        ),
        compiler_params=params(),
        cost_estimate=cost(40),
    )(meta, slopes, tokens, rows, cols, vecs, weight)


def mlp(meta, cot, att, packed, vecs, out_w, up_w, down_w, length):
    group, steps, padded, width = cot.shape
    rows = packed.shape[0]
    tiles = (rows - WINDOW) // TILE
    hidden = up_w.shape[1]
    parcel = (2 * width + hidden // 2 + width // 2) // BLOCKS
    def fwd_tile(s, meta):
        return (jnp.clip(s - steps, 0, meta[N_FWD] - 1), 0)

    def bwd_tile(s, meta):
        return (jnp.clip(s - steps, 0, jnp.maximum(meta[N_BWD] - 1, 0)), 0)

    return pl.pallas_call(
        functools.partial(mlp_kernel, CHUNK, length),
        out_shape=(
            jax.ShapeDtypeStruct(cot.shape, BF16),
            jax.ShapeDtypeStruct((rows, width), F32),
            jax.ShapeDtypeStruct((rows, width), BF16),
            jax.ShapeDtypeStruct((BLOCKS, parcel, width), BF16),
            jax.ShapeDtypeStruct((BLOCKS, parcel, width), BF16),
            jax.ShapeDtypeStruct((8, width), F32),
            jax.ShapeDtypeStruct((8, hidden), F32),
        ),
        grid_spec=pltpu.PrefetchScalarGridSpec(
            num_scalar_prefetch=1,
            grid=(2 * steps + tiles,),
            in_specs=[
                pl.BlockSpec(
                    (group, 1, padded, width), lambda s, meta: (0, jnp.minimum(s, steps - 1), 0, 0)
                ),
                pl.BlockSpec((TILE, width), fwd_tile),
                pl.BlockSpec((TILE, width), fwd_tile),
                whole(*vecs.shape),
                pl.BlockSpec(memory_space=pl.ANY),
                pl.BlockSpec(memory_space=pl.ANY),
                pl.BlockSpec(memory_space=pl.ANY),
            ],
            out_specs=[
                pl.BlockSpec(
                    (group, 1, padded, width),
                    lambda s, meta: (0, jnp.clip(s - steps - tiles, 0, steps - 1), 0, 0),
                ),
                pl.BlockSpec((TILE, width), bwd_tile),
                pl.BlockSpec((TILE, width), bwd_tile),
                pl.BlockSpec(memory_space=pl.ANY),
                pl.BlockSpec(memory_space=pl.ANY),
                whole(8, width),
                whole(8, hidden),
            ],
            scratch_shapes=[
                pltpu.VMEM((8, hidden), F32),
                pltpu.VMEM((rows, width), BF16),
                pltpu.VMEM((width, hidden), F32),
                pltpu.VMEM((width, hidden), F32),
                pltpu.VMEM((width, width), F32),
                pltpu.VMEM((TILE, width), BF16),
                pltpu.VMEM((width, TILE), BF16),
                pltpu.VMEM((width, TILE), BF16),
                pltpu.VMEM((TILE, width), F32),
                pltpu.VMEM((TILE, width), F32),
                pltpu.VMEM((width, width), BF16),
                pltpu.VMEM((width, hidden), BF16),
                pltpu.VMEM((hidden, width), BF16),
                pltpu.SemaphoreType.DMA((2, BLOCKS)),
                pltpu.SemaphoreType.DMA((3,)),
            ],
        ),
        compiler_params=params(),
        cost_estimate=cost(110),
    )(meta, cot, att, packed, vecs, out_w, up_w, down_w)


def attend_back(first, count, expected, meta, slopes, qkv, att_grad, totals, rows_in, cols_in, earlier):
    total, wide = qkv.shape
    width = wide // 3
    per, length = rows_in.shape[1:]

    def spot_of(s, meta):
        return jnp.clip(first + s, 0, jnp.maximum(meta[N_LIVE] - 1, 0))

    def by_offset(s, meta, slopes):
        return (aligned(meta[OFF + spot_of(s, meta)]), 0)

    spots = pl.BlockSpec(
        (1, per, length),
        lambda s, meta, slopes: (meta[IMG + spot_of(s, meta)] // per, 0, 0),
    )
    anywhere = pl.BlockSpec(memory_space=pl.ANY)
    return pl.pallas_call(
        functools.partial(attend_back_kernel, first, per),
        out_shape=jax.ShapeDtypeStruct((total, wide), BF16),
        grid_spec=pltpu.PrefetchScalarGridSpec(
            num_scalar_prefetch=2,
            grid=(count,),
            in_specs=[
                pl.BlockSpec((pl.Element(WINDOW), pl.Element(wide)), by_offset),
                pl.BlockSpec((pl.Element(WINDOW), pl.Element(width)), by_offset),
                pl.BlockSpec(
                    (1, HEADS // 2, 8, WINDOW),
                    lambda s, meta, slopes: (spot_of(s, meta), 0, 0, 0),
                ),
                spots,
                spots,
            ]
            + [anywhere] * len(earlier),
            out_specs=anywhere,
            scratch_shapes=[
                pltpu.VMEM((2, WINDOW, wide), BF16),
                pltpu.VMEM((WINDOW, WINDOW), F32),
                pltpu.SemaphoreType.DMA((2,)),
            ],
        ),
        input_output_aliases={7: 0} if earlier else {},
        compiler_params=params(),
        cost_estimate=cost(expected),
    )(meta, slopes, qkv, att_grad, totals, rows_in, cols_in, *earlier)


def bwd_tile(s, meta):
    return (jnp.clip(s, 0, jnp.maximum(meta[N_BWD] - 1, 0)), 0)


def qkv_grad(meta, packed_grad, packed, vecs):
    rows, width = packed.shape
    parcel = 3 * width // 2 // BLOCKS
    tiles = (rows - WINDOW) // TILE
    return pl.pallas_call(
        qkv_grad_kernel,
        out_shape=(
            jax.ShapeDtypeStruct((BLOCKS, parcel, width), BF16),
            jax.ShapeDtypeStruct((BLOCKS, parcel, width), BF16),
            jax.ShapeDtypeStruct((8, 3 * width), F32),
        ),
        grid_spec=pltpu.PrefetchScalarGridSpec(
            num_scalar_prefetch=1,
            grid=(tiles,),
            in_specs=[
                pl.BlockSpec((TILE, 3 * width), bwd_tile),
                pl.BlockSpec((TILE, width), bwd_tile),
                whole(*vecs.shape),
            ],
            out_specs=[
                pl.BlockSpec(memory_space=pl.ANY),
                pl.BlockSpec(memory_space=pl.ANY),
                whole(8, 3 * width),
            ],
            scratch_shapes=[
                pltpu.VMEM((width, 3 * width), F32),
                pltpu.VMEM((2, BLOCKS, parcel, width), BF16),
                pltpu.SemaphoreType.DMA((2,)),
            ],
        ),
        compiler_params=params(),
        cost_estimate=cost(15),
    )(meta, packed_grad, packed, vecs)


def token_grad(
    meta, packed_grad, packed, mid_grad, vecs, weight, bias_g, vec_two, upb_g, steps, length, images
):
    rows, width = packed.shape
    tiles = (rows - WINDOW) // TILE
    return pl.pallas_call(
        token_grad_kernel,
        out_shape=(
            jax.ShapeDtypeStruct((steps, length, images, width), F32),
            jax.ShapeDtypeStruct((16, width), F32),
        ),
        grid_spec=pltpu.PrefetchScalarGridSpec(
            num_scalar_prefetch=1,
            grid=(tiles + steps,),
            in_specs=[
                pl.BlockSpec((TILE, 3 * width), bwd_tile),
                pl.BlockSpec((TILE, width), bwd_tile),
                pl.BlockSpec((TILE, width), bwd_tile),
                whole(*vecs.shape),
                whole(width, 3 * width),
                whole(*bias_g.shape),
                whole(*vec_two.shape),
                whole(*upb_g.shape),
            ],
            out_specs=[
                pl.BlockSpec(
                    (1, length, images, width),
                    lambda s, meta: (jnp.clip(s - tiles, 0, steps - 1), 0, 0, 0),
                ),
                whole(16, width),
            ],
            scratch_shapes=[pltpu.VMEM((rows, width), F32)],
        ),
        compiler_params=params(),
        cost_estimate=cost(20),
    )(meta, packed_grad, packed, mid_grad, vecs, weight, bias_g, vec_two, upb_g)


def cost(microseconds):
    return pl.CostEstimate(
        flops=int(microseconds * 1e9), bytes_accessed=int(microseconds * 1e5), transcendentals=0
    )


def swap(block, axis, bit):
    size = lax.axis_size(axis)
    return lax.ppermute(block, axis, [(n, n ^ bit) for n in range(size)])


def bit_of(axis, bit):
    return lax.axis_index(axis) // bit % 2


def added(a, b):
    return (a.astype(F32) + b.astype(F32)).astype(BF16)


def unpacked(mine, other, shapes):
    swapped = bit_of("bal", 1) == 1
    first = jnp.where(swapped, other, mine)
    second = jnp.where(swapped, mine, other)
    lead, width = mine.shape[:-2], mine.shape[-1]
    out, at = [], 0
    for rows, columns, kind in shapes:
        wide = columns // width
        part = rows * wide // 2
        held = [half[..., at : at + part, :] for half in (first, second)]
        if kind == "rows":
            size = rows // 2
            parts = [
                jnp.concatenate(
                    [half[..., c * size : (c + 1) * size, :] for c in range(wide)], axis=-1
                )
                for half in held
            ]
            out.append(jnp.concatenate(parts, axis=-2))
        elif kind == "columns":
            parts = [
                half[..., c * rows : (c + 1) * rows, :] for half in held for c in range(wide // 2)
            ]
            out.append(jnp.concatenate(parts, axis=-1))
        else:
            size = width // 2
            tops = [half[..., :size] for half in held]
            bottoms = [half[..., size:] for half in held]
            out.append(
                jnp.concatenate(
                    [jnp.concatenate(tops, axis=-1), jnp.concatenate(bottoms, axis=-1)], axis=-2
                )
            )
        at += part
    return [matrix.reshape(lead[:-1] + (-1, matrix.shape[-1])) if lead else matrix for matrix in out]


def spread_sum(keep, send, shapes):
    return [
        lax.psum(lax.psum_scatter(matrix, "dp", scatter_dimension=0, tiled=True), "bal").astype(F32)
        for matrix in unpacked(keep, send, shapes)
    ]


def start_fold(block, bit):
    block = block.reshape((-1, 2) + block.shape[-2:])
    mine = bit_of("dp", bit)
    keep = lax.dynamic_index_in_dim(block, mine, 1, keepdims=False)
    send = lax.dynamic_index_in_dim(block, 1 - mine, 1, keepdims=False)
    return keep, swap(send, "dp", bit)


def after(value, *others):
    return lax.optimization_barrier((value,) + others)[0]


def doubled(block, round_no):
    bits = [("bal", 1), ("bal", 2)]
    bit = 1
    while bit < lax.axis_size("dp"):
        bits.append(("dp", bit))
        bit *= 2
    if round_no is None:
        return len(bits)
    axis, bit = bits[round_no]
    return block + swap(block, axis, bit)


def per_device(
    tokens,
    cotangent,
    counts,
    rows,
    cols,
    present,
    slots,
    first_gain,
    first_shift,
    qkv_weight,
    query_bias,
    value_bias,
    out_weight,
    out_bias,
    second_gain,
    second_shift,
    up_weight,
    up_bias,
    down_weight,
    down_bias,
):
    steps, images, length, width = tokens.shape
    hidden = up_weight.shape[1]
    group = lax.axis_size("bal")
    total = steps * images
    slopes = jnp.exp2(-8.0 * (jnp.arange(16, dtype=F32) + 1.0) / HEADS)

    def exchange(blocks):
        flat = blocks.reshape(group, -1, width)
        return lax.all_to_all(flat, "bal", split_axis=0, concat_axis=0, tiled=True)

    def turn(array):
        return jnp.transpose(array, (0, 2, 1, 3))

    meta, take, vecs, cot_send = prepare(
        [
            lax.ppermute(slots, "bal", [(a, (a + k) % group) for a in range(group)])
            for k in range(1, group)
        ],
        counts, present, slots,
        lax.axis_index("bal").astype(jnp.int32).reshape(1), turn(cotangent),
        first_gain, first_shift, query_bias, value_bias, out_bias, second_gain, second_shift,
        down_bias, up_bias,
    )
    cot_home = exchange(cot_send).reshape(group, steps, -1, width)
    packed, qkv, att, totals = first_half(meta, slopes, turn(tokens), rows, cols, vecs, qkv_weight)
    y_send, mid_grad, att_grad, keep_two, send_two, vec_two, upb_g = mlp(
        meta, cot_home, att, packed, vecs, out_weight, up_weight, down_weight, length
    )
    share, long = width // BLOCKS, hidden // BLOCKS
    shapes_two = ((share, hidden, "columns"), (long, width, "side"), (share, width, "rows"))
    shapes_one = ((share, 3 * width, "rows"),)
    direct = lax.axis_size("dp") == BLOCKS

    def back(first, count, expected, table, earlier):
        return attend_back(
            first, count, expected, table, slopes, qkv, att_grad, totals, rows, cols, earlier
        )

    lead = max(images // 2, 1)
    packed_grad = back(0, lead, 15, meta, ())
    table = meta
    if direct:
        sum_two = added(after(keep_two, packed_grad), swap(send_two, "bal", 1))
        share_two = lax.psum_scatter(sum_two, "dp", scatter_dimension=0, tiled=True)[0]
        table = after(meta, sum_two)
        y_send = after(y_send, sum_two)
    y_got = exchange(y_send)
    packed_grad = back(lead, total - lead, 500, table, (packed_grad,))
    keep_one, send_one, bias_g = qkv_grad(table, packed_grad, packed, vecs)
    output = place(after(take, keep_one), y_got.reshape(group, steps, -1, width), length)
    table = after(table, output)
    if direct:
        sum_one = added(keep_one, swap(send_one, "bal", 1))
        keep_y, crossing_y = start_fold(sum_one, 1)
        table = after(table, sum_one)
    input_grad, vectors = token_grad(
        table, packed_grad, packed, mid_grad, vecs, qkv_weight, bias_g, vec_two, upb_g,
        steps, length, images,
    )
    rounds = doubled(vectors, None)
    if direct:
        half_one = added(after(keep_y, vectors), crossing_y)
        keep, crossing = start_fold(half_one, 2)
        for n in range(rounds - 2):
            vectors = doubled(vectors, n)
        block = added(after(keep, vectors), crossing)
        keep, crossing = start_fold(block, 4)
        vectors = doubled(after(vectors, block), rounds - 2)
        across_two = swap(share_two, "bal", 2)
        block = added(after(keep, vectors, share_two), crossing).reshape(sum_one.shape[-2:])
        across_one = swap(block, "bal", 2)
        vectors = doubled(after(vectors, block), rounds - 1)
        full_one = added(after(block, vectors), across_one)
        full_two = added(after(share_two, full_one), across_two)
        (qkv_rows,) = [
            matrix.astype(F32)
            for matrix in unpacked(full_one, swap(full_one, "bal", 1), shapes_one)
        ]
        up_rows, down_rows, out_rows = [
            matrix.astype(F32)
            for matrix in unpacked(full_two, swap(full_two, "bal", 1), shapes_two)
        ]
    else:
        (qkv_rows,) = spread_sum(keep_one, send_one, shapes_one)
        up_rows, down_rows, out_rows = spread_sum(keep_two, send_two, shapes_two)
        for n in range(rounds):
            vectors = doubled(vectors, n)

    def vector(n):
        return vectors[n]

    return (
        turn(output),
        turn(input_grad),
        vector(0),
        vector(1),
        qkv_rows,
        vector(2),
        vector(3),
        out_rows,
        vector(6),
        vector(4),
        vector(5),
        up_rows,
        vectors[8 : 8 + hidden // width].reshape(-1),
        down_rows,
        vector(7),
    )


def solution(mesh):
    images = P(None, ("dp", "bal"), None, None)
    spots = P(None, ("dp", "bal"), None)
    flags = P(None, ("dp", "bal"))
    matrix = P("dp", None)
    return jax.shard_map(
        per_device,
        mesh=mesh,
        in_specs=(images, images, flags, spots, spots, flags, flags) + (P(),) * 13,
        out_specs=(
            images, images, P(), P(), matrix, P(), P(), matrix, P(), P(), P(), matrix, P(), matrix, P(),
        ),
        check_vma=False,
    )
```

```python
import functools
import math

import jax
import jax.numpy as jnp
from jax import lax
from jax.experimental import pallas as pl
from jax.experimental.pallas import tpu as pltpu
from jax.sharding import PartitionSpec as P

HEADS = 12
TILE = 256
WINDOW = 256
FAR = 1e12
EPS = 1e-06
BLOCKS = 8
CHUNK = 1024
VMEM_LIMIT = 60 * 1024 * 1024

F32 = jnp.float32
BF16 = jnp.bfloat16

OFF, CNT, IMG, LIVE, PEER, SPOT, MISC = 0, 16, 32, 48, 64, 80, 96
N_FWD, N_BWD, ROWS_FWD, ROWS_BWD, N_LIVE, CORE = range(MISC, MISC + 6)
PLACES = 128

GAIN_ONE, SHIFT_ONE, QKV_B, OUT_B, GAIN_TWO, SHIFT_TWO, DOWN_B, UP_B = 0, 1, 2, 5, 6, 7, 8, 9
VECTORS = (GAIN_ONE, SHIFT_ONE, QKV_B, QKV_B + 2, OUT_B, GAIN_TWO, SHIFT_TWO, DOWN_B, UP_B)


def dot(a, b):
    return jnp.dot(a, b, preferred_element_type=F32)


def dot_bt(a, b):
    return lax.dot_general(a, b, (((1,), (1,)), ((), ())), preferred_element_type=F32)


def turned(block):
    return block.astype(F32).T.astype(BF16)


def layer_norm(values):
    average = jnp.mean(values, axis=-1, keepdims=True)
    centred = values - average
    spread = jnp.mean(centred * centred, axis=-1, keepdims=True)
    inverse = lax.rsqrt(spread + EPS)
    return centred * inverse, inverse


def norm_back(out_grad, gain, unit, inverse):
    e = out_grad * gain
    mean_e = jnp.mean(e, axis=-1, keepdims=True)
    mean_eu = jnp.mean(e * unit, axis=-1, keepdims=True)
    return inverse * (e - mean_e - unit * mean_eu)


def gelu_parts(u):
    size = jnp.abs(u)
    t = 1.0 / (1.0 + (0.3275911 * math.sqrt(0.5)) * size)
    bell = jnp.exp2((-0.5 * math.log2(math.e)) * (u * u))
    poly = t * (
        0.5 * 0.254829592
        + t
        * (
            0.5 * -0.284496736
            + t * (0.5 * 1.421413741 + t * (0.5 * -1.453152027 + t * (0.5 * 1.061405429)))
        )
    )
    tail = poly * bell
    phi_sum = jnp.where(u >= 0, 1.0 - tail, tail)
    return phi_sum, u * bell * (1.0 / math.sqrt(2.0 * math.pi))


def put_rows(packed, off, count, block):
    rows = (block.shape[0] + 15) // 16 * 16
    if rows > block.shape[0]:
        more = jnp.zeros((rows - block.shape[0], block.shape[1]), block.dtype)
        block = jnp.concatenate([block, more], axis=0)
    ids = row_ids(0, rows)
    window = pl.ds(off, rows)
    block = jnp.where(ids < count, block, jnp.zeros_like(block))
    packed[window, :] = jnp.where(ids < (count + 15) // 16 * 16, block, packed[window, :])


def row_ids(start, rows):
    return start + lax.broadcasted_iota(jnp.int32, (rows, 1), 0)


def aligned(value, step=16):
    return pl.multiple_of(value, step)


def by_count(count, run):
    @pl.when(count <= 128)
    def _():
        run(128, 128)

    @pl.when(jnp.logical_and(count > 128, count <= 192))
    def _():
        run(192, 256)

    @pl.when(count > 192)
    def _():
        run(256, 256)


def distances(rows, cols, which, count, keys, queries):
    mine = lax.broadcasted_iota(jnp.int32, rows.shape, 0) == which
    row = jnp.sum(jnp.where(mine, rows, 0).astype(F32), axis=0, keepdims=True)
    col = jnp.sum(jnp.where(mine, cols, 0).astype(F32), axis=0, keepdims=True)
    spots = jnp.concatenate([row, col, jnp.zeros((6, row.shape[1]), F32)], axis=0)
    spots = jnp.concatenate([spots, jnp.zeros((8, WINDOW - row.shape[1]), F32)], axis=1)
    eye = jnp.where(
        lax.broadcasted_iota(jnp.int32, (keys, WINDOW), 0)
        == lax.broadcasted_iota(jnp.int32, (keys, WINDOW), 1),
        1.0,
        0.0,
    ).astype(BF16)
    turned_spots = dot_bt(eye, spots.astype(BF16))
    down = turned_spots[:, 0:1] - spots[0:1, :queries]
    across = turned_spots[:, 1:2] - spots[1:2, :queries]
    far = row_ids(0, keys) >= count
    return jnp.where(far, FAR, jnp.sqrt(down * down + across * across))


def prepare_kernel(group, counts, present, slots, me, cot, *rest):
    *rest, meta, take, vecs, send = rest
    every, lines = (slots,) + tuple(rest[: group - 1]), rest[group - 1 :]
    step = pl.program_id(0)
    steps, length, images, width = pl.num_programs(0), cot.shape[1], cot.shape[2], cot.shape[3]
    @pl.when(step == 0)
    def _():
        def fill(live):
            def body(img, carry):
                spot, off = carry
                m, i = img // images, img % images
                count = counts[m, i]
                mine = present[m, i] == live

                @pl.when(mine)
                def _():
                    meta[OFF + spot] = off
                    meta[CNT + spot] = count
                    meta[IMG + spot] = img
                    meta[LIVE + spot] = live
                    meta[PEER + spot] = slots[m, i] // images * steps + m
                    meta[SPOT + img] = spot

                padded = (count + 15) // 16 * 16
                return spot + mine.astype(jnp.int32), off + jnp.where(mine, padded, 0)

            return body

        meta[CORE] = me[0] % 2
        vecs[...] = jnp.zeros_like(vecs)
        for row, values in zip(VECTORS, lines):
            for n in range(values.shape[0] // width):
                piece = values[n * width : (n + 1) * width]
                vecs[row + n : row + n + 1, :] = piece.reshape(1, width)
        zero = jnp.int32(0)
        total = counts.shape[0] * images
        spot, off = lax.fori_loop(0, total, fill(1), (zero, zero))
        meta[N_LIVE] = spot
        meta[ROWS_BWD] = off
        meta[N_BWD] = (off + TILE - 1) // TILE
        spot, off = lax.fori_loop(0, total, fill(0), (spot, off))
        meta[ROWS_FWD] = off
        meta[N_FWD] = (off + TILE - 1) // TILE

        for back, theirs in enumerate(every):
            a = (me[0] + group - back) % group

            def land(n, carry):
                m, i = n // images, n % images
                slot = theirs[m, i]

                @pl.when(slot // images == me[0])
                def _():
                    take[m * images + slot % images] = a * steps + m

                return carry

            lax.fori_loop(0, total, land, 0)

    block = jnp.swapaxes(cot[0].astype(F32), 0, 1).astype(BF16)
    for place in range(images):
        peer = take[step * images + place] // steps
        send[peer, 0, :length, :] = block[place]


def place_kernel(take, got, out):
    step = pl.program_id(0)
    length, images = out.shape[1], out.shape[2]
    steps = pl.num_programs(0)
    parts = [
        got[take[step * images + place] // steps, 0, :length, :].astype(F32)
        for place in range(images)
    ]
    out[0] = jnp.swapaxes(jnp.stack(parts, axis=0), 0, 1).astype(out.dtype)


def attend_kernel(
    meta, slopes, tokens, rows_in, cols_in, vecs, weight,
    packed_out, qkv_out, att_out, total_out,
    packed, qkv, att, gaps, sem_packed, sem_qkv, sem_att,
):
    length, per, width = tokens.shape[1], tokens.shape[2], tokens.shape[3]
    steps = pl.num_programs(0) // (per + 1)
    images = steps * per
    now = pl.program_id(0)

    def tile_copy(which, t):
        src, dst, sem = (
            (packed, packed_out, sem_packed),
            (qkv, qkv_out, sem_qkv),
            (att, att_out, sem_att),
        )[which]
        rows = pl.ds(aligned(t * TILE, TILE), TILE)
        return pltpu.make_async_copy(src.at[rows], dst.at[rows], sem.at[t])

    @pl.when(now == 0)
    def _():
        packed[...] = jnp.zeros_like(packed)

    @pl.when(now < steps)
    def _():
        block = jnp.swapaxes(tokens[0].astype(F32), 0, 1).astype(BF16)
        for i in range(per):
            spot = meta[SPOT + now * per + i]
            put_rows(packed, aligned(meta[OFF + spot]), meta[CNT + spot], block[i])

    @pl.when(now == steps - 1)
    def _():

        def project(t, carry):
            rows = pl.ds(aligned(t * TILE, TILE), TILE)
            unit, _ = layer_norm(packed[rows, :].astype(F32))
            hidden = (
                unit * vecs[GAIN_ONE : GAIN_ONE + 1] + vecs[SHIFT_ONE : SHIFT_ONE + 1]
            ).astype(BF16)
            for part in range(3):
                cols = slice(part * width, (part + 1) * width)
                bias = vecs[QKV_B + part : QKV_B + part + 1]
                qkv[rows, cols] = (dot(hidden, weight[:, cols]) + bias).astype(BF16)
            tile_copy(0, t).start()
            tile_copy(1, t).start()
            return carry

        lax.fori_loop(0, meta[N_FWD], project, 0)

    @pl.when(now >= steps)
    def _():
        spot = now - steps
        off = aligned(meta[OFF + spot])
        count = meta[CNT + spot]

        def run(keys, queries):
            which = meta[IMG + spot] % per
            gaps[:keys, :queries] = distances(rows_in[0], cols_in[0], which, count, keys, queries)
            key_seen = row_ids(0, keys) < count
            query_seen = row_ids(0, queries) < count
            left = lax.broadcasted_iota(jnp.int32, (keys, 128), 1) < 64

            def pair(p, carry):
                lanes = aligned(p * 128, 128)
                q2 = qkv[pl.ds(off, queries), pl.ds(lanes, 128)] * 0.125
                k2 = qkv[pl.ds(off, keys), pl.ds(width + lanes, 128)]
                v2 = qkv[pl.ds(off, keys), pl.ds(2 * width + lanes, 128)]
                q2 = jnp.where(query_seen, q2, jnp.zeros_like(q2))
                k2 = jnp.where(key_seen, k2, jnp.zeros_like(k2))
                v2 = jnp.where(key_seen, v2, jnp.zeros_like(v2))
                v2t = v2.astype(F32).T.astype(BF16)
                raw = dot_bt(by_head(k2, left), q2)
                outs = []
                for half in range(2):
                    head = 2 * p + half
                    scores = raw[half * keys : (half + 1) * keys]
                    scores = scores - slopes[head] * gaps[:keys, :queries]
                    top = jnp.max(scores, axis=0, keepdims=True)
                    terms = jnp.exp(scores - top)
                    total = jnp.sum(terms, axis=0, keepdims=True)
                    heads_out = dot(v2t[half * 64 : half * 64 + 64], terms.astype(BF16))
                    outs.append(heads_out * (1.0 / total))
                    total_out[0, p, half : half + 1, :queries] = top + jnp.log(total)
                both = jnp.concatenate(outs, axis=0)
                att[pl.ds(off, queries), pl.ds(lanes, 128)] = both.T.astype(BF16)
                return carry

            lax.fori_loop(0, HEADS // 2, pair, 0, unroll=HEADS // 2)

        by_count(count, run)
        after = meta[OFF + jnp.minimum(spot + 1, images - 1)]
        end = jnp.where(spot == images - 1, meta[N_FWD], after // TILE)

        def send(t, carry):
            tile_copy(2, t).start()
            return carry

        lax.fori_loop(off // TILE, end, send, 0)

    @pl.when(now == pl.num_programs(0) - 1)
    def _():
        def finish(t, carry):
            for which in range(3):
                tile_copy(which, t).wait()
            return carry

        lax.fori_loop(0, meta[N_FWD], finish, 0)


def by_head(block, left):
    none = jnp.zeros_like(block)
    return jnp.concatenate([jnp.where(left, block, none), jnp.where(left, none, block)], axis=0)


def mlp_kernel(
    chunk, length, meta, cot_in, att_in, tokens_in,
    vecs, out_hbm, up_hbm, down_hbm,
    y_send, mid_grad, att_grad, keep_g, send_g, vec_g, upb_g,
    up_b, held, up_acc, down_acc, out_acc, h2_s, h2t_s, dzt_s, z_s, g_s,
    out_w, up_w, down_w, sem, sem_w,
):
    step = pl.program_id(0)
    tiles = held.shape[0] // TILE - WINDOW // TILE
    images = (pl.num_programs(0) - tiles) // 2
    per = cot_in.shape[0]
    width = cot_in.shape[3]
    hidden = up_w.shape[1]
    out_b, gain, shift, down_b = [
        vecs.at[pl.ds(n, 1)] for n in (OUT_B, GAIN_TWO, SHIFT_TWO, DOWN_B)
    ]

    def weight_copies():
        pairs = ((out_hbm, out_w), (up_hbm, up_w), (down_hbm, down_w))
        return [pltpu.make_async_copy(a, b, sem_w.at[n]) for n, (a, b) in enumerate(pairs)]

    @pl.when(step == 0)
    def _():
        for copy in weight_copies():
            copy.start()
        up_acc[...] = jnp.zeros_like(up_acc)
        down_acc[...] = jnp.zeros_like(down_acc)
        out_acc[...] = jnp.zeros_like(out_acc)
        vec_g[...] = jnp.zeros_like(vec_g)
        upb_g[...] = jnp.zeros_like(upb_g)
        for n in range(hidden // width):
            up_b[0:1, n * width : (n + 1) * width] = vecs[UP_B + n : UP_B + n + 1, :]

    @pl.when(step < images)
    def _():
        for i in range(per):
            spot = meta[SPOT + step * per + i]

            @pl.when(meta[LIVE + spot] == 1)
            def _():
                put_rows(
                    held, aligned(meta[OFF + spot]), meta[CNT + spot],
                    cot_in[meta[PEER + spot] // images, 0],
                )

    @pl.when(step == images)
    def _():
        for copy in weight_copies():
            copy.wait()

    def run_tile(t, both):
        rows = aligned(t * TILE, TILE)
        ids = row_ids(rows, TILE)
        att = att_in[...]
        att = jnp.where(ids < meta[ROWS_FWD], att, jnp.zeros_like(att))
        mid = tokens_in[...].astype(F32) + (dot(att, out_w[...]) + out_b[...])
        unit, inverse = layer_norm(mid)
        h2 = (unit * gain[...] + shift[...]).astype(BF16)
        h2_s[...] = h2
        z_s[...] = mid + down_b[...]
        if both:
            dz = held[pl.ds(rows, TILE), :]
            dz = jnp.where(ids < meta[ROWS_BWD], dz, jnp.zeros_like(dz))
            h2t_s[...] = turned(h2)
            dzt_s[...] = turned(dz)
            g_s[...] = jnp.zeros_like(g_s)

        def part(c, carry):
            cols = pl.ds(aligned(c * chunk, chunk), chunk)
            pre = dot(h2_s[...], up_w[:, cols]) + up_b[0:1, cols]
            share, slope = gelu_parts(pre)
            act = (pre * share).astype(BF16)
            z_s[...] += dot(act, down_w[cols, :])
            if both:
                pre_g = (dot_bt(dz, down_w[cols, :]) * (share + slope)).astype(BF16)
                up_acc[:, cols] += dot(h2t_s[...], pre_g)
                down_acc[:, cols] += dot(dzt_s[...], act)
                upb_g[0:1, cols] += jnp.sum(pre_g.astype(F32), axis=0, keepdims=True)
                g_s[...] += dot_bt(pre_g, up_w[:, cols])
            return carry

        lax.fori_loop(0, hidden // chunk, part, 0, unroll=True)
        held[pl.ds(rows, TILE), :] = z_s[...].astype(BF16)
        if both:
            dzf = dz.astype(F32)
            g2 = g_s[...]
            dmid = dzf + norm_back(g2, gain[...], unit, inverse)
            branch = dmid.astype(BF16)
            mid_grad[...] = dmid
            att_grad[...] = dot_bt(branch, out_w[...]).astype(BF16)
            out_acc[...] += dot(turned(att), branch)
            vec_g[0:1, :] += jnp.sum(g2 * unit, axis=0, keepdims=True)
            vec_g[1:2, :] += jnp.sum(g2, axis=0, keepdims=True)
            vec_g[2:3, :] += jnp.sum(branch.astype(F32), axis=0, keepdims=True)
            vec_g[3:4, :] += jnp.sum(dzf, axis=0, keepdims=True)

    tile = step - images

    @pl.when(jnp.logical_and(tile >= 0, tile < meta[N_BWD]))
    def _():
        run_tile(tile, True)

    @pl.when(
        jnp.logical_and(
            jnp.logical_and(tile >= meta[N_BWD], tile >= 0),
            jnp.logical_and(tile < meta[N_FWD], tile < tiles),
        )
    )
    def _():
        run_tile(tile, False)

    turn = step - images - tiles

    @pl.when(turn >= 0)
    def _():
        for i in range(per):
            spot = meta[SPOT + turn * per + i]
            block = held[pl.ds(aligned(meta[OFF + spot]), length), :]
            seen = row_ids(0, length) < meta[CNT + spot]
            y_send[meta[PEER + spot] // images, 0, :length, :] = jnp.where(
                seen, block, jnp.zeros_like(block)
            )

    @pl.when(step == pl.num_programs(0) - 1)
    def _():
        share = width // BLOCKS
        long = hidden // BLOCKS
        size = 2 * share + long // 2 + share // 2
        for turn, target in enumerate((send_g, keep_g)):
            h = meta[CORE] if turn else 1 - meta[CORE]
            side = aligned(h * (width // 2), 128)
            copies = []
            for n in range(BLOCKS):
                base = n * size
                if turn:
                    earlier[n].wait()
                for c in range(2):
                    cols = pl.ds(aligned((2 * h + c) * width, 128), width)
                    piece = up_acc[n * share : (n + 1) * share, cols]
                    held[base + c * share : base + (c + 1) * share, :] = piece.astype(BF16)
                base += 2 * share
                piece = down_acc[pl.ds(side, width // 2), n * long : (n + 1) * long]
                flipped = turned(piece.astype(BF16))
                held[base : base + long // 2, : width // 2] = flipped[: long // 2]
                held[base : base + long // 2, width // 2 :] = flipped[long // 2 :]
                base += long // 2
                rows = pl.ds(pl.multiple_of(n * share + h * (share // 2), 8), share // 2)
                held[base : base + share // 2, :] = out_acc[rows, :].astype(BF16)
                copy = pltpu.make_async_copy(
                    held.at[pl.ds(n * size, size)], target.at[n], sem.at[turn, n]
                )
                copy.start()
                copies.append(copy)
            earlier = copies
        for copy in earlier:
            copy.wait()


def attend_back_kernel(
    first, per, meta, slopes, qkv, att_grad, totals, rows_in, cols_in, *rest
):
    grads_out, grads, gaps, sem = rest[-4:]
    step = pl.program_id(0)
    width = att_grad.shape[1]
    spot = first + step
    live = spot < meta[N_LIVE]
    slot = step % 2

    def copy(at):
        rows = pl.ds(aligned(meta[OFF + first + at]), WINDOW)
        return pltpu.make_async_copy(grads.at[at % 2], grads_out.at[rows], sem.at[at % 2])

    @pl.when(live)
    def _():
        count = meta[CNT + spot]

        def run(keys, queries):
            which = meta[IMG + spot] % per
            gaps[:keys, :queries] = distances(rows_in[0], cols_in[0], which, count, keys, queries)
            key_seen = row_ids(0, keys) < count
            query_seen = row_ids(0, queries) < count
            left = lax.broadcasted_iota(jnp.int32, (keys, 128), 1) < 64

            def pair(p, carry):
                lanes = aligned(p * 128, 128)
                q2 = qkv[:queries, pl.ds(lanes, 128)] * 0.125
                k2 = qkv[:keys, pl.ds(width + lanes, 128)]
                v2 = qkv[:keys, pl.ds(2 * width + lanes, 128)]
                o2 = att_grad[:queries, pl.ds(lanes, 128)]
                q2 = jnp.where(query_seen, q2, jnp.zeros_like(q2))
                o2 = jnp.where(query_seen, o2, jnp.zeros_like(o2))
                k2 = jnp.where(key_seen, k2, jnp.zeros_like(k2))
                v2 = jnp.where(key_seen, v2, jnp.zeros_like(v2))
                k2t = k2.astype(F32).T.astype(BF16)
                raw = dot_bt(by_head(k2, left), q2)
                raw_g = dot_bt(by_head(v2, left), o2)
                dq_parts, probs_low, score_low = [], [], []
                for half in range(2):
                    head = 2 * p + half
                    rows = slice(half * keys, (half + 1) * keys)
                    scores = raw[rows] - slopes[head] * gaps[:keys, :queries]
                    probs = jnp.exp(scores - totals[0, p, half : half + 1, :queries])
                    prob_g = raw_g[rows]
                    inner = jnp.sum(probs * prob_g, axis=0, keepdims=True)
                    score_g = (probs * (prob_g - inner)).astype(BF16)
                    dq_parts.append(dot(k2t[half * 64 : half * 64 + 64], score_g) * 0.125)
                    probs_low.append(probs.astype(BF16))
                    score_low.append(score_g)
                dv = dot(jnp.concatenate(probs_low, axis=0), o2)
                dk = dot(jnp.concatenate(score_low, axis=0), q2)
                dv = jnp.where(left, dv[:keys], dv[keys:])
                dk = jnp.where(left, dk[:keys], dk[keys:])
                dq = jnp.concatenate(dq_parts, axis=0).T.astype(BF16)
                grads[slot, :queries, pl.ds(lanes, 128)] = dq
                grads[slot, :keys, pl.ds(width + lanes, 128)] = dk.astype(BF16)
                grads[slot, :keys, pl.ds(2 * width + lanes, 128)] = dv.astype(BF16)
                return carry

            lax.fori_loop(0, HEADS // 2, pair, 0, unroll=HEADS // 2)

        by_count(count, run)

        @pl.when(step > 0)
        def _():
            copy(step - 1).wait()

        copy(step).start()

        @pl.when(jnp.logical_or(step == pl.num_programs(0) - 1, spot == meta[N_LIVE] - 1))
        def _():
            copy(step).wait()


def qkv_grad_kernel(meta, packed_grad, tokens, vecs, keep_g, send_g, bias_g, acc, stage, sem):
    tile = pl.program_id(0)
    width = tokens.shape[1]

    @pl.when(tile == 0)
    def _():
        acc[...] = jnp.zeros_like(acc)
        bias_g[...] = jnp.zeros_like(bias_g)

    @pl.when(tile < meta[N_BWD])
    def _():
        ids = row_ids(tile * TILE, TILE)
        unit, _ = layer_norm(tokens[...].astype(F32))
        hidden = (
            unit * vecs[GAIN_ONE : GAIN_ONE + 1] + vecs[SHIFT_ONE : SHIFT_ONE + 1]
        ).astype(BF16)
        hidden_t = turned(hidden)
        for part in range(3):
            cols = slice(part * width, (part + 1) * width)
            block = packed_grad[:, cols]
            block = jnp.where(ids < meta[ROWS_BWD], block, jnp.zeros_like(block))
            acc[:, cols] += dot(hidden_t, block)
            bias_g[0:1, cols] += jnp.sum(block.astype(F32), axis=0, keepdims=True)

    @pl.when(tile == pl.num_programs(0) - 1)
    def _():
        rows = width // BLOCKS // 2
        for block in range(BLOCKS):
            for h in range(2):
                for c in range(3):
                    first = (2 * block + h) * rows
                    piece = acc[first : first + rows, c * width : (c + 1) * width]
                    stage[h, block, c * rows : (c + 1) * rows, :] = piece.astype(BF16)
        mine = meta[CORE]
        keep = pltpu.make_async_copy(stage.at[mine], keep_g, sem.at[0])
        send = pltpu.make_async_copy(stage.at[1 - mine], send_g, sem.at[1])
        keep.start()
        send.start()
        keep.wait()
        send.wait()


def token_grad_kernel(
    meta, packed_grad, tokens, mid_grad, vecs, weight, bias_g, vec_two, upb_g, out, vec_g, held
):
    step = pl.program_id(0)
    tiles = held.shape[0] // TILE - WINDOW // TILE
    length, images = out.shape[1], out.shape[2]

    @pl.when(step == 0)
    def _():
        width = vec_g.shape[1]
        vec_g[...] = jnp.zeros_like(vec_g)
        vec_g[2:3, :] = bias_g[0:1, :width]
        vec_g[3:4, :] = bias_g[0:1, 2 * width :]
        vec_g[4:8, :] = vec_two[0:4, :]
        for n in range(upb_g.shape[1] // width):
            vec_g[8 + n : 9 + n, :] = upb_g[0:1, n * width : (n + 1) * width]

    @pl.when(jnp.logical_and(step < tiles, step < meta[N_BWD]))
    def _():
        rows = aligned(step * TILE, TILE)
        ids = row_ids(rows, TILE)
        unit, inverse = layer_norm(tokens[...].astype(F32))
        block = packed_grad[...]
        block = jnp.where(ids < meta[ROWS_BWD], block, jnp.zeros_like(block))
        g1 = dot_bt(block, weight[...])
        back = norm_back(g1, vecs[GAIN_ONE : GAIN_ONE + 1], unit, inverse)
        held[pl.ds(rows, TILE), :] = mid_grad[...] + back
        vec_g[0:1, :] += jnp.sum(g1 * unit, axis=0, keepdims=True)
        vec_g[1:2, :] += jnp.sum(g1, axis=0, keepdims=True)

    @pl.when(step >= tiles)
    def _():
        parts = []
        for i in range(images):
            spot = meta[SPOT + (step - tiles) * images + i]
            off = aligned(meta[OFF + spot])
            limit = meta[CNT + spot] * meta[LIVE + spot]
            block = held[pl.ds(off, length), :]
            parts.append(jnp.where(row_ids(0, length) < limit, block, 0.0))
        out[0] = jnp.swapaxes(jnp.stack(parts, axis=0), 0, 1)


def whole(*shape):
    return pl.BlockSpec(shape, lambda *_: (0,) * len(shape), pipeline_mode=pl.Buffered(1))


def params():
    return pltpu.CompilerParams(vmem_limit_bytes=VMEM_LIMIT)


def small():
    return pl.BlockSpec(memory_space=pltpu.SMEM)


def prepare(others, counts, present, slots, me, cotangent, *vectors):
    steps, length, images, width = cotangent.shape
    group = len(others) + 1
    padded = (length + 7) // 8 * 8
    return pl.pallas_call(
        functools.partial(prepare_kernel, group),
        out_shape=(
            jax.ShapeDtypeStruct((PLACES,), jnp.int32),
            jax.ShapeDtypeStruct((steps * images,), jnp.int32),
            jax.ShapeDtypeStruct((16, width), F32),
            jax.ShapeDtypeStruct((group, steps, padded, width), BF16),
        ),
        grid=(steps,),
        in_specs=[small()] * 4
        + [pl.BlockSpec((1, length, images, width), lambda m: (m, 0, 0, 0))]
        + [small()] * len(others)
        + [whole(*vector.shape) for vector in vectors],
        out_specs=[
            small(),
            small(),
            whole(16, width),
            pl.BlockSpec((group, 1, padded, width), lambda m: (0, m, 0, 0)),
        ],
        compiler_params=params(),
    )(counts, present, slots, me, cotangent, *others, *vectors)


def place(take, got, length):
    group, steps, padded, width = got.shape
    return pl.pallas_call(
        place_kernel,
        out_shape=jax.ShapeDtypeStruct((steps, length, group, width), BF16),
        grid=(steps,),
        in_specs=[small(), pl.BlockSpec((group, 1, padded, width), lambda m: (0, m, 0, 0))],
        out_specs=pl.BlockSpec((1, length, group, width), lambda m: (m, 0, 0, 0)),
        compiler_params=params(),
    )(take, got)


def first_half(meta, slopes, tokens, rows, cols, vecs, weight):
    steps, length, per, width = tokens.shape
    images = steps * per
    tiles = -(-images * ((length + 15) // 16 * 16) // TILE)
    total = tiles * TILE + WINDOW
    spots = pl.BlockSpec(
        (1, per, length),
        lambda s, meta, slopes: (meta[IMG + jnp.maximum(s - steps, 0)] // per, 0, 0),
    )
    return pl.pallas_call(
        attend_kernel,
        out_shape=(
            jax.ShapeDtypeStruct((total, width), BF16),
            jax.ShapeDtypeStruct((total, 3 * width), BF16),
            jax.ShapeDtypeStruct((total, width), BF16),
            jax.ShapeDtypeStruct((images, HEADS // 2, 8, WINDOW), F32),
        ),
        grid_spec=pltpu.PrefetchScalarGridSpec(
            num_scalar_prefetch=2,
            grid=(steps + images,),
            in_specs=[
                pl.BlockSpec(
                    (1, length, per, width),
                    lambda s, meta, slopes: (jnp.minimum(s, steps - 1), 0, 0, 0),
                ),
                spots,
                spots,
                whole(*vecs.shape),
                whole(width, 3 * width),
            ],
            out_specs=[
                pl.BlockSpec(memory_space=pl.ANY),
                pl.BlockSpec(memory_space=pl.ANY),
                pl.BlockSpec(memory_space=pl.ANY),
                pl.BlockSpec(
                    (1, HEADS // 2, 8, WINDOW),
                    lambda s, meta, slopes: (jnp.maximum(s - steps, 0), 0, 0, 0),
                ),
            ],
            scratch_shapes=[
                pltpu.VMEM((total, width), BF16),
                pltpu.VMEM((total, 3 * width), BF16),
                pltpu.VMEM((total, width), BF16),
                pltpu.VMEM((WINDOW, WINDOW), F32),
                pltpu.SemaphoreType.DMA((tiles,)),
                pltpu.SemaphoreType.DMA((tiles,)),
                pltpu.SemaphoreType.DMA((tiles,)),
            ],
        ),
        compiler_params=params(),
        cost_estimate=cost(40),
    )(meta, slopes, tokens, rows, cols, vecs, weight)


def mlp(meta, cot, att, packed, vecs, out_w, up_w, down_w, length):
    group, steps, padded, width = cot.shape
    rows = packed.shape[0]
    tiles = (rows - WINDOW) // TILE
    hidden = up_w.shape[1]
    parcel = (2 * width + hidden // 2 + width // 2) // BLOCKS
    def fwd_tile(s, meta):
        return (jnp.clip(s - steps, 0, meta[N_FWD] - 1), 0)

    def bwd_tile(s, meta):
        return (jnp.clip(s - steps, 0, jnp.maximum(meta[N_BWD] - 1, 0)), 0)

    return pl.pallas_call(
        functools.partial(mlp_kernel, CHUNK, length),
        out_shape=(
            jax.ShapeDtypeStruct(cot.shape, BF16),
            jax.ShapeDtypeStruct((rows, width), F32),
            jax.ShapeDtypeStruct((rows, width), BF16),
            jax.ShapeDtypeStruct((BLOCKS, parcel, width), BF16),
            jax.ShapeDtypeStruct((BLOCKS, parcel, width), BF16),
            jax.ShapeDtypeStruct((8, width), F32),
            jax.ShapeDtypeStruct((8, hidden), F32),
        ),
        grid_spec=pltpu.PrefetchScalarGridSpec(
            num_scalar_prefetch=1,
            grid=(2 * steps + tiles,),
            in_specs=[
                pl.BlockSpec(
                    (group, 1, padded, width), lambda s, meta: (0, jnp.minimum(s, steps - 1), 0, 0)
                ),
                pl.BlockSpec((TILE, width), fwd_tile),
                pl.BlockSpec((TILE, width), fwd_tile),
                whole(*vecs.shape),
                pl.BlockSpec(memory_space=pl.ANY),
                pl.BlockSpec(memory_space=pl.ANY),
                pl.BlockSpec(memory_space=pl.ANY),
            ],
            out_specs=[
                pl.BlockSpec(
                    (group, 1, padded, width),
                    lambda s, meta: (0, jnp.clip(s - steps - tiles, 0, steps - 1), 0, 0),
                ),
                pl.BlockSpec((TILE, width), bwd_tile),
                pl.BlockSpec((TILE, width), bwd_tile),
                pl.BlockSpec(memory_space=pl.ANY),
                pl.BlockSpec(memory_space=pl.ANY),
                whole(8, width),
                whole(8, hidden),
            ],
            scratch_shapes=[
                pltpu.VMEM((8, hidden), F32),
                pltpu.VMEM((rows, width), BF16),
                pltpu.VMEM((width, hidden), F32),
                pltpu.VMEM((width, hidden), F32),
                pltpu.VMEM((width, width), F32),
                pltpu.VMEM((TILE, width), BF16),
                pltpu.VMEM((width, TILE), BF16),
                pltpu.VMEM((width, TILE), BF16),
                pltpu.VMEM((TILE, width), F32),
                pltpu.VMEM((TILE, width), F32),
                pltpu.VMEM((width, width), BF16),
                pltpu.VMEM((width, hidden), BF16),
                pltpu.VMEM((hidden, width), BF16),
                pltpu.SemaphoreType.DMA((2, BLOCKS)),
                pltpu.SemaphoreType.DMA((3,)),
            ],
        ),
        compiler_params=params(),
        cost_estimate=cost(110),
    )(meta, cot, att, packed, vecs, out_w, up_w, down_w)


def attend_back(first, count, expected, meta, slopes, qkv, att_grad, totals, rows_in, cols_in, earlier):
    total, wide = qkv.shape
    width = wide // 3
    per, length = rows_in.shape[1:]

    def spot_of(s, meta):
        return jnp.clip(first + s, 0, jnp.maximum(meta[N_LIVE] - 1, 0))

    def by_offset(s, meta, slopes):
        return (aligned(meta[OFF + spot_of(s, meta)]), 0)

    spots = pl.BlockSpec(
        (1, per, length),
        lambda s, meta, slopes: (meta[IMG + spot_of(s, meta)] // per, 0, 0),
    )
    anywhere = pl.BlockSpec(memory_space=pl.ANY)
    return pl.pallas_call(
        functools.partial(attend_back_kernel, first, per),
        out_shape=jax.ShapeDtypeStruct((total, wide), BF16),
        grid_spec=pltpu.PrefetchScalarGridSpec(
            num_scalar_prefetch=2,
            grid=(count,),
            in_specs=[
                pl.BlockSpec((pl.Element(WINDOW), pl.Element(wide)), by_offset),
                pl.BlockSpec((pl.Element(WINDOW), pl.Element(width)), by_offset),
                pl.BlockSpec(
                    (1, HEADS // 2, 8, WINDOW),
                    lambda s, meta, slopes: (spot_of(s, meta), 0, 0, 0),
                ),
                spots,
                spots,
            ]
            + [anywhere] * len(earlier),
            out_specs=anywhere,
            scratch_shapes=[
                pltpu.VMEM((2, WINDOW, wide), BF16),
                pltpu.VMEM((WINDOW, WINDOW), F32),
                pltpu.SemaphoreType.DMA((2,)),
            ],
        ),
        input_output_aliases={7: 0} if earlier else {},
        compiler_params=params(),
        cost_estimate=cost(expected),
    )(meta, slopes, qkv, att_grad, totals, rows_in, cols_in, *earlier)


def bwd_tile(s, meta):
    return (jnp.clip(s, 0, jnp.maximum(meta[N_BWD] - 1, 0)), 0)


def qkv_grad(meta, packed_grad, packed, vecs):
    rows, width = packed.shape
    parcel = 3 * width // 2 // BLOCKS
    tiles = (rows - WINDOW) // TILE
    return pl.pallas_call(
        qkv_grad_kernel,
        out_shape=(
            jax.ShapeDtypeStruct((BLOCKS, parcel, width), BF16),
            jax.ShapeDtypeStruct((BLOCKS, parcel, width), BF16),
            jax.ShapeDtypeStruct((8, 3 * width), F32),
        ),
        grid_spec=pltpu.PrefetchScalarGridSpec(
            num_scalar_prefetch=1,
            grid=(tiles,),
            in_specs=[
                pl.BlockSpec((TILE, 3 * width), bwd_tile),
                pl.BlockSpec((TILE, width), bwd_tile),
                whole(*vecs.shape),
            ],
            out_specs=[
                pl.BlockSpec(memory_space=pl.ANY),
                pl.BlockSpec(memory_space=pl.ANY),
                whole(8, 3 * width),
            ],
            scratch_shapes=[
                pltpu.VMEM((width, 3 * width), F32),
                pltpu.VMEM((2, BLOCKS, parcel, width), BF16),
                pltpu.SemaphoreType.DMA((2,)),
            ],
        ),
        compiler_params=params(),
        cost_estimate=cost(15),
    )(meta, packed_grad, packed, vecs)


def token_grad(
    meta, packed_grad, packed, mid_grad, vecs, weight, bias_g, vec_two, upb_g, steps, length, images
):
    rows, width = packed.shape
    tiles = (rows - WINDOW) // TILE
    return pl.pallas_call(
        token_grad_kernel,
        out_shape=(
            jax.ShapeDtypeStruct((steps, length, images, width), F32),
            jax.ShapeDtypeStruct((16, width), F32),
        ),
        grid_spec=pltpu.PrefetchScalarGridSpec(
            num_scalar_prefetch=1,
            grid=(tiles + steps,),
            in_specs=[
                pl.BlockSpec((TILE, 3 * width), bwd_tile),
                pl.BlockSpec((TILE, width), bwd_tile),
                pl.BlockSpec((TILE, width), bwd_tile),
                whole(*vecs.shape),
                whole(width, 3 * width),
                whole(*bias_g.shape),
                whole(*vec_two.shape),
                whole(*upb_g.shape),
            ],
            out_specs=[
                pl.BlockSpec(
                    (1, length, images, width),
                    lambda s, meta: (jnp.clip(s - tiles, 0, steps - 1), 0, 0, 0),
                ),
                whole(16, width),
            ],
            scratch_shapes=[pltpu.VMEM((rows, width), F32)],
        ),
        compiler_params=params(),
        cost_estimate=cost(20),
    )(meta, packed_grad, packed, mid_grad, vecs, weight, bias_g, vec_two, upb_g)


def cost(microseconds):
    return pl.CostEstimate(
        flops=int(microseconds * 1e9), bytes_accessed=int(microseconds * 1e5), transcendentals=0
    )


def swap(block, axis, bit):
    size = lax.axis_size(axis)
    return lax.ppermute(block, axis, [(n, n ^ bit) for n in range(size)])


def bit_of(axis, bit):
    return lax.axis_index(axis) // bit % 2


def added(a, b):
    return (a.astype(F32) + b.astype(F32)).astype(BF16)


def unpacked(mine, other, shapes):
    swapped = bit_of("bal", 1) == 1
    first = jnp.where(swapped, other, mine)
    second = jnp.where(swapped, mine, other)
    lead, width = mine.shape[:-2], mine.shape[-1]
    out, at = [], 0
    for rows, columns, kind in shapes:
        wide = columns // width
        part = rows * wide // 2
        held = [half[..., at : at + part, :] for half in (first, second)]
        if kind == "rows":
            size = rows // 2
            parts = [
                jnp.concatenate(
                    [half[..., c * size : (c + 1) * size, :] for c in range(wide)], axis=-1
                )
                for half in held
            ]
            out.append(jnp.concatenate(parts, axis=-2))
        elif kind == "columns":
            parts = [
                half[..., c * rows : (c + 1) * rows, :] for half in held for c in range(wide // 2)
            ]
            out.append(jnp.concatenate(parts, axis=-1))
        else:
            size = width // 2
            tops = [half[..., :size] for half in held]
            bottoms = [half[..., size:] for half in held]
            out.append(
                jnp.concatenate(
                    [jnp.concatenate(tops, axis=-1), jnp.concatenate(bottoms, axis=-1)], axis=-2
                )
            )
        at += part
    return [matrix.reshape(lead[:-1] + (-1, matrix.shape[-1])) if lead else matrix for matrix in out]


def spread_sum(keep, send, shapes):
    return [
        lax.psum(lax.psum_scatter(matrix, "dp", scatter_dimension=0, tiled=True), "bal").astype(F32)
        for matrix in unpacked(keep, send, shapes)
    ]


def start_fold(block, bit):
    block = block.reshape((-1, 2) + block.shape[-2:])
    mine = bit_of("dp", bit)
    keep = lax.dynamic_index_in_dim(block, mine, 1, keepdims=False)
    send = lax.dynamic_index_in_dim(block, 1 - mine, 1, keepdims=False)
    return keep, swap(send, "dp", bit)


def after(value, *others):
    return lax.optimization_barrier((value,) + others)[0]


def doubled(block, round_no):
    bits = [("bal", 1), ("bal", 2)]
    bit = 1
    while bit < lax.axis_size("dp"):
        bits.append(("dp", bit))
        bit *= 2
    if round_no is None:
        return len(bits)
    axis, bit = bits[round_no]
    return block + swap(block, axis, bit)


def per_device(
    tokens,
    cotangent,
    counts,
    rows,
    cols,
    present,
    slots,
    first_gain,
    first_shift,
    qkv_weight,
    query_bias,
    value_bias,
    out_weight,
    out_bias,
    second_gain,
    second_shift,
    up_weight,
    up_bias,
    down_weight,
    down_bias,
):
    steps, images, length, width = tokens.shape
    hidden = up_weight.shape[1]
    group = lax.axis_size("bal")
    total = steps * images
    slopes = jnp.exp2(-8.0 * (jnp.arange(16, dtype=F32) + 1.0) / HEADS)

    def exchange(blocks):
        flat = blocks.reshape(group, -1, width)
        return lax.all_to_all(flat, "bal", split_axis=0, concat_axis=0, tiled=True)

    def turn(array):
        return jnp.transpose(array, (0, 2, 1, 3))

    meta, take, vecs, cot_send = prepare(
        [
            lax.ppermute(slots, "bal", [(a, (a + k) % group) for a in range(group)])
            for k in range(1, group)
        ],
        counts, present, slots,
        lax.axis_index("bal").astype(jnp.int32).reshape(1), turn(cotangent),
        first_gain, first_shift, query_bias, value_bias, out_bias, second_gain, second_shift,
        down_bias, up_bias,
    )
    cot_home = exchange(cot_send).reshape(group, steps, -1, width)
    packed, qkv, att, totals = first_half(meta, slopes, turn(tokens), rows, cols, vecs, qkv_weight)
    y_send, mid_grad, att_grad, keep_two, send_two, vec_two, upb_g = mlp(
        meta, cot_home, att, packed, vecs, out_weight, up_weight, down_weight, length
    )
    share, long = width // BLOCKS, hidden // BLOCKS
    shapes_two = ((share, hidden, "columns"), (long, width, "side"), (share, width, "rows"))
    shapes_one = ((share, 3 * width, "rows"),)
    direct = lax.axis_size("dp") == BLOCKS

    def back(first, count, expected, table, earlier):
        return attend_back(
            first, count, expected, table, slopes, qkv, att_grad, totals, rows, cols, earlier
        )

    lead = max(images // 2, 1)
    packed_grad = back(0, lead, 15, meta, ())
    table = meta
    if direct:
        sum_two = added(after(keep_two, packed_grad), swap(send_two, "bal", 1))
        share_two = lax.psum_scatter(sum_two, "dp", scatter_dimension=0, tiled=True)[0]
        table = after(meta, sum_two)
        y_send = after(y_send, sum_two)
    y_got = exchange(y_send)
    packed_grad = back(lead, total - lead, 500, table, (packed_grad,))
    keep_one, send_one, bias_g = qkv_grad(table, packed_grad, packed, vecs)
    output = place(after(take, keep_one), y_got.reshape(group, steps, -1, width), length)
    table = after(table, output)
    if direct:
        sum_one = added(keep_one, swap(send_one, "bal", 1))
        keep_y, crossing_y = start_fold(sum_one, 1)
        table = after(table, sum_one)
    input_grad, vectors = token_grad(
        table, packed_grad, packed, mid_grad, vecs, qkv_weight, bias_g, vec_two, upb_g,
        steps, length, images,
    )
    rounds = doubled(vectors, None)
    if direct:
        half_one = added(after(keep_y, vectors), crossing_y)
        keep, crossing = start_fold(half_one, 2)
        for n in range(rounds - 2):
            vectors = doubled(vectors, n)
        block = added(after(keep, vectors), crossing)
        keep, crossing = start_fold(block, 4)
        across_two = swap(share_two, "bal", 2)
        vectors = doubled(after(vectors, block, share_two), rounds - 2)
        block = added(after(keep, vectors), crossing).reshape(sum_one.shape[-2:])
        across_one = swap(block, "bal", 2)
        vectors = doubled(after(vectors, block), rounds - 1)
        full_one = added(after(block, vectors), across_one)
        full_two = added(after(share_two, full_one), across_two)
        (qkv_rows,) = [
            matrix.astype(F32)
            for matrix in unpacked(full_one, swap(full_one, "bal", 1), shapes_one)
        ]
        up_rows, down_rows, out_rows = [
            matrix.astype(F32)
            for matrix in unpacked(full_two, swap(full_two, "bal", 1), shapes_two)
        ]
    else:
        (qkv_rows,) = spread_sum(keep_one, send_one, shapes_one)
        up_rows, down_rows, out_rows = spread_sum(keep_two, send_two, shapes_two)
        for n in range(rounds):
            vectors = doubled(vectors, n)

    def vector(n):
        return vectors[n]

    return (
        turn(output),
        turn(input_grad),
        vector(0),
        vector(1),
        qkv_rows,
        vector(2),
        vector(3),
        out_rows,
        vector(6),
        vector(4),
        vector(5),
        up_rows,
        vectors[8 : 8 + hidden // width].reshape(-1),
        down_rows,
        vector(7),
    )


def solution(mesh):
    images = P(None, ("dp", "bal"), None, None)
    spots = P(None, ("dp", "bal"), None)
    flags = P(None, ("dp", "bal"))
    matrix = P("dp", None)
    return jax.shard_map(
        per_device,
        mesh=mesh,
        in_specs=(images, images, flags, spots, spots, flags, flags) + (P(),) * 13,
        out_specs=(
            images, images, P(), P(), matrix, P(), P(), matrix, P(), P(), P(), matrix, P(), matrix, P(),
        ),
        check_vma=False,
    )
```

```python
import functools
import math

import jax
import jax.numpy as jnp
from jax import lax
from jax.experimental import pallas as pl
from jax.experimental.pallas import tpu as pltpu
from jax.sharding import PartitionSpec as P

HEADS = 12
TILE = 256
WINDOW = 256
FAR = 1e12
EPS = 1e-06
BLOCKS = 8
CHUNK = 1024
VMEM_LIMIT = 60 * 1024 * 1024

F32 = jnp.float32
BF16 = jnp.bfloat16

OFF, CNT, IMG, LIVE, PEER, SPOT, MISC = 0, 16, 32, 48, 64, 80, 96
N_FWD, N_BWD, ROWS_FWD, ROWS_BWD, N_LIVE, CORE = range(MISC, MISC + 6)
PLACES = 128

GAIN_ONE, SHIFT_ONE, QKV_B, OUT_B, GAIN_TWO, SHIFT_TWO, DOWN_B, UP_B = 0, 1, 2, 5, 6, 7, 8, 9
VECTORS = (GAIN_ONE, SHIFT_ONE, QKV_B, QKV_B + 2, OUT_B, GAIN_TWO, SHIFT_TWO, DOWN_B, UP_B)


def dot(a, b):
    return jnp.dot(a, b, preferred_element_type=F32)


def dot_bt(a, b):
    return lax.dot_general(a, b, (((1,), (1,)), ((), ())), preferred_element_type=F32)


def turned(block):
    return block.astype(F32).T.astype(BF16)


def layer_norm(values):
    average = jnp.mean(values, axis=-1, keepdims=True)
    centred = values - average
    spread = jnp.mean(centred * centred, axis=-1, keepdims=True)
    inverse = lax.rsqrt(spread + EPS)
    return centred * inverse, inverse


def norm_back(out_grad, gain, unit, inverse):
    e = out_grad * gain
    mean_e = jnp.mean(e, axis=-1, keepdims=True)
    mean_eu = jnp.mean(e * unit, axis=-1, keepdims=True)
    return inverse * (e - mean_e - unit * mean_eu)


def gelu_parts(u):
    size = jnp.abs(u)
    t = 1.0 / (1.0 + (0.3275911 * math.sqrt(0.5)) * size)
    bell = jnp.exp2((-0.5 * math.log2(math.e)) * (u * u))
    poly = t * (
        0.5 * 0.254829592
        + t
        * (
            0.5 * -0.284496736
            + t * (0.5 * 1.421413741 + t * (0.5 * -1.453152027 + t * (0.5 * 1.061405429)))
        )
    )
    tail = poly * bell
    phi_sum = jnp.where(u >= 0, 1.0 - tail, tail)
    return phi_sum, u * bell * (1.0 / math.sqrt(2.0 * math.pi))


def put_rows(packed, off, count, block):
    rows = (block.shape[0] + 15) // 16 * 16
    if rows > block.shape[0]:
        more = jnp.zeros((rows - block.shape[0], block.shape[1]), block.dtype)
        block = jnp.concatenate([block, more], axis=0)
    ids = row_ids(0, rows)
    window = pl.ds(off, rows)
    block = jnp.where(ids < count, block, jnp.zeros_like(block))
    packed[window, :] = jnp.where(ids < (count + 15) // 16 * 16, block, packed[window, :])


def row_ids(start, rows):
    return start + lax.broadcasted_iota(jnp.int32, (rows, 1), 0)


def aligned(value, step=16):
    return pl.multiple_of(value, step)


def by_count(count, run):
    @pl.when(count <= 128)
    def _():
        run(128, 128)

    @pl.when(jnp.logical_and(count > 128, count <= 192))
    def _():
        run(192, 256)

    @pl.when(count > 192)
    def _():
        run(256, 256)


def distances(rows, cols, which, count, keys, queries):
    mine = lax.broadcasted_iota(jnp.int32, rows.shape, 0) == which
    row = jnp.sum(jnp.where(mine, rows, 0).astype(F32), axis=0, keepdims=True)
    col = jnp.sum(jnp.where(mine, cols, 0).astype(F32), axis=0, keepdims=True)
    spots = jnp.concatenate([row, col, jnp.zeros((6, row.shape[1]), F32)], axis=0)
    spots = jnp.concatenate([spots, jnp.zeros((8, WINDOW - row.shape[1]), F32)], axis=1)
    eye = jnp.where(
        lax.broadcasted_iota(jnp.int32, (keys, WINDOW), 0)
        == lax.broadcasted_iota(jnp.int32, (keys, WINDOW), 1),
        1.0,
        0.0,
    ).astype(BF16)
    turned_spots = dot_bt(eye, spots.astype(BF16))
    down = turned_spots[:, 0:1] - spots[0:1, :queries]
    across = turned_spots[:, 1:2] - spots[1:2, :queries]
    far = row_ids(0, keys) >= count
    return jnp.where(far, FAR, jnp.sqrt(down * down + across * across))


def prepare_kernel(group, counts, present, slots, me, cot, *rest):
    *rest, meta, take, vecs, send = rest
    every, lines = (slots,) + tuple(rest[: group - 1]), rest[group - 1 :]
    step = pl.program_id(0)
    steps, length, images, width = pl.num_programs(0), cot.shape[1], cot.shape[2], cot.shape[3]
    @pl.when(step == 0)
    def _():
        def fill(live):
            def body(img, carry):
                spot, off = carry
                m, i = img // images, img % images
                count = counts[m, i]
                mine = present[m, i] == live

                @pl.when(mine)
                def _():
                    meta[OFF + spot] = off
                    meta[CNT + spot] = count
                    meta[IMG + spot] = img
                    meta[LIVE + spot] = live
                    meta[PEER + spot] = slots[m, i] // images * steps + m
                    meta[SPOT + img] = spot

                padded = (count + 15) // 16 * 16
                return spot + mine.astype(jnp.int32), off + jnp.where(mine, padded, 0)

            return body

        meta[CORE] = me[0] % 2
        vecs[...] = jnp.zeros_like(vecs)
        for row, values in zip(VECTORS, lines):
            for n in range(values.shape[0] // width):
                piece = values[n * width : (n + 1) * width]
                vecs[row + n : row + n + 1, :] = piece.reshape(1, width)
        zero = jnp.int32(0)
        total = counts.shape[0] * images
        spot, off = lax.fori_loop(0, total, fill(1), (zero, zero))
        meta[N_LIVE] = spot
        meta[ROWS_BWD] = off
        meta[N_BWD] = (off + TILE - 1) // TILE
        spot, off = lax.fori_loop(0, total, fill(0), (spot, off))
        meta[ROWS_FWD] = off
        meta[N_FWD] = (off + TILE - 1) // TILE

        for back, theirs in enumerate(every):
            a = (me[0] + group - back) % group

            def land(n, carry):
                m, i = n // images, n % images
                slot = theirs[m, i]

                @pl.when(slot // images == me[0])
                def _():
                    take[m * images + slot % images] = a * steps + m

                return carry

            lax.fori_loop(0, total, land, 0)

    block = jnp.swapaxes(cot[0].astype(F32), 0, 1).astype(BF16)
    for place in range(images):
        peer = take[step * images + place] // steps
        send[peer, 0, :length, :] = block[place]


def place_kernel(take, got, out):
    step = pl.program_id(0)
    length, images = out.shape[1], out.shape[2]
    steps = pl.num_programs(0)
    parts = [
        got[take[step * images + place] // steps, 0, :length, :].astype(F32)
        for place in range(images)
    ]
    out[0] = jnp.swapaxes(jnp.stack(parts, axis=0), 0, 1).astype(out.dtype)


def attend_kernel(
    meta, slopes, tokens, rows_in, cols_in, vecs, weight,
    packed_out, qkv_out, att_out, total_out,
    packed, qkv, att, gaps, sem_packed, sem_qkv, sem_att,
):
    length, per, width = tokens.shape[1], tokens.shape[2], tokens.shape[3]
    steps = pl.num_programs(0) // (per + 1)
    images = steps * per
    now = pl.program_id(0)

    def tile_copy(which, t):
        src, dst, sem = (
            (packed, packed_out, sem_packed),
            (qkv, qkv_out, sem_qkv),
            (att, att_out, sem_att),
        )[which]
        rows = pl.ds(aligned(t * TILE, TILE), TILE)
        return pltpu.make_async_copy(src.at[rows], dst.at[rows], sem.at[t])

    @pl.when(now == 0)
    def _():
        packed[...] = jnp.zeros_like(packed)

    @pl.when(now < steps)
    def _():
        block = jnp.swapaxes(tokens[0].astype(F32), 0, 1).astype(BF16)
        for i in range(per):
            spot = meta[SPOT + now * per + i]
            put_rows(packed, aligned(meta[OFF + spot]), meta[CNT + spot], block[i])

    @pl.when(now == steps - 1)
    def _():

        def project(t, carry):
            rows = pl.ds(aligned(t * TILE, TILE), TILE)
            unit, _ = layer_norm(packed[rows, :].astype(F32))
            hidden = (
                unit * vecs[GAIN_ONE : GAIN_ONE + 1] + vecs[SHIFT_ONE : SHIFT_ONE + 1]
            ).astype(BF16)
            for part in range(3):
                cols = slice(part * width, (part + 1) * width)
                bias = vecs[QKV_B + part : QKV_B + part + 1]
                qkv[rows, cols] = (dot(hidden, weight[:, cols]) + bias).astype(BF16)
            tile_copy(0, t).start()
            tile_copy(1, t).start()
            return carry

        lax.fori_loop(0, meta[N_FWD], project, 0)

    @pl.when(now >= steps)
    def _():
        spot = now - steps
        off = aligned(meta[OFF + spot])
        count = meta[CNT + spot]

        def run(keys, queries):
            which = meta[IMG + spot] % per
            gaps[:keys, :queries] = distances(rows_in[0], cols_in[0], which, count, keys, queries)
            key_seen = row_ids(0, keys) < count
            query_seen = row_ids(0, queries) < count
            left = lax.broadcasted_iota(jnp.int32, (keys, 128), 1) < 64

            def pair(p, carry):
                lanes = aligned(p * 128, 128)
                q2 = qkv[pl.ds(off, queries), pl.ds(lanes, 128)] * 0.125
                k2 = qkv[pl.ds(off, keys), pl.ds(width + lanes, 128)]
                v2 = qkv[pl.ds(off, keys), pl.ds(2 * width + lanes, 128)]
                q2 = jnp.where(query_seen, q2, jnp.zeros_like(q2))
                k2 = jnp.where(key_seen, k2, jnp.zeros_like(k2))
                v2 = jnp.where(key_seen, v2, jnp.zeros_like(v2))
                v2t = v2.astype(F32).T.astype(BF16)
                raw = dot_bt(by_head(k2, left), q2)
                outs = []
                for half in range(2):
                    head = 2 * p + half
                    scores = raw[half * keys : (half + 1) * keys]
                    scores = scores - slopes[head] * gaps[:keys, :queries]
                    top = jnp.max(scores, axis=0, keepdims=True)
                    terms = jnp.exp(scores - top)
                    total = jnp.sum(terms, axis=0, keepdims=True)
                    heads_out = dot(v2t[half * 64 : half * 64 + 64], terms.astype(BF16))
                    outs.append(heads_out * (1.0 / total))
                    total_out[0, p, half : half + 1, :queries] = top + jnp.log(total)
                both = jnp.concatenate(outs, axis=0)
                att[pl.ds(off, queries), pl.ds(lanes, 128)] = both.T.astype(BF16)
                return carry

            lax.fori_loop(0, HEADS // 2, pair, 0, unroll=HEADS // 2)

        by_count(count, run)
        after = meta[OFF + jnp.minimum(spot + 1, images - 1)]
        end = jnp.where(spot == images - 1, meta[N_FWD], after // TILE)

        def send(t, carry):
            tile_copy(2, t).start()
            return carry

        lax.fori_loop(off // TILE, end, send, 0)

    @pl.when(now == pl.num_programs(0) - 1)
    def _():
        def finish(t, carry):
            for which in range(3):
                tile_copy(which, t).wait()
            return carry

        lax.fori_loop(0, meta[N_FWD], finish, 0)


def by_head(block, left):
    none = jnp.zeros_like(block)
    return jnp.concatenate([jnp.where(left, block, none), jnp.where(left, none, block)], axis=0)


def mlp_kernel(
    chunk, length, meta, cot_in, att_in, tokens_in,
    vecs, out_hbm, up_hbm, down_hbm,
    y_send, mid_grad, att_grad, keep_g, send_g, vec_g, upb_g,
    up_b, held, up_acc, down_acc, out_acc, h2_s, h2t_s, dzt_s, z_s, g_s,
    out_w, up_w, down_w, sem, sem_w,
):
    step = pl.program_id(0)
    tiles = held.shape[0] // TILE - WINDOW // TILE
    images = (pl.num_programs(0) - tiles) // 2
    per = cot_in.shape[0]
    width = cot_in.shape[3]
    hidden = up_w.shape[1]
    out_b, gain, shift, down_b = [
        vecs.at[pl.ds(n, 1)] for n in (OUT_B, GAIN_TWO, SHIFT_TWO, DOWN_B)
    ]

    def weight_copies():
        pairs = ((out_hbm, out_w), (up_hbm, up_w), (down_hbm, down_w))
        return [pltpu.make_async_copy(a, b, sem_w.at[n]) for n, (a, b) in enumerate(pairs)]

    @pl.when(step == 0)
    def _():
        for copy in weight_copies():
            copy.start()
        up_acc[...] = jnp.zeros_like(up_acc)
        down_acc[...] = jnp.zeros_like(down_acc)
        out_acc[...] = jnp.zeros_like(out_acc)
        vec_g[...] = jnp.zeros_like(vec_g)
        upb_g[...] = jnp.zeros_like(upb_g)
        for n in range(hidden // width):
            up_b[0:1, n * width : (n + 1) * width] = vecs[UP_B + n : UP_B + n + 1, :]

    @pl.when(step < images)
    def _():
        for i in range(per):
            spot = meta[SPOT + step * per + i]

            @pl.when(meta[LIVE + spot] == 1)
            def _():
                put_rows(
                    held, aligned(meta[OFF + spot]), meta[CNT + spot],
                    cot_in[meta[PEER + spot] // images, 0],
                )

    @pl.when(step == images)
    def _():
        for copy in weight_copies():
            copy.wait()

    def run_tile(t, both):
        rows = aligned(t * TILE, TILE)
        ids = row_ids(rows, TILE)
        att = att_in[...]
        att = jnp.where(ids < meta[ROWS_FWD], att, jnp.zeros_like(att))
        mid = tokens_in[...].astype(F32) + (dot(att, out_w[...]) + out_b[...])
        unit, inverse = layer_norm(mid)
        h2 = (unit * gain[...] + shift[...]).astype(BF16)
        h2_s[...] = h2
        z_s[...] = mid + down_b[...]
        if both:
            dz = held[pl.ds(rows, TILE), :]
            dz = jnp.where(ids < meta[ROWS_BWD], dz, jnp.zeros_like(dz))
            h2t_s[...] = turned(h2)
            dzt_s[...] = turned(dz)
            g_s[...] = jnp.zeros_like(g_s)

        def part(c, carry):
            cols = pl.ds(aligned(c * chunk, chunk), chunk)
            pre = dot(h2_s[...], up_w[:, cols]) + up_b[0:1, cols]
            share, slope = gelu_parts(pre)
            act = (pre * share).astype(BF16)
            z_s[...] += dot(act, down_w[cols, :])
            if both:
                pre_g = (dot_bt(dz, down_w[cols, :]) * (share + slope)).astype(BF16)
                up_acc[:, cols] += dot(h2t_s[...], pre_g)
                down_acc[:, cols] += dot(dzt_s[...], act)
                upb_g[0:1, cols] += jnp.sum(pre_g.astype(F32), axis=0, keepdims=True)
                g_s[...] += dot_bt(pre_g, up_w[:, cols])
            return carry

        lax.fori_loop(0, hidden // chunk, part, 0, unroll=True)
        held[pl.ds(rows, TILE), :] = z_s[...].astype(BF16)
        if both:
            dzf = dz.astype(F32)
            g2 = g_s[...]
            dmid = dzf + norm_back(g2, gain[...], unit, inverse)
            branch = dmid.astype(BF16)
            mid_grad[...] = dmid
            att_grad[...] = dot_bt(branch, out_w[...]).astype(BF16)
            out_acc[...] += dot(turned(att), branch)
            vec_g[0:1, :] += jnp.sum(g2 * unit, axis=0, keepdims=True)
            vec_g[1:2, :] += jnp.sum(g2, axis=0, keepdims=True)
            vec_g[2:3, :] += jnp.sum(branch.astype(F32), axis=0, keepdims=True)
            vec_g[3:4, :] += jnp.sum(dzf, axis=0, keepdims=True)

    tile = step - images

    @pl.when(jnp.logical_and(tile >= 0, tile < meta[N_BWD]))
    def _():
        run_tile(tile, True)

    @pl.when(
        jnp.logical_and(
            jnp.logical_and(tile >= meta[N_BWD], tile >= 0),
            jnp.logical_and(tile < meta[N_FWD], tile < tiles),
        )
    )
    def _():
        run_tile(tile, False)

    turn = step - images - tiles

    @pl.when(turn >= 0)
    def _():
        for i in range(per):
            spot = meta[SPOT + turn * per + i]
            block = held[pl.ds(aligned(meta[OFF + spot]), length), :]
            seen = row_ids(0, length) < meta[CNT + spot]
            y_send[meta[PEER + spot] // images, 0, :length, :] = jnp.where(
                seen, block, jnp.zeros_like(block)
            )

    @pl.when(step == pl.num_programs(0) - 1)
    def _():
        share = width // BLOCKS
        long = hidden // BLOCKS
        size = 2 * share + long // 2 + share // 2
        for turn, target in enumerate((send_g, keep_g)):
            h = meta[CORE] if turn else 1 - meta[CORE]
            side = aligned(h * (width // 2), 128)
            copies = []
            for n in range(BLOCKS):
                base = n * size
                if turn:
                    earlier[n].wait()
                for c in range(2):
                    cols = pl.ds(aligned((2 * h + c) * width, 128), width)
                    piece = up_acc[n * share : (n + 1) * share, cols]
                    held[base + c * share : base + (c + 1) * share, :] = piece.astype(BF16)
                base += 2 * share
                piece = down_acc[pl.ds(side, width // 2), n * long : (n + 1) * long]
                flipped = turned(piece.astype(BF16))
                held[base : base + long // 2, : width // 2] = flipped[: long // 2]
                held[base : base + long // 2, width // 2 :] = flipped[long // 2 :]
                base += long // 2
                rows = pl.ds(pl.multiple_of(n * share + h * (share // 2), 8), share // 2)
                held[base : base + share // 2, :] = out_acc[rows, :].astype(BF16)
                copy = pltpu.make_async_copy(
                    held.at[pl.ds(n * size, size)], target.at[n], sem.at[turn, n]
                )
                copy.start()
                copies.append(copy)
            earlier = copies
        for copy in earlier:
            copy.wait()


def attend_back_kernel(
    first, per, meta, slopes, qkv, att_grad, totals, rows_in, cols_in, *rest
):
    grads_out, grads, gaps, sem = rest[-4:]
    step = pl.program_id(0)
    width = att_grad.shape[1]
    spot = first + step
    live = spot < meta[N_LIVE]
    slot = step % 2

    def copy(at):
        rows = pl.ds(aligned(meta[OFF + first + at]), WINDOW)
        return pltpu.make_async_copy(grads.at[at % 2], grads_out.at[rows], sem.at[at % 2])

    @pl.when(live)
    def _():
        count = meta[CNT + spot]

        def run(keys, queries):
            which = meta[IMG + spot] % per
            gaps[:keys, :queries] = distances(rows_in[0], cols_in[0], which, count, keys, queries)
            key_seen = row_ids(0, keys) < count
            query_seen = row_ids(0, queries) < count
            left = lax.broadcasted_iota(jnp.int32, (keys, 128), 1) < 64

            def pair(p, carry):
                lanes = aligned(p * 128, 128)
                q2 = qkv[:queries, pl.ds(lanes, 128)] * 0.125
                k2 = qkv[:keys, pl.ds(width + lanes, 128)]
                v2 = qkv[:keys, pl.ds(2 * width + lanes, 128)]
                o2 = att_grad[:queries, pl.ds(lanes, 128)]
                q2 = jnp.where(query_seen, q2, jnp.zeros_like(q2))
                o2 = jnp.where(query_seen, o2, jnp.zeros_like(o2))
                k2 = jnp.where(key_seen, k2, jnp.zeros_like(k2))
                v2 = jnp.where(key_seen, v2, jnp.zeros_like(v2))
                k2t = k2.astype(F32).T.astype(BF16)
                raw = dot_bt(by_head(k2, left), q2)
                raw_g = dot_bt(by_head(v2, left), o2)
                dq_parts, probs_low, score_low = [], [], []
                for half in range(2):
                    head = 2 * p + half
                    rows = slice(half * keys, (half + 1) * keys)
                    scores = raw[rows] - slopes[head] * gaps[:keys, :queries]
                    probs = jnp.exp(scores - totals[0, p, half : half + 1, :queries])
                    prob_g = raw_g[rows]
                    inner = jnp.sum(probs * prob_g, axis=0, keepdims=True)
                    score_g = (probs * (prob_g - inner)).astype(BF16)
                    dq_parts.append(dot(k2t[half * 64 : half * 64 + 64], score_g) * 0.125)
                    probs_low.append(probs.astype(BF16))
                    score_low.append(score_g)
                dv = dot(jnp.concatenate(probs_low, axis=0), o2)
                dk = dot(jnp.concatenate(score_low, axis=0), q2)
                dv = jnp.where(left, dv[:keys], dv[keys:])
                dk = jnp.where(left, dk[:keys], dk[keys:])
                dq = jnp.concatenate(dq_parts, axis=0).T.astype(BF16)
                grads[slot, :queries, pl.ds(lanes, 128)] = dq
                grads[slot, :keys, pl.ds(width + lanes, 128)] = dk.astype(BF16)
                grads[slot, :keys, pl.ds(2 * width + lanes, 128)] = dv.astype(BF16)
                return carry

            lax.fori_loop(0, HEADS // 2, pair, 0, unroll=HEADS // 2)

        by_count(count, run)

        @pl.when(step > 0)
        def _():
            copy(step - 1).wait()

        copy(step).start()

        @pl.when(jnp.logical_or(step == pl.num_programs(0) - 1, spot == meta[N_LIVE] - 1))
        def _():
            copy(step).wait()


def qkv_grad_kernel(meta, packed_grad, tokens, vecs, keep_g, send_g, bias_g, acc, stage, sem):
    tile = pl.program_id(0)
    width = tokens.shape[1]

    @pl.when(tile == 0)
    def _():
        acc[...] = jnp.zeros_like(acc)
        bias_g[...] = jnp.zeros_like(bias_g)

    @pl.when(tile < meta[N_BWD])
    def _():
        ids = row_ids(tile * TILE, TILE)
        unit, _ = layer_norm(tokens[...].astype(F32))
        hidden = (
            unit * vecs[GAIN_ONE : GAIN_ONE + 1] + vecs[SHIFT_ONE : SHIFT_ONE + 1]
        ).astype(BF16)
        hidden_t = turned(hidden)
        for part in range(3):
            cols = slice(part * width, (part + 1) * width)
            block = packed_grad[:, cols]
            block = jnp.where(ids < meta[ROWS_BWD], block, jnp.zeros_like(block))
            acc[:, cols] += dot(hidden_t, block)
            bias_g[0:1, cols] += jnp.sum(block.astype(F32), axis=0, keepdims=True)

    @pl.when(tile == pl.num_programs(0) - 1)
    def _():
        rows = width // BLOCKS // 2
        for block in range(BLOCKS):
            for h in range(2):
                for c in range(3):
                    first = (2 * block + h) * rows
                    piece = acc[first : first + rows, c * width : (c + 1) * width]
                    stage[h, block, c * rows : (c + 1) * rows, :] = piece.astype(BF16)
        mine = meta[CORE]
        keep = pltpu.make_async_copy(stage.at[mine], keep_g, sem.at[0])
        send = pltpu.make_async_copy(stage.at[1 - mine], send_g, sem.at[1])
        keep.start()
        send.start()
        keep.wait()
        send.wait()


def token_grad_kernel(
    meta, packed_grad, tokens, mid_grad, vecs, weight, bias_g, vec_two, upb_g, out, vec_g, held
):
    step = pl.program_id(0)
    tiles = held.shape[0] // TILE - WINDOW // TILE
    length, images = out.shape[1], out.shape[2]

    @pl.when(step == 0)
    def _():
        width = vec_g.shape[1]
        vec_g[...] = jnp.zeros_like(vec_g)
        vec_g[2:3, :] = bias_g[0:1, :width]
        vec_g[3:4, :] = bias_g[0:1, 2 * width :]
        vec_g[4:8, :] = vec_two[0:4, :]
        for n in range(upb_g.shape[1] // width):
            vec_g[8 + n : 9 + n, :] = upb_g[0:1, n * width : (n + 1) * width]

    @pl.when(jnp.logical_and(step < tiles, step < meta[N_BWD]))
    def _():
        rows = aligned(step * TILE, TILE)
        ids = row_ids(rows, TILE)
        unit, inverse = layer_norm(tokens[...].astype(F32))
        block = packed_grad[...]
        block = jnp.where(ids < meta[ROWS_BWD], block, jnp.zeros_like(block))
        g1 = dot_bt(block, weight[...])
        back = norm_back(g1, vecs[GAIN_ONE : GAIN_ONE + 1], unit, inverse)
        held[pl.ds(rows, TILE), :] = mid_grad[...] + back
        vec_g[0:1, :] += jnp.sum(g1 * unit, axis=0, keepdims=True)
        vec_g[1:2, :] += jnp.sum(g1, axis=0, keepdims=True)

    @pl.when(step >= tiles)
    def _():
        parts = []
        for i in range(images):
            spot = meta[SPOT + (step - tiles) * images + i]
            off = aligned(meta[OFF + spot])
            limit = meta[CNT + spot] * meta[LIVE + spot]
            block = held[pl.ds(off, length), :]
            parts.append(jnp.where(row_ids(0, length) < limit, block, 0.0))
        out[0] = jnp.swapaxes(jnp.stack(parts, axis=0), 0, 1)


def whole(*shape):
    return pl.BlockSpec(shape, lambda *_: (0,) * len(shape), pipeline_mode=pl.Buffered(1))


def params():
    return pltpu.CompilerParams(vmem_limit_bytes=VMEM_LIMIT)


def small():
    return pl.BlockSpec(memory_space=pltpu.SMEM)


def prepare(others, counts, present, slots, me, cotangent, *vectors):
    steps, length, images, width = cotangent.shape
    group = len(others) + 1
    padded = (length + 7) // 8 * 8
    return pl.pallas_call(
        functools.partial(prepare_kernel, group),
        out_shape=(
            jax.ShapeDtypeStruct((PLACES,), jnp.int32),
            jax.ShapeDtypeStruct((steps * images,), jnp.int32),
            jax.ShapeDtypeStruct((16, width), F32),
            jax.ShapeDtypeStruct((group, steps, padded, width), BF16),
        ),
        grid=(steps,),
        in_specs=[small()] * 4
        + [pl.BlockSpec((1, length, images, width), lambda m: (m, 0, 0, 0))]
        + [small()] * len(others)
        + [whole(*vector.shape) for vector in vectors],
        out_specs=[
            small(),
            small(),
            whole(16, width),
            pl.BlockSpec((group, 1, padded, width), lambda m: (0, m, 0, 0)),
        ],
        compiler_params=params(),
    )(counts, present, slots, me, cotangent, *others, *vectors)


def place(take, got, length):
    group, steps, padded, width = got.shape
    return pl.pallas_call(
        place_kernel,
        out_shape=jax.ShapeDtypeStruct((steps, length, group, width), BF16),
        grid=(steps,),
        in_specs=[small(), pl.BlockSpec((group, 1, padded, width), lambda m: (0, m, 0, 0))],
        out_specs=pl.BlockSpec((1, length, group, width), lambda m: (m, 0, 0, 0)),
        compiler_params=params(),
    )(take, got)


def first_half(meta, slopes, tokens, rows, cols, vecs, weight):
    steps, length, per, width = tokens.shape
    images = steps * per
    tiles = -(-images * ((length + 15) // 16 * 16) // TILE)
    total = tiles * TILE + WINDOW
    spots = pl.BlockSpec(
        (1, per, length),
        lambda s, meta, slopes: (meta[IMG + jnp.maximum(s - steps, 0)] // per, 0, 0),
    )
    return pl.pallas_call(
        attend_kernel,
        out_shape=(
            jax.ShapeDtypeStruct((total, width), BF16),
            jax.ShapeDtypeStruct((total, 3 * width), BF16),
            jax.ShapeDtypeStruct((total, width), BF16),
            jax.ShapeDtypeStruct((images, HEADS // 2, 8, WINDOW), F32),
        ),
        grid_spec=pltpu.PrefetchScalarGridSpec(
            num_scalar_prefetch=2,
            grid=(steps + images,),
            in_specs=[
                pl.BlockSpec(
                    (1, length, per, width),
                    lambda s, meta, slopes: (jnp.minimum(s, steps - 1), 0, 0, 0),
                ),
                spots,
                spots,
                whole(*vecs.shape),
                whole(width, 3 * width),
            ],
            out_specs=[
                pl.BlockSpec(memory_space=pl.ANY),
                pl.BlockSpec(memory_space=pl.ANY),
                pl.BlockSpec(memory_space=pl.ANY),
                pl.BlockSpec(
                    (1, HEADS // 2, 8, WINDOW),
                    lambda s, meta, slopes: (jnp.maximum(s - steps, 0), 0, 0, 0),
                ),
            ],
            scratch_shapes=[
                pltpu.VMEM((total, width), BF16),
                pltpu.VMEM((total, 3 * width), BF16),
                pltpu.VMEM((total, width), BF16),
                pltpu.VMEM((WINDOW, WINDOW), F32),
                pltpu.SemaphoreType.DMA((tiles,)),
                pltpu.SemaphoreType.DMA((tiles,)),
                pltpu.SemaphoreType.DMA((tiles,)),
            ],
        ),
        compiler_params=params(),
        cost_estimate=cost(40),
    )(meta, slopes, tokens, rows, cols, vecs, weight)


def mlp(meta, cot, att, packed, vecs, out_w, up_w, down_w, length):
    group, steps, padded, width = cot.shape
    rows = packed.shape[0]
    tiles = (rows - WINDOW) // TILE
    hidden = up_w.shape[1]
    parcel = (2 * width + hidden // 2 + width // 2) // BLOCKS
    def fwd_tile(s, meta):
        return (jnp.clip(s - steps, 0, meta[N_FWD] - 1), 0)

    def bwd_tile(s, meta):
        return (jnp.clip(s - steps, 0, jnp.maximum(meta[N_BWD] - 1, 0)), 0)

    return pl.pallas_call(
        functools.partial(mlp_kernel, CHUNK, length),
        out_shape=(
            jax.ShapeDtypeStruct(cot.shape, BF16),
            jax.ShapeDtypeStruct((rows, width), F32),
            jax.ShapeDtypeStruct((rows, width), BF16),
            jax.ShapeDtypeStruct((BLOCKS, parcel, width), BF16),
            jax.ShapeDtypeStruct((BLOCKS, parcel, width), BF16),
            jax.ShapeDtypeStruct((8, width), F32),
            jax.ShapeDtypeStruct((8, hidden), F32),
        ),
        grid_spec=pltpu.PrefetchScalarGridSpec(
            num_scalar_prefetch=1,
            grid=(2 * steps + tiles,),
            in_specs=[
                pl.BlockSpec(
                    (group, 1, padded, width), lambda s, meta: (0, jnp.minimum(s, steps - 1), 0, 0)
                ),
                pl.BlockSpec((TILE, width), fwd_tile),
                pl.BlockSpec((TILE, width), fwd_tile),
                whole(*vecs.shape),
                pl.BlockSpec(memory_space=pl.ANY),
                pl.BlockSpec(memory_space=pl.ANY),
                pl.BlockSpec(memory_space=pl.ANY),
            ],
            out_specs=[
                pl.BlockSpec(
                    (group, 1, padded, width),
                    lambda s, meta: (0, jnp.clip(s - steps - tiles, 0, steps - 1), 0, 0),
                ),
                pl.BlockSpec((TILE, width), bwd_tile),
                pl.BlockSpec((TILE, width), bwd_tile),
                pl.BlockSpec(memory_space=pl.ANY),
                pl.BlockSpec(memory_space=pl.ANY),
                whole(8, width),
                whole(8, hidden),
            ],
            scratch_shapes=[
                pltpu.VMEM((8, hidden), F32),
                pltpu.VMEM((rows, width), BF16),
                pltpu.VMEM((width, hidden), F32),
                pltpu.VMEM((width, hidden), F32),
                pltpu.VMEM((width, width), F32),
                pltpu.VMEM((TILE, width), BF16),
                pltpu.VMEM((width, TILE), BF16),
                pltpu.VMEM((width, TILE), BF16),
                pltpu.VMEM((TILE, width), F32),
                pltpu.VMEM((TILE, width), F32),
                pltpu.VMEM((width, width), BF16),
                pltpu.VMEM((width, hidden), BF16),
                pltpu.VMEM((hidden, width), BF16),
                pltpu.SemaphoreType.DMA((2, BLOCKS)),
                pltpu.SemaphoreType.DMA((3,)),
            ],
        ),
        compiler_params=params(),
        cost_estimate=cost(110),
    )(meta, cot, att, packed, vecs, out_w, up_w, down_w)


def attend_back(first, count, expected, meta, slopes, qkv, att_grad, totals, rows_in, cols_in, earlier):
    total, wide = qkv.shape
    width = wide // 3
    per, length = rows_in.shape[1:]

    def spot_of(s, meta):
        return jnp.clip(first + s, 0, jnp.maximum(meta[N_LIVE] - 1, 0))

    def by_offset(s, meta, slopes):
        return (aligned(meta[OFF + spot_of(s, meta)]), 0)

    spots = pl.BlockSpec(
        (1, per, length),
        lambda s, meta, slopes: (meta[IMG + spot_of(s, meta)] // per, 0, 0),
    )
    anywhere = pl.BlockSpec(memory_space=pl.ANY)
    return pl.pallas_call(
        functools.partial(attend_back_kernel, first, per),
        out_shape=jax.ShapeDtypeStruct((total, wide), BF16),
        grid_spec=pltpu.PrefetchScalarGridSpec(
            num_scalar_prefetch=2,
            grid=(count,),
            in_specs=[
                pl.BlockSpec((pl.Element(WINDOW), pl.Element(wide)), by_offset),
                pl.BlockSpec((pl.Element(WINDOW), pl.Element(width)), by_offset),
                pl.BlockSpec(
                    (1, HEADS // 2, 8, WINDOW),
                    lambda s, meta, slopes: (spot_of(s, meta), 0, 0, 0),
                ),
                spots,
                spots,
            ]
            + [anywhere] * len(earlier),
            out_specs=anywhere,
            scratch_shapes=[
                pltpu.VMEM((2, WINDOW, wide), BF16),
                pltpu.VMEM((WINDOW, WINDOW), F32),
                pltpu.SemaphoreType.DMA((2,)),
            ],
        ),
        input_output_aliases={7: 0} if earlier else {},
        compiler_params=params(),
        cost_estimate=cost(expected),
    )(meta, slopes, qkv, att_grad, totals, rows_in, cols_in, *earlier)


def bwd_tile(s, meta):
    return (jnp.clip(s, 0, jnp.maximum(meta[N_BWD] - 1, 0)), 0)


def qkv_grad(meta, packed_grad, packed, vecs):
    rows, width = packed.shape
    parcel = 3 * width // 2 // BLOCKS
    tiles = (rows - WINDOW) // TILE
    return pl.pallas_call(
        qkv_grad_kernel,
        out_shape=(
            jax.ShapeDtypeStruct((BLOCKS, parcel, width), BF16),
            jax.ShapeDtypeStruct((BLOCKS, parcel, width), BF16),
            jax.ShapeDtypeStruct((8, 3 * width), F32),
        ),
        grid_spec=pltpu.PrefetchScalarGridSpec(
            num_scalar_prefetch=1,
            grid=(tiles,),
            in_specs=[
                pl.BlockSpec((TILE, 3 * width), bwd_tile),
                pl.BlockSpec((TILE, width), bwd_tile),
                whole(*vecs.shape),
            ],
            out_specs=[
                pl.BlockSpec(memory_space=pl.ANY),
                pl.BlockSpec(memory_space=pl.ANY),
                whole(8, 3 * width),
            ],
            scratch_shapes=[
                pltpu.VMEM((width, 3 * width), F32),
                pltpu.VMEM((2, BLOCKS, parcel, width), BF16),
                pltpu.SemaphoreType.DMA((2,)),
            ],
        ),
        compiler_params=params(),
        cost_estimate=cost(15),
    )(meta, packed_grad, packed, vecs)


def token_grad(
    meta, packed_grad, packed, mid_grad, vecs, weight, bias_g, vec_two, upb_g, steps, length, images
):
    rows, width = packed.shape
    tiles = (rows - WINDOW) // TILE
    return pl.pallas_call(
        token_grad_kernel,
        out_shape=(
            jax.ShapeDtypeStruct((steps, length, images, width), F32),
            jax.ShapeDtypeStruct((16, width), F32),
        ),
        grid_spec=pltpu.PrefetchScalarGridSpec(
            num_scalar_prefetch=1,
            grid=(tiles + steps,),
            in_specs=[
                pl.BlockSpec((TILE, 3 * width), bwd_tile),
                pl.BlockSpec((TILE, width), bwd_tile),
                pl.BlockSpec((TILE, width), bwd_tile),
                whole(*vecs.shape),
                whole(width, 3 * width),
                whole(*bias_g.shape),
                whole(*vec_two.shape),
                whole(*upb_g.shape),
            ],
            out_specs=[
                pl.BlockSpec(
                    (1, length, images, width),
                    lambda s, meta: (jnp.clip(s - tiles, 0, steps - 1), 0, 0, 0),
                ),
                whole(16, width),
            ],
            scratch_shapes=[pltpu.VMEM((rows, width), F32)],
        ),
        compiler_params=params(),
        cost_estimate=cost(20),
    )(meta, packed_grad, packed, mid_grad, vecs, weight, bias_g, vec_two, upb_g)


def cost(microseconds):
    return pl.CostEstimate(
        flops=int(microseconds * 1e9), bytes_accessed=int(microseconds * 1e5), transcendentals=0
    )


def add_kernel(a, b, out):
    out[...] = (a[...].astype(F32) + b[...].astype(F32)).astype(BF16)


def added_parcels(a, b):
    block = pl.BlockSpec((1,) + a.shape[1:], lambda n: (n, 0, 0))
    return pl.pallas_call(
        add_kernel,
        out_shape=jax.ShapeDtypeStruct(a.shape, BF16),
        grid=a.shape[:1],
        in_specs=[block, block],
        out_specs=block,
        compiler_params=params(),
        cost_estimate=cost(5),
    )(a, b)


def swap(block, axis, bit):
    size = lax.axis_size(axis)
    return lax.ppermute(block, axis, [(n, n ^ bit) for n in range(size)])


def bit_of(axis, bit):
    return lax.axis_index(axis) // bit % 2


def added(a, b):
    return (a.astype(F32) + b.astype(F32)).astype(BF16)


def unpacked(mine, other, shapes):
    swapped = bit_of("bal", 1) == 1
    first = jnp.where(swapped, other, mine)
    second = jnp.where(swapped, mine, other)
    lead, width = mine.shape[:-2], mine.shape[-1]
    out, at = [], 0
    for rows, columns, kind in shapes:
        wide = columns // width
        part = rows * wide // 2
        held = [half[..., at : at + part, :] for half in (first, second)]
        if kind == "rows":
            size = rows // 2
            parts = [
                jnp.concatenate(
                    [half[..., c * size : (c + 1) * size, :] for c in range(wide)], axis=-1
                )
                for half in held
            ]
            out.append(jnp.concatenate(parts, axis=-2))
        elif kind == "columns":
            parts = [
                half[..., c * rows : (c + 1) * rows, :] for half in held for c in range(wide // 2)
            ]
            out.append(jnp.concatenate(parts, axis=-1))
        else:
            size = width // 2
            tops = [half[..., :size] for half in held]
            bottoms = [half[..., size:] for half in held]
            out.append(
                jnp.concatenate(
                    [jnp.concatenate(tops, axis=-1), jnp.concatenate(bottoms, axis=-1)], axis=-2
                )
            )
        at += part
    return [matrix.reshape(lead[:-1] + (-1, matrix.shape[-1])) if lead else matrix for matrix in out]


def spread_sum(keep, send, shapes):
    return [
        lax.psum(lax.psum_scatter(matrix, "dp", scatter_dimension=0, tiled=True), "bal").astype(F32)
        for matrix in unpacked(keep, send, shapes)
    ]


def start_fold(block, bit):
    block = block.reshape((-1, 2) + block.shape[-2:])
    mine = bit_of("dp", bit)
    keep = lax.dynamic_index_in_dim(block, mine, 1, keepdims=False)
    send = lax.dynamic_index_in_dim(block, 1 - mine, 1, keepdims=False)
    return keep, swap(send, "dp", bit)


def after(value, *others):
    return lax.optimization_barrier((value,) + others)[0]


def doubled(block, round_no):
    bits = [("bal", 1), ("bal", 2)]
    bit = 1
    while bit < lax.axis_size("dp"):
        bits.append(("dp", bit))
        bit *= 2
    if round_no is None:
        return len(bits)
    axis, bit = bits[round_no]
    return block + swap(block, axis, bit)


def per_device(
    tokens,
    cotangent,
    counts,
    rows,
    cols,
    present,
    slots,
    first_gain,
    first_shift,
    qkv_weight,
    query_bias,
    value_bias,
    out_weight,
    out_bias,
    second_gain,
    second_shift,
    up_weight,
    up_bias,
    down_weight,
    down_bias,
):
    steps, images, length, width = tokens.shape
    hidden = up_weight.shape[1]
    group = lax.axis_size("bal")
    total = steps * images
    slopes = jnp.exp2(-8.0 * (jnp.arange(16, dtype=F32) + 1.0) / HEADS)

    def exchange(blocks):
        flat = blocks.reshape(group, -1, width)
        return lax.all_to_all(flat, "bal", split_axis=0, concat_axis=0, tiled=True)

    def turn(array):
        return jnp.transpose(array, (0, 2, 1, 3))

    meta, take, vecs, cot_send = prepare(
        [
            lax.ppermute(slots, "bal", [(a, (a + k) % group) for a in range(group)])
            for k in range(1, group)
        ],
        counts, present, slots,
        lax.axis_index("bal").astype(jnp.int32).reshape(1), turn(cotangent),
        first_gain, first_shift, query_bias, value_bias, out_bias, second_gain, second_shift,
        down_bias, up_bias,
    )
    cot_home = exchange(cot_send).reshape(group, steps, -1, width)
    packed, qkv, att, totals = first_half(meta, slopes, turn(tokens), rows, cols, vecs, qkv_weight)
    y_send, mid_grad, att_grad, keep_two, send_two, vec_two, upb_g = mlp(
        meta, cot_home, att, packed, vecs, out_weight, up_weight, down_weight, length
    )
    share, long = width // BLOCKS, hidden // BLOCKS
    shapes_two = ((share, hidden, "columns"), (long, width, "side"), (share, width, "rows"))
    shapes_one = ((share, 3 * width, "rows"),)
    direct = lax.axis_size("dp") == BLOCKS

    def back(first, count, expected, table, earlier):
        return attend_back(
            first, count, expected, table, slopes, qkv, att_grad, totals, rows, cols, earlier
        )

    lead = max(images // 2, 1)
    packed_grad = back(0, lead, 15, meta, ())
    table = meta
    if direct:
        sum_two = added_parcels(after(keep_two, packed_grad), swap(send_two, "bal", 1))
        share_two = lax.psum_scatter(sum_two, "dp", scatter_dimension=0, tiled=True)[0]
        table = after(meta, sum_two)
        y_send = after(y_send, sum_two)
    y_got = exchange(y_send)
    packed_grad = back(lead, total - lead, 500, table, (packed_grad,))
    keep_one, send_one, bias_g = qkv_grad(table, packed_grad, packed, vecs)
    output = place(after(take, keep_one), y_got.reshape(group, steps, -1, width), length)
    table = after(table, output)
    if direct:
        sum_one = added(keep_one, swap(send_one, "bal", 1))
        keep_y, crossing_y = start_fold(sum_one, 1)
        table = after(table, sum_one)
    input_grad, vectors = token_grad(
        table, packed_grad, packed, mid_grad, vecs, qkv_weight, bias_g, vec_two, upb_g,
        steps, length, images,
    )
    rounds = doubled(vectors, None)
    if direct:
        half_one = added(after(keep_y, vectors), crossing_y)
        keep, crossing = start_fold(half_one, 2)
        for n in range(rounds - 2):
            vectors = doubled(vectors, n)
        block = added(after(keep, vectors), crossing)
        keep, crossing = start_fold(block, 4)
        across_two = swap(share_two, "bal", 2)
        vectors = doubled(after(vectors, block, share_two), rounds - 2)
        block = added(after(keep, vectors), crossing).reshape(sum_one.shape[-2:])
        across_one = swap(block, "bal", 2)
        vectors = doubled(after(vectors, block), rounds - 1)
        full_one = added(after(block, vectors), across_one)
        full_two = added(after(share_two, full_one), across_two)
        (qkv_rows,) = [
            matrix.astype(F32)
            for matrix in unpacked(full_one, swap(full_one, "bal", 1), shapes_one)
        ]
        up_rows, down_rows, out_rows = [
            matrix.astype(F32)
            for matrix in unpacked(full_two, swap(full_two, "bal", 1), shapes_two)
        ]
    else:
        (qkv_rows,) = spread_sum(keep_one, send_one, shapes_one)
        up_rows, down_rows, out_rows = spread_sum(keep_two, send_two, shapes_two)
        for n in range(rounds):
            vectors = doubled(vectors, n)

    def vector(n):
        return vectors[n]

    return (
        turn(output),
        turn(input_grad),
        vector(0),
        vector(1),
        qkv_rows,
        vector(2),
        vector(3),
        out_rows,
        vector(6),
        vector(4),
        vector(5),
        up_rows,
        vectors[8 : 8 + hidden // width].reshape(-1),
        down_rows,
        vector(7),
    )


def solution(mesh):
    images = P(None, ("dp", "bal"), None, None)
    spots = P(None, ("dp", "bal"), None)
    flags = P(None, ("dp", "bal"))
    matrix = P("dp", None)
    return jax.shard_map(
        per_device,
        mesh=mesh,
        in_specs=(images, images, flags, spots, spots, flags, flags) + (P(),) * 13,
        out_specs=(
            images, images, P(), P(), matrix, P(), P(), matrix, P(), P(), P(), matrix, P(), matrix, P(),
        ),
        check_vma=False,
    )
```
